32 devices in a mesh: fsdp: 4 (over y, x), ctx: 2 (over core), tp: 4 (over z).
Axes of the slice: x: 2, y: 2, z: 4, core: 2. Of those that a mesh axis runs over, the one named last changes fastest.
Arguments:
- inputs: float32 [2048, 2048], P(('fsdp', 'ctx')), may hold values from -6 to 6
- cotangent: float32 [2048, 2048], P(('fsdp', 'ctx')), may hold values from -6 to 6
- seq_lengths: int32 [4, 4], P('fsdp'), may hold values from 0 to 512, as said below
- slots: int32 [2048], P(('fsdp', 'ctx')), may hold values from 0 to 2047, as said below
- gain_in: float32 [2048], replicated, may hold values from 0.5 to 1.5
- w_z: float32 [2048, 4096], P(('fsdp', 'ctx'), 'tp'), may hold values from -0.125 to 0.125
- w_x: float32 [2048, 4096], P(('fsdp', 'ctx'), 'tp'), may hold values from -0.125 to 0.125
- w_dt: float32 [2048, 64], P(('fsdp', 'ctx'), 'tp'), may hold values from -0.125 to 0.125
- w_bc: float32 [2048, 256], P(('fsdp', 'ctx')), may hold values from -0.125 to 0.125
- w_out: float32 [2048, 4096], P(('fsdp', 'ctx'), 'tp'), may hold values from -0.09375 to 0.09375
- conv_x: float32 [4, 4096], P(None, 'tp'), may hold values from -3 to 3
- conv_x_bias: float32 [4096], P('tp'), may hold values from -3 to 3
- conv_bc: float32 [4, 256], replicated, may hold values from -3 to 3
- conv_bc_bias: float32 [256], replicated, may hold values from -3 to 3
- dt_bias: float32 [64], P('tp'), may hold values from -8 to -3
- a_log: float32 [64], P('tp'), may hold values from 0 to 2.5
- d_skip: float32 [64], P('tp'), may hold values from 0.5 to 1.5
- gate_gain: float32 [4096], P('tp'), may hold values from 0.5 to 1.5
Outputs:
- result: float32 [2048, 2048], P(('fsdp', 'ctx'), 'tp')
- grad_input: float32 [2048, 2048], P(('fsdp', 'ctx'), 'tp')
- grad_w_z: float32 [2048, 4096], P(('fsdp', 'ctx'), 'tp')
- grad_w_x: float32 [2048, 4096], P(('fsdp', 'ctx'), 'tp')
- grad_w_dt: float32 [2048, 64], P(('fsdp', 'ctx'), 'tp')
- grad_w_bc: float32 [2048, 256], P(('fsdp', 'ctx'))
- grad_w_out: float32 [2048, 4096], P(('fsdp', 'ctx'), 'tp')
- grad_conv_x: float32 [4, 4096], P(None, 'tp')
- grad_conv_x_bias: float32 [4096], P('tp')
- grad_conv_bc: float32 [4, 256], replicated
- grad_conv_bc_bias: float32 [256], replicated
- grad_dt_bias: float32 [64], P('tp')
- grad_a_log: float32 [64], P('tp')
- grad_d_skip: float32 [64], P('tp')
- grad_gate_gain: float32 [4096], P('tp')
- grad_gain_in: float32 [2048], P('tp')
The draws below stay inside these ranges and needn't reach their ends.
Inputs may be any that keep to these rules, and one draw needn't show every extreme that they name: `seq_lengths`: the lengths of each row sum to 512; a length of zero is an empty slot; in every row one sequence covers positions 255 and 256. The slots are a permutation. The 256 tokens of arrival positions i * 256 to (i + 1) * 256 - 1 go to all 8 half rows (slot // 256), exactly 32 to each, so every half row receives exactly 32 tokens from each such block.
All inputs are finite; a program needn't handle non-finite values.
Results may differ from the reference program's by a relative error of at most 0.0003.
Values sent between devices are 32-bit elements; how exact they have to be, the bound alone decides.
A program may use at most 192 MiB of HBM per device.

```python
import jax
import jax.numpy as jnp
from jax import lax

D = 2048
H = 64
N = 128
CONV = 4
SPAN = 256
TOK_DEV = 256
INNER = 4096
ROWS = 4
ROW_LEN = 512
TOKENS = 2048
N_FSDP = 4
N_CTX = 2


def draw_seq_lengths(key, part):
    key = jax.random.fold_in(key, 11)
    row_len = TOK_DEV * N_CTX
    subkeys = jax.random.split(key, 4)
    starts = jax.random.randint(subkeys[0], (N_FSDP,), 0, TOK_DEV - TOK_DEV // 4 + 1)
    stops = jax.random.randint(subkeys[1], (N_FSDP,), TOK_DEV + TOK_DEV // 4, row_len + 1)
    whole_row = jax.random.randint(subkeys[2], (), 0, N_FSDP)
    is_whole = jnp.arange(N_FSDP) == whole_row
    starts = jnp.where(is_whole, 0, starts)
    stops = jnp.where(is_whole, row_len, stops)
    front_raw = jax.random.randint(subkeys[3], (N_FSDP, 1), 0, row_len + 1)
    front_cuts = jnp.remainder(front_raw, starts[:, None] + 1)
    zero_col = jnp.zeros((N_FSDP, 1), jnp.int32)
    front_edges = jnp.concatenate([zero_col, front_cuts, starts[:, None]], axis=1)
    front_len = front_edges[:, 1:] - front_edges[:, :-1]
    middle = (stops - starts)[:, None]
    back_len = (row_len - stops)[:, None]
    return jnp.concatenate([front_len, middle, back_len], axis=1).astype(jnp.int32)


def draw_slots(key, part):
    key = jax.random.fold_in(key, 23)
    groups = N_FSDP * N_CTX
    spread = groups
    per_pair = TOK_DEV // spread
    subkeys = jax.random.split(key, 3)
    offsets = jax.random.permutation(subkeys[0], groups)[:spread]
    source_order = jax.vmap(lambda sub: jax.random.permutation(sub, TOK_DEV))(jax.random.split(subkeys[1], groups))
    target_order = jax.vmap(lambda sub: jax.random.permutation(sub, TOK_DEV))(jax.random.split(subkeys[2], groups))
    sources = jnp.arange(groups)[:, None]
    blocks_of = source_order // per_pair
    targets = jnp.remainder(sources + offsets[blocks_of], groups)
    places = target_order[targets, source_order]
    return (targets * TOK_DEV + places).reshape(-1).astype(jnp.int32)


def level_of(stream_key, dims, shards, least, high):
    factor_of = 1.0
    for dim, blocks in shards:
        draws = jax.random.uniform(jax.random.fold_in(jax.random.fold_in(stream_key, 6), dim), (blocks,), jnp.float32, least / len(shards), high / len(shards))
        factor_of = factor_of * jnp.repeat(jnp.exp(draws), dims[dim] // blocks).reshape((-1,) + (1,) * (len(dims) - 1 - dim))
    return factor_of


def bell_draw(key, dims, scale, most, cuts=(), kind=jnp.bfloat16):
    values = jax.random.normal(key, dims, jnp.float32) * scale
    if len(cuts) > 0:
        values = level_of(key, dims, cuts, -0.22, 0.18) * values
    return jnp.clip(values, min=-most, max=most).astype(kind)


def setup_inputs(seed: int = 0) -> dict:
    arg_keys = jax.random.split(jax.random.key(seed), 19)
    inputs = bell_draw(arg_keys[0], (TOKENS, D), 1.0, 6.0, ((0, 8),), jnp.float32)
    cotangent = bell_draw(arg_keys[1], (TOKENS, D), 1.0, 6.0, ((0, 8),), jnp.float32)
    seq_lengths = draw_seq_lengths(jax.random.fold_in(arg_keys[18], 71), 0)
    slots = draw_slots(jax.random.fold_in(arg_keys[18], 71), 0)
    gain_in = jnp.clip(1.0 + 0.1 * jax.random.normal(arg_keys[4], (D,), jnp.float32), 0.5, 1.5)
    w_z = bell_draw(arg_keys[5], (D, INNER), D ** -0.5, 0.125, ((0, 8), (1, 4)), jnp.float32)
    w_x = bell_draw(arg_keys[6], (D, INNER), D ** -0.5, 0.125, ((0, 8), (1, 4)), jnp.float32)
    w_dt = bell_draw(arg_keys[7], (D, H), D ** -0.5, 0.125, ((0, 8), (1, 4)), jnp.float32)
    w_bc = bell_draw(arg_keys[8], (D, 2 * N), D ** -0.5, 0.125, ((0, 8),), jnp.float32)
    w_out = bell_draw(arg_keys[9], (D, INNER), INNER ** -0.5, 0.09375, ((0, 8), (1, 4)), jnp.float32)
    conv_x = bell_draw(arg_keys[10], (CONV, INNER), CONV ** -0.5, 3.0, ((1, 4),), jnp.float32)
    conv_x_bias = bell_draw(arg_keys[11], (INNER,), 0.5, 3.0, ((0, 4),), jnp.float32)
    conv_bc = bell_draw(arg_keys[12], (CONV, 2 * N), CONV ** -0.5, 3.0, (), jnp.float32)
    conv_bc_bias = bell_draw(arg_keys[13], (2 * N,), 0.5, 3.0, (), jnp.float32)
    dt_bias = jnp.clip(-8.0 + 5.0 * jax.random.uniform(arg_keys[14], (H,), jnp.float32) ** level_of(arg_keys[14], (H,), ((0, 4),), -0.2, 0.2), -8.0, -3.0)
    a_log = jnp.clip(2.5 * jax.random.uniform(arg_keys[15], (H,), jnp.float32) ** level_of(arg_keys[15], (H,), ((0, 4),), -0.2, 0.2), 0.0, 2.5)
    d_skip = jnp.clip(0.5 + 1.0 * jax.random.uniform(arg_keys[16], (H,), jnp.float32) ** level_of(arg_keys[16], (H,), ((0, 4),), -0.2, 0.2), 0.5, 1.5)
    gate_gain = jnp.clip(1.0 + 0.1 * jax.random.normal(arg_keys[17], (INNER,), jnp.float32), 0.5, 1.5)
    return dict(inputs=inputs, cotangent=cotangent, seq_lengths=seq_lengths, slots=slots, gain_in=gain_in, w_z=w_z, w_x=w_x, w_dt=w_dt, w_bc=w_bc, w_out=w_out, conv_x=conv_x, conv_x_bias=conv_x_bias, conv_bc=conv_bc, conv_bc_bias=conv_bc_bias, dt_bias=dt_bias, a_log=a_log, d_skip=d_skip, gate_gain=gate_gain)


HIGH = lax.Precision.HIGHEST
EPSILON = 1e-05

@jax.custom_vjp
def low(v):
    return lax.optimization_barrier(v.astype(jnp.bfloat16)).astype(jnp.float32)

@jax.custom_vjp
def low_back(v):
    return v

def low_keep(v):
    return (low(v), None)

def low_pass(kept, grad):
    return (grad,)

def back_keep(v):
    return (v, None)

def back_low(kept, grad):
    return (low(grad),)
low.defvjp(low_keep, low_pass)
low_back.defvjp(back_keep, back_low)

def matmul(left, right):
    return jnp.dot(left, right, precision=HIGH)

def matmul_nt(left, right):
    return lax.dot_general(left, right, (((1,), (1,)), ((), ())), precision=HIGH)

def silu_f(value):
    return value * jax.nn.sigmoid(value)

def segment_of(positions, lengths):
    bounds = jnp.cumsum(lengths.astype(jnp.int32)).astype(jnp.int32)
    hits = (bounds[None, :] <= positions.astype(jnp.int32)[:, None]).astype(jnp.int32)
    return lax.optimization_barrier(jnp.sum(hits, axis=1)).astype(jnp.int32)

def norm_in(tokens, gain):
    scale = lax.rsqrt(lax.optimization_barrier(jnp.mean(tokens * tokens, axis=1, keepdims=True)) + EPSILON)
    return tokens * scale * gain[None, :]

def conv_act(pre, tail, taps, bias, raw_dt, dt_bias, a_log, segs, tail_segs, n_inner, n_state):
    extended = jnp.concatenate([tail, pre], axis=0)
    ext_segs = jnp.concatenate([tail_segs, segs]).astype(jnp.int32)
    length = pre.shape[0]
    summed = jnp.zeros_like(pre) + bias[None, :]
    for offset_k in range(taps.shape[0]):
        moved = lax.slice_in_dim(extended, offset_k, offset_k + length, axis=0)
        same_doc = (lax.slice_in_dim(ext_segs, offset_k, offset_k + length, axis=0) == segs).astype(jnp.float32)
        summed = summed + taps[offset_k][None, :] * moved * same_doc[:, None]
    activated = silu_f(summed)
    xs = activated[:, :n_inner]
    bm = activated[:, n_inner:n_inner + n_state]
    cm = activated[:, n_inner + n_state:]
    step_size = jax.nn.softplus(raw_dt + dt_bias[None, :])
    decay_rate = -jnp.exp(a_log)
    return (xs, bm, cm, step_size, decay_rate)

def block_ssd(xs, step_size, decay_rate, bm, cm, d_skip, segs, seg_before, block_len):
    length, heads = step_size.shape
    head_width = xs.shape[1] // heads
    count = length // block_len
    x_blocks = xs.reshape(count, block_len, heads, head_width)
    log_blocks = (step_size * decay_rate[None, :]).reshape(count, block_len, heads)
    step_blocks = step_size.reshape(count, block_len, heads)
    b_blocks = bm.reshape(count, block_len, bm.shape[1])
    c_blocks = cm.reshape(count, block_len, cm.shape[1])
    seg_blocks = segs.reshape(count, block_len).astype(jnp.int32)
    seg_prev = jnp.concatenate([jnp.reshape(seg_before, (1,)).astype(jnp.int32), seg_blocks[:-1, -1]]).astype(jnp.int32)
    rows_i = lax.broadcasted_iota(jnp.int32, (block_len, block_len), 0)
    cols_j = lax.broadcasted_iota(jnp.int32, (block_len, block_len), 1)

    def one_block(state, item):
        x_block, log_block, step_block, b_block, c_block, seg_block, seg_last_prev = item
        cumulative = jnp.cumsum(log_block, axis=0).T
        causal_same = (seg_block[:, None] == seg_block[None, :]) & (rows_i >= cols_j)
        gaps = cumulative[:, :, None] - cumulative[:, None, :]
        decays = jnp.where(causal_same[None], jnp.exp(jnp.where(causal_same[None], gaps, 0.0)), 0.0)
        scores = matmul_nt(c_block, b_block)
        weights = decays * scores[None] * step_block.T[:, None, :]
        mixed_out = jnp.einsum('hij,jhp->ihp', weights, x_block, precision=HIGH)
        keep_in = (seg_block == seg_last_prev).astype(jnp.float32)
        reading = jnp.exp(cumulative).T * keep_in[:, None]
        mixed_out = mixed_out + reading[:, :, None] * jnp.einsum('in,hpn->ihp', c_block, state, precision=HIGH)
        last_seg = seg_block[-1]
        tail_w = jnp.exp(cumulative[:, -1:] - cumulative).T * (seg_block == last_seg).astype(jnp.float32)[:, None] * step_block
        carried = (jnp.exp(cumulative[:, -1]) * (last_seg == seg_last_prev).astype(jnp.float32))[:, None, None] * state
        carried = carried + jnp.einsum('jh,jhp,jn->hpn', tail_w, x_block, b_block, precision=HIGH)
        mixed_out = mixed_out + d_skip[None, :, None] * x_block
        return (carried, mixed_out.reshape(block_len, heads * head_width))
    start_state = jnp.zeros((heads, head_width, bm.shape[1]), jnp.float32)
    end_state, outs = lax.scan(jax.checkpoint(one_block), start_state, (x_blocks, log_blocks, step_blocks, b_blocks, c_blocks, seg_blocks, seg_prev))
    return (outs.reshape(length, heads * head_width), end_state)

def layer_row(u_row, lengths, gain_in, w_z, w_x, w_dt, w_bc, w_out, conv_x, conv_x_bias, conv_bc, conv_bc_bias, dt_bias, a_log, d_skip, gate_gain):
    positions = jnp.arange(u_row.shape[0], dtype=jnp.int32)
    segs = segment_of(positions, lengths)
    normed = norm_in(u_row, gain_in)
    gate_pre = matmul(normed, w_z)
    pre = jnp.concatenate([matmul(normed, w_x), matmul(normed, w_bc)], axis=1)
    raw_dt = matmul(normed, w_dt)
    width = conv_x.shape[0]
    tail = jnp.zeros((width - 1, pre.shape[1]), jnp.float32)
    tail_segs = jnp.full((width - 1,), -1, jnp.int32)
    taps = jnp.concatenate([conv_x, conv_bc], axis=1)
    bias = jnp.concatenate([conv_x_bias, conv_bc_bias])
    xs, bm, cm, step_size, decay_rate = conv_act(pre, tail, taps, bias, raw_dt, dt_bias, a_log, segs, tail_segs, INNER, N)
    mixed, end_state = block_ssd(xs, step_size, decay_rate, bm, cm, d_skip, segs, jnp.int32(-1), SPAN)
    gated = mixed * silu_f(gate_pre)
    gscale = lax.rsqrt(lax.optimization_barrier(jnp.mean(gated * gated, axis=1)) + EPSILON)
    normal_y = gated * gscale[:, None] * gate_gain[None, :]
    return u_row + matmul_nt(normal_y, w_out)

def reference(inputs, cotangent, seq_lengths, slots, gain_in, w_z, w_x, w_dt, w_bc, w_out, conv_x, conv_x_bias, conv_bc, conv_bc_bias, dt_bias, a_log, d_skip, gate_gain):
    tokens_all = inputs.shape[0]
    inverse = jnp.zeros((tokens_all,), jnp.int32).at[slots].set(jnp.arange(tokens_all, dtype=jnp.int32))

    def forward(inputs, gain_in, w_z, w_x, w_dt, w_bc, w_out, conv_x, conv_x_bias, conv_bc, conv_bc_bias, dt_bias, a_log, d_skip, gate_gain):
        packed = inputs[inverse].reshape(ROWS, ROW_LEN, D)

        def one_row(carried, item):
            u_row, lengths = item
            row_out = layer_row(u_row, lengths, gain_in, w_z, w_x, w_dt, w_bc, w_out, conv_x, conv_x_bias, conv_bc, conv_bc_bias, dt_bias, a_log, d_skip, gate_gain)
            return (carried, row_out)
        unused, rows_out = lax.scan(jax.checkpoint(one_row), jnp.float32(0.0), (packed, seq_lengths))
        return rows_out.reshape(tokens_all, D)[slots]
    result, pullback = jax.vjp(forward, inputs, gain_in, w_z, w_x, w_dt, w_bc, w_out, conv_x, conv_x_bias, conv_bc, conv_bc_bias, dt_bias, a_log, d_skip, gate_gain)
    grads = pullback(cotangent)
    return (result, grads[0], grads[2], grads[3], grads[4], grads[5], grads[6], grads[7], grads[8], grads[9], grads[10], grads[11], grads[12], grads[13], grads[14], grads[1])
```

```python
import functools
import math

import jax
import jax.numpy as jnp
from jax import lax
from jax.experimental import pallas as pl
from jax.experimental.pallas import tpu as pltpu
from jax.sharding import PartitionSpec as P

N = 128
SPAN = 256
INNER = 4096
EPSILON = 1e-05
F32 = jnp.float32
BF16 = jnp.bfloat16
MESH = pl.DeviceIdType.MESH
NN = (((1,), (0,)), ((), ()))
NT = (((1,), (1,)), ((), ()))
TN = (((0,), (0,)), ((), ()))
VMEM_LIMIT = 62 << 20


def split2(value):
    high = value.astype(BF16)
    return high, (value - high.astype(F32)).astype(BF16)


def split3(value):
    high = value.astype(BF16)
    rest = value - high.astype(F32)
    middle = rest.astype(BF16)
    return high, middle, (rest - middle.astype(F32)).astype(BF16)


def dot1(left, right, dims):
    return lax.dot_general(left, right, dims, preferred_element_type=F32)


def dot_split(left, right, dims):
    (lh, ll), (rh, rl) = left, right
    return dot1(lh, rh, dims) + (dot1(lh, rl, dims) + dot1(ll, rh, dims))


def dot3(left, right, dims):
    return dot_split(split2(left), split2(right), dims)


def pick(table, value, dims):
    parts = split3(value)
    return dot1(table, parts[0], dims) + dot1(table, parts[1], dims) + dot1(table, parts[2], dims)


def iota(shape, dim):
    return lax.broadcasted_iota(jnp.int32, shape, dim)


class Place:
    def __init__(self, fsdp, ctx, tp):
        self.fsdp, self.n_ctx, self.tp = fsdp, ctx, tp
        self.side = math.isqrt(fsdp)
        assert self.side * self.side == fsdp and ctx == 2
        self.f = lax.axis_index("fsdp")
        self.c = lax.axis_index("ctx")
        self.z = lax.axis_index("tp")
        self.y, self.x = self.f // self.side, self.f % self.side

    def chip(self, dy, dx):
        side = self.side
        return ((self.y + dy + side) % side) * side + (self.x + dx + side) % side

    def block(self, dy, dx, core):
        return self.chip(dy, dx) * 2 + core

    def at(self, dy, dx):
        return (self.chip(dy, dx), self.c, self.z)

    def sibling(self):
        return (self.f, 1 - self.c, self.z)

    def plane(self):
        out = []
        for df in range(self.fsdp):
            for dc in range(2):
                if df or dc:
                    to_f = (self.f + df) % self.fsdp
                    from_f = (self.f - df + self.fsdp) % self.fsdp
                    core = (self.c + dc) % 2
                    out.append(((to_f, core, self.z), to_f * 2 + core, from_f * 2 + core))
        return out

    def column(self):
        out = []
        for dz in range(1, self.tp):
            to_z = (self.z + dz) % self.tp
            out.append(((self.f, self.c, to_z), to_z, (self.z - dz + self.tp) % self.tp))
        return out


class Links:
    def __init__(self, send, recv, local):
        self.send, self.recv, self.local = send, recv, local
        self.used, self.used_local = 0, 0
        self.open = []

    def remote(self, src, dst, device):
        k = self.used
        self.used += 1
        copy = pltpu.make_async_remote_copy(
            src_ref=src,
            dst_ref=dst,
            send_sem=self.send.at[k],
            recv_sem=self.recv.at[k],
            device_id=device,
            device_id_type=MESH,
        )
        copy.start()
        self.open.append(copy)
        return copy

    def move(self, src, dst):
        k = self.used_local
        self.used_local += 1
        copy = pltpu.make_async_copy(src, dst, self.local.at[k])
        copy.start()
        return copy

    def finish(self):
        for copy in self.open:
            copy.wait_send()


def greet(devices):
    barrier = pltpu.get_barrier_semaphore()
    for device in devices:
        pl.semaphore_signal(barrier, inc=1, device_id=device, device_id_type=MESH)
    pl.semaphore_wait(barrier, len(devices))


class Gather:
    def __init__(self, place, links, shard, whole):
        self.place, self.links, self.shard, self.whole = place, links, shard, whole
        self.rows = shard.shape[0]

    def rows_of(self, block, start=0, count=None):
        count = self.rows if count is None else count
        return self.whole.at[pl.ds(pl.multiple_of(block * self.rows + start, 8), count)]

    def start(self):
        p, steps = self.place, range(1, self.place.side)
        mine = self.rows_of(p.block(0, 0, p.c))
        self.row = [self.links.remote(self.shard, mine, p.at(0, d)) for d in steps]
        self.col = [self.links.remote(self.shard, mine, p.at(d, 0)) for d in steps]
        self.pair = [self.links.remote(self.shard, mine, p.sibling())]
        self.own = self.links.move(self.shard, mine)

    def forward(self):
        p, steps, half = self.place, range(1, self.place.side), self.rows // 2
        self.half_a, self.half_b = [], []
        for k, d in enumerate(steps):
            self.row[k].wait_recv()
            block = p.block(0, -d, p.c)
            part = self.rows_of(block, 0, half)
            self.half_a += [self.links.remote(part, part, p.at(e, 0)) for e in steps]
            whole = self.rows_of(block)
            self.pair.append(self.links.remote(whole, whole, p.sibling()))
        for k, e in enumerate(steps):
            self.col[k].wait_recv()
            block = p.block(-e, 0, p.c)
            part = self.rows_of(block, half, half)
            self.half_b += [self.links.remote(part, part, p.at(0, d)) for d in steps]
            whole = self.rows_of(block)
            self.pair.append(self.links.remote(whole, whole, p.sibling()))

    def share(self):
        p, steps, half = self.place, range(1, self.place.side), self.rows // 2
        k = 0
        for d in steps:
            for e in steps:
                self.half_a[k].wait_recv()
                part = self.rows_of(p.block(-e, -d, p.c), 0, half)
                self.pair.append(self.links.remote(part, part, p.sibling()))
                k += 1
        k = 0
        for e in steps:
            for d in steps:
                self.half_b[k].wait_recv()
                part = self.rows_of(p.block(-e, -d, p.c), half, half)
                self.pair.append(self.links.remote(part, part, p.sibling()))
                k += 1

    def finish(self):
        self.own.wait()
        for copy in self.pair:
            copy.wait_recv()


def gather_copies(side):
    steps = side - 1
    return 4 * steps + 1 + 4 * steps * steps


def project(left_high, left_low, whole, out, tile):
    slices, _, width = left_high.shape

    @pl.loop(0, whole.shape[1] // tile)
    def _(n):
        cols = pl.ds(pl.multiple_of(n * tile, 128), tile)
        total = jnp.zeros((left_high.shape[1], tile), F32)
        for k in range(slices):
            right = split2(whole[k * width : (k + 1) * width, cols])
            total = total + dot_split((left_high[k], left_low[k]), right, NN)
        out[:, cols] = total


def forward_kernel(
    sizes,
    slots_in,
    gain,
    x_in,
    c_in,
    w_x,
    w_s,
    w_z,
    w_out,
    tokens_out,
    upstream_out,
    p_recv,
    pre_x,
    pre_s,
    gate_pre,
    d_normal,
    wx_out,
    ws_out,
    wz_out,
    wo_out,
    wx,
    ws,
    wz,
    wo,
    x_own,
    c_own,
    x_sort,
    c_sort,
    p_sort,
    x_recv,
    c_recv,
    tokens,
    upstream,
    n_high,
    n_low,
    send,
    recv,
    local,
):
    place = Place(*sizes)
    links = Links(send, recv, local)
    tok, groups = x_own.shape[0], 2 * place.fsdp
    per_pair = tok // groups
    slice_width = x_own.shape[1]
    slice_cols = pl.ds(pl.multiple_of(place.z * slice_width, 128), slice_width)
    load_x = links.move(x_in.at[:, slice_cols], x_own)
    load_c = links.move(c_in.at[:, slice_cols], c_own)
    plane, column = place.plane(), place.column()
    greet([entry[0] for entry in plane] + [entry[0] for entry in column])

    gathers = [Gather(place, links, shard, whole) for shard, whole in ((w_x, wx), (w_s, ws), (w_z, wz), (w_out, wo))]
    g_x, g_s, g_z, g_o = gathers
    g_x.start()
    g_s.start()

    slots = slots_in[...]
    targets = slots >> (tok.bit_length() - 1)
    member = (targets == iota((tok, 128), 1)).astype(F32)
    earlier = (iota((tok, tok), 0) > iota((tok, tok), 1)).astype(BF16)
    ranks = jnp.sum(dot1(earlier, member.astype(BF16), NN) * member, axis=1, keepdims=True)
    send_at = (targets[:, :1] * per_pair).astype(F32) + ranks
    leave = (send_at == iota((tok, tok), 1).astype(F32)).astype(BF16)
    place_of = (slots - targets * tok).astype(F32).astype(BF16)
    p_sort[...] = dot1(leave, place_of, TN)
    load_x.wait()
    x_sort[...] = pick(leave, x_own[...], TN)

    def rows(group):
        return pl.ds(pl.multiple_of(group * per_pair, 8), per_pair)

    def route(source, target):
        mine = rows(place.f * 2 + place.c)
        copies = [links.remote(source.at[rows(to)], target.at[mine], device) for device, to, _ in plane]
        return copies, links.move(source.at[mine], target.at[mine])

    routes_x = [route(p_sort, p_recv), route(x_sort, x_recv.at[place.z])]
    load_c.wait()
    c_sort[...] = pick(leave, c_own[...], TN)
    routes_c = [route(c_sort, c_recv.at[place.z])]
    g_z.start()

    def arrive(routes):
        for copies, own in routes:
            own.wait()
            for copy in copies:
                copy.wait_recv()

    def spread(received):
        mine = received.at[place.z]
        return [links.remote(mine, mine, device) for device, _, _ in column]

    arrive(routes_x)
    spread_x = spread(x_recv)
    g_x.forward()
    g_s.forward()
    g_o.start()
    arrive(routes_c)
    spread_c = spread(c_recv)
    g_x.share()
    g_s.share()

    for copy in spread_x:
        copy.wait_recv()
    settle = (p_recv[:, :1] == iota((tok, tok), 1).astype(F32)).astype(BF16)
    squares = jnp.zeros((tok, 1), F32)
    for k in range(place.tp):
        value = pick(settle, x_recv[k], TN)
        tokens[k] = value
        squares = squares + jnp.sum(value * value, axis=1, keepdims=True)
    scale = lax.rsqrt(squares / (place.tp * slice_width) + EPSILON)
    for k in range(place.tp):
        high, low = split2(tokens[k] * scale * gain[:, k * slice_width : (k + 1) * slice_width])
        n_high[k] = high
        n_low[k] = low
    stores = []
    for k in range(place.tp):
        stores.append(links.move(tokens.at[k], tokens_out.at[:, k * slice_width : (k + 1) * slice_width]))

    g_z.forward()
    g_x.finish()
    g_s.finish()
    stores += [links.move(wx, wx_out), links.move(ws, ws_out)]
    project(n_high, n_low, wx, pre_x, 256)
    project(n_high, n_low, ws, pre_s, 128)
    g_z.share()
    g_o.forward()
    g_z.finish()
    stores += [links.move(wz, wz_out)]
    project(n_high, n_low, wz, gate_pre, 256)

    for copy in spread_c:
        copy.wait_recv()
    for k in range(place.tp):
        upstream[k] = pick(settle, c_recv[k], TN)
        stores.append(links.move(upstream.at[k], upstream_out.at[:, k * slice_width : (k + 1) * slice_width]))
    for k in range(place.tp):
        high, low = split2(upstream[k])
        n_high[k] = high
        n_low[k] = low
    g_o.share()
    g_o.finish()
    stores += [links.move(wo, wo_out)]
    project(n_high, n_low, wo, d_normal, 256)
    for store in stores:
        store.wait()
    links.finish()


def forward_call(sizes, slots, gain_in, inputs, cotangent, w_x, w_s, w_z, w_out):
    fsdp, _, tp = sizes
    tok, width = inputs.shape
    shard, inner = w_x.shape
    side = w_s.shape[1]
    depth = shard * 2 * fsdp
    part = width // tp
    grid_side = math.isqrt(fsdp)
    copies = 4 * gather_copies(grid_side) + 3 * (2 * fsdp - 1) + 2 * (tp - 1)
    anywhere = pl.BlockSpec(memory_space=pl.ANY)
    inside = pl.BlockSpec(memory_space=pltpu.VMEM)

    def shape(*dims):
        return jax.ShapeDtypeStruct(dims, F32)

    return pl.pallas_call(
        functools.partial(forward_kernel, sizes),
        out_shape=(
            shape(tok, width),
            shape(tok, width),
            shape(tok, 128),
            shape(tok, inner),
            shape(tok, side),
            shape(tok, inner),
            shape(tok, inner),
            shape(depth, inner),
            shape(depth, side),
            shape(depth, inner),
            shape(depth, inner),
        ),
        in_specs=[inside, inside] + [anywhere] * 6,
        out_specs=(anywhere, anywhere, inside, inside, inside, inside, inside, anywhere, anywhere, anywhere, anywhere),
        scratch_shapes=[
            pltpu.VMEM((depth, inner), F32),
            pltpu.VMEM((depth, side), F32),
            pltpu.VMEM((depth, inner), F32),
            pltpu.VMEM((depth, inner), F32),
            pltpu.VMEM((tok, part), F32),
            pltpu.VMEM((tok, part), F32),
            pltpu.VMEM((tok, part), F32),
            pltpu.VMEM((tok, part), F32),
            pltpu.VMEM((tok, 128), F32),
            pltpu.VMEM((tp, tok, part), F32),
            pltpu.VMEM((tp, tok, part), F32),
            pltpu.VMEM((tp, tok, part), F32),
            pltpu.VMEM((tp, tok, part), F32),
            pltpu.VMEM((tp, tok, part), BF16),
            pltpu.VMEM((tp, tok, part), BF16),
            pltpu.SemaphoreType.DMA((copies,)),
            pltpu.SemaphoreType.DMA((copies,)),
            pltpu.SemaphoreType.DMA((2 + 3 + 4 + 2 * tp + 4,)),
        ],
        compiler_params=pltpu.CompilerParams(collective_id=0, has_side_effects=True, vmem_limit_bytes=VMEM_LIMIT),
        name="gather_project",
    )(slots, gain_in, inputs, cotangent, w_x, w_s, w_z, w_out)


HIGH = lax.Precision.HIGH


def passed_along(block, axis, distance):
    devices = range(lax.axis_size(axis))
    route = [(i - distance, i) for i in devices if i - distance in devices]
    return lax.ppermute(block, axis, route)


def matmul(left, right):
    return jnp.dot(left, right, precision=HIGH)


def matmul_nt(left, right):
    return lax.dot_general(left, right, (((1,), (1,)), ((), ())), precision=HIGH)


def matmul_tn(left, right):
    return lax.dot_general(left, right, (((0,), (0,)), ((), ())), precision=HIGH)


def silu_f(value):
    return value * jax.nn.sigmoid(value)


def segment_of(positions, lengths):
    bounds = jnp.cumsum(lengths)
    hits = (bounds[None, :] <= positions[:, None]).astype(jnp.int32)
    return jnp.sum(hits, axis=1)


def norm_in(tokens, gain):
    scale = lax.rsqrt(jnp.mean(tokens * tokens, axis=1, keepdims=True) + EPSILON)
    return tokens * scale * gain[None, :]


def conv_act(pre, tail, taps, bias, raw_dt, dt_bias, a_log, segs, tail_segs, n_inner, n_state):
    extended = jnp.concatenate([tail, pre], axis=0)
    ext_segs = jnp.concatenate([tail_segs, segs])
    length = pre.shape[0]
    summed = jnp.zeros_like(pre) + bias[None, :]
    for offset_k in range(taps.shape[0]):
        moved = lax.slice_in_dim(extended, offset_k, offset_k + length, axis=0)
        same_doc = (lax.slice_in_dim(ext_segs, offset_k, offset_k + length, axis=0) == segs).astype(
            jnp.float32
        )
        summed = summed + taps[offset_k][None, :] * moved * same_doc[:, None]
    activated = silu_f(summed)
    xs = activated[:, :n_inner]
    bm = activated[:, n_inner : n_inner + n_state]
    cm = activated[:, n_inner + n_state :]
    step_size = jax.nn.softplus(raw_dt + dt_bias[None, :])
    decay_rate = -jnp.exp(a_log)
    return (xs, bm, cm, step_size, decay_rate)


def block_ssd(xs, step_size, decay_rate, bm, cm, d_skip, segs, seg_before, block_len):
    length, heads = step_size.shape
    head_width = xs.shape[1] // heads
    count = length // block_len
    x_blocks = xs.reshape(count, block_len, heads, head_width)
    log_blocks = (step_size * decay_rate[None, :]).reshape(count, block_len, heads)
    step_blocks = step_size.reshape(count, block_len, heads)
    b_blocks = bm.reshape(count, block_len, bm.shape[1])
    c_blocks = cm.reshape(count, block_len, cm.shape[1])
    seg_blocks = segs.reshape(count, block_len)
    seg_prev = jnp.concatenate([jnp.reshape(seg_before, (1,)), seg_blocks[:-1, -1]])
    rows_i = lax.broadcasted_iota(jnp.int32, (block_len, block_len), 0)
    cols_j = lax.broadcasted_iota(jnp.int32, (block_len, block_len), 1)

    def one_block(state, item):
        x_block, log_block, step_block, b_block, c_block, seg_block, seg_last_prev = item
        cumulative = jnp.cumsum(log_block, axis=0).T
        causal_same = (seg_block[:, None] == seg_block[None, :]) & (rows_i >= cols_j)
        gaps = cumulative[:, :, None] - cumulative[:, None, :]
        decays = jnp.where(causal_same[None], jnp.exp(jnp.where(causal_same[None], gaps, 0.0)), 0.0)
        scores = matmul_nt(c_block, b_block)
        weights = decays * scores[None] * step_block.T[:, None, :]
        mixed_out = jnp.einsum("hij,jhp->ihp", weights, x_block, precision=HIGH)
        keep_in = (seg_block == seg_last_prev).astype(jnp.float32)
        reading = jnp.exp(cumulative).T * keep_in[:, None]
        mixed_out = mixed_out + reading[:, :, None] * jnp.einsum(
            "in,hpn->ihp", c_block, state, precision=HIGH
        )
        last_seg = seg_block[-1]
        tail_w = (
            jnp.exp(cumulative[:, -1:] - cumulative).T
            * (seg_block == last_seg).astype(jnp.float32)[:, None]
            * step_block
        )
        carried = (jnp.exp(cumulative[:, -1]) * (last_seg == seg_last_prev).astype(jnp.float32))[
            :, None, None
        ] * state
        carried = carried + jnp.einsum("jh,jhp,jn->hpn", tail_w, x_block, b_block, precision=HIGH)
        mixed_out = mixed_out + d_skip[None, :, None] * x_block
        return (carried, mixed_out.reshape(block_len, heads * head_width))

    start_state = jnp.zeros((heads, head_width, bm.shape[1]), jnp.float32)
    end_state, outs = lax.scan(
        jax.checkpoint(one_block),
        start_state,
        (x_blocks, log_blocks, step_blocks, b_blocks, c_blocks, seg_blocks, seg_prev),
    )
    return (outs.reshape(length, heads * head_width), end_state)


def state_read(state, cm, step_size, decay_rate, segs, seg_before):
    cumulative = jnp.cumsum(step_size * decay_rate[None, :], axis=0)
    keep_in = (segs == seg_before).astype(jnp.float32)
    reading = jnp.exp(cumulative) * keep_in[:, None]
    read_out = reading[:, :, None] * jnp.einsum("in,hpn->ihp", cm, state, precision=HIGH)
    return read_out.reshape(cm.shape[0], -1)


def shards(
    inputs,
    cotangent,
    seq_lengths,
    slots,
    gain_in,
    w_z,
    w_x,
    w_dt,
    w_bc,
    w_out,
    conv_x,
    conv_x_bias,
    conv_bc,
    conv_bc_bias,
    dt_bias,
    a_log,
    d_skip,
    gate_gain,
):
    tok_count = inputs.shape[0]
    model_width = inputs.shape[1]
    groups = lax.axis_size(("fsdp", "ctx"))
    per_pair = tok_count // groups
    tp_count = lax.axis_size("tp")
    tp_index = lax.axis_index("tp")
    slice_width = model_width // tp_count
    targets = slots // tok_count
    onehot = (targets[:, None] == jnp.arange(groups, dtype=jnp.int32)[None, :]).astype(jnp.int32)
    ranks = jnp.sum((jnp.cumsum(onehot, axis=0) - onehot) * onehot, axis=1)
    send_at = targets * per_pair + ranks
    places = slots - targets * tok_count
    lead = (lax.axis_size("fsdp"), lax.axis_size("ctx"), tp_count)
    heads = w_dt.shape[1]
    w_side = jnp.concatenate([w_bc, w_dt, jnp.zeros((w_dt.shape[0], 128 - heads), jnp.float32)], axis=1)
    slots_wide = jnp.broadcast_to(slots[:, None], (tok_count, 128))
    tokens, upstream, p_recv, pre_x, pre_s, gate_pre, d_normal, chan_w, side_w, gate_w, proj_w = forward_call(
        lead, slots_wide, gain_in[None, :], inputs, cotangent, w_x, w_side, w_z, w_out
    )
    state_w, step_w = side_w[:, : 2 * N], side_w[:, 2 * N : 2 * N + heads]
    p_flat = p_recv[:, 0].astype(jnp.int32)
    inner_local = gate_w.shape[1]
    lengths = seq_lengths[0]
    offset = lax.axis_index("ctx") * tok_count
    width = conv_x.shape[0]
    segs = segment_of(offset + jnp.arange(tok_count, dtype=jnp.int32), lengths)
    tail_segs = segment_of(offset - width + 1 + jnp.arange(width - 1, dtype=jnp.int32), lengths)
    seg_before = segment_of(jnp.reshape(offset - 1, (1,)), lengths)[0]
    normed, norm_back = jax.vjp(norm_in, tokens, gain_in)
    pre = jnp.concatenate([pre_x, pre_s[:, : 2 * N]], axis=1)
    raw_dt = pre_s[:, 2 * N : 2 * N + heads]
    tail = passed_along(pre[tok_count - width + 1 :], "ctx", 1)
    taps = jnp.concatenate([conv_x, conv_bc], axis=1)
    bias = jnp.concatenate([conv_x_bias, conv_bc_bias])

    def act_fn(pre, tail, taps, bias, raw_dt, dt_bias, a_log):
        return conv_act(
            pre, tail, taps, bias, raw_dt, dt_bias, a_log, segs, tail_segs, inner_local, N
        )

    (xs, bm, cm, step_size, decay_rate), act_back = jax.vjp(
        act_fn, pre, tail, taps, bias, raw_dt, dt_bias, a_log
    )

    def ssd_fn(xs, step_size, decay_rate, bm, cm, d_skip):
        return block_ssd(xs, step_size, decay_rate, bm, cm, d_skip, segs, seg_before, SPAN)

    (y_own, end_state), ssd_back = jax.vjp(ssd_fn, xs, step_size, decay_rate, bm, cm, d_skip)
    state_in = passed_along(end_state, "ctx", 1)

    def read_fn(state, cm, step_size, decay_rate):
        return state_read(state, cm, step_size, decay_rate, segs, seg_before)

    y_read, read_back = jax.vjp(read_fn, state_in, cm, step_size, decay_rate)
    mixed = y_own + y_read
    gate_act = silu_f(gate_pre)
    gated = mixed * gate_act
    squares = jnp.sum(gated * gated, axis=1)
    shaped = gated * gate_gain[None, :]
    gscale = lax.rsqrt(lax.psum(squares, "tp") / INNER + EPSILON)
    shaped = shaped * gscale[:, None]
    partial_out = matmul_nt(shaped, proj_w)
    reduced = (lax.psum_scatter(partial_out, "tp", scatter_dimension=1, tiled=True),)
    branch_out = reduced[0]
    normal_y = gated * gscale[:, None] * gate_gain[None, :]
    own_cols = lax.dynamic_slice_in_dim(tokens, tp_index * slice_width, slice_width, 1)
    result_rows = own_cols + branch_out
    g_out = matmul_tn(upstream, normal_y)
    g_gate_gain = jnp.sum(d_normal * gated * gscale[:, None], axis=0)
    inner_part = jnp.sum(d_normal * gate_gain[None, :] * gated, axis=1)
    inner_total = lax.psum(inner_part, "tp")
    d_gated = (
        gscale[:, None] * gate_gain[None, :] * d_normal
        - gated * (gscale * gscale * gscale * inner_total / INNER)[:, None]
    )
    d_mixed = d_gated * gate_act
    sigmoid_z = jax.nn.sigmoid(gate_pre)
    d_gate_pre = d_gated * mixed * sigmoid_z * (1.0 + gate_pre * (1.0 - sigmoid_z))
    d_state_in, d_cm_read, d_step_read, d_rate_read = read_back(d_mixed)
    d_state_end = passed_along(d_state_in, "ctx", -1)
    d_xs, d_step_ssd, d_rate_ssd, d_bm_part, d_cm_ssd, g_skip = ssd_back((d_mixed, d_state_end))
    d_bm, d_cm = lax.psum((d_bm_part, d_cm_ssd + d_cm_read), "tp")
    d_pre, d_tail, g_taps, g_bias, d_raw_dt, g_dt_bias, g_a_log = act_back(
        (d_xs, d_bm, d_cm, d_step_ssd + d_step_read, d_rate_ssd + d_rate_read)
    )
    d_tail_in = passed_along(d_tail, "ctx", -1)
    d_pre = d_pre.at[tok_count - width + 1 :].add(d_tail_in)
    d_pre_x = d_pre[:, :inner_local]
    d_pre_bc = d_pre[:, inner_local:]
    lead_mask = (tp_index == 0).astype(jnp.float32)
    d_normed = (
        matmul_nt(d_gate_pre, gate_w)
        + matmul_nt(d_pre_x, chan_w)
        + matmul_nt(d_raw_dt, step_w)
        + matmul_nt(d_pre_bc * lead_mask, state_w)
    )
    g_gate_w = matmul_tn(normed, d_gate_pre)
    g_chan_w = matmul_tn(normed, d_pre_x)
    g_step_w = matmul_tn(normed, d_raw_dt)
    g_state_w = matmul_tn(normed, d_pre_bc)
    d_tokens_part, d_gain_part = norm_back(d_normed)
    d_tokens_own, d_gain_own = (
        lax.psum_scatter(d_tokens_part, "tp", scatter_dimension=1, tiled=True),
        lax.psum_scatter(d_gain_part, "tp", scatter_dimension=0, tiled=True),
    )
    up_cols = lax.dynamic_slice_in_dim(upstream, tp_index * slice_width, slice_width, 1)
    dx_rows = up_cols + d_tokens_own
    pad_row = jnp.zeros((1, slice_width), jnp.float32)
    out_send = jnp.concatenate([result_rows, pad_row], axis=0)[p_flat]
    dx_send = jnp.concatenate([dx_rows, pad_row], axis=0)[p_flat]
    out_back, dx_back = (
        lax.all_to_all(
            out_send.reshape(groups, per_pair, slice_width),
            ("fsdp", "ctx"),
            split_axis=0,
            concat_axis=0,
            tiled=True,
        ),
        lax.all_to_all(
            dx_send.reshape(groups, per_pair, slice_width),
            ("fsdp", "ctx"),
            split_axis=0,
            concat_axis=0,
            tiled=True,
        ),
    )
    result = out_back.reshape(-1, slice_width)[send_at]
    grad_input = dx_back.reshape(-1, slice_width)[send_at]
    s_gate_w, s_chan_w, s_step_w, s_state_w, s_out_w = (
        lax.psum_scatter(g_gate_w, ("fsdp", "ctx"), scatter_dimension=0, tiled=True),
        lax.psum_scatter(g_chan_w, ("fsdp", "ctx"), scatter_dimension=0, tiled=True),
        lax.psum_scatter(g_step_w, ("fsdp", "ctx"), scatter_dimension=0, tiled=True),
        lax.psum_scatter(g_state_w, ("fsdp", "ctx"), scatter_dimension=0, tiled=True),
        lax.psum_scatter(g_out, ("fsdp", "ctx"), scatter_dimension=0, tiled=True),
    )
    small_grads = lax.psum(
        (
            g_taps[:, :inner_local],
            g_bias[:inner_local],
            g_taps[:, inner_local:],
            g_bias[inner_local:],
            g_dt_bias,
            g_a_log,
            g_skip,
            g_gate_gain,
            d_gain_own,
        ),
        ("fsdp", "ctx"),
    )
    return (
        result,
        grad_input,
        s_gate_w,
        s_chan_w,
        s_step_w,
        s_state_w,
        s_out_w,
        small_grads[0],
        small_grads[1],
        small_grads[2],
        small_grads[3],
        small_grads[4],
        small_grads[5],
        small_grads[6],
        small_grads[7],
        small_grads[8],
    )


def solution(mesh):
    return jax.shard_map(
        shards,
        mesh=mesh,
        in_specs=(
            P(("fsdp", "ctx"), None),
            P(("fsdp", "ctx"), None),
            P("fsdp", None),
            P(("fsdp", "ctx")),
            P(),
            P(("fsdp", "ctx"), "tp"),
            P(("fsdp", "ctx"), "tp"),
            P(("fsdp", "ctx"), "tp"),
            P(("fsdp", "ctx"), None),
            P(("fsdp", "ctx"), "tp"),
            P(None, "tp"),
            P("tp"),
            P(),
            P(),
            P("tp"),
            P("tp"),
            P("tp"),
            P("tp"),
        ),
        out_specs=(
            P(("fsdp", "ctx"), "tp"),
            P(("fsdp", "ctx"), "tp"),
            P(("fsdp", "ctx"), "tp"),
            P(("fsdp", "ctx"), "tp"),
            P(("fsdp", "ctx"), "tp"),
            P(("fsdp", "ctx"), None),
            P(("fsdp", "ctx"), "tp"),
            P(None, "tp"),
            P("tp"),
            P(),
            P(),
            P("tp"),
            P("tp"),
            P("tp"),
            P("tp"),
            P("tp"),
        ),
        check_vma=False,
    )
```

```python
import functools
import math

import jax
import jax.numpy as jnp
from jax import lax
from jax.experimental import pallas as pl
from jax.experimental.pallas import tpu as pltpu
from jax.sharding import PartitionSpec as P

N = 128
SPAN = 256
INNER = 4096
EPSILON = 1e-05
F32 = jnp.float32
BF16 = jnp.bfloat16
MESH = pl.DeviceIdType.MESH
NN = (((1,), (0,)), ((), ()))
NT = (((1,), (1,)), ((), ()))
TN = (((0,), (0,)), ((), ()))
VMEM_LIMIT = 62 << 20


def split2(value):
    high = value.astype(BF16)
    return high, (value - high.astype(F32)).astype(BF16)


def split3(value):
    high = value.astype(BF16)
    rest = value - high.astype(F32)
    middle = rest.astype(BF16)
    return high, middle, (rest - middle.astype(F32)).astype(BF16)


def dot1(left, right, dims):
    return lax.dot_general(left, right, dims, preferred_element_type=F32)


def dot_split(left, right, dims):
    (lh, ll), (rh, rl) = left, right
    return dot1(lh, rh, dims) + (dot1(lh, rl, dims) + dot1(ll, rh, dims))


def dot3(left, right, dims):
    return dot_split(split2(left), split2(right), dims)


def pick(table, value, dims):
    parts = split3(value)
    return dot1(table, parts[0], dims) + dot1(table, parts[1], dims) + dot1(table, parts[2], dims)


def iota(shape, dim):
    return lax.broadcasted_iota(jnp.int32, shape, dim)


class Place:
    def __init__(self, fsdp, ctx, tp):
        self.fsdp, self.n_ctx, self.tp = fsdp, ctx, tp
        self.side = math.isqrt(fsdp)
        assert self.side * self.side == fsdp and ctx == 2
        self.f = lax.axis_index("fsdp")
        self.c = lax.axis_index("ctx")
        self.z = lax.axis_index("tp")
        self.y, self.x = self.f // self.side, self.f % self.side

    def chip(self, dy, dx):
        side = self.side
        return ((self.y + dy + side) % side) * side + (self.x + dx + side) % side

    def block(self, dy, dx, core):
        return self.chip(dy, dx) * 2 + core

    def at(self, dy, dx):
        return (self.chip(dy, dx), self.c, self.z)

    def sibling(self):
        return (self.f, 1 - self.c, self.z)

    def plane(self):
        out = []
        for df in range(self.fsdp):
            for dc in range(2):
                if df or dc:
                    to_f = (self.f + df) % self.fsdp
                    from_f = (self.f - df + self.fsdp) % self.fsdp
                    core = (self.c + dc) % 2
                    out.append(((to_f, core, self.z), to_f * 2 + core, from_f * 2 + core))
        return out

    def column(self):
        out = []
        for dz in range(1, self.tp):
            to_z = (self.z + dz) % self.tp
            out.append(((self.f, self.c, to_z), to_z, (self.z - dz + self.tp) % self.tp))
        return out


class Links:
    def __init__(self, send, recv, local):
        self.send, self.recv, self.local = send, recv, local
        self.used, self.used_local = 0, 0
        self.open = []

    def remote(self, src, dst, device):
        k = self.used
        self.used += 1
        copy = pltpu.make_async_remote_copy(
            src_ref=src,
            dst_ref=dst,
            send_sem=self.send.at[k],
            recv_sem=self.recv.at[k],
            device_id=device,
            device_id_type=MESH,
        )
        copy.start()
        self.open.append(copy)
        return copy

    def move(self, src, dst):
        k = self.used_local
        self.used_local += 1
        copy = pltpu.make_async_copy(src, dst, self.local.at[k])
        copy.start()
        return copy

    def settle(self, copies):
        for copy in copies:
            copy.wait_send()
            self.open = [other for other in self.open if other is not copy]

    def finish(self):
        self.settle(list(self.open))


def greet(devices):
    barrier = pltpu.get_barrier_semaphore()
    for device in devices:
        pl.semaphore_signal(barrier, inc=1, device_id=device, device_id_type=MESH)
    pl.semaphore_wait(barrier, len(devices))


class Gather:
    def __init__(self, place, links, shard, whole):
        self.place, self.links, self.shard, self.whole = place, links, shard, whole
        self.rows = shard.shape[0]

    def rows_of(self, block, start=0, count=None):
        count = self.rows if count is None else count
        return self.whole.at[pl.ds(pl.multiple_of(block * self.rows + start, 8), count)]

    def start(self):
        p, steps = self.place, range(1, self.place.side)
        mine = self.rows_of(p.block(0, 0, p.c))
        self.row = [self.links.remote(self.shard, mine, p.at(0, d)) for d in steps]
        self.col = [self.links.remote(self.shard, mine, p.at(d, 0)) for d in steps]
        self.pair = [self.links.remote(self.shard, mine, p.sibling())]
        self.own = self.links.move(self.shard, mine)

    def forward(self):
        p, steps, half = self.place, range(1, self.place.side), self.rows // 2
        self.half_a, self.half_b = [], []
        for k, d in enumerate(steps):
            self.row[k].wait_recv()
            block = p.block(0, -d, p.c)
            part = self.rows_of(block, 0, half)
            self.half_a += [self.links.remote(part, part, p.at(e, 0)) for e in steps]
            whole = self.rows_of(block)
            self.pair.append(self.links.remote(whole, whole, p.sibling()))
        for k, e in enumerate(steps):
            self.col[k].wait_recv()
            block = p.block(-e, 0, p.c)
            part = self.rows_of(block, half, half)
            self.half_b += [self.links.remote(part, part, p.at(0, d)) for d in steps]
            whole = self.rows_of(block)
            self.pair.append(self.links.remote(whole, whole, p.sibling()))

    def share(self):
        p, steps, half = self.place, range(1, self.place.side), self.rows // 2
        k = 0
        for d in steps:
            for e in steps:
                self.half_a[k].wait_recv()
                part = self.rows_of(p.block(-e, -d, p.c), 0, half)
                self.pair.append(self.links.remote(part, part, p.sibling()))
                k += 1
        k = 0
        for e in steps:
            for d in steps:
                self.half_b[k].wait_recv()
                part = self.rows_of(p.block(-e, -d, p.c), half, half)
                self.pair.append(self.links.remote(part, part, p.sibling()))
                k += 1

    def finish(self):
        self.own.wait()
        for copy in self.pair:
            copy.wait_recv()


def gather_copies(side):
    steps = side - 1
    return 4 * steps + 1 + 4 * steps * steps


def leaving(slots, tok, groups):
    targets = slots >> (tok.bit_length() - 1)
    member = (targets == iota((tok, 128), 1)).astype(F32)
    earlier = (iota((tok, tok), 0) > iota((tok, tok), 1)).astype(BF16)
    ranks = jnp.sum(dot1(earlier, member.astype(BF16), NN) * member, axis=1, keepdims=True)
    send_at = (targets[:, :1] * (tok // groups)).astype(F32) + ranks
    return (send_at == iota((tok, tok), 1).astype(F32)).astype(BF16)


def settling(places, tok):
    return (places[:, :1] == iota((tok, tok), 1).astype(F32)).astype(BF16)


def silu_slope(value):
    gate = jax.nn.sigmoid(value)
    return gate * (1.0 + value * (1.0 - gate))


def softplus(value):
    return jnp.maximum(value, 0.0) + jnp.log1p(jnp.exp(-jnp.abs(value)))


def segments(lengths, position):
    bound, seg = 0, jnp.zeros_like(position)
    for k in range(lengths.shape[1]):
        bound = bound + lengths[0, k]
        seg = seg + (bound <= position).astype(jnp.int32)
    return seg


def same_before(lengths, first, tok, distance):
    position = first + iota((tok, 128), 0)
    return (segments(lengths, position) == segments(lengths, position - distance)).astype(F32)


def wide(table, width):
    return jnp.concatenate([table] * (width // 128), axis=1)


def column_of(table, head):
    lanes = iota(table.shape, 1)
    return jnp.sum(jnp.where(lanes == head, table, 0.0), axis=1, keepdims=True)


def pair_columns(table, pair):
    first, second = column_of(table, 2 * pair), column_of(table, 2 * pair + 1)
    return jnp.where(iota(table.shape, 1) < 64, first, second)


class Steps:
    def __init__(self, raw, params_s, lengths, first):
        tok = raw.shape[0]
        shifted = raw + params_s[5:6, :128]
        self.slope = jax.nn.sigmoid(shifted)
        self.step = softplus(shifted)
        self.rate = -jnp.exp(params_s[6:7, :128])
        until = (iota((tok, tok), 0) >= iota((tok, tok), 1)).astype(BF16)
        self.total = pick(until, self.step * self.rate, NN)
        position = first + iota((tok, 128), 0)
        seg = segments(lengths, position)
        before = segments(lengths, jnp.full((tok, 128), first - 1, jnp.int32))
        last = segments(lengths, jnp.full((tok, 128), first + tok - 1, jnp.int32))
        self.reading = jnp.exp(self.total) * (seg == before).astype(F32)
        self.fading = jnp.exp(self.total[tok - 1 : tok] - self.total) * (seg == last).astype(F32)
        self.tail = self.fading * self.step


def closed(lengths, first, tok, flipped):
    rows, cols = first + iota((tok, tok), 0), first + iota((tok, tok), 1)
    order = rows <= cols if flipped else rows >= cols
    seg_rows = segments(lengths, first + iota((tok, 1), 0))
    seg_cols = segments(lengths, first + iota((1, tok), 1))
    return jnp.where(order & (seg_rows == seg_cols), 0.0, -1e30)


def project(left_high, left_low, whole, out, tile, first_row):
    slices, rows, width = left_high.shape

    @pl.loop(0, whole.shape[1] // tile)
    def _(n):
        cols = pl.ds(pl.multiple_of(n * tile, 128), tile)
        total = jnp.zeros((rows, tile), F32)
        for k in range(slices):
            right = split2(whole[k * width : (k + 1) * width, cols])
            total = total + dot_split((left_high[k], left_low[k]), right, NN)
        out[first_row : first_row + rows, cols] = total


def convolve(padded, params, lengths, first, conv, act):
    tok, tile = conv.shape[0], 128
    same = [same_before(lengths, first, tok, 3 - k) for k in range(3)]

    @pl.loop(0, conv.shape[1] // tile)
    def _(n):
        cols = pl.ds(pl.multiple_of(n * tile, 128), tile)
        total = params[4:5, cols] + params[3:4, cols] * padded[8 : 8 + tok, cols]
        for k in range(3):
            total = total + params[k : k + 1, cols] * (padded[5 + k : 5 + k + tok, cols] * same[k])
        conv[:, cols] = total
        act[:, cols] = total * jax.nn.sigmoid(total)


def forward_kernel(
    sizes,
    lengths,
    slots_in,
    gain,
    params_c,
    params_s,
    x_in,
    c_in,
    w_x,
    w_s,
    w_z,
    w_out,
    tokens_out,
    up_out,
    n_pairs_out,
    c_pairs_out,
    p_recv,
    pre_x_out,
    pre_s_out,
    conv_x_out,
    conv_s_out,
    ny_out,
    dz_out,
    dmix_out,
    state_out,
    gain_out,
    wx_out,
    ws_out,
    wz_out,
    wo_out,
    wx,
    ws,
    wz,
    wo,
    x_own,
    c_own,
    x_sort,
    c_sort,
    p_sort,
    x_recv,
    c_recv,
    tokens,
    n_high,
    n_low,
    turned,
    n_pairs,
    c_pairs,
    pre_x,
    pre_s,
    tail_x,
    tail_s,
    conv_x,
    conv_s,
    act_x,
    act_s,
    totals,
    step_rows,
    open_,
    scores,
    state,
    state_in,
    mixed,
    gate_pre,
    d_normal,
    sums,
    sums_recv,
    send,
    recv,
    local,
):
    place = Place(*sizes)
    links = Links(send, recv, local)
    tok, groups = x_own.shape[0], 2 * place.fsdp
    per_pair = tok // groups
    part = x_own.shape[1]
    inner = act_x.shape[1]
    pairs = inner // 128
    first = place.c * tok
    part_cols = pl.ds(pl.multiple_of(place.z * part, 128), part)
    load_x = links.move(x_in.at[:, part_cols], x_own)
    load_c = links.move(c_in.at[:, part_cols], c_own)
    plane, column = place.plane(), place.column()
    greet([entry[0] for entry in plane] + [entry[0] for entry in column])

    g_x, g_s, g_z, g_o = [Gather(place, links, shard, whole) for shard, whole in ((w_x, wx), (w_s, ws), (w_z, wz), (w_out, wo))]
    g_x.start()
    g_s.start()

    slots = slots_in[...]
    leave = leaving(slots, tok, groups)
    targets = slots >> (tok.bit_length() - 1)
    place_of = (slots - targets * tok).astype(F32).astype(BF16)
    p_sort[...] = dot1(leave, place_of, TN)
    load_x.wait()
    x_sort[...] = pick(leave, x_own[...], TN)

    def rows(group):
        return pl.ds(pl.multiple_of(group * per_pair, 8), per_pair)

    def route(source, target):
        mine = rows(place.f * 2 + place.c)
        copies = [links.remote(source.at[rows(to)], target.at[mine], device) for device, to, _ in plane]
        return copies, links.move(source.at[mine], target.at[mine])

    routes_x = [route(p_sort, p_recv), route(x_sort, x_recv.at[place.z])]
    load_c.wait()
    c_sort[...] = pick(leave, c_own[...], TN)
    routes_c = [route(c_sort, c_recv.at[place.z])]
    g_z.start()

    def arrive(routes):
        for copies, own in routes:
            own.wait()
            for copy in copies:
                copy.wait_recv()

    def spread(received):
        mine = received.at[place.z]
        return [links.remote(mine, mine, device) for device, _, _ in column]

    arrive(routes_x)
    spread_x = spread(x_recv)
    g_x.forward()
    g_s.forward()
    g_o.start()
    arrive(routes_c)
    spread_c = spread(c_recv)
    g_x.share()
    g_s.share()

    stores = []
    shard_rows = n_pairs.shape[1]
    for copy in spread_x:
        copy.wait_recv()
    settle = settling(p_recv, tok)
    squares = jnp.zeros((tok, 1), F32)
    for k in range(place.tp):
        value = pick(settle, x_recv[k], TN)
        tokens[k] = value
        squares = squares + jnp.sum(value * value, axis=1, keepdims=True)
    scale = lax.rsqrt(squares / (place.tp * part) + EPSILON)
    own_cols = pl.ds(pl.multiple_of(place.c * tok, 128), tok)

    def exchange_blocks(pairs_ref):
        copies = []
        for q in range(place.fsdp):
            there = turned.at[pl.ds(pl.multiple_of((2 * q + 1 - place.c) * shard_rows, 8), shard_rows)]
            here = turned.at[pl.ds(pl.multiple_of((2 * q + place.c) * shard_rows, 8), shard_rows)]
            copies.append(links.remote(there, pairs_ref.at[q, :, own_cols], place.sibling()))
            stores.append(links.move(here, pairs_ref.at[q, :, own_cols]))
        return copies

    for k in range(place.tp):
        normed = tokens[k] * scale * gain[:, k * part : (k + 1) * part]
        n_high[k], n_low[k] = split2(normed)
        turned[k * part : (k + 1) * part, :] = normed.T
    pairs_n = exchange_blocks(n_pairs)
    stores.append(links.move(tokens, tokens_out))

    g_x.finish()
    g_s.finish()
    stores += [links.move(wx, wx_out), links.move(ws, ws_out)]
    project(n_high, n_low, ws, pre_s, 128, 8)
    g_z.forward()
    project(n_high, n_low, wx, pre_x, 256, 8)
    halo = [
        links.remote(pre_x.at[pl.ds(tok, 8)], tail_x, place.sibling()),
        links.remote(pre_s.at[pl.ds(tok, 8)], tail_s, place.sibling()),
    ]

    steps = Steps(pre_s[8 : 8 + tok, pre_s.shape[1] - 128 :], params_s, lengths, first)
    totals[...] = steps.total
    totals_rows = steps.total.T
    step_rows[0] = totals_rows
    step_rows[1] = steps.step.T
    open_[...] = closed(lengths, first, tok, False)
    for copy in halo:
        copy.wait_recv()
    second = (place.c > 0).astype(F32)
    pre_x[0:8, :] = tail_x[...] * second
    pre_s[0:8, :] = tail_s[...] * second
    convolve(pre_s, params_s, lengths, first, conv_s, act_s)
    convolve(pre_x, params_c, lengths, first, conv_x, act_x)
    b_parts = split2(act_s[:, :N])
    c_parts = split2(act_s[:, N:])
    scores[...] = dot_split(c_parts, b_parts, NT)
    tail_table, reading_table = steps.tail, steps.reading

    @pl.loop(0, pairs)
    def _(q):
        cols = pl.ds(pl.multiple_of(q * 128, 128), 128)
        faded = act_x[:, cols] * pair_columns(tail_table, q)
        state[cols, :] = dot_split(split2(faded), b_parts, TN)

    pass_state = links.remote(state, state_in, place.sibling())
    g_z.share()
    g_o.forward()
    pass_state.wait_recv()
    @pl.loop(0, pairs)
    def _(q):
        cols = pl.ds(pl.multiple_of(q * 128, 128), 128)
        channels = act_x[:, cols]
        entered = state_in[cols, :] * second
        state_in[cols, :] = entered
        out = params_c[5:6, cols] * channels
        out = out + pair_columns(reading_table, q) * dot_split(c_parts, split2(entered), NT)
        lanes = iota((tok, 128), 1)
        for s in range(2):
            head = 2 * q + s
            gaps = column_of(totals[...], head) - step_rows[0, pl.ds(head, 1), :] + open_[...]
            weights = jnp.exp(gaps) * scores[...] * step_rows[1, pl.ds(head, 1), :]
            own = jnp.where((lanes < 64) == (s == 0), channels, 0.0)
            out = out + dot3(weights, own, NN)
        mixed[:, cols] = out

    stores += [
        links.move(pre_x, pre_x_out),
        links.move(pre_s, pre_s_out),
        links.move(conv_x, conv_x_out),
        links.move(conv_s, conv_s_out),
        links.move(state_in, state_out),
    ]
    g_z.finish()
    stores.append(links.move(wz, wz_out))
    project(n_high, n_low, wz, gate_pre, 256, 0)

    for copy in spread_c:
        copy.wait_recv()
    for copy in pairs_n:
        copy.wait_recv()
    links.settle(pairs_n)
    for k in range(place.fsdp):
        stores[k].wait()
    del stores[: place.fsdp]
    stores.append(links.move(n_pairs, n_pairs_out))
    for k in range(place.tp):
        upstream = pick(settle, c_recv[k], TN)
        n_high[k], n_low[k] = split2(upstream)
        turned[k * part : (k + 1) * part, :] = upstream.T

        @pl.when(place.z == k)
        def _():
            x_own[...] = upstream

    moved = len(stores)
    pairs_c = exchange_blocks(c_pairs)
    stores.append(links.move(x_own, up_out))
    g_o.share()
    g_o.finish()
    stores.append(links.move(wo, wo_out))
    project(n_high, n_low, wo, d_normal, 256, 0)

    def over_tiles(body, carry):
        def step(n, carry):
            return body(pl.ds(pl.multiple_of(n * 128, 128), 128), carry)

        return lax.fori_loop(0, pairs, step, carry)

    def add_up(cols, carry):
        z = gate_pre[:, cols]
        gated = mixed[:, cols] * (z * jax.nn.sigmoid(z))
        return carry[0] + gated * gated, carry[1] + d_normal[:, cols] * params_c[6:7, cols] * gated

    zeros = jnp.zeros((tok, 128), F32)
    square_sum, inner_sum = over_tiles(add_up, (zeros, zeros))
    lanes = iota((tok, 128), 1)
    both = jnp.where(lanes == 0, jnp.sum(square_sum, axis=1, keepdims=True), jnp.sum(inner_sum, axis=1, keepdims=True))
    sums[...] = both.T[0:8, :]
    copies = [links.remote(sums, sums_recv.at[k], device) for k, (device, _, _) in enumerate(column)]
    for copy in copies:
        copy.wait_recv()
    total = sums[...]
    for k in range(place.tp - 1):
        total = total + sums_recv[k]
    total = jnp.concatenate([total, jnp.zeros((120, tok), F32)], axis=0).T
    gscale = lax.rsqrt(total[:, 0:1] / INNER + EPSILON)
    pull = gscale * gscale * gscale * total[:, 1:2] / INNER

    def shape_all(cols, carry):
        z, y, upward, weight = gate_pre[:, cols], mixed[:, cols], d_normal[:, cols], params_c[6:7, cols]
        gate = jax.nn.sigmoid(z)
        act = z * gate
        gated = y * act
        d_gated = gscale * weight * upward - gated * pull
        mixed[:, cols] = gated * gscale * weight
        d_normal[:, cols] = d_gated * act
        gate_pre[:, cols] = d_gated * y * gate * (1.0 + z * (1.0 - gate))
        gain_out[:, cols] = jnp.sum(upward * gated * gscale, axis=0, keepdims=True)
        return carry

    over_tiles(shape_all, 0)
    stores += [links.move(mixed, ny_out), links.move(gate_pre, dz_out), links.move(d_normal, dmix_out)]
    for copy in pairs_c:
        copy.wait_recv()
    for k in range(place.fsdp):
        stores[moved + k].wait()
    del stores[moved : moved + place.fsdp]
    stores.append(links.move(c_pairs, c_pairs_out))
    for store in stores:
        store.wait()
    links.finish()


class Scatter:
    def __init__(self, place, links, blocks, first_a, first_b, second_a, second_b):
        self.place, self.links, self.blocks = place, links, blocks
        self.first = (first_a, first_b)
        self.second = (second_a, second_b)
        self.half = blocks.shape[1] // 2
        self.copies_a, self.copies_b = {}, {}

    def order(self):
        side = self.place.side
        hops = [(dy, dx) for dy in range(side) for dx in range(side)]
        return sorted(hops, key=lambda hop: -(hop[0] > 0) - (hop[1] > 0))

    def halves(self, dy, dx):
        ref = self.blocks.at[self.place.chip(dy, dx)]
        return ref.at[pl.ds(0, self.half)], ref.at[pl.ds(self.half, self.half)]

    def send(self, dy, dx):
        p, side = self.place, self.place.side
        upper, lower = self.halves(dy, dx)
        if dy:
            target = self.first[0].at[dy - 1, (p.x + dx) % side]
            self.copies_a[dy, dx] = self.links.remote(upper, target, p.at(dy, 0))
        if dx:
            target = self.first[1].at[dx - 1, (p.y + dy) % side]
            self.copies_b[dy, dx] = self.links.remote(lower, target, p.at(0, dx))

    def pass_on(self):
        p, side = self.place, self.place.side
        self.last_a, self.last_b = [], []
        for d in list(range(1, side)) + [0]:
            upper, _ = self.halves(0, d)
            total = upper[...]
            for e in range(1, side):
                self.copies_a[e, d].wait_recv()
                total = total + self.first[0][e - 1, (p.x + d) % side]
            upper[...] = total
            if d:
                self.last_a.append(self.links.remote(upper, self.second[0].at[d - 1], p.at(0, d)))
            _, lower = self.halves(d, 0)
            total = lower[...]
            for e in range(1, side):
                self.copies_b[d, e].wait_recv()
                total = total + self.first[1][e - 1, (p.y + d) % side]
            lower[...] = total
            if d:
                self.last_b.append(self.links.remote(lower, self.second[1].at[d - 1], p.at(d, 0)))

    def finish(self):
        for k, (copies, part) in enumerate(zip((self.last_a, self.last_b), self.halves(0, 0))):
            total = part[...]
            for d, copy in enumerate(copies):
                copy.wait_recv()
                total = total + self.second[k][d]
            part[...] = total
        return self.blocks.at[self.place.chip(0, 0)]


def halve(value_ref, high, low):
    tile = 128

    @pl.loop(0, value_ref.shape[1] // tile)
    def _(n):
        cols = pl.ds(pl.multiple_of(n * tile, 128), tile)
        high[:, cols], low[:, cols] = split2(value_ref[:, cols])


def weight_block(left_ref, high, low, left_high, left_low, out):
    left_high[...], left_low[...] = split2(left_ref[...])
    tile = 256

    @pl.loop(0, high.shape[1] // tile)
    def _(n):
        cols = pl.ds(pl.multiple_of(n * tile, 128), tile)
        out[:, cols] = dot_split((left_high[...], left_low[...]), (high[:, cols], low[:, cols]), NN)


def times_rows(high, low, rows_ref, out, fresh):
    tile = min(256, rows_ref.shape[0])
    for n in range(rows_ref.shape[0] // tile):
        at = slice(n * tile, (n + 1) * tile)
        value = dot_split((high[...], low[...]), split2(rows_ref[at, :]), NT)
        out[:, at] = value if fresh else out[:, at] + value


def backward_kernel(
    sizes,
    heads,
    lengths,
    slots_in,
    p_recv,
    gain,
    params_c,
    params_s,
    gain_row,
    tokens_in,
    up_in,
    n_pairs_in,
    c_pairs_in,
    pre_x_in,
    pre_s_in,
    conv_x_in,
    conv_s_in,
    ny_in,
    dz_in,
    dmix_in,
    state_in_hbm,
    wx_in,
    ws_in,
    wz_in,
    wo_in,
    result,
    grad_input,
    grad_z,
    grad_x,
    grad_bc,
    grad_dt,
    grad_out,
    small_out,
    tokens,
    n_pairs,
    c_pairs,
    pre_x,
    pre_s,
    conv_x,
    conv_s,
    state_in,
    ny_both,
    dz_both,
    ds_both,
    high,
    low,
    left_high,
    left_low,
    blocks_o,
    blocks_z,
    blocks_s,
    o1a, o1b, o2a, o2b,
    z1a, z1b, z2a, z2b,
    x1a, x1b, x2a, x2b,
    s1a, s1b, s2a, s2b,
    blocks_x,
    stream,
    ws,
    ds,
    ds_high,
    ds_low,
    bc_rows,
    bc_recv,
    bc_grad,
    part_r,
    part_spare,
    recv_r,
    recv_t,
    row_sums,
    row_recv,
    home_r,
    home_t,
    back_r,
    back_t,
    d_state,
    d_state_recv,
    d_b,
    d_c,
    pad_x,
    pad_s,
    head_x,
    head_s,
    open_,
    scores,
    d_scores,
    totals,
    steps_col,
    total_rows,
    grad_total,
    grad_step,
    grad_tail,
    grad_rows,
    skip_row,
    small,
    small_recv,
    small_z,
    send,
    recv,
    local,
):
    place = Place(*sizes)
    links = Links(send, recv, local)
    tok, groups = tokens.shape[1], 2 * place.fsdp
    per_pair = tok // groups
    part = tokens.shape[2]
    part_t = c_pairs if c_pairs.shape == tokens.shape else part_spare
    inner = conv_x.shape[1]
    pairs = inner // 128
    first = place.c * tok
    own_rows = pl.ds(pl.multiple_of(place.c * tok, 128), tok)
    plane, column = place.plane(), place.column()

    loads = {}
    for name, src, dst in (
        ("pre_s", pre_s_in, pre_s),
        ("conv_s", conv_s_in, conv_s),
        ("dmix", dmix_in, pad_x.at[pl.ds(0, tok)]),
        ("state", state_in_hbm, state_in),
        ("ny", ny_in, ny_both.at[own_rows]),
        ("c_pairs", c_pairs_in, c_pairs),
        ("dz", dz_in, dz_both.at[own_rows]),
        ("n_pairs", n_pairs_in, n_pairs),
        ("conv_x", conv_x_in, conv_x),
        ("pre_x", pre_x_in, pre_x),
        ("tokens", tokens_in, tokens),
        ("up", up_in, home_t),
    ):
        loads[name] = links.move(src, dst)

    turns = [(place.z + d + 1) % place.tp for d in range(place.tp)]
    schedule = [(weight, turn) for weight in (wo_in, wz_in, wx_in) for turn in turns]
    fetched = []

    def fetch():
        k = len(fetched)
        if k < len(schedule):
            weight, turn = schedule[k]
            src = weight.at[pl.ds(pl.multiple_of(turn * part, 8), part)]
            fetched.append(links.move(src, stream.at[k % 2]))

    fetch()
    fetch()

    def weight_slice(k):
        fetched[k].wait()
        return stream.at[k % 2]

    greet([entry[0] for entry in plane] + [entry[0] for entry in column])
    give_ny = links.remote(ny_in, ny_both.at[own_rows], place.sibling())
    give_dz = links.remote(dz_in, dz_both.at[own_rows], place.sibling())

    loads["pre_s"].wait()
    loads["conv_s"].wait()
    side = pre_s.shape[1]
    steps = Steps(pre_s[8 : 8 + tok, side - 128 :], params_s, lengths, first)
    totals[...] = steps.total
    steps_col[...] = steps.step
    total_rows[...] = steps.total.T
    open_[...] = closed(lengths, first, tok, True)
    act_s = conv_s[...] * jax.nn.sigmoid(conv_s[...])
    b_parts, c_parts = split2(act_s[:, :N]), split2(act_s[:, N:])
    scores[...] = dot_split(b_parts, c_parts, NT)
    reading_table, tail_table = steps.reading, steps.tail
    grad_total[...] = jnp.zeros((tok, 128), F32)
    grad_step[...] = jnp.zeros((tok, 128), F32)
    grad_tail[...] = jnp.zeros((tok, 128), F32)
    d_c[...] = jnp.zeros((tok, N), F32)
    d_b[...] = jnp.zeros((tok, N), F32)
    d_scores[...] = jnp.zeros((tok, tok), F32)
    grad_rows[...] = jnp.zeros((128, tok), F32)
    lanes = iota((tok, 128), 1)

    def put(ref, head, value):
        ref[...] = ref[...] + jnp.where(lanes == head, value, 0.0)

    def by_head(value, s):
        return jnp.sum(jnp.where((lanes < 64) == (s == 0), value, 0.0), axis=1, keepdims=True)

    loads["dmix"].wait()
    loads["state"].wait()

    @pl.loop(0, pairs)
    def _(q):
        cols = pl.ds(pl.multiple_of(q * 128, 128), 128)
        upward = pad_x[0:tok, cols] * pair_columns(reading_table, q)
        parts = split2(upward)
        entered = split2(state_in[cols, :])
        d_c[...] = d_c[...] + dot_split(parts, entered, NN)
        d_state[cols, :] = dot_split(parts, c_parts, TN)
        read = upward * dot_split(c_parts, entered, NT)
        for s in range(2):
            put(grad_total, 2 * q + s, by_head(read, s))

    give_state = links.remote(d_state, d_state_recv, place.sibling())

    def spread_blocks(scatter, pairs_ref, both):
        halve(both, high, low)
        for hop in scatter.order():
            block = place.chip(*hop)
            weight_block(pairs_ref.at[block], high, low, left_high, left_low, scatter.blocks.at[block])
            scatter.send(*hop)

    loads["ny"].wait()
    loads["c_pairs"].wait()
    give_ny.wait_recv()
    sum_o = Scatter(place, links, blocks_o, o1a, o1b, o2a, o2b)
    spread_blocks(sum_o, c_pairs, ny_both)

    def product(k, turn, fresh, out):
        ref = weight_slice(k)
        times_rows(high.at[own_rows], low.at[own_rows], ref, out, fresh)
        fetch()

    shares_r = []
    for k, turn in enumerate(turns):
        product(k, turn, True, part_r.at[turn])
        if k < place.tp - 1:
            shares_r.append(links.remote(part_r.at[turn], recv_r.at[k], column[k][0]))

    loads["dz"].wait()
    loads["n_pairs"].wait()
    give_dz.wait_recv()
    sum_z = Scatter(place, links, blocks_z, z1a, z1b, z2a, z2b)
    spread_blocks(sum_z, n_pairs, dz_both)
    for k, turn in enumerate(turns):
        product(place.tp + k, turn, True, part_t.at[turn])

    loads["conv_x"].wait()
    give_state.wait_recv()
    first_half = (place.c == 0).astype(F32)

    @pl.loop(0, pairs)
    def _(q):
        cols = pl.ds(pl.multiple_of(q * 128, 128), 128)
        conv = conv_x[:, cols]
        gate = jax.nn.sigmoid(conv)
        channels = conv * gate
        upward = pad_x[0:tok, cols]
        ended = split2(d_state_recv[cols, :] * first_half)
        tail = pair_columns(tail_table, q)
        from_end = dot_split(b_parts, ended, NT)
        d_b[...] = d_b[...] + dot_split(split2(channels * tail), ended, NN)
        into = params_c[5:6, cols] * upward + tail * from_end
        skip_row[:, cols] = jnp.sum(upward * channels, axis=0, keepdims=True)
        end_part = channels * from_end
        x_parts = split2(channels)
        for s in range(2):
            head = 2 * q + s
            put(grad_tail, head, by_head(end_part, s))
            step_col = column_of(steps_col[...], head)
            gaps = total_rows[pl.ds(head, 1), :] - column_of(totals[...], head) + open_[...]
            decay = jnp.exp(gaps)
            up_parts = split2(jnp.where((lanes < 64) == (s == 0), upward, 0.0))
            reach = dot_split(x_parts, up_parts, NT) * decay
            d_scores[...] = d_scores[...] + reach * step_col
            reach = reach * scores[...]
            put(grad_step, head, jnp.sum(reach, axis=1, keepdims=True))
            grad_rows[pl.ds(head, 1), :] = jnp.sum(reach * step_col, axis=0, keepdims=True)
            into = into + dot3(decay * scores[...] * step_col, jnp.where((lanes < 64) == (s == 0), upward, 0.0), NN)
        pad_x[0:tok, cols] = into * gate * (1.0 + conv * (1.0 - gate))

    sum_o.pass_on()

    score_parts = split2(d_scores[...])
    slope_s = silu_slope(conv_s[...])
    pad_s[0:tok, 0:N] = (d_b[...] + dot_split(score_parts, c_parts, NN)) * slope_s[:, :N]
    pad_s[0:tok, N : 2 * N] = (d_c[...] + dot_split(score_parts, b_parts, TN)) * slope_s[:, N:]
    halo = [
        links.remote(pad_x.at[pl.ds(0, 8)], head_x, place.sibling()),
        links.remote(pad_s.at[pl.ds(0, 8)], head_s, place.sibling()),
    ]
    step_now = steps_col[...]
    faded = grad_tail[...] * tail_table
    d_total = grad_total[...] + grad_rows[...].T - grad_step[...] * step_now - faded
    at_end = iota((tok, 128), 0) == tok - 1
    d_total = d_total + jnp.where(at_end, jnp.sum(faded, axis=0, keepdims=True), 0.0)
    onward = (iota((tok, tok), 1) >= iota((tok, tok), 0)).astype(BF16)
    d_log = pick(onward, d_total, NN)
    d_step = grad_step[...] + grad_tail[...] * steps.fading + d_log * steps.rate
    d_raw = jnp.where(lanes < heads, d_step * steps.slope, 0.0)
    ds[:, 2 * N :] = d_raw
    small[...] = jnp.zeros_like(small)
    small[5:6, inner : inner + 128] = jnp.sum(d_raw, axis=0, keepdims=True)
    small[6:7, inner : inner + 128] = jnp.sum(d_log * step_now, axis=0, keepdims=True) * steps.rate
    head_of = (iota((inner, 128), 0) // (inner // heads) == iota((inner, 128), 1)).astype(BF16)
    skips = jnp.broadcast_to(skip_row[...], (8, inner))
    small[7:8, inner : inner + 128] = sum(dot1(piece, head_of, NN) for piece in split3(skips))[0:1]
    small[5:6, 0:inner] = gain_row[...]

    loads["pre_x"].wait()
    for copy in halo:
        copy.wait_recv()
    pad_x[tok : tok + 8, :] = head_x[...] * first_half
    pad_s[tok : tok + 8, :] = head_s[...] * first_half
    dx_both = ny_both
    same = [same_before(lengths, first, tok, 3 - k) for k in range(3)]
    same_next = [same_before(lengths, first + 3 - k, tok, 3 - k) for k in range(3)]

    def back(padded, pre, params, out, start, n):
        cols = pl.ds(pl.multiple_of(n * 128, 128), 128)
        small_cols = pl.ds(pl.multiple_of(start + n * 128, 128), 128)
        here = padded[0:tok, cols]
        total = params[3:4, cols] * here
        small[3:4, small_cols] = jnp.sum(here * pre[8 : 8 + tok, cols], axis=0, keepdims=True)
        small[4:5, small_cols] = jnp.sum(here, axis=0, keepdims=True)
        for k in range(3):
            total = total + params[k : k + 1, cols] * (padded[3 - k : 3 - k + tok, cols] * same_next[k])
            value = here * (pre[5 + k : 5 + k + tok, cols] * same[k])
            small[k : k + 1, small_cols] = jnp.sum(value, axis=0, keepdims=True)
        out[:, cols] = total

    @pl.loop(0, pairs)
    def _(n):
        back(pad_x, pre_x, params_c, dx_both.at[own_rows], 0, n)

    give_dx = links.remote(dx_both.at[own_rows], dx_both.at[own_rows], place.sibling())

    @pl.loop(0, 2 * N // 128)
    def _(n):
        back(pad_s, pre_s, params_s, ds, inner, n)

    share = 2 * N // place.tp
    bc_rows[...] = ds[:, : 2 * N].T

    def share_of(turn):
        return pl.ds(pl.multiple_of(turn * share, 8), share)

    give_bc = [
        links.remote(bc_rows.at[share_of(to_z)], bc_recv.at[k], device) for k, (device, to_z, _) in enumerate(column)
    ]

    give_dx.wait_recv()
    sum_x = Scatter(place, links, blocks_x, x1a, x1b, x2a, x2b)
    spread_blocks(sum_x, n_pairs, dx_both)
    sum_z.pass_on()

    loads["tokens"].wait()

    def fetch_side(k):
        return links.move(ws_in.at[pl.ds(pl.multiple_of(turns[k] * part, 8), part)], ws.at[k % 2])

    side_copies = [fetch_side(0), fetch_side(1)]
    ds_high[...], ds_low[...] = split2(ds[...])
    shares_t = []
    row_sum = jnp.zeros((tok, 1), F32)
    squares = jnp.zeros((tok, 1), F32)
    for k, turn in enumerate(turns):
        out = part_t.at[turn]
        product(2 * place.tp + k, turn, False, out)
        side_copies[k].wait()
        times_rows(ds_high, ds_low, ws.at[k % 2], out, False)
        if k + 2 < place.tp:
            side_copies.append(fetch_side(k + 2))
        if k < place.tp - 1:
            shares_t.append(links.remote(out, recv_t.at[k], column[k][0]))
        value = tokens[turn]
        row_sum = row_sum + jnp.sum(out[...] * gain[turn] * value, axis=1, keepdims=True)
        squares = squares + jnp.sum(value * value, axis=1, keepdims=True)
    row_sums[...] = jnp.where(lanes == 0, row_sum, 0.0).T[0:8, :]
    give_rows = [links.remote(row_sums, row_recv.at[k], device) for k, (device, _, _) in enumerate(column)]

    for copy in give_bc:
        copy.wait_recv()
    summed = bc_rows[share_of(place.z), :]
    for k in range(place.tp - 1):
        summed = summed + bc_recv[k]
    own_cols = pl.ds(pl.multiple_of(place.c * tok, 128), tok)
    ds_both[0:heads, own_cols] = ds[:, 2 * N :].T[0:heads, :]
    ds_both[heads : heads + share, own_cols] = summed
    ds_both[heads + share :, own_cols] = jnp.zeros((128 - heads - share, tok), F32)
    give_ds = links.remote(ds_both.at[:, own_cols], ds_both.at[:, own_cols], place.sibling())

    stores = [links.move(sum_o.finish(), grad_out)]

    settle = settling(p_recv, tok)

    def rows(group):
        return pl.ds(pl.multiple_of(group * per_pair, 8), per_pair)

    def homeward(value, home, back_ref):
        home[...] = pick(settle, value, NN)
        at = rows(place.f * 2 + place.c)
        copies = [links.remote(home.at[rows(to)], back_ref.at[at], device) for device, to, _ in plane]
        return copies + [links.move(home.at[at], back_ref.at[at])]

    value = tokens[place.z] + part_r[place.z]
    for k, copy in enumerate(shares_r):
        copy.wait_recv()
        value = value + recv_r[k]
    way_r = homeward(value, home_r, back_r)

    give_ds.wait_recv()
    sum_s = Scatter(place, links, blocks_s, s1a, s1b, s2a, s2b)
    ds_parts = split2(ds_both[...])
    for hop in sum_s.order():
        block = place.chip(*hop)
        sum_s.blocks[block] = dot_split(ds_parts, split2(n_pairs[block]), NT)
        sum_s.send(*hop)
    stores.append(links.move(sum_z.finish(), grad_z))
    sum_x.pass_on()

    for copy in shares_t + give_rows:
        copy.wait_recv()
    total = row_sums[...]
    d_normed = part_t[place.z]
    for k in range(place.tp - 1):
        total = total + row_recv[k]
        d_normed = d_normed + recv_t[k]
    row_sum = jnp.concatenate([total, jnp.zeros((120, tok), F32)], axis=0).T[:, 0:1]
    width = place.tp * part
    scale = lax.rsqrt(squares / width + EPSILON)
    scaled = tokens[place.z] * scale
    small[0:1, inner + 2 * N :] = jnp.sum(d_normed * scaled, axis=0, keepdims=True)
    loads["up"].wait()
    value = home_t[...] + scale * gain[place.z] * d_normed - scaled * (scale * scale * row_sum / width)
    way_t = homeward(value, home_t, back_t)
    sum_s.pass_on()

    steps_of = [[place.sibling()]]
    steps_of.append([place.at(0, d) for d in range(1, place.side)])
    steps_of.append([place.at(d, 0) for d in range(1, place.side)])
    slot = 0
    for devices in steps_of:
        copies = [links.remote(small, small_recv.at[slot + k], device) for k, device in enumerate(devices)]
        for copy in copies:
            copy.wait_recv()
        links.settle(copies)
        total = small[...]
        for k in range(len(devices)):
            total = total + small_recv[slot + k]
        small[...] = total
        slot += len(devices)
    bc_cols = pl.ds(inner, 2 * N)
    give_small = [links.remote(small.at[:, bc_cols], small_z.at[k], device) for k, (device, _, _) in enumerate(column)]

    stores.append(links.move(sum_x.finish(), grad_x))
    last = sum_s.finish()
    give_grad = [
        links.remote(last.at[pl.ds(heads, share)], bc_grad.at[share_of(place.z)], device) for device, _, _ in column
    ]
    bc_grad[share_of(place.z), :] = last[heads : heads + share, :]
    grad_dt[...] = last[...].T[:, :heads]

    leave = leaving(slots_in[...], tok, groups)
    for way, home, back_ref, out in ((way_r, home_r, back_r, result), (way_t, home_t, back_t, grad_input)):
        for copy in way[:-1]:
            copy.wait_recv()
        way[-1].wait()
        links.settle(way[:-1])
        home[...] = pick(leave, back_ref[...], NN)
        stores.append(links.move(home, out))
    for copy in give_small:
        copy.wait_recv()
    small_out[...] = small[...]
    over_tp = small[0:5, inner : inner + 2 * N]
    for k in range(place.tp - 1):
        over_tp = over_tp + small_z[k, 0:5, :]
    small_out[0:5, inner : inner + 2 * N] = over_tp
    for copy in give_grad:
        copy.wait_recv()
    grad_bc[...] = bc_grad[...].T
    for store in stores:
        store.wait()
    links.finish()


ANYWHERE = pl.BlockSpec(memory_space=pl.ANY)
INSIDE = pl.BlockSpec(memory_space=pltpu.VMEM)
SCALARS = pl.BlockSpec(memory_space=pltpu.SMEM)


def shape(*dims):
    return jax.ShapeDtypeStruct(dims, F32)


def floats(*dims):
    return pltpu.VMEM(dims, F32)


def halves(*dims):
    return pltpu.VMEM(dims, BF16)


def forward_call(sizes, lengths, slots, gain, params_c, params_s, inputs, cotangent, w_x, w_s, w_z, w_out):
    fsdp, _, tp = sizes
    tok, width = inputs.shape
    shard, inner = w_x.shape
    side = w_s.shape[1]
    depth = shard * 2 * fsdp
    part = width // tp
    copies = 4 * gather_copies(math.isqrt(fsdp)) + 3 * (2 * fsdp - 1) + 3 * (tp - 1) + 2 * fsdp + 3
    return pl.pallas_call(
        functools.partial(forward_kernel, sizes),
        out_shape=(
            shape(tp, tok, part),
            shape(tok, part),
            shape(fsdp, shard, 2 * tok),
            shape(fsdp, shard, 2 * tok),
            shape(tok, 128),
            shape(8 + tok, inner),
            shape(8 + tok, side),
            shape(tok, inner),
            shape(tok, 2 * N),
            shape(tok, inner),
            shape(tok, inner),
            shape(tok, inner),
            shape(inner, N),
            shape(1, inner),
            shape(depth, inner),
            shape(depth, side),
            shape(depth, inner),
            shape(depth, inner),
        ),
        in_specs=[SCALARS] + [INSIDE] * 4 + [ANYWHERE] * 6,
        out_specs=(
            [ANYWHERE] * 4 + [INSIDE] + [ANYWHERE] * 8 + [INSIDE] + [ANYWHERE] * 4
        ),
        scratch_shapes=[
            floats(depth, inner),
            floats(depth, side),
            floats(depth, inner),
            floats(depth, inner),
            floats(tok, part),
            floats(tok, part),
            floats(tok, part),
            floats(tok, part),
            floats(tok, 128),
            floats(tp, tok, part),
            floats(tp, tok, part),
            floats(tp, tok, part),
            halves(tp, tok, part),
            halves(tp, tok, part),
            floats(width, tok),
            floats(fsdp, shard, 2 * tok),
            floats(fsdp, shard, 2 * tok),
            floats(8 + tok, inner),
            floats(8 + tok, side),
            floats(8, inner),
            floats(8, side),
            floats(tok, inner),
            floats(tok, 2 * N),
            floats(tok, inner),
            floats(tok, 2 * N),
            floats(tok, 128),
            floats(2, 128, tok),
            floats(tok, tok),
            floats(tok, tok),
            floats(inner, N),
            floats(inner, N),
            floats(tok, inner),
            floats(tok, inner),
            floats(tok, inner),
            floats(8, tok),
            floats(tp - 1, 8, tok),
            pltpu.SemaphoreType.DMA((copies,)),
            pltpu.SemaphoreType.DMA((copies,)),
            pltpu.SemaphoreType.DMA((40 + 2 * fsdp,)),
        ],
        compiler_params=pltpu.CompilerParams(collective_id=0, has_side_effects=True, vmem_limit_bytes=VMEM_LIMIT),
        name="forward",
    )(lengths, slots, gain, params_c, params_s, inputs, cotangent, w_x, w_s, w_z, w_out)


def backward_call(sizes, heads, operands, tok, width, shard, inner, side):
    fsdp, _, tp = sizes
    grid = math.isqrt(fsdp)
    part = width // tp
    share = 2 * N // tp
    small_width = inner + 2 * N + part
    hops = grid - 1
    copies = 6 + 4 * (2 * hops * grid + 2 * hops) + 6 * tp + 2 * (2 * fsdp) + 2 * hops + 4

    def landing(rows, columns):
        return [
            floats(hops, grid, rows // 2, columns),
            floats(hops, grid, rows // 2, columns),
            floats(hops, rows // 2, columns),
            floats(hops, rows // 2, columns),
        ]

    return pl.pallas_call(
        functools.partial(backward_kernel, sizes, heads),
        out_shape=(
            shape(tok, part),
            shape(tok, part),
            shape(shard, inner),
            shape(shard, inner),
            shape(shard, 2 * N),
            shape(shard, heads),
            shape(shard, inner),
            shape(8, small_width),
        ),
        in_specs=[SCALARS] + [INSIDE] * 6 + [ANYWHERE] * 16,
        out_specs=(ANYWHERE, ANYWHERE, ANYWHERE, ANYWHERE, INSIDE, INSIDE, ANYWHERE, INSIDE),
        scratch_shapes=[
            floats(tp, tok, part),
            floats(fsdp, shard, 2 * tok),
            floats(fsdp, shard, 2 * tok),
            floats(8 + tok, inner),
            floats(8 + tok, side),
            floats(tok, inner),
            floats(tok, 2 * N),
            floats(inner, N),
            floats(2 * tok, inner),
            floats(2 * tok, inner),
            floats(128, 2 * tok),
            halves(2 * tok, inner),
            halves(2 * tok, inner),
            halves(shard, 2 * tok),
            halves(shard, 2 * tok),
            floats(fsdp, shard, inner),
            floats(fsdp, shard, inner),
            floats(fsdp, 128, shard),
            *landing(shard, inner),
            *landing(shard, inner),
            *landing(shard, inner),
            *landing(128, shard),
            floats(fsdp, shard, inner),
            floats(2, part, inner),
            floats(2, part, side),
            floats(tok, side),
            halves(tok, side),
            halves(tok, side),
            floats(2 * N, tok),
            floats(tp - 1, share, tok),
            floats(2 * N, shard),
            floats(tp, tok, part),
            floats(*((8, 128) if (fsdp, shard, 2 * tok) == (tp, tok, part) else (tp, tok, part))),
            floats(tp - 1, tok, part),
            floats(tp - 1, tok, part),
            floats(8, tok),
            floats(tp - 1, 8, tok),
            floats(tok, part),
            floats(tok, part),
            floats(tok, part),
            floats(tok, part),
            floats(inner, N),
            floats(inner, N),
            floats(tok, N),
            floats(tok, N),
            floats(8 + tok, inner),
            floats(8 + tok, 2 * N),
            floats(8, inner),
            floats(8, 2 * N),
            floats(tok, tok),
            floats(tok, tok),
            floats(tok, tok),
            floats(tok, 128),
            floats(tok, 128),
            floats(128, tok),
            floats(tok, 128),
            floats(tok, 128),
            floats(tok, 128),
            floats(128, tok),
            floats(1, inner),
            floats(8, small_width),
            floats(1 + 2 * hops, 8, small_width),
            floats(tp - 1, 8, 2 * N),
            pltpu.SemaphoreType.DMA((copies,)),
            pltpu.SemaphoreType.DMA((copies,)),
            pltpu.SemaphoreType.DMA((24 + 4 * tp,)),
        ],
        compiler_params=pltpu.CompilerParams(collective_id=1, has_side_effects=True, vmem_limit_bytes=VMEM_LIMIT),
        name="backward",
    )(*operands)


def shards(
    inputs,
    cotangent,
    seq_lengths,
    slots,
    gain_in,
    w_z,
    w_x,
    w_dt,
    w_bc,
    w_out,
    conv_x,
    conv_x_bias,
    conv_bc,
    conv_bc_bias,
    dt_bias,
    a_log,
    d_skip,
    gate_gain,
):
    sizes = (lax.axis_size("fsdp"), lax.axis_size("ctx"), lax.axis_size("tp"))
    tok, width = inputs.shape
    shard, inner = w_x.shape
    heads = w_dt.shape[1]
    tp = sizes[2]

    def lane_pad(value, lanes):
        return jnp.pad(value, ((0, 0), (0, lanes - value.shape[1])))

    w_s = jnp.concatenate([w_bc, lane_pad(w_dt, 128)], axis=1)
    slots_wide = jnp.broadcast_to(slots[:, None], (tok, 128))
    skip_wide = jnp.repeat(d_skip, inner // heads)
    params_c = jnp.concatenate(
        [conv_x, conv_x_bias[None], skip_wide[None], gate_gain[None], jnp.zeros((1, inner), F32)], axis=0
    )
    params_s = jnp.concatenate(
        [conv_bc, conv_bc_bias[None], lane_pad(dt_bias[None], 2 * N), lane_pad(a_log[None], 2 * N), jnp.zeros((1, 2 * N), F32)],
        axis=0,
    )
    (
        tokens,
        up,
        n_pairs,
        c_pairs,
        p_recv,
        pre_x,
        pre_s,
        conv_x_kept,
        conv_s_kept,
        normal_y,
        d_gate,
        d_mixed,
        state_in,
        gain_row,
        wx,
        ws,
        wz,
        wo,
    ) = forward_call(sizes, seq_lengths, slots_wide, gain_in[None], params_c, params_s, inputs, cotangent, w_x, w_s, w_z, w_out)
    operands = (
        seq_lengths,
        slots_wide,
        p_recv,
        gain_in.reshape(tp, 1, width // tp),
        params_c,
        params_s,
        gain_row,
        tokens,
        up,
        n_pairs,
        c_pairs,
        pre_x,
        pre_s,
        conv_x_kept,
        conv_s_kept,
        normal_y,
        d_gate,
        d_mixed,
        state_in,
        wx,
        ws,
        wz,
        wo,
    )
    result, grad_input, grad_z, grad_x, grad_bc, grad_dt, grad_out, small = backward_call(
        sizes, heads, operands, tok, width, shard, inner, w_s.shape[1]
    )
    bc = slice(inner, inner + 2 * N)
    head = slice(inner, inner + heads)
    return (
        result,
        grad_input,
        grad_z,
        grad_x,
        grad_dt,
        grad_bc,
        grad_out,
        small[0:4, :inner],
        small[4, :inner],
        small[0:4, bc],
        small[4, bc],
        small[5, head],
        small[6, head],
        small[7, head],
        small[5, :inner],
        small[0, inner + 2 * N :],
    )


def solution(mesh):
    return jax.shard_map(
        shards,
        mesh=mesh,
        in_specs=(
            P(("fsdp", "ctx"), None),
            P(("fsdp", "ctx"), None),
            P("fsdp", None),
            P(("fsdp", "ctx")),
            P(),
            P(("fsdp", "ctx"), "tp"),
            P(("fsdp", "ctx"), "tp"),
            P(("fsdp", "ctx"), "tp"),
            P(("fsdp", "ctx"), None),
            P(("fsdp", "ctx"), "tp"),
            P(None, "tp"),
            P("tp"),
            P(),
            P(),
            P("tp"),
            P("tp"),
            P("tp"),
            P("tp"),
        ),
        out_specs=(
            P(("fsdp", "ctx"), "tp"),
            P(("fsdp", "ctx"), "tp"),
            P(("fsdp", "ctx"), "tp"),
            P(("fsdp", "ctx"), "tp"),
            P(("fsdp", "ctx"), "tp"),
            P(("fsdp", "ctx"), None),
            P(("fsdp", "ctx"), "tp"),
            P(None, "tp"),
            P("tp"),
            P(),
            P(),
            P("tp"),
            P("tp"),
            P("tp"),
            P("tp"),
            P("tp"),
        ),
        check_vma=False,
    )
```

```python
import functools
import math

import jax
import jax.numpy as jnp
from jax import lax
from jax.experimental import pallas as pl
from jax.experimental.pallas import tpu as pltpu
from jax.sharding import PartitionSpec as P

N = 128
SPAN = 256
INNER = 4096
EPSILON = 1e-05
F32 = jnp.float32
BF16 = jnp.bfloat16
MESH = pl.DeviceIdType.MESH
NN = (((1,), (0,)), ((), ()))
NT = (((1,), (1,)), ((), ()))
TN = (((0,), (0,)), ((), ()))
VMEM_LIMIT = 62 << 20


def split2(value):
    high = value.astype(BF16)
    return high, (value - high.astype(F32)).astype(BF16)


def split3(value):
    high = value.astype(BF16)
    rest = value - high.astype(F32)
    middle = rest.astype(BF16)
    return high, middle, (rest - middle.astype(F32)).astype(BF16)


def dot1(left, right, dims):
    return lax.dot_general(left, right, dims, preferred_element_type=F32)


def dot_split(left, right, dims):
    (lh, ll), (rh, rl) = left, right
    return dot1(lh, rh, dims) + (dot1(lh, rl, dims) + dot1(ll, rh, dims))


def dot3(left, right, dims):
    return dot_split(split2(left), split2(right), dims)


def pick(table, value, dims):
    parts = split3(value)
    return dot1(table, parts[0], dims) + dot1(table, parts[1], dims) + dot1(table, parts[2], dims)


def iota(shape, dim):
    return lax.broadcasted_iota(jnp.int32, shape, dim)


class Place:
    def __init__(self, fsdp, ctx, tp):
        self.fsdp, self.n_ctx, self.tp = fsdp, ctx, tp
        self.side = math.isqrt(fsdp)
        assert self.side * self.side == fsdp and ctx == 2
        self.f = lax.axis_index("fsdp")
        self.c = lax.axis_index("ctx")
        self.z = lax.axis_index("tp")
        self.y, self.x = self.f // self.side, self.f % self.side

    def chip(self, dy, dx):
        side = self.side
        return ((self.y + dy + side) % side) * side + (self.x + dx + side) % side

    def block(self, dy, dx, core):
        return self.chip(dy, dx) * 2 + core

    def at(self, dy, dx):
        return (self.chip(dy, dx), self.c, self.z)

    def sibling(self):
        return (self.f, 1 - self.c, self.z)

    def plane(self):
        out = []
        for df in range(self.fsdp):
            for dc in range(2):
                if df or dc:
                    to_f = (self.f + df) % self.fsdp
                    from_f = (self.f - df + self.fsdp) % self.fsdp
                    core = (self.c + dc) % 2
                    out.append(((to_f, core, self.z), to_f * 2 + core, from_f * 2 + core))
        return out

    def column(self):
        out = []
        for dz in range(1, self.tp):
            to_z = (self.z + dz) % self.tp
            out.append(((self.f, self.c, to_z), to_z, (self.z - dz + self.tp) % self.tp))
        return out


class Links:
    def __init__(self, send, recv, local):
        self.send, self.recv, self.local = send, recv, local
        self.used, self.used_local = 0, 0
        self.open = []

    def remote(self, src, dst, device):
        k = self.used
        self.used += 1
        copy = pltpu.make_async_remote_copy(
            src_ref=src,
            dst_ref=dst,
            send_sem=self.send.at[k],
            recv_sem=self.recv.at[k],
            device_id=device,
            device_id_type=MESH,
        )
        copy.start()
        self.open.append(copy)
        return copy

    def plan(self, src, dst, device, lands_as=None):
        k = self.used
        self.used += 1
        copy = pltpu.make_async_remote_copy(
            src_ref=src,
            dst_ref=dst,
            send_sem=self.send.at[k],
            recv_sem=self.recv.at[k if lands_as is None else lands_as.slot],
            device_id=device,
            device_id_type=MESH,
        )
        copy.slot = k
        return copy

    def move(self, src, dst):
        k = self.used_local
        self.used_local += 1
        copy = pltpu.make_async_copy(src, dst, self.local.at[k])
        copy.start()
        return copy

    def settle(self, copies):
        for copy in copies:
            copy.wait_send()
            self.open = [other for other in self.open if other is not copy]

    def finish(self):
        assert self.used <= self.send.shape[0] and self.used_local <= self.local.shape[0]
        self.settle(list(self.open))


def greet(devices):
    barrier = pltpu.get_barrier_semaphore()
    for device in devices:
        pl.semaphore_signal(barrier, inc=1, device_id=device, device_id_type=MESH)


def greeted(devices):
    pl.semaphore_wait(pltpu.get_barrier_semaphore(), len(devices))


class Spread:
    def __init__(self, place, links, slices):
        self.place, self.links, self.slices = place, links, slices
        self.line = place.tp == 4
        z, mine = place.z, slices.at[place.z]
        if not self.line:
            self.copies = [links.remote(mine, mine, device) for device, _, _ in place.column()]
            return
        self.copies = [links.remote(mine, mine, (place.f, place.c, z ^ d)) for d in (1, 2)]
        self.inner = (z == 1) | (z == 2)
        across = links.plan(mine, mine, (place.f, place.c, 3 - z))
        onward = slices.at[z ^ 2]
        self.onward = links.plan(onward, onward, (place.f, place.c, z ^ 1), across)
        self.across = across

        @pl.when(self.inner)
        def _():
            across.start()

    def forward(self):
        if self.line:
            self.copies.pop().wait_recv()

            @pl.when(self.inner)
            def _():
                self.onward.start()

    def finish(self):
        for copy in self.copies:
            copy.wait_recv()
        if self.line:
            self.across.wait_recv()

            @pl.when(self.inner)
            def _():
                self.across.wait_send()
                self.onward.wait_send()


class Gather:
    def __init__(self, place, links, shard, whole):
        self.place, self.links, self.shard, self.whole = place, links, shard, whole
        self.rows = shard.shape[0]
        self.near = 0

    def rows_of(self, block, start=0, count=None):
        count = self.rows if count is None else count
        return self.whole.at[pl.ds(pl.multiple_of(block * self.rows + start, 8), count)]

    def start(self):
        p, steps = self.place, range(1, self.place.side)
        mine = self.rows_of(p.block(0, 0, p.c))
        self.row = [self.links.remote(self.shard, mine, p.at(0, d)) for d in steps]
        self.col = [self.links.remote(self.shard, mine, p.at(d, 0)) for d in steps]
        self.pair = [self.links.remote(self.shard, mine, p.sibling())]
        self.own = self.links.move(self.shard, mine)

    def forward(self):
        p, steps, half = self.place, range(1, self.place.side), self.rows // 2
        self.half_a, self.half_b = [], []
        for k, d in enumerate(steps):
            self.row[k].wait_recv()
            block = p.block(0, -d, p.c)
            part = self.rows_of(block, 0, half)
            self.half_a += [self.links.remote(part, part, p.at(e, 0)) for e in steps]
            whole = self.rows_of(block)
            self.pair.append(self.links.remote(whole, whole, p.sibling()))
        for k, e in enumerate(steps):
            self.col[k].wait_recv()
            block = p.block(-e, 0, p.c)
            part = self.rows_of(block, half, half)
            self.half_b += [self.links.remote(part, part, p.at(0, d)) for d in steps]
            whole = self.rows_of(block)
            self.pair.append(self.links.remote(whole, whole, p.sibling()))

    def share(self):
        p, steps, half = self.place, range(1, self.place.side), self.rows // 2
        k = 0
        for d in steps:
            for e in steps:
                self.half_a[k].wait_recv()
                part = self.rows_of(p.block(-e, -d, p.c), 0, half)
                self.pair.append(self.links.remote(part, part, p.sibling()))
                k += 1
        k = 0
        for e in steps:
            for d in steps:
                self.half_b[k].wait_recv()
                part = self.rows_of(p.block(-e, -d, p.c), half, half)
                self.pair.append(self.links.remote(part, part, p.sibling()))
                k += 1

    def finish_near(self):
        self.own.wait()
        self.near = 1 + 2 * (self.place.side - 1)
        for copy in self.pair[: self.near]:
            copy.wait_recv()

    def finish(self):
        if self.near == 0:
            self.finish_near()
        for copy in self.pair[self.near :]:
            copy.wait_recv()


def gather_copies(side):
    steps = side - 1
    return 4 * steps + 1 + 4 * steps * steps


def down_lanes(row):
    return jnp.broadcast_to(row, (128, row.shape[1])).T


def leaving(slots, tok, groups):
    slots = down_lanes(slots.astype(F32)).astype(jnp.int32)
    targets = slots >> (tok.bit_length() - 1)
    member = (targets == iota((tok, 128), 1)).astype(F32)
    earlier = (iota((tok, tok), 0) > iota((tok, tok), 1)).astype(BF16)
    ranks = jnp.sum(dot1(earlier, member.astype(BF16), NN) * member, axis=1, keepdims=True)
    send_at = (targets[:, :1] * (tok // groups)).astype(F32) + ranks
    leave = (send_at == iota((tok, tok), 1).astype(F32)).astype(BF16)
    return leave, (slots - targets * tok).astype(F32)


def settling(places, tok):
    return (places[:, :1] == iota((tok, tok), 1).astype(F32)).astype(BF16)


def halve(value_ref, high, low):
    @pl.loop(0, value_ref.shape[1] // 128)
    def _(n):
        cols = pl.ds(pl.multiple_of(n * 128, 128), 128)
        high[:, cols], low[:, cols] = split2(value_ref[:, cols])


def project(left_high, left_low, whole, chips, out, tile, first_row, fresh):
    _, rows, width = left_high.shape

    @pl.loop(0, whole.shape[1] // tile)
    def _(n):
        cols = pl.ds(pl.multiple_of(n * tile, 128), tile)
        total = jnp.zeros((rows, tile), F32) if fresh else out[first_row : first_row + rows, cols]
        for chip in chips:
            at = pl.ds(chip * width if isinstance(chip, int) else pl.multiple_of(chip * width, 8), width)
            total = total + dot_split((left_high[chip], left_low[chip]), split2(whole[at, cols]), NN)
        out[first_row : first_row + rows, cols] = total


def weight_block(left_ref, high, low, left_high, left_low, out):
    left_high[...], left_low[...] = split2(left_ref[...])

    @pl.loop(0, high.shape[1] // 256)
    def _(n):
        cols = pl.ds(pl.multiple_of(n * 256, 128), 256)
        out[:, cols] = dot_split((left_high[...], left_low[...]), (high[:, cols], low[:, cols]), NN)


def times_rows(high, low, rows_ref, out, fresh):
    tile = min(256, rows_ref.shape[0])
    for n in range(rows_ref.shape[0] // tile):
        at = slice(n * tile, (n + 1) * tile)
        value = dot_split((high[...], low[...]), split2(rows_ref[at, :]), NT)
        out[:, at] = value if fresh else out[:, at] + value


def silu_slope(value):
    gate = jax.nn.sigmoid(value)
    return gate * (1.0 + value * (1.0 - gate))


def softplus(value):
    return jnp.maximum(value, 0.0) + jnp.log1p(jnp.exp(-jnp.abs(value)))


def segments(lengths, position):
    bound, seg = 0, jnp.zeros_like(position)
    for k in range(lengths.shape[1]):
        bound = bound + lengths[0, k]
        seg = seg + (bound <= position).astype(jnp.int32)
    return seg


def same_before(lengths, first, tok, distance):
    position = first + iota((tok, 128), 0)
    return (segments(lengths, position) == segments(lengths, position - distance)).astype(F32)


def wide(table, width):
    return jnp.concatenate([table] * (width // 128), axis=1)


def column_of(table, head):
    lanes = iota(table.shape, 1)
    return jnp.sum(jnp.where(lanes == head, table, 0.0), axis=1, keepdims=True)


def pair_columns(table, pair):
    first, second = column_of(table, 2 * pair), column_of(table, 2 * pair + 1)
    return jnp.where(iota(table.shape, 1) < 64, first, second)


class Steps:
    def __init__(self, raw, params_s, lengths, first):
        tok = raw.shape[0]
        shifted = raw + params_s[5:6, :128]
        self.slope = jax.nn.sigmoid(shifted)
        self.step = softplus(shifted)
        self.rate = -jnp.exp(params_s[6:7, :128])
        until = (iota((tok, tok), 0) >= iota((tok, tok), 1)).astype(BF16)
        self.total = pick(until, self.step * self.rate, NN)
        position = first + iota((tok, 128), 0)
        seg = segments(lengths, position)
        before = segments(lengths, jnp.full((tok, 128), first - 1, jnp.int32))
        last = segments(lengths, jnp.full((tok, 128), first + tok - 1, jnp.int32))
        self.reading = jnp.exp(self.total) * (seg == before).astype(F32)
        self.fading = jnp.exp(self.total[tok - 1 : tok] - self.total) * (seg == last).astype(F32)
        self.tail = self.fading * self.step


def closed(lengths, first, tok, flipped):
    rows, cols = first + iota((tok, tok), 0), first + iota((tok, tok), 1)
    order = rows <= cols if flipped else rows >= cols
    seg_rows = segments(lengths, first + iota((tok, 1), 0))
    seg_cols = segments(lengths, first + iota((1, tok), 1))
    return jnp.where(order & (seg_rows == seg_cols), 0.0, -1e30)


def convolve(padded, params, lengths, first, conv, act):
    tok, tile = conv.shape[0], 128
    same = [same_before(lengths, first, tok, 3 - k) for k in range(3)]

    @pl.loop(0, conv.shape[1] // tile)
    def _(n):
        cols = pl.ds(pl.multiple_of(n * tile, 128), tile)
        total = params[4:5, cols] + params[3:4, cols] * padded[8 : 8 + tok, cols]
        for k in range(3):
            total = total + params[k : k + 1, cols] * (padded[5 + k : 5 + k + tok, cols] * same[k])
        conv[:, cols] = total
        act[:, cols] = total * jax.nn.sigmoid(total)


def forward_kernel(
    sizes,
    lengths,
    slots_in,
    gain,
    taps_x,
    bias_x,
    taps_s,
    bias_s,
    dt_bias,
    a_log,
    d_skip,
    gate_gain,
    w_bc,
    w_dt,
    x_in,
    c_in,
    w_x,
    w_z,
    w_out,
    params_c,
    params_s,
    tokens_out,
    up_out,
    n_pairs_out,
    p_recv,
    pre_x_out,
    pre_s_out,
    raw_out,
    conv_x_out,
    conv_s_out,
    ny_out,
    z_out,
    mixed_out,
    dn_out,
    gscale_out,
    inner_out,
    state_out,
    g_out,
    wx_out,
    ws_out,
    wz_out,
    wo_out,
    wx,
    ws,
    wz,
    wo,
    ws_own,
    ws_turned,
    x_own,
    c_own,
    x_sort,
    c_sort,
    p_sort,
    x_recv,
    c_recv,
    tokens,
    n_high,
    n_low,
    turned,
    n_pairs,
    c_pairs,
    pre_x,
    pre_s,
    raw,
    bc_rows,
    tail_x,
    tail_s,
    conv_x,
    conv_s,
    act_x,
    act_s,
    totals,
    step_rows,
    open_,
    scores,
    state,
    state_in,
    mixed,
    gate_pre,
    d_normal,
    ny_both,
    high,
    low,
    left_high,
    left_low,
    block_out,
    sums,
    sums_recv,
    send,
    recv,
    local,
):
    place = Place(*sizes)
    links = Links(send, recv, local)
    tok, groups = x_own.shape[0], 2 * place.fsdp
    per_pair = tok // groups
    part = x_own.shape[1]
    inner = act_x.shape[1]
    pairs = inner // 128
    heads = d_skip.shape[1]
    share = 2 * N // place.tp
    shard_rows = n_pairs.shape[1]
    chip_rows = 2 * shard_rows
    first = place.c * tok
    lanes = iota((tok, 128), 1)
    part_cols = pl.ds(pl.multiple_of(place.z * part, 128), part)
    load_x = links.move(x_in.at[:, part_cols], x_own)
    load_c = links.move(c_in.at[:, part_cols], c_own)
    plane, column = place.plane(), place.column()
    partners = [entry[0] for entry in plane] + [entry[0] for entry in column]
    greet(partners)

    leave, place_of = leaving(slots_in[...], tok, groups)
    p_sort[...] = dot1(leave, place_of.astype(BF16), TN)
    load_x.wait()
    x_sort[...] = pick(leave, x_own[...], TN)

    def share_of(turn):
        return pl.ds(pl.multiple_of(turn * share, 8), share)

    bc_rows[:, 0:shard_rows] = w_bc[...].T
    ws_own[...] = jnp.zeros_like(ws_own)
    ws_own[:, 0:heads] = w_dt[...]
    ws_turned[...] = ws_own[...].T
    ws_turned[heads : heads + share, :] = bc_rows[share_of(place.z), 0:shard_rows]
    ws_own[...] = ws_turned[...].T

    greeted(partners)
    g_x, g_s, g_z, g_o = [Gather(place, links, shard, whole) for shard, whole in ((w_x, wx), (ws_own, ws), (w_z, wz), (w_out, wo))]

    def rows(group):
        return pl.ds(pl.multiple_of(group * per_pair, 8), per_pair)

    def route(source, target):
        mine = rows(place.f * 2 + place.c)
        copies = [links.remote(source.at[rows(to)], target.at[mine], device) for device, to, _ in plane]
        return copies, links.move(source.at[mine], target.at[mine])

    routes_x = [route(p_sort, p_recv), route(x_sort, x_recv.at[place.z])]
    g_x.start()
    g_s.start()
    load_c.wait()
    c_sort[...] = pick(leave, c_own[...], TN)
    routes_c = [route(c_sort, c_recv.at[place.z])]

    params_c[0:4, :] = taps_x[...]
    params_c[4:5, :] = bias_x[...]
    params_c[6:7, :] = gate_gain[...]
    params_c[7:8, :] = jnp.zeros((1, inner), F32)
    for q in range(pairs):
        both = [d_skip[0:1, 2 * q + s : 2 * q + s + 1] for s in range(2)]
        params_c[5:6, q * 128 : (q + 1) * 128] = jnp.where(lanes[0:1] < 64, both[0], both[1])
    params_s[...] = jnp.zeros_like(params_s)
    params_s[0:4, :] = taps_s[...]
    params_s[4:5, :] = bias_s[...]
    params_s[5:6, 0:heads] = dt_bias[...]
    params_s[6:7, 0:heads] = a_log[...]

    def arrive(routes):
        for copies, own in routes:
            own.wait()
            for copy in copies:
                copy.wait_recv()

    arrive(routes_x)
    spread_x = Spread(place, links, x_recv)
    g_x.forward()
    g_s.forward()
    g_z.start()
    spread_x.forward()
    arrive(routes_c)
    g_s.share()
    stores = []
    spread_x.finish()
    settle = settling(p_recv, tok)
    squares = jnp.zeros((tok, 1), F32)
    for k in range(place.tp):
        value = pick(settle, x_recv[k], TN)
        tokens[k] = value
        squares = squares + jnp.sum(value * value, axis=1, keepdims=True)
    scale = lax.rsqrt(squares / (place.tp * part) + EPSILON)
    own_cols = pl.ds(pl.multiple_of(place.c * tok, 128), tok)
    own_rows = pl.ds(pl.multiple_of(place.c * tok, 128), tok)
    chips_here = part // chip_rows

    def keep_left(k, value):
        for j in range(chips_here):
            piece = value[:, j * chip_rows : (j + 1) * chip_rows]
            n_high[k * chips_here + j], n_low[k * chips_here + j] = split2(piece)
        turned[k * part : (k + 1) * part, :] = value.T

    def exchange_blocks(pairs_ref):
        copies, kept = [], []
        for q in range(place.fsdp):
            there = turned.at[pl.ds(pl.multiple_of((2 * q + 1 - place.c) * shard_rows, 8), shard_rows)]
            here = turned.at[pl.ds(pl.multiple_of((2 * q + place.c) * shard_rows, 8), shard_rows)]
            copies.append(links.remote(there, pairs_ref.at[q, :, own_cols], place.sibling()))
            kept.append(links.move(here, pairs_ref.at[q, :, own_cols]))
        return copies, kept

    for k in range(place.tp):
        keep_left(k, tokens[k] * scale * gain[:, k * part : (k + 1) * part])
    pairs_n, kept_n = exchange_blocks(n_pairs)
    stores.append(links.move(tokens, tokens_out))

    every = list(range(place.fsdp))
    g_s.finish()
    project(n_high, n_low, ws, every, raw, 128, 0, True)
    bc_turned = raw[...].T
    bc_rows[share_of(place.z), :] = bc_turned[heads : heads + share]
    mine = bc_rows.at[share_of(place.z)]
    spread_bc = [links.remote(mine, mine, device) for device, _, _ in column]
    spread_c = Spread(place, links, c_recv)
    g_x.share()
    g_x.finish()
    stores += [links.move(wx, wx_out), links.move(ws, ws_out)]
    project(n_high, n_low, wx, every, pre_x, 256, 8, True)
    halo = [links.remote(pre_x.at[pl.ds(tok, 8)], tail_x, place.sibling())]
    g_z.forward()
    g_o.start()

    raw[...] = jnp.where(lanes < heads, raw[...], 0.0)
    steps = Steps(raw[...], params_s, lengths, first)
    totals[...] = steps.total
    step_rows[0] = steps.total.T
    step_rows[1] = steps.step.T
    open_[...] = closed(lengths, first, tok, False)
    for copy in spread_bc:
        copy.wait_recv()
    pre_s[8 : 8 + tok, :] = bc_rows[...].T
    halo.append(links.remote(pre_s.at[pl.ds(tok, 8)], tail_s, place.sibling()))
    for copy in halo:
        copy.wait_recv()
    second = (place.c > 0).astype(F32)
    pre_x[0:8, :] = tail_x[...] * second
    pre_s[0:8, :] = tail_s[...] * second
    convolve(pre_s, params_s, lengths, first, conv_s, act_s)
    convolve(pre_x, params_c, lengths, first, conv_x, act_x)
    b_parts = split2(act_s[:, :N])
    c_parts = split2(act_s[:, N:])
    scores[...] = dot_split(c_parts, b_parts, NT)
    tail_table, reading_table = steps.tail, steps.reading

    @pl.loop(0, pairs)
    def _(q):
        cols = pl.ds(pl.multiple_of(q * 128, 128), 128)
        faded = act_x[:, cols] * pair_columns(tail_table, q)
        state[cols, :] = dot_split(split2(faded), b_parts, TN)

    pass_state = links.remote(state, state_in, place.sibling())
    spread_c.forward()
    pass_state.wait_recv()

    @pl.loop(0, pairs)
    def _(q):
        cols = pl.ds(pl.multiple_of(q * 128, 128), 128)
        channels = act_x[:, cols]
        entered = state_in[cols, :] * second
        state_in[cols, :] = entered
        out = params_c[5:6, cols] * channels
        out = out + pair_columns(reading_table, q) * dot_split(c_parts, split2(entered), NT)
        for s in range(2):
            head = 2 * q + s
            gaps = column_of(totals[...], head) - step_rows[0, pl.ds(head, 1), :] + open_[...]
            weights = jnp.exp(gaps) * scores[...] * step_rows[1, pl.ds(head, 1), :]
            own = jnp.where((lanes < 64) == (s == 0), channels, 0.0)
            out = out + dot3(weights, own, NN)
        mixed[:, cols] = out

    stores += [
        links.move(pre_x, pre_x_out),
        links.move(pre_s, pre_s_out),
        links.move(raw, raw_out),
        links.move(conv_x, conv_x_out),
        links.move(conv_s, conv_s_out),
        links.move(state_in, state_out),
        links.move(mixed, mixed_out),
    ]
    g_z.share()
    g_z.finish()
    stores.append(links.move(wz, wz_out))
    project(n_high, n_low, wz, every, gate_pre, 256, 0, True)
    stores.append(links.move(gate_pre, z_out))

    def over_tiles(body, carry):
        def step(n, carry):
            return body(pl.ds(pl.multiple_of(n * 128, 128), 128), carry)

        return lax.fori_loop(0, pairs, step, carry)

    def gated_at(cols):
        z = gate_pre[:, cols]
        return mixed[:, cols] * (z * jax.nn.sigmoid(z))

    def add_squares(cols, total):
        gated = gated_at(cols)
        return total + gated * gated

    zeros = jnp.zeros((tok, 128), F32)
    square_sum = over_tiles(add_squares, zeros)
    sums[...] = jnp.broadcast_to(jnp.sum(square_sum, axis=1, keepdims=True), (tok, 128)).T[0:8, :]
    copies = [links.remote(sums, sums_recv.at[k], device) for k, (device, _, _) in enumerate(column)]

    spread_c.finish()
    for copy in pairs_n:
        copy.wait_recv()
    links.settle(pairs_n)
    for copy in kept_n:
        copy.wait()
    stores.append(links.move(n_pairs, n_pairs_out))
    for k in range(place.tp):
        upstream = pick(settle, c_recv[k], TN)
        keep_left(k, upstream)

        @pl.when(place.z == k)
        def _():
            x_own[...] = upstream

    pairs_c, kept_c = exchange_blocks(c_pairs)
    stores.append(links.move(x_own, up_out))

    for copy in copies:
        copy.wait_recv()
    total = sums[...]
    for k in range(place.tp - 1):
        total = total + sums_recv[k]
    gscale = lax.rsqrt(down_lanes(total[0:1]) / INNER + EPSILON)
    gscale_out[...] = gscale

    def normalise(cols, carry):
        ny_both[own_rows, cols] = gated_at(cols) * gscale * params_c[6:7, cols]
        return carry

    over_tiles(normalise, 0)
    g_o.forward()
    give_ny = links.remote(ny_both.at[own_rows], ny_both.at[own_rows], place.sibling())
    stores.append(links.move(ny_both.at[own_rows], ny_out))

    near = [place.f] + [place.chip(0, d) for d in range(1, place.side)] + [place.chip(d, 0) for d in range(1, place.side)]
    far = [place.chip(e, d) for e in range(1, place.side) for d in range(1, place.side)]
    for copy in kept_c:
        copy.wait()
    for copy in pairs_c:
        copy.wait_recv()
    give_ny.wait_recv()
    halve(ny_both, high, low)
    saved = []
    for q in range(place.fsdp):
        if q >= 2:
            saved[q - 2].wait()
        weight_block(c_pairs.at[q], high, low, left_high, left_low, block_out.at[q % 2])
        saved.append(links.move(block_out.at[q % 2], g_out.at[q]))
    stores += saved[-2:]
    g_o.share()
    g_o.finish_near()
    project(n_high, n_low, wo, near, d_normal, 256, 0, True)
    g_o.finish()
    project(n_high, n_low, wo, far, d_normal, 256, 0, False)
    stores.append(links.move(wo, wo_out))
    stores.append(links.move(d_normal, dn_out))

    def add_inner(cols, total):
        return total + d_normal[:, cols] * params_c[6:7, cols] * gated_at(cols)

    inner_sum = over_tiles(add_inner, zeros)
    inner_out[...] = jnp.broadcast_to(jnp.sum(inner_sum, axis=1, keepdims=True), (tok, 128)).T[0:8, :]
    for store in stores:
        store.wait()
    links.finish()


class Scatter:
    def __init__(self, place, links, blocks, first_a, first_b, second_a, second_b):
        self.place, self.links, self.blocks = place, links, blocks
        self.first = (first_a, first_b)
        self.second = (second_a, second_b)
        self.half = blocks.shape[1] // 2
        self.source = blocks
        self.copies_a, self.copies_b = {}, {}

    def order(self):
        side = self.place.side
        hops = [(dy, dx) for dy in range(side) for dx in range(side)]
        return sorted(hops, key=lambda hop: -(hop[0] > 0) - (hop[1] > 0))

    def halves(self, dy, dx, source=None):
        ref = (self.blocks if source is None else source).at[self.place.chip(dy, dx)]
        return ref.at[pl.ds(0, self.half)], ref.at[pl.ds(self.half, self.half)]

    def send(self, dy, dx):
        p, side = self.place, self.place.side
        upper, lower = self.halves(dy, dx, self.source)
        if dy:
            target = self.first[0].at[dy - 1, (p.x + dx) % side]
            self.copies_a[dy, dx] = self.links.remote(upper, target, p.at(dy, 0))
        if dx:
            target = self.first[1].at[dx - 1, (p.y + dy) % side]
            self.copies_b[dy, dx] = self.links.remote(lower, target, p.at(0, dx))

    def pass_on(self):
        p, side = self.place, self.place.side
        self.last_a, self.last_b = [], []
        for d in list(range(1, side)) + [0]:
            upper, _ = self.halves(0, d)
            total = upper[...]
            for e in range(1, side):
                self.copies_a[e, d].wait_recv()
                total = total + self.first[0][e - 1, (p.x + d) % side]
            upper[...] = total
            if d:
                self.last_a.append(self.links.remote(upper, self.second[0].at[d - 1], p.at(0, d)))
            _, lower = self.halves(d, 0)
            total = lower[...]
            for e in range(1, side):
                self.copies_b[d, e].wait_recv()
                total = total + self.first[1][e - 1, (p.y + d) % side]
            lower[...] = total
            if d:
                self.last_b.append(self.links.remote(lower, self.second[1].at[d - 1], p.at(d, 0)))

    def finish(self):
        for k, (copies, part) in enumerate(zip((self.last_a, self.last_b), self.halves(0, 0))):
            total = part[...]
            for d, copy in enumerate(copies):
                copy.wait_recv()
                total = total + self.second[k][d]
            part[...] = total
        return self.blocks.at[self.place.chip(0, 0)]


def backward_kernel(
    sizes,
    heads,
    lengths,
    slots_in,
    p_recv,
    gain,
    params_c,
    params_s,
    gscale_in,
    inner_in,
    tokens_in,
    up_in,
    n_pairs_in,
    pre_x_in,
    pre_s_in,
    raw_in,
    conv_x_in,
    conv_s_in,
    ny_in,
    z_in,
    mixed_in,
    dn_in,
    state_in_hbm,
    g_in,
    wx_in,
    ws_in,
    wz_in,
    wo_in,
    result,
    grad_input,
    grad_z,
    grad_x,
    grad_bc,
    grad_dt,
    grad_out,
    small_out,
    gain_out,
    tokens,
    n_pairs,
    pre_x,
    pre_s,
    raw,
    conv_x,
    conv_s,
    state_in,
    dx_both,
    dz_both,
    ds_both,
    high,
    low,
    left_high,
    left_low,
    blocks_o,
    blocks_z,
    blocks_s,
    o1a, o1b, o2a, o2b,
    z1a, z1b, z2a, z2b,
    x1a, x1b, x2a, x2b,
    s1a, s1b, s2a, s2b,
    blocks_x,
    stream,
    ws,
    d_bc,
    ds_high,
    ds_low,
    bc_rows,
    bc_recv,
    bc_grad,
    part_r,
    part_t,
    recv_r,
    recv_t,
    row_sums,
    row_recv,
    inner_recv,
    home_r,
    home_t,
    back_r,
    back_t,
    d_state,
    d_state_recv,
    d_b,
    d_c,
    pad_x,
    pad_s,
    head_x,
    head_s,
    open_,
    scores,
    d_scores,
    totals,
    steps_col,
    total_rows,
    grad_total,
    grad_step,
    grad_tail,
    grad_rows,
    skip_row,
    gain_row,
    small,
    small_recv,
    small_z,
    gain_own,
    gain_recv,
    send,
    recv,
    local,
):
    place = Place(*sizes)
    links = Links(send, recv, local)
    tok, groups = tokens.shape[1], 2 * place.fsdp
    per_pair = tok // groups
    part = tokens.shape[2]
    inner = conv_x.shape[1]
    pairs = inner // 128
    first = place.c * tok
    own_rows = pl.ds(pl.multiple_of(place.c * tok, 128), tok)
    plane, column = place.plane(), place.column()

    partners = [entry[0] for entry in plane] + [entry[0] for entry in column]
    greet(partners)
    dz_own, dm_own = dz_both.at[own_rows], pad_x.at[pl.ds(0, tok)]

    loads = {}
    for name, src, dst in (
        ("ny", ny_in, dx_both.at[own_rows]),
        ("raw", raw_in, raw),
        ("conv_s", conv_s_in, conv_s),
        ("mixed", mixed_in, conv_x),
        ("z", z_in, dz_own),
        ("dn", dn_in, dm_own),
        ("state", state_in_hbm, state_in),
        ("n_pairs", n_pairs_in, n_pairs),
        ("g", g_in, blocks_o),
        ("pre_x", pre_x_in, pre_x),
        ("pre_s", pre_s_in, pre_s),
        ("tokens", tokens_in, tokens),
        ("up", up_in, home_t),
        ("ws", ws_in, ws),
    ):
        loads[name] = links.move(src, dst)

    turns = [(place.z + d + 1) % place.tp for d in range(place.tp)]
    schedule = [(weight, turn) for weight in (wo_in, wz_in, wx_in) for turn in turns]
    fetched = []

    def fetch():
        k = len(fetched)
        if k < len(schedule):
            weight, turn = schedule[k]
            src = weight.at[pl.ds(pl.multiple_of(turn * part, 8), part)]
            fetched.append(links.move(src, stream.at[k % 2]))

    fetch()
    fetch()

    def weight_slice(k):
        fetched[k].wait()
        return stream.at[k % 2]

    greeted(partners)
    sum_o = Scatter(place, links, blocks_o, o1a, o1b, o2a, o2b)
    sum_o.source = g_in
    give_inner = [links.remote(inner_in, inner_recv.at[k], device) for k, (device, _, _) in enumerate(column)]
    for hop in sum_o.order():
        sum_o.send(*hop)

    loads["raw"].wait()
    loads["conv_s"].wait()
    steps = Steps(raw[...], params_s, lengths, first)
    totals[...] = steps.total
    steps_col[...] = steps.step
    total_rows[...] = steps.total.T
    open_[...] = closed(lengths, first, tok, True)
    act_s = conv_s[...] * jax.nn.sigmoid(conv_s[...])
    b_parts, c_parts = split2(act_s[:, :N]), split2(act_s[:, N:])
    scores[...] = dot_split(b_parts, c_parts, NT)
    reading_table, tail_table = steps.reading, steps.tail
    grad_total[...] = jnp.zeros((tok, 128), F32)
    grad_step[...] = jnp.zeros((tok, 128), F32)
    grad_tail[...] = jnp.zeros((tok, 128), F32)
    d_c[...] = jnp.zeros((tok, N), F32)
    d_b[...] = jnp.zeros((tok, N), F32)
    d_scores[...] = jnp.zeros((tok, tok), F32)
    grad_rows[...] = jnp.zeros((128, tok), F32)
    lanes = iota((tok, 128), 1)

    def put(ref, head, value):
        ref[...] = ref[...] + jnp.where(lanes == head, value, 0.0)

    def by_head(value, s):
        return jnp.sum(jnp.where((lanes < 64) == (s == 0), value, 0.0), axis=1, keepdims=True)

    loads["ny"].wait()
    halve(dx_both.at[own_rows], high.at[own_rows], low.at[own_rows])

    def product(k, turn, fresh, out):
        ref = weight_slice(k)
        times_rows(high.at[own_rows], low.at[own_rows], ref, out, fresh)
        fetch()

    shares_r = []
    for k, turn in enumerate(turns):
        product(k, turn, True, part_r.at[turn])
        if k < place.tp - 1:
            shares_r.append(links.remote(part_r.at[turn], recv_r.at[k], column[k][0]))

    for copy in give_inner:
        copy.wait_recv()
    for name in ("mixed", "z", "dn"):
        loads[name].wait()
    total = inner_in[...]
    for k in range(place.tp - 1):
        total = total + inner_recv[k]
    gscale = gscale_in[...]
    pull = gscale * gscale * gscale * down_lanes(total[0:1]) / INNER

    @pl.loop(0, pairs)
    def _(n):
        cols = pl.ds(pl.multiple_of(n * 128, 128), 128)
        z, y, upward, weight = dz_own[:, cols], conv_x[:, cols], dm_own[:, cols], params_c[6:7, cols]
        gate = jax.nn.sigmoid(z)
        act = z * gate
        gated = y * act
        d_gated = gscale * weight * upward - gated * pull
        dm_own[:, cols] = d_gated * act
        dz_own[:, cols] = d_gated * y * gate * (1.0 + z * (1.0 - gate))
        gain_row[:, cols] = jnp.sum(upward * gated * gscale, axis=0, keepdims=True)

    give_dz = links.remote(dz_own, dz_own, place.sibling())
    loads["conv_x"] = links.move(conv_x_in, conv_x)

    loads["state"].wait()

    @pl.loop(0, pairs)
    def _(q):
        cols = pl.ds(pl.multiple_of(q * 128, 128), 128)
        upward = pad_x[0:tok, cols] * pair_columns(reading_table, q)
        parts = split2(upward)
        entered = split2(state_in[cols, :])
        d_c[...] = d_c[...] + dot_split(parts, entered, NN)
        d_state[cols, :] = dot_split(parts, c_parts, TN)
        read = upward * dot_split(c_parts, entered, NT)
        for s in range(2):
            put(grad_total, 2 * q + s, by_head(read, s))

    give_state = links.remote(d_state, d_state_recv, place.sibling())

    def spread_blocks(scatter, pairs_ref, both):
        halve(both, high, low)
        for hop in scatter.order():
            block = place.chip(*hop)
            weight_block(pairs_ref.at[block], high, low, left_high, left_low, scatter.blocks.at[block])
            scatter.send(*hop)

    loads["n_pairs"].wait()
    give_dz.wait_recv()
    sum_z = Scatter(place, links, blocks_z, z1a, z1b, z2a, z2b)
    spread_blocks(sum_z, n_pairs, dz_both)
    for k, turn in enumerate(turns):
        product(place.tp + k, turn, True, part_t.at[turn])

    loads["conv_x"].wait()
    give_state.wait_recv()
    first_half = (place.c == 0).astype(F32)

    @pl.loop(0, pairs)
    def _(q):
        cols = pl.ds(pl.multiple_of(q * 128, 128), 128)
        conv = conv_x[:, cols]
        gate = jax.nn.sigmoid(conv)
        channels = conv * gate
        upward = pad_x[0:tok, cols]
        ended = split2(d_state_recv[cols, :] * first_half)
        tail = pair_columns(tail_table, q)
        from_end = dot_split(b_parts, ended, NT)
        d_b[...] = d_b[...] + dot_split(split2(channels * tail), ended, NN)
        into = params_c[5:6, cols] * upward + tail * from_end
        skip_row[:, cols] = jnp.sum(upward * channels, axis=0, keepdims=True)
        end_part = channels * from_end
        x_parts = split2(channels)
        for s in range(2):
            head = 2 * q + s
            put(grad_tail, head, by_head(end_part, s))
            step_col = column_of(steps_col[...], head)
            gaps = total_rows[pl.ds(head, 1), :] - column_of(totals[...], head) + open_[...]
            decay = jnp.exp(gaps)
            up_parts = split2(jnp.where((lanes < 64) == (s == 0), upward, 0.0))
            reach = dot_split(x_parts, up_parts, NT) * decay
            d_scores[...] = d_scores[...] + reach * step_col
            reach = reach * scores[...]
            put(grad_step, head, jnp.sum(reach, axis=1, keepdims=True))
            grad_rows[pl.ds(head, 1), :] = jnp.sum(reach * step_col, axis=0, keepdims=True)
            into = into + dot3(decay * scores[...] * step_col, jnp.where((lanes < 64) == (s == 0), upward, 0.0), NN)
        pad_x[0:tok, cols] = into * gate * (1.0 + conv * (1.0 - gate))

    loads["g"].wait()
    sum_o.pass_on()

    score_parts = split2(d_scores[...])
    slope_s = silu_slope(conv_s[...])
    pad_s[0:tok, 0:N] = (d_b[...] + dot_split(score_parts, c_parts, NN)) * slope_s[:, :N]
    pad_s[0:tok, N : 2 * N] = (d_c[...] + dot_split(score_parts, b_parts, TN)) * slope_s[:, N:]
    halo = [
        links.remote(pad_x.at[pl.ds(0, 8)], head_x, place.sibling()),
        links.remote(pad_s.at[pl.ds(0, 8)], head_s, place.sibling()),
    ]
    step_now = steps_col[...]
    faded = grad_tail[...] * tail_table
    d_total = grad_total[...] + grad_rows[...].T - grad_step[...] * step_now - faded
    at_end = iota((tok, 128), 0) == tok - 1
    d_total = d_total + jnp.where(at_end, jnp.sum(faded, axis=0, keepdims=True), 0.0)
    onward = (iota((tok, tok), 1) >= iota((tok, tok), 0)).astype(BF16)
    d_log = pick(onward, d_total, NN)
    d_step = grad_step[...] + grad_tail[...] * steps.fading + d_log * steps.rate
    d_raw = jnp.where(lanes < heads, d_step * steps.slope, 0.0)
    small[...] = jnp.zeros_like(small)
    small[5:6, inner : inner + 128] = jnp.sum(d_raw, axis=0, keepdims=True)
    small[6:7, inner : inner + 128] = jnp.sum(d_log * step_now, axis=0, keepdims=True) * steps.rate
    head_of = (iota((inner, 128), 0) // (inner // heads) == iota((inner, 128), 1)).astype(BF16)
    skips = jnp.broadcast_to(skip_row[...], (8, inner))
    small[7:8, inner : inner + 128] = sum(dot1(piece, head_of, NN) for piece in split3(skips))[0:1]
    small[5:6, 0:inner] = gain_row[...]

    loads["pre_x"].wait()
    loads["pre_s"].wait()
    for copy in halo:
        copy.wait_recv()
    pad_x[tok : tok + 8, :] = head_x[...] * first_half
    pad_s[tok : tok + 8, :] = head_s[...] * first_half
    same = [same_before(lengths, first, tok, 3 - k) for k in range(3)]
    same_next = [same_before(lengths, first + 3 - k, tok, 3 - k) for k in range(3)]

    def back(padded, pre, params, out, start, n):
        cols = pl.ds(pl.multiple_of(n * 128, 128), 128)
        small_cols = pl.ds(pl.multiple_of(start + n * 128, 128), 128)
        here = padded[0:tok, cols]
        total = params[3:4, cols] * here
        small[3:4, small_cols] = jnp.sum(here * pre[8 : 8 + tok, cols], axis=0, keepdims=True)
        small[4:5, small_cols] = jnp.sum(here, axis=0, keepdims=True)
        for k in range(3):
            total = total + params[k : k + 1, cols] * (padded[3 - k : 3 - k + tok, cols] * same_next[k])
            value = here * (pre[5 + k : 5 + k + tok, cols] * same[k])
            small[k : k + 1, small_cols] = jnp.sum(value, axis=0, keepdims=True)
        out[:, cols] = total

    @pl.loop(0, pairs)
    def _(n):
        back(pad_x, pre_x, params_c, dx_both.at[own_rows], 0, n)

    give_dx = links.remote(dx_both.at[own_rows], dx_both.at[own_rows], place.sibling())

    @pl.loop(0, 2 * N // 128)
    def _(n):
        back(pad_s, pre_s, params_s, d_bc, inner, n)

    share = 2 * N // place.tp
    bc_rows[...] = d_bc[...].T

    def share_of(turn):
        return pl.ds(pl.multiple_of(turn * share, 8), share)

    give_bc = [
        links.remote(bc_rows.at[share_of(to_z)], bc_recv.at[k], device) for k, (device, to_z, _) in enumerate(column)
    ]

    hops_of = [
        [place.sibling()],
        [place.at(0, d) for d in range(1, place.side)],
        [place.at(d, 0) for d in range(1, place.side)],
    ]
    small_copies = []

    def hop_small(step):
        slot = sum(len(devices) for devices in hops_of[:step])
        for device in hops_of[step]:
            small_copies.append(links.remote(small, small_recv.at[slot], device))
            slot += 1

    def land_small(step):
        slot = sum(len(devices) for devices in hops_of[:step])
        total = small[...]
        links.settle(small_copies[slot:])
        for copy in small_copies[slot:]:
            copy.wait_recv()
            total = total + small_recv[slot]
            slot += 1
        small[...] = total

    hop_small(0)
    give_dx.wait_recv()
    sum_x = Scatter(place, links, blocks_x, x1a, x1b, x2a, x2b)
    spread_blocks(sum_x, n_pairs, dx_both)
    land_small(0)
    hop_small(1)
    sum_z.pass_on()

    loads["tokens"].wait()
    loads["ws"].wait()
    for copy in give_bc:
        copy.wait_recv()
    summed = bc_rows[share_of(place.z), :]
    for k in range(place.tp - 1):
        summed = summed + bc_recv[k]
    own_cols = pl.ds(pl.multiple_of(place.c * tok, 128), tok)
    ds_both[0:heads, own_cols] = d_raw.T[0:heads, :]
    ds_both[heads : heads + share, own_cols] = summed
    ds_both[heads + share :, own_cols] = jnp.zeros((128 - heads - share, tok), F32)
    give_ds = links.remote(ds_both.at[:, own_cols], ds_both.at[:, own_cols], place.sibling())
    ds_high[...], ds_low[...] = split2(ds_both[:, own_cols].T)
    shares_t = []
    row_sum = jnp.zeros((tok, 1), F32)
    squares = jnp.zeros((tok, 1), F32)
    for k, turn in enumerate(turns):
        out = part_t.at[turn]
        product(2 * place.tp + k, turn, False, out)
        times_rows(ds_high, ds_low, ws.at[pl.ds(pl.multiple_of(turn * part, 8), part)], out, False)
        if k < place.tp - 1:
            shares_t.append(links.remote(out, recv_t.at[k], column[k][0]))
        value = tokens[turn]
        row_sum = row_sum + jnp.sum(out[...] * gain[turn] * value, axis=1, keepdims=True)
        squares = squares + jnp.sum(value * value, axis=1, keepdims=True)
    row_sums[...] = jnp.where(lanes == 0, row_sum, 0.0).T[0:8, :]
    give_rows = [links.remote(row_sums, row_recv.at[k], device) for k, (device, _, _) in enumerate(column)]

    land_small(1)
    hop_small(2)
    stores = [links.move(sum_o.finish(), grad_out)]

    settle = settling(p_recv, tok)

    def rows(group):
        return pl.ds(pl.multiple_of(group * per_pair, 8), per_pair)

    def homeward(value, home, back_ref):
        home[...] = pick(settle, value, NN)
        at = rows(place.f * 2 + place.c)
        copies = [links.remote(home.at[rows(to)], back_ref.at[at], device) for device, to, _ in plane]
        return copies + [links.move(home.at[at], back_ref.at[at])]

    value = tokens[place.z] + part_r[place.z]
    for k, copy in enumerate(shares_r):
        copy.wait_recv()
        value = value + recv_r[k]
    way_r = homeward(value, home_r, back_r)

    give_ds.wait_recv()
    sum_s = Scatter(place, links, blocks_s, s1a, s1b, s2a, s2b)
    ds_parts = split2(ds_both[...])
    for hop in sum_s.order():
        block = place.chip(*hop)
        sum_s.blocks[block] = dot_split(ds_parts, split2(n_pairs[block]), NT)
        sum_s.send(*hop)
    stores.append(links.move(sum_z.finish(), grad_z))
    sum_x.pass_on()

    land_small(2)
    bc_cols = pl.ds(inner, 2 * N)
    give_small = [links.remote(small.at[:, bc_cols], small_z.at[j], device) for j, (device, _, _) in enumerate(column)]
    for copy in shares_t + give_rows:
        copy.wait_recv()
    total = row_sums[...]
    d_normed = part_t[place.z]
    for k in range(place.tp - 1):
        total = total + row_recv[k]
        d_normed = d_normed + recv_t[k]
    row_sum = jnp.concatenate([total, jnp.zeros((120, tok), F32)], axis=0).T[:, 0:1]
    width = place.tp * part
    scale = lax.rsqrt(squares / width + EPSILON)
    scaled = tokens[place.z] * scale
    gain_own[...] = jnp.sum(d_normed * scaled, axis=0, keepdims=True)
    give_gain = [links.remote(gain_own, gain_recv.at[j], device) for j, (device, _, _) in enumerate(plane)]
    loads["up"].wait()
    value = home_t[...] + scale * gain[place.z] * d_normed - scaled * (scale * scale * row_sum / width)
    way_t = homeward(value, home_t, back_t)
    sum_s.pass_on()

    stores.append(links.move(sum_x.finish(), grad_x))
    last = sum_s.finish()
    give_grad = [
        links.remote(last.at[pl.ds(heads, share)], bc_grad.at[share_of(place.z)], device) for device, _, _ in column
    ]
    bc_grad[share_of(place.z), :] = last[heads : heads + share, :]
    grad_dt[...] = last[...].T[:, :heads]

    leave, _ = leaving(slots_in[...], tok, groups)
    for way, home, back_ref, out in ((way_r, home_r, back_r, result), (way_t, home_t, back_t, grad_input)):
        for copy in way[:-1]:
            copy.wait_recv()
        way[-1].wait()
        links.settle(way[:-1])
        home[...] = pick(leave, back_ref[...], NN)
        stores.append(links.move(home, out))
    total = gain_own[...]
    for j, copy in enumerate(give_gain):
        copy.wait_recv()
        total = total + gain_recv[j]
    gain_out[...] = total
    for copy in give_small:
        copy.wait_recv()
    small_out[...] = small[...]
    over_tp = small[0:5, inner : inner + 2 * N]
    for k in range(place.tp - 1):
        over_tp = over_tp + small_z[k, 0:5, :]
    small_out[0:5, inner : inner + 2 * N] = over_tp
    for copy in give_grad:
        copy.wait_recv()
    grad_bc[...] = bc_grad[...].T
    for store in stores:
        store.wait()
    links.finish()


ANYWHERE = pl.BlockSpec(memory_space=pl.ANY)
INSIDE = pl.BlockSpec(memory_space=pltpu.VMEM)
SCALARS = pl.BlockSpec(memory_space=pltpu.SMEM)


def shape(*dims):
    return jax.ShapeDtypeStruct(dims, F32)


def floats(*dims):
    return pltpu.VMEM(dims, F32)


def halves(*dims):
    return pltpu.VMEM(dims, BF16)


def forward_call(sizes, operands, heads):
    fsdp, _, tp = sizes
    inputs, w_x = operands[13], operands[15]
    tok, width = inputs.shape
    shard, inner = w_x.shape
    depth = shard * 2 * fsdp
    part = width // tp
    copies = 4 * gather_copies(math.isqrt(fsdp)) + 3 * (2 * fsdp - 1) + 6 * tp + 2 * fsdp + 4
    outs = [
        (shape(8, inner), INSIDE),
        (shape(8, 2 * N), INSIDE),
        (shape(tp, tok, part), ANYWHERE),
        (shape(tok, part), ANYWHERE),
        (shape(fsdp, shard, 2 * tok), ANYWHERE),
        (shape(tok, 128), INSIDE),
        (shape(8 + tok, inner), ANYWHERE),
        (shape(8 + tok, 2 * N), ANYWHERE),
        (shape(tok, 128), ANYWHERE),
        (shape(tok, inner), ANYWHERE),
        (shape(tok, 2 * N), ANYWHERE),
        (shape(tok, inner), ANYWHERE),
        (shape(tok, inner), ANYWHERE),
        (shape(tok, inner), ANYWHERE),
        (shape(tok, inner), ANYWHERE),
        (shape(tok, 128), INSIDE),
        (shape(8, tok), INSIDE),
        (shape(inner, N), ANYWHERE),
        (shape(fsdp, shard, inner), ANYWHERE),
        (shape(depth, inner), ANYWHERE),
        (shape(depth, 128), ANYWHERE),
        (shape(depth, inner), ANYWHERE),
        (shape(depth, inner), ANYWHERE),
    ]
    return pl.pallas_call(
        functools.partial(forward_kernel, sizes),
        out_shape=tuple(out for out, _ in outs),
        in_specs=[SCALARS] + [INSIDE] * 12 + [ANYWHERE] * 5,
        out_specs=tuple(spec for _, spec in outs),
        scratch_shapes=[
            floats(depth, inner),
            floats(depth, 128),
            floats(depth, inner),
            floats(depth, inner),
            floats(shard, 128),
            floats(128, shard),
            floats(tok, part),
            floats(tok, part),
            floats(tok, part),
            floats(tok, part),
            floats(tok, 128),
            floats(tp, tok, part),
            floats(tp, tok, part),
            floats(tp, tok, part),
            halves(fsdp, tok, 2 * shard),
            halves(fsdp, tok, 2 * shard),
            floats(width, tok),
            floats(fsdp, shard, 2 * tok),
            floats(fsdp, shard, 2 * tok),
            floats(8 + tok, inner),
            floats(8 + tok, 2 * N),
            floats(tok, 128),
            floats(2 * N, max(tok, shard)),
            floats(8, inner),
            floats(8, 2 * N),
            floats(tok, inner),
            floats(tok, 2 * N),
            floats(tok, inner),
            floats(tok, 2 * N),
            floats(tok, 128),
            floats(2, 128, tok),
            floats(tok, tok),
            floats(tok, tok),
            floats(inner, N),
            floats(inner, N),
            floats(tok, inner),
            floats(tok, inner),
            floats(tok, inner),
            floats(2 * tok, inner),
            halves(2 * tok, inner),
            halves(2 * tok, inner),
            halves(shard, 2 * tok),
            halves(shard, 2 * tok),
            floats(2, shard, inner),
            floats(8, tok),
            floats(tp - 1, 8, tok),
            pltpu.SemaphoreType.DMA((copies,)),
            pltpu.SemaphoreType.DMA((copies,)),
            pltpu.SemaphoreType.DMA((48 + 3 * fsdp,)),
        ],
        compiler_params=pltpu.CompilerParams(collective_id=0, has_side_effects=True, vmem_limit_bytes=VMEM_LIMIT),
        name="forward",
    )(*operands)


def backward_call(sizes, heads, operands, tok, width, shard, inner):
    fsdp, _, tp = sizes
    grid = math.isqrt(fsdp)
    part = width // tp
    share = 2 * N // tp
    hops = grid - 1
    copies = 4 + 4 * (2 * hops * grid + 2 * hops) + 7 * tp + 3 * (2 * fsdp) + 2 * hops + 4

    def landing(rows, columns):
        return [
            floats(hops, grid, rows // 2, columns),
            floats(hops, grid, rows // 2, columns),
            floats(hops, rows // 2, columns),
            floats(hops, rows // 2, columns),
        ]

    return pl.pallas_call(
        functools.partial(backward_kernel, sizes, heads),
        out_shape=(
            shape(tok, part),
            shape(tok, part),
            shape(shard, inner),
            shape(shard, inner),
            shape(shard, 2 * N),
            shape(shard, heads),
            shape(shard, inner),
            shape(8, inner + 2 * N),
            shape(1, part),
        ),
        in_specs=[SCALARS] + [INSIDE] * 7 + [ANYWHERE] * 18,
        out_specs=(ANYWHERE, ANYWHERE, ANYWHERE, ANYWHERE, INSIDE, INSIDE, ANYWHERE, INSIDE, INSIDE),
        scratch_shapes=[
            floats(tp, tok, part),
            floats(fsdp, shard, 2 * tok),
            floats(8 + tok, inner),
            floats(8 + tok, 2 * N),
            floats(tok, 128),
            floats(tok, inner),
            floats(tok, 2 * N),
            floats(inner, N),
            floats(2 * tok, inner),
            floats(2 * tok, inner),
            floats(128, 2 * tok),
            halves(2 * tok, inner),
            halves(2 * tok, inner),
            halves(shard, 2 * tok),
            halves(shard, 2 * tok),
            floats(fsdp, shard, inner),
            floats(fsdp, shard, inner),
            floats(fsdp, 128, shard),
            *landing(shard, inner),
            *landing(shard, inner),
            *landing(shard, inner),
            *landing(128, shard),
            floats(fsdp, shard, inner),
            floats(2, part, inner),
            floats(width, 128),
            floats(tok, 2 * N),
            halves(tok, 128),
            halves(tok, 128),
            floats(2 * N, tok),
            floats(tp - 1, share, tok),
            floats(2 * N, shard),
            floats(tp, tok, part),
            floats(tp, tok, part),
            floats(tp - 1, tok, part),
            floats(tp - 1, tok, part),
            floats(8, tok),
            floats(tp - 1, 8, tok),
            floats(tp - 1, 8, tok),
            floats(tok, part),
            floats(tok, part),
            floats(tok, part),
            floats(tok, part),
            floats(inner, N),
            floats(inner, N),
            floats(tok, N),
            floats(tok, N),
            floats(8 + tok, inner),
            floats(8 + tok, 2 * N),
            floats(8, inner),
            floats(8, 2 * N),
            floats(tok, tok),
            floats(tok, tok),
            floats(tok, tok),
            floats(tok, 128),
            floats(tok, 128),
            floats(128, tok),
            floats(tok, 128),
            floats(tok, 128),
            floats(tok, 128),
            floats(128, tok),
            floats(1, inner),
            floats(1, inner),
            floats(8, inner + 2 * N),
            floats(1 + 2 * hops, 8, inner + 2 * N),
            floats(tp - 1, 8, 2 * N),
            floats(1, part),
            floats(2 * fsdp - 1, 1, part),
            pltpu.SemaphoreType.DMA((copies,)),
            pltpu.SemaphoreType.DMA((copies,)),
            pltpu.SemaphoreType.DMA((24 + 3 * tp,)),
        ],
        compiler_params=pltpu.CompilerParams(collective_id=1, has_side_effects=True, vmem_limit_bytes=VMEM_LIMIT),
        name="backward",
    )(*operands)


def last_kernel(heads, small, gain, bc, dt, *refs):
    large, outs, held, sems = refs[:5], refs[5:21], refs[21:26], refs[26]
    loads = [pltpu.make_async_copy(src, dst, sems.at[0, k]) for k, (src, dst) in enumerate(zip(large, held))]
    stores = [pltpu.make_async_copy(src, dst, sems.at[1, k]) for k, (src, dst) in enumerate(zip(held, outs))]
    for load in loads:
        load.start()
    for load, store in zip(loads, stores):
        load.wait()
        store.start()
    grad_bc, grad_dt, taps_x, bias_x, taps_s, bias_s, dt_bias, a_log, d_skip, gate_gain, gain_in = outs[5:]
    inner = taps_x.shape[1]
    grad_bc[...] = bc[...]
    grad_dt[...] = dt[...]
    taps_x[...] = small[0:4, 0:inner]
    bias_x[...] = small[4:5, 0:inner]
    taps_s[...] = small[0:4, inner : inner + 2 * N]
    bias_s[...] = small[4:5, inner : inner + 2 * N]
    dt_bias[...] = small[5:6, inner : inner + heads]
    a_log[...] = small[6:7, inner : inner + heads]
    d_skip[...] = small[7:8, inner : inner + heads]
    gate_gain[...] = small[5:6, 0:inner]
    gain_in[...] = gain[...]
    for store in stores:
        store.wait()


def last_call(heads, small, gain, bc, dt, *large):
    inner, part = small.shape[1] - 2 * N, gain.shape[1]
    few = [
        bc.shape,
        dt.shape,
        (4, inner),
        (1, inner),
        (4, 2 * N),
        (1, 2 * N),
        (1, heads),
        (1, heads),
        (1, heads),
        (1, inner),
        (1, part),
    ]
    return pl.pallas_call(
        functools.partial(last_kernel, heads),
        out_shape=tuple([shape(*value.shape) for value in large] + [shape(*dims) for dims in few]),
        in_specs=[INSIDE] * 4 + [ANYWHERE] * 5,
        out_specs=tuple([ANYWHERE] * 5 + [INSIDE] * len(few)),
        scratch_shapes=[floats(*value.shape) for value in large] + [pltpu.SemaphoreType.DMA((2, 5))],
        compiler_params=pltpu.CompilerParams(vmem_limit_bytes=VMEM_LIMIT),
        name="results",
    )(small, gain, bc, dt, *large)


def shards(
    inputs,
    cotangent,
    seq_lengths,
    slots,
    gain_in,
    w_z,
    w_x,
    w_dt,
    w_bc,
    w_out,
    conv_x,
    conv_x_bias,
    conv_bc,
    conv_bc_bias,
    dt_bias,
    a_log,
    d_skip,
    gate_gain,
):
    sizes = (lax.axis_size("fsdp"), lax.axis_size("ctx"), lax.axis_size("tp"))
    tok, width = inputs.shape
    shard, inner = w_x.shape
    heads = w_dt.shape[1]
    tp = sizes[2]
    operands = (
        seq_lengths,
        slots[None],
        gain_in[None],
        conv_x,
        conv_x_bias[None],
        conv_bc,
        conv_bc_bias[None],
        dt_bias[None],
        a_log[None],
        d_skip[None],
        gate_gain[None],
        w_bc,
        w_dt,
        inputs,
        cotangent,
        w_x,
        w_z,
        w_out,
    )
    params_c, params_s, tokens, up, n_pairs, p_recv, *kept = forward_call(sizes, operands, heads)
    pre_x, pre_s, raw, conv_x_kept, conv_s_kept, normal_y, gate_pre, mixed, d_normal, gscale, inner_sum, *rest = kept
    operands = (
        seq_lengths,
        slots[None],
        p_recv,
        gain_in.reshape(tp, 1, width // tp),
        params_c,
        params_s,
        gscale,
        inner_sum,
        tokens,
        up,
        n_pairs,
        pre_x,
        pre_s,
        raw,
        conv_x_kept,
        conv_s_kept,
        normal_y,
        gate_pre,
        mixed,
        d_normal,
        *rest,
    )
    result, grad_input, grad_z, grad_x, grad_bc, grad_dt, grad_out, small, gain = backward_call(
        sizes, heads, operands, tok, width, shard, inner
    )
    outs = last_call(heads, small, gain, grad_bc, grad_dt, result, grad_input, grad_z, grad_x, grad_out)
    result, grad_input, grad_z, grad_x, grad_out, grad_bc, grad_dt, taps_x, bias_x, taps_s, bias_s, *few = outs
    return (
        result,
        grad_input,
        grad_z,
        grad_x,
        grad_dt,
        grad_bc,
        grad_out,
        taps_x,
        bias_x[0],
        taps_s,
        bias_s[0],
        *[value[0] for value in few],
    )


def solution(mesh):
    return jax.shard_map(
        shards,
        mesh=mesh,
        in_specs=(
            P(("fsdp", "ctx"), None),
            P(("fsdp", "ctx"), None),
            P("fsdp", None),
            P(("fsdp", "ctx")),
            P(),
            P(("fsdp", "ctx"), "tp"),
            P(("fsdp", "ctx"), "tp"),
            P(("fsdp", "ctx"), "tp"),
            P(("fsdp", "ctx"), None),
            P(("fsdp", "ctx"), "tp"),
            P(None, "tp"),
            P("tp"),
            P(),
            P(),
            P("tp"),
            P("tp"),
            P("tp"),
            P("tp"),
        ),
        out_specs=(
            P(("fsdp", "ctx"), "tp"),
            P(("fsdp", "ctx"), "tp"),
            P(("fsdp", "ctx"), "tp"),
            P(("fsdp", "ctx"), "tp"),
            P(("fsdp", "ctx"), "tp"),
            P(("fsdp", "ctx"), None),
            P(("fsdp", "ctx"), "tp"),
            P(None, "tp"),
            P("tp"),
            P(),
            P(),
            P("tp"),
            P("tp"),
            P("tp"),
            P("tp"),
            P("tp"),
        ),
        check_vma=False,
    )
```

```python
import functools
import math

import jax
import jax.numpy as jnp
from jax import lax
from jax.experimental import pallas as pl
from jax.experimental.pallas import tpu as pltpu
from jax.sharding import PartitionSpec as P

N = 128
SPAN = 256
INNER = 4096
EPSILON = 1e-05
F32 = jnp.float32
BF16 = jnp.bfloat16
MESH = pl.DeviceIdType.MESH
NN = (((1,), (0,)), ((), ()))
NT = (((1,), (1,)), ((), ()))
TN = (((0,), (0,)), ((), ()))
VMEM_LIMIT = 62 << 20


def split2(value):
    high = value.astype(BF16)
    return high, (value - high.astype(F32)).astype(BF16)


def split3(value):
    high = value.astype(BF16)
    rest = value - high.astype(F32)
    middle = rest.astype(BF16)
    return high, middle, (rest - middle.astype(F32)).astype(BF16)


def dot1(left, right, dims):
    return lax.dot_general(left, right, dims, preferred_element_type=F32)


def dot_split(left, right, dims):
    (lh, ll), (rh, rl) = left, right
    return dot1(lh, rh, dims) + (dot1(lh, rl, dims) + dot1(ll, rh, dims))


def dot3(left, right, dims):
    return dot_split(split2(left), split2(right), dims)


def pick(table, value, dims):
    parts = split3(value)
    return dot1(table, parts[0], dims) + dot1(table, parts[1], dims) + dot1(table, parts[2], dims)


def iota(shape, dim):
    return lax.broadcasted_iota(jnp.int32, shape, dim)


class Place:
    def __init__(self, fsdp, ctx, tp):
        self.fsdp, self.n_ctx, self.tp = fsdp, ctx, tp
        self.side = math.isqrt(fsdp)
        assert self.side * self.side == fsdp and ctx == 2
        self.f = lax.axis_index("fsdp")
        self.c = lax.axis_index("ctx")
        self.z = lax.axis_index("tp")
        self.y, self.x = self.f // self.side, self.f % self.side

    def chip(self, dy, dx):
        side = self.side
        return ((self.y + dy + side) % side) * side + (self.x + dx + side) % side

    def block(self, dy, dx, core):
        return self.chip(dy, dx) * 2 + core

    def at(self, dy, dx):
        return (self.chip(dy, dx), self.c, self.z)

    def sibling(self):
        return (self.f, 1 - self.c, self.z)

    def plane(self):
        out = []
        for df in range(self.fsdp):
            for dc in range(2):
                if df or dc:
                    to_f = (self.f + df) % self.fsdp
                    from_f = (self.f - df + self.fsdp) % self.fsdp
                    core = (self.c + dc) % 2
                    out.append(((to_f, core, self.z), to_f * 2 + core, from_f * 2 + core))
        return out

    def column(self):
        out = []
        for dz in range(1, self.tp):
            to_z = (self.z + dz) % self.tp
            out.append(((self.f, self.c, to_z), to_z, (self.z - dz + self.tp) % self.tp))
        return out


class Links:
    def __init__(self, send, recv, local):
        self.send, self.recv, self.local = send, recv, local
        self.used, self.used_local = 0, 0
        self.open = []

    def remote(self, src, dst, device):
        k = self.used
        self.used += 1
        copy = pltpu.make_async_remote_copy(
            src_ref=src,
            dst_ref=dst,
            send_sem=self.send.at[k],
            recv_sem=self.recv.at[k],
            device_id=device,
            device_id_type=MESH,
        )
        copy.start()
        self.open.append(copy)
        return copy

    def plan(self, src, dst, device, lands_as=None):
        k = self.used
        self.used += 1
        copy = pltpu.make_async_remote_copy(
            src_ref=src,
            dst_ref=dst,
            send_sem=self.send.at[k],
            recv_sem=self.recv.at[k if lands_as is None else lands_as.slot],
            device_id=device,
            device_id_type=MESH,
        )
        copy.slot = k
        return copy

    def move(self, src, dst):
        k = self.used_local
        self.used_local += 1
        copy = pltpu.make_async_copy(src, dst, self.local.at[k])
        copy.start()
        return copy

    def settle(self, copies):
        for copy in copies:
            copy.wait_send()
            self.open = [other for other in self.open if other is not copy]

    def finish(self):
        assert self.used <= self.send.shape[0] and self.used_local <= self.local.shape[0]
        self.settle(list(self.open))


def greet(devices):
    barrier = pltpu.get_barrier_semaphore()
    for device in devices:
        pl.semaphore_signal(barrier, inc=1, device_id=device, device_id_type=MESH)


def greeted(devices):
    pl.semaphore_wait(pltpu.get_barrier_semaphore(), len(devices))


class Spread:
    def __init__(self, place, links, slices):
        self.place, self.links, self.slices = place, links, slices
        self.line = place.tp == 4
        z, mine = place.z, slices.at[place.z]
        if not self.line:
            self.copies = [links.remote(mine, mine, device) for device, _, _ in place.column()]
            return
        self.copies = [links.remote(mine, mine, (place.f, place.c, z ^ d)) for d in (1, 2)]
        self.inner = (z == 1) | (z == 2)
        across = links.plan(mine, mine, (place.f, place.c, 3 - z))
        onward = slices.at[z ^ 2]
        self.onward = links.plan(onward, onward, (place.f, place.c, z ^ 1), across)
        self.across = across

        @pl.when(self.inner)
        def _():
            across.start()

    def forward(self):
        if self.line:
            self.copies.pop().wait_recv()

            @pl.when(self.inner)
            def _():
                self.onward.start()

    def finish(self):
        for copy in self.copies:
            copy.wait_recv()
        if self.line:
            self.across.wait_recv()

            @pl.when(self.inner)
            def _():
                self.across.wait_send()
                self.onward.wait_send()


class Gather:
    def __init__(self, place, links, shard, whole):
        self.place, self.links, self.shard, self.whole = place, links, shard, whole
        self.rows = shard.shape[0]
        self.near = 0

    def rows_of(self, block, start=0, count=None):
        count = self.rows if count is None else count
        return self.whole.at[pl.ds(pl.multiple_of(block * self.rows + start, 8), count)]

    def part(self, block, half):
        return self.rows_of(block, half * (self.rows // 2), self.rows // 2)

    def start(self):
        p, steps = self.place, range(1, self.place.side)
        me = p.block(0, 0, p.c)
        self.row, self.col = [[], []], [[], []]
        for turn in range(2):
            for d in steps:
                shard = self.shard.at[pl.ds(turn * (self.rows // 2), self.rows // 2)]
                self.row[turn].append(self.links.remote(shard, self.part(me, turn), p.at(0, d)))
                shard = self.shard.at[pl.ds((1 - turn) * (self.rows // 2), self.rows // 2)]
                self.col[turn].append(self.links.remote(shard, self.part(me, 1 - turn), p.at(d, 0)))
        mine = self.rows_of(me)
        self.pair = [self.links.remote(self.shard, mine, p.sibling())]
        self.own = self.links.move(self.shard, mine)

    def forward(self):
        p, steps = self.place, range(1, self.place.side)
        self.half_a, self.half_b = [], []
        for k, d in enumerate(steps):
            self.row[0][k].wait_recv()
            part = self.part(p.block(0, -d, p.c), 0)
            self.half_a += [self.links.remote(part, part, p.at(e, 0)) for e in steps]
        for k, e in enumerate(steps):
            self.col[0][k].wait_recv()
            part = self.part(p.block(-e, 0, p.c), 1)
            self.half_b += [self.links.remote(part, part, p.at(0, d)) for d in steps]
        for k, d in enumerate(steps):
            self.row[1][k].wait_recv()
            whole = self.rows_of(p.block(0, -d, p.c))
            self.pair.append(self.links.remote(whole, whole, p.sibling()))
        for k, e in enumerate(steps):
            self.col[1][k].wait_recv()
            whole = self.rows_of(p.block(-e, 0, p.c))
            self.pair.append(self.links.remote(whole, whole, p.sibling()))

    def share(self):
        p, steps, half = self.place, range(1, self.place.side), self.rows // 2
        k = 0
        for d in steps:
            for e in steps:
                self.half_a[k].wait_recv()
                part = self.rows_of(p.block(-e, -d, p.c), 0, half)
                self.pair.append(self.links.remote(part, part, p.sibling()))
                k += 1
        k = 0
        for e in steps:
            for d in steps:
                self.half_b[k].wait_recv()
                part = self.rows_of(p.block(-e, -d, p.c), half, half)
                self.pair.append(self.links.remote(part, part, p.sibling()))
                k += 1

    def finish_near(self):
        self.own.wait()
        self.near = 1 + 2 * (self.place.side - 1)
        for copy in self.pair[: self.near]:
            copy.wait_recv()

    def finish(self):
        if self.near == 0:
            self.finish_near()
        for copy in self.pair[self.near :]:
            copy.wait_recv()


def gather_copies(side):
    steps = side - 1
    return 6 * steps + 1 + 4 * steps * steps


def down_lanes(row):
    return jnp.broadcast_to(row, (128, row.shape[1])).T


def leaving(slots, tok, groups):
    slots = down_lanes(slots.astype(F32)).astype(jnp.int32)
    targets = slots >> (tok.bit_length() - 1)
    lanes = iota((tok, 128), 1)
    member = (targets == lanes).astype(F32)
    earlier = (iota((tok, tok), 0) > iota((tok, tok), 1)).astype(BF16)
    ranks = jnp.sum(dot1(earlier, member.astype(BF16), NN) * member, axis=1, keepdims=True)
    send_at = (targets[:, :1] * (tok // groups)).astype(F32) + ranks
    leave = (send_at == iota((tok, tok), 1).astype(F32)).astype(BF16)
    places = jnp.where(ranks == lanes.astype(F32), (slots - targets * tok).astype(F32), 0.0)
    return leave, dot1(member.astype(BF16), places.astype(BF16), TN)


def arrived(rows, tok, per_pair):
    groups = rows.shape[0]
    rows = jnp.concatenate([rows, jnp.zeros((128 - groups, 128), F32)], axis=0)
    token, lanes = iota((tok, 128), 0), iota((tok, 128), 1)
    spread = dot1((token // per_pair == lanes).astype(BF16), rows.astype(BF16), NN)
    place = jnp.sum(jnp.where(token % per_pair == lanes, spread, 0.0), axis=1, keepdims=True)
    return jnp.broadcast_to(place, (tok, 128))


def settling(places, tok):
    return (places[:, :1] == iota((tok, tok), 1).astype(F32)).astype(BF16)


def halve(value_ref, high, low):
    @pl.loop(0, value_ref.shape[1] // 128)
    def _(n):
        cols = pl.ds(pl.multiple_of(n * 128, 128), 128)
        high[:, cols], low[:, cols] = split2(value_ref[:, cols])


def project(left_high, left_low, whole, chips, out, tile, first_row, fresh):
    _, rows, width = left_high.shape

    @pl.loop(0, whole.shape[1] // tile)
    def _(n):
        cols = pl.ds(pl.multiple_of(n * tile, 128), tile)
        total = jnp.zeros((rows, tile), F32) if fresh else out[first_row : first_row + rows, cols]
        for chip in chips:
            at = pl.ds(chip * width if isinstance(chip, int) else pl.multiple_of(chip * width, 8), width)
            total = total + dot_split((left_high[chip], left_low[chip]), split2(whole[at, cols]), NN)
        out[first_row : first_row + rows, cols] = total


def weight_block(left_ref, high, low, left_high, left_low, out):
    left_high[...], left_low[...] = split2(left_ref[...])

    @pl.loop(0, high.shape[1] // 512)
    def _(n):
        cols = pl.ds(pl.multiple_of(n * 512, 128), 512)
        out[:, cols] = dot_split((left_high[...], left_low[...]), (high[:, cols], low[:, cols]), NN)


def times_rows(high, low, rows_ref, out, fresh):
    tile = min(256, rows_ref.shape[0])
    for n in range(rows_ref.shape[0] // tile):
        at = slice(n * tile, (n + 1) * tile)
        value = dot_split((high[...], low[...]), split2(rows_ref[at, :]), NT)
        out[:, at] = value if fresh else out[:, at] + value


class Scatter:
    def __init__(self, place, links, source, blocks, first, second=None):
        self.place, self.links, self.blocks = place, links, blocks
        self.first, self.second = first, second
        self.half = source.shape[1] // 2
        self.source = source
        self.copies_a, self.copies_b = {}, {}

    def order(self):
        side = self.place.side
        hops = [(dy, dx) for dy in range(side) for dx in range(side)]
        return sorted(hops, key=lambda hop: -(hop[0] > 0) - (hop[1] > 0))

    def halves(self, dy, dx, blocks=None):
        ref = (self.blocks if blocks is None else blocks).at[self.place.chip(dy, dx)]
        return ref.at[pl.ds(0, self.half)], ref.at[pl.ds(self.half, self.half)]

    def send(self, dy, dx):
        p, side = self.place, self.place.side
        upper, lower = self.halves(dy, dx, self.source)
        if dy:
            target = self.first[0].at[dy - 1, (p.x + dx) % side]
            self.copies_a[dy, dx] = self.links.remote(upper, target, p.at(dy, 0))
        if dx:
            target = self.first[1].at[dx - 1, (p.y + dy) % side]
            self.copies_b[dy, dx] = self.links.remote(lower, target, p.at(0, dx))

    def send_all(self):
        for hop in self.order():
            self.send(*hop)

    def land(self):
        for copy in [*self.copies_a.values(), *self.copies_b.values()]:
            copy.wait_recv()

    def pass_on(self):
        p, side = self.place, self.place.side
        self.last_a, self.last_b = [], []
        for d in list(range(1, side)) + [0]:
            upper, _ = self.halves(0, d)
            total = upper[...]
            for e in range(1, side):
                if (e, d) in self.copies_a:
                    self.copies_a[e, d].wait_recv()
                total = total + self.first[0][e - 1, (p.x + d) % side]
            upper[...] = total
            if d:
                self.last_a.append(self.links.remote(upper, self.second[0].at[d - 1], p.at(0, d)))
            _, lower = self.halves(d, 0)
            total = lower[...]
            for e in range(1, side):
                if (d, e) in self.copies_b:
                    self.copies_b[d, e].wait_recv()
                total = total + self.first[1][e - 1, (p.y + d) % side]
            lower[...] = total
            if d:
                self.last_b.append(self.links.remote(lower, self.second[1].at[d - 1], p.at(d, 0)))

    def finish(self):
        for k, (copies, part) in enumerate(zip((self.last_a, self.last_b), self.halves(0, 0))):
            total = part[...]
            for d, copy in enumerate(copies):
                copy.wait_recv()
                total = total + self.second[k][d]
            part[...] = total
        return self.blocks.at[self.place.chip(0, 0)]


class Shares:
    def __init__(self, place, links, parts, landing):
        self.place, self.links, self.parts, self.landing = place, links, parts, landing
        self.line = place.tp == 4
        z = place.z
        self.copies = []
        if self.line:
            self.turns = [z ^ 3, z ^ 2, z ^ 1, z]
            self.inner = (z == 1) | (z == 2)
        else:
            self.turns = [(z + d + 1) % place.tp for d in range(place.tp)]

    def send(self, k):
        place, z = self.place, self.place.z
        if k == place.tp - 1:
            return
        part = self.parts.at[self.turns[k]]
        if not self.line:
            self.copies.append(self.links.remote(part, self.landing.at[k], (place.f, place.c, self.turns[k])))
            return
        if k == 0:
            self.direct = self.links.plan(part, self.landing.at[2], (place.f, place.c, z ^ 3))
            self.extra = self.links.plan(part, self.landing.at[3], (place.f, place.c, z ^ 1))

            @pl.when(self.inner)
            def _():
                self.direct.start()

            @pl.when(jnp.logical_not(self.inner))
            def _():
                self.extra.start()

        elif k == 1:
            self.across = self.links.plan(part, self.landing.at[1], (place.f, place.c, z ^ 2))

            @pl.when(jnp.logical_not(self.inner))
            def _():
                self.across.start()

        else:
            self.copies.append(self.links.remote(part, self.landing.at[0], (place.f, place.c, z ^ 1)))

    def forward(self):
        if self.line:

            @pl.when(self.inner)
            def _():
                self.extra.wait_recv()
                part = self.parts.at[self.place.z ^ 2]
                part[...] = part[...] + self.landing[3]
                self.across.start()

    def finish(self):
        own = self.parts.at[self.place.z]
        total = own[...]
        for k, copy in enumerate(self.copies):
            copy.wait_recv()
            total = total + self.landing[k]
        if self.line:
            self.across.wait_recv()
            total = total + self.landing[1]
            self.across.wait_send()
        own[...] = total
        if self.line:

            @pl.when(self.inner)
            def _():
                self.direct.wait()
                own[...] = own[...] + self.landing[2]

            @pl.when(jnp.logical_not(self.inner))
            def _():
                self.extra.wait_send()


def silu_slope(value):
    gate = jax.nn.sigmoid(value)
    return gate * (1.0 + value * (1.0 - gate))


def softplus(value):
    return jnp.maximum(value, 0.0) + jnp.log1p(jnp.exp(-jnp.abs(value)))


def segments(lengths, position):
    bound, seg = 0, jnp.zeros_like(position)
    for k in range(lengths.shape[1]):
        bound = bound + lengths[0, k]
        seg = seg + (bound <= position).astype(jnp.int32)
    return seg


def same_before(lengths, first, tok, distance):
    position = first + iota((tok, 128), 0)
    return (segments(lengths, position) == segments(lengths, position - distance)).astype(F32)


def wide(table, width):
    return jnp.concatenate([table] * (width // 128), axis=1)


def column_of(table, head):
    lanes = iota(table.shape, 1)
    return jnp.sum(jnp.where(lanes == head, table, 0.0), axis=1, keepdims=True)


def pair_columns(table, pair):
    first, second = column_of(table, 2 * pair), column_of(table, 2 * pair + 1)
    return jnp.where(iota(table.shape, 1) < 64, first, second)


class Steps:
    def __init__(self, raw, params_s, lengths, first):
        tok = raw.shape[0]
        shifted = raw + params_s[5:6, :128]
        self.slope = jax.nn.sigmoid(shifted)
        self.step = softplus(shifted)
        self.rate = -jnp.exp(params_s[6:7, :128])
        until = (iota((tok, tok), 0) >= iota((tok, tok), 1)).astype(BF16)
        self.total = pick(until, self.step * self.rate, NN)
        position = first + iota((tok, 128), 0)
        seg = segments(lengths, position)
        before = segments(lengths, jnp.full((tok, 128), first - 1, jnp.int32))
        last = segments(lengths, jnp.full((tok, 128), first + tok - 1, jnp.int32))
        self.reading = jnp.exp(self.total) * (seg == before).astype(F32)
        self.fading = jnp.exp(self.total[tok - 1 : tok] - self.total) * (seg == last).astype(F32)
        self.tail = self.fading * self.step


def closed(lengths, first, tok, flipped):
    rows, cols = first + iota((tok, tok), 0), first + iota((tok, tok), 1)
    order = rows <= cols if flipped else rows >= cols
    seg_rows = segments(lengths, first + iota((tok, 1), 0))
    seg_cols = segments(lengths, first + iota((1, tok), 1))
    return jnp.where(order & (seg_rows == seg_cols), 0.0, -1e30)


def convolve(padded, params, lengths, first, conv, act):
    tok, tile = conv.shape[0], 128
    same = [same_before(lengths, first, tok, 3 - k) for k in range(3)]

    @pl.loop(0, conv.shape[1] // tile)
    def _(n):
        cols = pl.ds(pl.multiple_of(n * tile, 128), tile)
        total = params[4:5, cols] + params[3:4, cols] * padded[8 : 8 + tok, cols]
        for k in range(3):
            total = total + params[k : k + 1, cols] * (padded[5 + k : 5 + k + tok, cols] * same[k])
        conv[:, cols] = total
        act[:, cols] = total * jax.nn.sigmoid(total)


def forward_kernel(
    sizes,
    lengths,
    slots_in,
    gain,
    taps_x,
    bias_x,
    taps_s,
    bias_s,
    dt_bias,
    a_log,
    d_skip,
    gate_gain,
    w_bc,
    w_dt,
    x_in,
    c_in,
    w_x,
    w_z,
    w_out,
    params_c,
    params_s,
    tokens_out,
    up_out,
    n_pairs_out,
    p_out,
    pre_x_out,
    pre_s_out,
    raw_out,
    conv_x_out,
    conv_s_out,
    ny_out,
    dz_out,
    dmix_out,
    gain_row,
    state_out,
    g_out,
    gz_out,
    land_a,
    land_b,
    wx_out,
    ws_out,
    wz_out,
    wo_out,
    wx,
    ws,
    wz,
    wo,
    ws_own,
    x_own,
    c_own,
    x_sort,
    c_sort,
    p_sort,
    p_recv,
    x_recv,
    c_recv,
    tokens,
    n_high,
    n_low,
    turned,
    n_pairs,
    c_pairs,
    pre_x,
    pre_s,
    raw,
    bc_rows,
    tail_x,
    tail_s,
    conv_x,
    conv_s,
    act_x,
    act_s,
    totals,
    step_rows,
    open_,
    scores,
    state,
    state_in,
    mixed,
    gate_pre,
    d_normal,
    ny_both,
    high,
    low,
    left_high,
    left_low,
    sums,
    sums_recv,
    inner_sums,
    inner_recv,
    send,
    recv,
    local,
):
    place = Place(*sizes)
    links = Links(send, recv, local)
    tok, groups = x_own.shape[0], 2 * place.fsdp
    per_pair = tok // groups
    part = x_own.shape[1]
    inner = act_x.shape[1]
    pairs = inner // 128
    heads = d_skip.shape[1]
    share = 2 * N // place.tp
    shard_rows = n_pairs.shape[1]
    chip_rows = 2 * shard_rows
    first = place.c * tok
    lanes = iota((tok, 128), 1)
    part_cols = pl.ds(pl.multiple_of(place.z * part, 128), part)
    load_x = links.move(x_in.at[:, part_cols], x_own)
    load_c = links.move(c_in.at[:, part_cols], c_own)
    plane, column = place.plane(), place.column()
    partners = [entry[0] for entry in plane] + [entry[0] for entry in column]
    greet(partners)

    leave, places = leaving(slots_in[...], tok, groups)
    p_sort[...] = jnp.broadcast_to(places[0:groups, None, :], (groups, 8, 128))
    load_x.wait()
    x_sort[...] = pick(leave, x_own[...], TN)
    greeted(partners)
    g_x, g_s, g_z, g_o = [Gather(place, links, shard, whole) for shard, whole in ((w_x, wx), (ws_own, ws), (w_z, wz), (w_out, wo))]

    def rows(group):
        return pl.ds(pl.multiple_of(group * per_pair, 8), per_pair)

    def route(source, target, at):
        mine = at(place.f * 2 + place.c)
        copies = [links.remote(source.at[at(to)], target.at[mine], device) for device, to, _ in plane]
        return copies, links.move(source.at[mine], target.at[mine])

    routes_x = [route(p_sort, p_recv, lambda group: group), route(x_sort, x_recv.at[place.z], rows)]
    g_x.start()

    def share_of(turn):
        return pl.ds(pl.multiple_of(turn * share, 8), share)

    bc_rows[:, 0:shard_rows] = w_bc[...].T
    ws_own[...] = jnp.zeros_like(ws_own)
    ws_own[0:heads, :] = w_dt[...]
    ws_own[heads : heads + share, :] = bc_rows[share_of(place.z), 0:shard_rows]
    g_s.start()
    load_c.wait()
    c_sort[...] = pick(leave, c_own[...], TN)
    routes_c = [route(c_sort, c_recv.at[place.z], rows)]

    params_c[0:4, :] = taps_x[...]
    params_c[4:5, :] = bias_x[...]
    params_c[6:7, :] = gate_gain[...]
    params_c[7:8, :] = jnp.zeros((1, inner), F32)
    for q in range(pairs):
        both = [d_skip[0:1, 2 * q + s : 2 * q + s + 1] for s in range(2)]
        params_c[5:6, q * 128 : (q + 1) * 128] = jnp.where(lanes[0:1] < 64, both[0], both[1])
    params_s[...] = jnp.zeros_like(params_s)
    params_s[0:4, :] = taps_s[...]
    params_s[4:5, :] = bias_s[...]
    params_s[5:6, 0:heads] = dt_bias[...]
    params_s[6:7, 0:heads] = a_log[...]

    def arrive(routes):
        for copies, own in routes:
            own.wait()
            for copy in copies:
                copy.wait_recv()

    arrive(routes_x)
    spread_x = Spread(place, links, x_recv)
    g_x.forward()
    g_s.forward()
    g_z.start()
    spread_x.forward()
    arrive(routes_c)
    g_s.share()
    stores = []
    spread_x.finish()
    p_out[...] = arrived(p_recv[:, 0, :], tok, per_pair)
    settle = settling(p_out, tok)
    squares = jnp.zeros((tok, 1), F32)
    for k in range(place.tp):
        value = pick(settle, x_recv[k], TN)
        tokens[k] = value
        squares = squares + jnp.sum(value * value, axis=1, keepdims=True)
    scale = lax.rsqrt(squares / (place.tp * part) + EPSILON)
    own_cols = pl.ds(pl.multiple_of(place.c * tok, 128), tok)
    own_rows = pl.ds(pl.multiple_of(place.c * tok, 128), tok)
    chips_here = part // chip_rows

    def keep_left(k, value):
        for j in range(chips_here):
            piece = value[:, j * chip_rows : (j + 1) * chip_rows]
            n_high[k * chips_here + j], n_low[k * chips_here + j] = split2(piece)
        turned[k * part : (k + 1) * part, :] = value.T

    def exchange_blocks(pairs_ref):
        copies, kept = [], []
        for q in range(place.fsdp):
            there = turned.at[pl.ds(pl.multiple_of((2 * q + 1 - place.c) * shard_rows, 8), shard_rows)]
            here = turned.at[pl.ds(pl.multiple_of((2 * q + place.c) * shard_rows, 8), shard_rows)]
            copies.append(links.remote(there, pairs_ref.at[q, :, own_cols], place.sibling()))
            kept.append(links.move(here, pairs_ref.at[q, :, own_cols]))
        return copies, kept

    for k in range(place.tp):
        keep_left(k, tokens[k] * scale * gain[:, k * part : (k + 1) * part])
    pairs_n, kept_n = exchange_blocks(n_pairs)
    stores.append(links.move(tokens, tokens_out))

    every = list(range(place.fsdp))
    g_s.finish()
    raw[...] = jnp.zeros_like(raw)
    side_rows = ws_own.shape[0]
    total = jnp.zeros((tok, side_rows), F32)
    for block in range(2 * place.fsdp):
        at = slice(block % 2 * shard_rows, (block % 2 + 1) * shard_rows)
        left = (n_high[block // 2, :, at], n_low[block // 2, :, at])
        total = total + dot_split(left, split2(ws[block * side_rows : (block + 1) * side_rows, :]), NT)
    raw[:, 0:side_rows] = total
    bc_turned = raw[...].T
    bc_rows[share_of(place.z), :] = bc_turned[heads : heads + share]
    mine = bc_rows.at[share_of(place.z)]
    spread_bc = [links.remote(mine, mine, device) for device, _, _ in column]
    spread_c = Spread(place, links, c_recv)
    g_x.share()
    g_x.finish()
    keep_wx = links.move(wx, wx_out)
    stores += [links.move(ws, ws_out)]
    project(n_high, n_low, wx, every, pre_x, 512, 8, True)
    halo = [links.remote(pre_x.at[pl.ds(tok, 8)], tail_x, place.sibling())]
    g_z.forward()
    g_o.start()

    raw[...] = jnp.where(lanes < heads, raw[...], 0.0)
    steps = Steps(raw[...], params_s, lengths, first)
    totals[...] = steps.total
    step_rows[0] = steps.total.T
    step_rows[1] = steps.step.T
    open_[...] = closed(lengths, first, tok, False)
    for copy in spread_bc:
        copy.wait_recv()
    pre_s[8 : 8 + tok, :] = bc_rows[...].T
    halo.append(links.remote(pre_s.at[pl.ds(tok, 8)], tail_s, place.sibling()))
    for copy in halo:
        copy.wait_recv()
    second = (place.c > 0).astype(F32)
    pre_x[0:8, :] = tail_x[...] * second
    pre_s[0:8, :] = tail_s[...] * second
    convolve(pre_s, params_s, lengths, first, conv_s, act_s)
    convolve(pre_x, params_c, lengths, first, conv_x, act_x)
    b_parts = split2(act_s[:, :N])
    c_parts = split2(act_s[:, N:])
    scores[...] = dot_split(c_parts, b_parts, NT)
    tail_table, reading_table = steps.tail, steps.reading

    @pl.loop(0, pairs)
    def _(q):
        cols = pl.ds(pl.multiple_of(q * 128, 128), 128)
        faded = act_x[:, cols] * pair_columns(tail_table, q)
        state[cols, :] = dot_split(split2(faded), b_parts, TN)

    pass_state = links.remote(state, state_in, place.sibling())
    spread_c.forward()
    pass_state.wait_recv()

    @pl.loop(0, pairs)
    def _(q):
        cols = pl.ds(pl.multiple_of(q * 128, 128), 128)
        channels = act_x[:, cols]
        entered = state_in[cols, :] * second
        state_in[cols, :] = entered
        out = params_c[5:6, cols] * channels
        out = out + pair_columns(reading_table, q) * dot_split(c_parts, split2(entered), NT)
        for s in range(2):
            head = 2 * q + s
            gaps = column_of(totals[...], head) - step_rows[0, pl.ds(head, 1), :] + open_[...]
            weights = jnp.exp(gaps) * scores[...] * step_rows[1, pl.ds(head, 1), :]
            own = jnp.where((lanes < 64) == (s == 0), channels, 0.0)
            out = out + dot3(weights, own, NN)
        mixed[:, cols] = out

    stores += [
        links.move(pre_x, pre_x_out),
        links.move(pre_s, pre_s_out),
        links.move(raw, raw_out),
        links.move(conv_x, conv_x_out),
        links.move(conv_s, conv_s_out),
        links.move(state_in, state_out),
    ]
    g_z.share()
    g_z.finish()
    stores.append(links.move(wz, wz_out))
    project(n_high, n_low, wz, every, gate_pre, 512, 0, True)

    def over_tiles(body, carry):
        def step(n, carry):
            return body(pl.ds(pl.multiple_of(n * 128, 128), 128), carry)

        return lax.fori_loop(0, pairs, step, carry)

    def gated_at(cols):
        z = gate_pre[:, cols]
        return mixed[:, cols] * (z * jax.nn.sigmoid(z))

    def add_squares(cols, total):
        gated = gated_at(cols)
        return total + gated * gated

    zeros = jnp.zeros((tok, 128), F32)
    square_sum = over_tiles(add_squares, zeros)
    sums[...] = jnp.broadcast_to(jnp.sum(square_sum, axis=1, keepdims=True), (tok, 128)).T[0:8, :]
    copies = [links.remote(sums, sums_recv.at[k], device) for k, (device, _, _) in enumerate(column)]

    spread_c.finish()
    for copy in pairs_n:
        copy.wait_recv()
    links.settle(pairs_n)
    for copy in kept_n:
        copy.wait()
    stores.append(links.move(n_pairs, n_pairs_out))
    for k in range(place.tp):
        upstream = pick(settle, c_recv[k], TN)
        keep_left(k, upstream)

        @pl.when(place.z == k)
        def _():
            x_own[...] = upstream

    pairs_c, kept_c = exchange_blocks(c_pairs)
    stores.append(links.move(x_own, up_out))

    for copy in copies:
        copy.wait_recv()
    total = sums[...]
    for k in range(place.tp - 1):
        total = total + sums_recv[k]
    gscale = lax.rsqrt(down_lanes(total[0:1]) / INNER + EPSILON)

    def normalise(cols, carry):
        ny_both[own_rows, cols] = gated_at(cols) * gscale * params_c[6:7, cols]
        return carry

    over_tiles(normalise, 0)
    g_o.forward()
    give_ny = links.remote(ny_both.at[own_rows], ny_both.at[own_rows], place.sibling())
    keep_ny = links.move(ny_both.at[own_rows], ny_out)

    near = [place.f] + [place.chip(0, d) for d in range(1, place.side)] + [place.chip(d, 0) for d in range(1, place.side)]
    far = [place.chip(e, d) for e in range(1, place.side) for d in range(1, place.side)]
    for copy in kept_c:
        copy.wait()
    for copy in pairs_c:
        copy.wait_recv()
    give_ny.wait_recv()
    halve(ny_both, high, low)
    keep_wx.wait()
    links.settle(g_x.half_a + g_x.half_b + g_x.pair)
    blocks_o = wx.reshape(2, place.fsdp, shard_rows, inner).at[0]
    blocks_z = wx.reshape(2, place.fsdp, shard_rows, inner).at[1]
    for q in range(place.fsdp):
        weight_block(c_pairs.at[q], high, low, left_high, left_low, blocks_o.at[q])
    stores.append(links.move(blocks_o, g_out))
    def keep_rows(chip):
        at = pl.ds(pl.multiple_of(chip * chip_rows, 8), chip_rows)
        stores.append(links.move(wo.at[at], wo_out.at[at]))

    g_o.finish_near()
    for chip in near:
        keep_rows(chip)
    project(n_high, n_low, wo, near, d_normal, 512, 0, True)
    g_o.share()
    sum_o = Scatter(place, links, blocks_o, blocks_o, (land_a, land_b))
    sum_o.send_all()
    g_o.finish()
    for chip in far:
        keep_rows(chip)
    project(n_high, n_low, wo, far, d_normal, 512, 0, False)

    def add_inner(cols, total):
        return total + d_normal[:, cols] * params_c[6:7, cols] * gated_at(cols)

    inner_sum = over_tiles(add_inner, zeros)
    inner_sums[...] = jnp.broadcast_to(jnp.sum(inner_sum, axis=1, keepdims=True), (tok, 128)).T[0:8, :]
    copies = [links.remote(inner_sums, inner_recv.at[k], device) for k, (device, _, _) in enumerate(column)]
    links.settle([give_ny])
    keep_ny.wait()
    for copy in copies:
        copy.wait_recv()
    total = inner_sums[...]
    for k in range(place.tp - 1):
        total = total + inner_recv[k]
    pull = gscale * gscale * gscale * down_lanes(total[0:1]) / INNER

    def shape_all(cols, carry):
        z, y, upward, weight = gate_pre[:, cols], mixed[:, cols], d_normal[:, cols], params_c[6:7, cols]
        gate = jax.nn.sigmoid(z)
        act = z * gate
        gated = y * act
        d_gated = gscale * weight * upward - gated * pull
        d_normal[:, cols] = d_gated * act
        ny_both[own_rows, cols] = d_gated * y * gate * (1.0 + z * (1.0 - gate))
        gain_row[:, cols] = jnp.sum(upward * gated * gscale, axis=0, keepdims=True)
        return carry

    over_tiles(shape_all, 0)
    give_dz = links.remote(ny_both.at[own_rows], ny_both.at[own_rows], place.sibling())
    stores += [links.move(ny_both.at[own_rows], dz_out), links.move(d_normal, dmix_out)]
    give_dz.wait_recv()
    halve(ny_both, high, low)
    for q in range(place.fsdp):
        weight_block(n_pairs.at[q], high, low, left_high, left_low, blocks_z.at[q])
        stores.append(links.move(blocks_z.at[q], gz_out.at[q]))
    sum_o.land()
    for store in stores:
        store.wait()
    links.finish()


def backward_kernel(
    sizes,
    heads,
    lengths,
    slots_in,
    p_recv,
    gain,
    params_c,
    params_s,
    gain_row,
    tokens_in,
    up_in,
    n_pairs_in,
    pre_x_in,
    pre_s_in,
    raw_in,
    conv_x_in,
    conv_s_in,
    ny_in,
    dz_in,
    dmix_in,
    state_in_hbm,
    g_in,
    gz_in,
    land_a_in,
    land_b_in,
    wx_in,
    ws_in,
    wz_in,
    wo_in,
    result,
    grad_input,
    grad_z,
    grad_x,
    grad_bc,
    grad_dt,
    grad_out,
    small_out,
    gain_out,
    tokens,
    n_pairs,
    pre_x,
    pre_s,
    raw,
    conv_x,
    conv_s,
    state_in,
    dx_both,
    ds_both,
    high,
    low,
    left_high,
    left_low,
    blocks_o,
    blocks_z,
    blocks_s,
    o1a, o1b, o2a, o2b,
    z1a, z1b, z2a, z2b,
    x1a, x1b, x2a, x2b,
    s1a, s1b, s2a, s2b,
    blocks_x,
    stream,
    ws,
    d_bc,
    ds_high,
    ds_low,
    bc_rows,
    bc_recv,
    bc_grad,
    part_r,
    part_t,
    recv_r,
    recv_t,
    row_sums,
    row_recv,
    home_r,
    home_t,
    back_r,
    back_t,
    d_state,
    d_state_recv,
    d_b,
    d_c,
    pad_x,
    pad_s,
    head_x,
    head_s,
    open_,
    scores,
    d_scores,
    totals,
    steps_col,
    total_rows,
    grad_total,
    grad_step,
    grad_tail,
    grad_rows,
    skip_row,
    small,
    small_recv,
    small_z,
    gain_own,
    gain_recv,
    send,
    recv,
    local,
):
    place = Place(*sizes)
    links = Links(send, recv, local)
    tok, groups = tokens.shape[1], 2 * place.fsdp
    per_pair = tok // groups
    part = tokens.shape[2]
    inner = conv_x.shape[1]
    pairs = inner // 128
    first = place.c * tok
    own_rows = pl.ds(pl.multiple_of(place.c * tok, 128), tok)
    plane, column = place.plane(), place.column()

    partners = [entry[0] for entry in plane] + [entry[0] for entry in column]
    greet(partners)
    shares_r, shares_t = Shares(place, links, part_r, recv_r), Shares(place, links, part_t, recv_t)
    turns = shares_r.turns
    schedule = [(weight, turn) for weight in (wo_in, wz_in, wx_in) for turn in turns]
    fetched = []

    def fetch():
        k = len(fetched)
        if k < len(schedule):
            weight, turn = schedule[k]
            src = weight.at[pl.ds(pl.multiple_of(turn * part, 8), part)]
            fetched.append(links.move(src, stream.at[k % 2]))

    def weight_slice(k):
        fetched[k].wait()
        return stream.at[k % 2]

    greeted(partners)
    sum_o = Scatter(place, links, g_in, blocks_o, (o1a, o1b), (o2a, o2b))
    sum_z = Scatter(place, links, gz_in, blocks_z, (z1a, z1b), (z2a, z2b))
    sum_z.send_all()
    loads = {}
    for name, src, dst in (
        ("g", g_in, blocks_o),
        ("land_a", land_a_in, o1a),
        ("land_b", land_b_in, o1b),
        ("ny", ny_in, dx_both.at[own_rows]),
        ("raw", raw_in, raw),
        ("conv_s", conv_s_in, conv_s),
        ("dmix", dmix_in, pad_x.at[pl.ds(0, tok)]),
        ("state", state_in_hbm, state_in),
        ("conv_x", conv_x_in, conv_x),
        ("n_pairs", n_pairs_in, n_pairs),
        ("gz", gz_in, blocks_z),
        ("pre_x", pre_x_in, pre_x),
        ("pre_s", pre_s_in, pre_s),
        ("tokens", tokens_in, tokens),
        ("up", up_in, home_t),
        ("ws", ws_in, ws),
    ):
        loads[name] = links.move(src, dst)
    fetch()
    fetch()
    for name in ("g", "land_a", "land_b"):
        loads[name].wait()
    sum_o.pass_on()

    loads["raw"].wait()
    loads["conv_s"].wait()
    steps = Steps(raw[...], params_s, lengths, first)
    totals[...] = steps.total
    steps_col[...] = steps.step
    total_rows[...] = steps.total.T
    open_[...] = closed(lengths, first, tok, True)
    act_s = conv_s[...] * jax.nn.sigmoid(conv_s[...])
    b_parts, c_parts = split2(act_s[:, :N]), split2(act_s[:, N:])
    scores[...] = dot_split(b_parts, c_parts, NT)
    reading_table, tail_table = steps.reading, steps.tail
    grad_total[...] = jnp.zeros((tok, 128), F32)
    grad_step[...] = jnp.zeros((tok, 128), F32)
    grad_tail[...] = jnp.zeros((tok, 128), F32)
    d_c[...] = jnp.zeros((tok, N), F32)
    d_b[...] = jnp.zeros((tok, N), F32)
    d_scores[...] = jnp.zeros((tok, tok), F32)
    grad_rows[...] = jnp.zeros((128, tok), F32)
    lanes = iota((tok, 128), 1)

    def put(ref, head, value):
        ref[...] = ref[...] + jnp.where(lanes == head, value, 0.0)

    def by_head(value, s):
        return jnp.sum(jnp.where((lanes < 64) == (s == 0), value, 0.0), axis=1, keepdims=True)

    loads["ny"].wait()
    halve(dx_both.at[own_rows], high.at[own_rows], low.at[own_rows])

    def product(k, turn, fresh, out):
        ref = weight_slice(k)
        times_rows(high.at[own_rows], low.at[own_rows], ref, out, fresh)
        fetch()

    for k, turn in enumerate(turns):
        product(k, turn, True, part_r.at[turn])
        shares_r.send(k)

    loads["dmix"].wait()
    loads["state"].wait()

    @pl.loop(0, pairs)
    def _(q):
        cols = pl.ds(pl.multiple_of(q * 128, 128), 128)
        upward = pad_x[0:tok, cols] * pair_columns(reading_table, q)
        parts = split2(upward)
        entered = split2(state_in[cols, :])
        d_c[...] = d_c[...] + dot_split(parts, entered, NN)
        d_state[cols, :] = dot_split(parts, c_parts, TN)
        read = upward * dot_split(c_parts, entered, NT)
        for s in range(2):
            put(grad_total, 2 * q + s, by_head(read, s))

    give_state = links.remote(d_state, d_state_recv, place.sibling())

    loads["dz"] = links.move(dz_in, dx_both.at[own_rows])
    loads["dz"].wait()
    halve(dx_both.at[own_rows], high.at[own_rows], low.at[own_rows])
    for k, turn in enumerate(turns):
        product(place.tp + k, turn, True, part_t.at[turn])
    shares_r.forward()

    loads["conv_x"].wait()
    give_state.wait_recv()
    first_half = (place.c == 0).astype(F32)

    @pl.loop(0, pairs)
    def _(q):
        cols = pl.ds(pl.multiple_of(q * 128, 128), 128)
        conv = conv_x[:, cols]
        gate = jax.nn.sigmoid(conv)
        channels = conv * gate
        upward = pad_x[0:tok, cols]
        ended = split2(d_state_recv[cols, :] * first_half)
        tail = pair_columns(tail_table, q)
        from_end = dot_split(b_parts, ended, NT)
        d_b[...] = d_b[...] + dot_split(split2(channels * tail), ended, NN)
        into = params_c[5:6, cols] * upward + tail * from_end
        skip_row[:, cols] = jnp.sum(upward * channels, axis=0, keepdims=True)
        end_part = channels * from_end
        x_parts = split2(channels)
        for s in range(2):
            head = 2 * q + s
            put(grad_tail, head, by_head(end_part, s))
            step_col = column_of(steps_col[...], head)
            gaps = total_rows[pl.ds(head, 1), :] - column_of(totals[...], head) + open_[...]
            decay = jnp.exp(gaps)
            up_parts = split2(jnp.where((lanes < 64) == (s == 0), upward, 0.0))
            reach = dot_split(x_parts, up_parts, NT) * decay
            d_scores[...] = d_scores[...] + reach * step_col
            reach = reach * scores[...]
            put(grad_step, head, jnp.sum(reach, axis=1, keepdims=True))
            grad_rows[pl.ds(head, 1), :] = jnp.sum(reach * step_col, axis=0, keepdims=True)
            into = into + dot3(decay * scores[...] * step_col, jnp.where((lanes < 64) == (s == 0), upward, 0.0), NN)
        pad_x[0:tok, cols] = into * gate * (1.0 + conv * (1.0 - gate))


    score_parts = split2(d_scores[...])
    slope_s = silu_slope(conv_s[...])
    pad_s[0:tok, 0:N] = (d_b[...] + dot_split(score_parts, c_parts, NN)) * slope_s[:, :N]
    pad_s[0:tok, N : 2 * N] = (d_c[...] + dot_split(score_parts, b_parts, TN)) * slope_s[:, N:]
    halo = [
        links.remote(pad_x.at[pl.ds(0, 8)], head_x, place.sibling()),
        links.remote(pad_s.at[pl.ds(0, 8)], head_s, place.sibling()),
    ]
    step_now = steps_col[...]
    faded = grad_tail[...] * tail_table
    d_total = grad_total[...] + grad_rows[...].T - grad_step[...] * step_now - faded
    at_end = iota((tok, 128), 0) == tok - 1
    d_total = d_total + jnp.where(at_end, jnp.sum(faded, axis=0, keepdims=True), 0.0)
    onward = (iota((tok, tok), 1) >= iota((tok, tok), 0)).astype(BF16)
    d_log = pick(onward, d_total, NN)
    d_step = grad_step[...] + grad_tail[...] * steps.fading + d_log * steps.rate
    d_raw = jnp.where(lanes < heads, d_step * steps.slope, 0.0)
    small[...] = jnp.zeros_like(small)
    small[5:6, inner : inner + 128] = jnp.sum(d_raw, axis=0, keepdims=True)
    small[6:7, inner : inner + 128] = jnp.sum(d_log * step_now, axis=0, keepdims=True) * steps.rate
    head_of = (iota((inner, 128), 0) // (inner // heads) == iota((inner, 128), 1)).astype(BF16)
    skips = jnp.broadcast_to(skip_row[...], (8, inner))
    small[7:8, inner : inner + 128] = sum(dot1(piece, head_of, NN) for piece in split3(skips))[0:1]
    small[5:6, 0:inner] = gain_row[...]

    loads["pre_x"].wait()
    loads["pre_s"].wait()
    for copy in halo:
        copy.wait_recv()
    pad_x[tok : tok + 8, :] = head_x[...] * first_half
    pad_s[tok : tok + 8, :] = head_s[...] * first_half
    same = [same_before(lengths, first, tok, 3 - k) for k in range(3)]
    same_next = [same_before(lengths, first + 3 - k, tok, 3 - k) for k in range(3)]

    def back(padded, pre, params, out, start, n):
        cols = pl.ds(pl.multiple_of(n * 128, 128), 128)
        small_cols = pl.ds(pl.multiple_of(start + n * 128, 128), 128)
        here = padded[0:tok, cols]
        total = params[3:4, cols] * here
        small[3:4, small_cols] = jnp.sum(here * pre[8 : 8 + tok, cols], axis=0, keepdims=True)
        small[4:5, small_cols] = jnp.sum(here, axis=0, keepdims=True)
        for k in range(3):
            total = total + params[k : k + 1, cols] * (padded[3 - k : 3 - k + tok, cols] * same_next[k])
            value = here * (pre[5 + k : 5 + k + tok, cols] * same[k])
            small[k : k + 1, small_cols] = jnp.sum(value, axis=0, keepdims=True)
        out[:, cols] = total

    @pl.loop(0, pairs)
    def _(n):
        back(pad_x, pre_x, params_c, dx_both.at[own_rows], 0, n)

    give_dx = links.remote(dx_both.at[own_rows], dx_both.at[own_rows], place.sibling())

    @pl.loop(0, 2 * N // 128)
    def _(n):
        back(pad_s, pre_s, params_s, d_bc, inner, n)

    share = 2 * N // place.tp
    bc_rows[...] = d_bc[...].T

    def share_of(turn):
        return pl.ds(pl.multiple_of(turn * share, 8), share)

    give_bc = [
        links.remote(bc_rows.at[share_of(to_z)], bc_recv.at[k], device) for k, (device, to_z, _) in enumerate(column)
    ]

    hops_of = [
        [place.sibling()],
        [place.at(0, d) for d in range(1, place.side)],
        [place.at(d, 0) for d in range(1, place.side)],
    ]
    small_copies = []

    def hop_small(step):
        slot = sum(len(devices) for devices in hops_of[:step])
        for device in hops_of[step]:
            small_copies.append(links.remote(small, small_recv.at[slot], device))
            slot += 1

    def land_small(step):
        slot = sum(len(devices) for devices in hops_of[:step])
        total = small[...]
        links.settle(small_copies[slot:])
        for copy in small_copies[slot:]:
            copy.wait_recv()
            total = total + small_recv[slot]
            slot += 1
        small[...] = total

    hop_small(0)
    give_dx.wait_recv()
    loads["n_pairs"].wait()
    sum_x = Scatter(place, links, blocks_x, blocks_x, (x1a, x1b), (x2a, x2b))
    halve(dx_both, high, low)
    for hop in sum_x.order():
        block = place.chip(*hop)
        weight_block(n_pairs.at[block], high, low, left_high, left_low, blocks_x.at[block])
        sum_x.send(*hop)
    loads["gz"].wait()
    sum_z.pass_on()
    land_small(0)
    hop_small(1)

    loads["tokens"].wait()
    loads["ws"].wait()
    for copy in give_bc:
        copy.wait_recv()
    summed = bc_rows[share_of(place.z), :]
    for k in range(place.tp - 1):
        summed = summed + bc_recv[k]
    own_cols = pl.ds(pl.multiple_of(place.c * tok, 128), tok)
    ds_both[0:heads, own_cols] = d_raw.T[0:heads, :]
    ds_both[heads : heads + share, own_cols] = summed
    side_rows = ds_both.shape[0]
    if side_rows > heads + share:
        ds_both[heads + share :, own_cols] = jnp.zeros((side_rows - heads - share, tok), F32)
    give_ds = links.remote(ds_both.at[:, own_cols], ds_both.at[:, own_cols], place.sibling())
    ds_high[...], ds_low[...] = split2(ds_both[:, own_cols].T)
    give_ds.wait_recv()
    sum_s = Scatter(place, links, blocks_s, blocks_s, (s1a, s1b), (s2a, s2b))
    ds_parts = split2(ds_both[...])
    for hop in sum_s.order():
        block = place.chip(*hop)
        sum_s.blocks[block] = dot_split(ds_parts, split2(n_pairs[block]), NT)
        sum_s.send(*hop)
    row_sum = jnp.zeros((tok, 1), F32)
    squares = jnp.zeros((tok, 1), F32)
    for k, turn in enumerate(turns):
        out = part_t.at[turn]
        product(2 * place.tp + k, turn, False, out)
        shard_rows = ws.shape[1]
        for j in range(part // shard_rows):
            at = pl.ds(pl.multiple_of((turn * (part // shard_rows) + j) * side_rows, 8), side_rows)
            cols = slice(j * shard_rows, (j + 1) * shard_rows)
            out[:, cols] = out[:, cols] + dot_split((ds_high[...], ds_low[...]), split2(ws[at, :]), NN)
        shares_t.send(k)
        value = tokens[turn]
        row_sum = row_sum + jnp.sum(out[...] * gain[turn] * value, axis=1, keepdims=True)
        squares = squares + jnp.sum(value * value, axis=1, keepdims=True)
    row_sums[...] = jnp.where(lanes == 0, row_sum, 0.0).T[0:8, :]
    give_rows = [links.remote(row_sums, row_recv.at[k], device) for k, (device, _, _) in enumerate(column)]

    land_small(1)
    hop_small(2)
    stores = [links.move(sum_o.finish(), grad_out)]

    settle = settling(p_recv, tok)

    def rows(group):
        return pl.ds(pl.multiple_of(group * per_pair, 8), per_pair)

    def homeward(value, home, back_ref):
        home[...] = pick(settle, value, NN)
        at = rows(place.f * 2 + place.c)
        copies = [links.remote(home.at[rows(to)], back_ref.at[at], device) for device, to, _ in plane]
        return copies + [links.move(home.at[at], back_ref.at[at])]

    shares_r.finish()
    value = tokens[place.z] + part_r[place.z]
    way_r = homeward(value, home_r, back_r)

    sum_s.pass_on()
    shares_t.forward()
    sum_x.pass_on()
    stores.append(links.move(sum_z.finish(), grad_z))

    land_small(2)
    bc_cols = pl.ds(inner, 2 * N)
    give_small = [links.remote(small.at[:, bc_cols], small_z.at[j], device) for j, (device, _, _) in enumerate(column)]
    last = sum_s.finish()
    give_grad = [
        links.remote(last.at[pl.ds(heads, share)], bc_grad.at[share_of(place.z)], device) for device, _, _ in column
    ]
    bc_grad[share_of(place.z), :] = last[heads : heads + share, :]
    grad_dt[...] = last[0:heads, :]
    for copy in give_rows:
        copy.wait_recv()
    total = row_sums[...]
    for k in range(place.tp - 1):
        total = total + row_recv[k]
    shares_t.finish()
    d_normed = part_t[place.z]
    row_sum = jnp.concatenate([total, jnp.zeros((120, tok), F32)], axis=0).T[:, 0:1]
    width = place.tp * part
    scale = lax.rsqrt(squares / width + EPSILON)
    scaled = tokens[place.z] * scale
    gain_own[...] = jnp.sum(d_normed * scaled, axis=0, keepdims=True)
    give_gain = [links.remote(gain_own, gain_recv.at[j], device) for j, (device, _, _) in enumerate(plane)]
    loads["up"].wait()
    value = home_t[...] + scale * gain[place.z] * d_normed - scaled * (scale * scale * row_sum / width)
    way_t = homeward(value, home_t, back_t)

    stores.append(links.move(sum_x.finish(), grad_x))
    leave, _ = leaving(slots_in[...], tok, groups)
    for way, home, back_ref, out in ((way_r, home_r, back_r, result), (way_t, home_t, back_t, grad_input)):
        for copy in way[:-1]:
            copy.wait_recv()
        way[-1].wait()
        links.settle(way[:-1])
        home[...] = pick(leave, back_ref[...], NN)
        stores.append(links.move(home, out))
    total = gain_own[...]
    for j, copy in enumerate(give_gain):
        copy.wait_recv()
        total = total + gain_recv[j]
    gain_out[...] = total
    for copy in give_small:
        copy.wait_recv()
    small_out[...] = small[...]
    over_tp = small[0:5, inner : inner + 2 * N]
    for k in range(place.tp - 1):
        over_tp = over_tp + small_z[k, 0:5, :]
    small_out[0:5, inner : inner + 2 * N] = over_tp
    for copy in give_grad:
        copy.wait_recv()
    grad_bc[...] = bc_grad[...].T
    for store in stores:
        store.wait()
    links.finish()


ANYWHERE = pl.BlockSpec(memory_space=pl.ANY)
INSIDE = pl.BlockSpec(memory_space=pltpu.VMEM)
SCALARS = pl.BlockSpec(memory_space=pltpu.SMEM)


def shape(*dims):
    return jax.ShapeDtypeStruct(dims, F32)


def floats(*dims):
    return pltpu.VMEM(dims, F32)


def halves(*dims):
    return pltpu.VMEM(dims, BF16)


def side_height(heads, tp):
    return -(-(heads + 2 * N // tp) // 16) * 16


def forward_call(sizes, operands, heads):
    fsdp, _, tp = sizes
    inputs, w_x = operands[13], operands[15]
    tok, width = inputs.shape
    shard, inner = w_x.shape
    depth = shard * 2 * fsdp
    part = width // tp
    side = side_height(heads, tp)
    copies = 4 * gather_copies(math.isqrt(fsdp)) + 3 * (2 * fsdp - 1) + 8 * tp + 4 * fsdp + 8
    grid = math.isqrt(fsdp)
    landing = (grid - 1, grid, shard // 2, inner)
    outs = [
        (shape(8, inner), INSIDE),
        (shape(8, 2 * N), INSIDE),
        (shape(tp, tok, part), ANYWHERE),
        (shape(tok, part), ANYWHERE),
        (shape(fsdp, shard, 2 * tok), ANYWHERE),
        (shape(tok, 128), INSIDE),
        (shape(8 + tok, inner), ANYWHERE),
        (shape(8 + tok, 2 * N), ANYWHERE),
        (shape(tok, 128), ANYWHERE),
        (shape(tok, inner), ANYWHERE),
        (shape(tok, 2 * N), ANYWHERE),
        (shape(tok, inner), ANYWHERE),
        (shape(tok, inner), ANYWHERE),
        (shape(tok, inner), ANYWHERE),
        (shape(1, inner), INSIDE),
        (shape(inner, N), ANYWHERE),
        (shape(fsdp, shard, inner), ANYWHERE),
        (shape(fsdp, shard, inner), ANYWHERE),
        (shape(*landing), ANYWHERE),
        (shape(*landing), ANYWHERE),
        (shape(depth, inner), ANYWHERE),
        (shape(2 * fsdp * side, shard), ANYWHERE),
        (shape(depth, inner), ANYWHERE),
        (shape(depth, inner), ANYWHERE),
    ]
    return pl.pallas_call(
        functools.partial(forward_kernel, sizes),
        out_shape=tuple(out for out, _ in outs),
        in_specs=[SCALARS] + [INSIDE] * 12 + [ANYWHERE] * 5,
        out_specs=tuple(spec for _, spec in outs),
        scratch_shapes=[
            floats(depth, inner),
            floats(2 * fsdp * side, shard),
            floats(depth, inner),
            floats(depth, inner),
            floats(side, shard),
            floats(tok, part),
            floats(tok, part),
            floats(tok, part),
            floats(tok, part),
            floats(2 * fsdp, 8, 128),
            floats(2 * fsdp, 8, 128),
            floats(tp, tok, part),
            floats(tp, tok, part),
            floats(tp, tok, part),
            halves(fsdp, tok, 2 * shard),
            halves(fsdp, tok, 2 * shard),
            floats(width, tok),
            floats(fsdp, shard, 2 * tok),
            floats(fsdp, shard, 2 * tok),
            floats(8 + tok, inner),
            floats(8 + tok, 2 * N),
            floats(tok, 128),
            floats(2 * N, max(tok, shard)),
            floats(8, inner),
            floats(8, 2 * N),
            floats(tok, inner),
            floats(tok, 2 * N),
            floats(tok, inner),
            floats(tok, 2 * N),
            floats(tok, 128),
            floats(2, 128, tok),
            floats(tok, tok),
            floats(tok, tok),
            floats(inner, N),
            floats(inner, N),
            floats(tok, inner),
            floats(tok, inner),
            floats(tok, inner),
            floats(2 * tok, inner),
            halves(2 * tok, inner),
            halves(2 * tok, inner),
            halves(shard, 2 * tok),
            halves(shard, 2 * tok),
            floats(8, tok),
            floats(tp - 1, 8, tok),
            floats(8, tok),
            floats(tp - 1, 8, tok),
            pltpu.SemaphoreType.DMA((copies,)),
            pltpu.SemaphoreType.DMA((copies,)),
            pltpu.SemaphoreType.DMA((48 + 3 * fsdp,)),
        ],
        compiler_params=pltpu.CompilerParams(collective_id=0, has_side_effects=True, vmem_limit_bytes=VMEM_LIMIT),
        name="forward",
    )(*operands)


def backward_call(sizes, heads, operands, tok, width, shard, inner):
    fsdp, _, tp = sizes
    grid = math.isqrt(fsdp)
    part = width // tp
    share = 2 * N // tp
    side = side_height(heads, tp)
    hops = grid - 1
    copies = 4 + 4 * (2 * hops * grid + 2 * hops) + 9 * tp + 3 * (2 * fsdp) + 2 * hops + 4

    def landing(rows, columns):
        return [
            floats(hops, grid, rows // 2, columns),
            floats(hops, grid, rows // 2, columns),
            floats(hops, rows // 2, columns),
            floats(hops, rows // 2, columns),
        ]

    return pl.pallas_call(
        functools.partial(backward_kernel, sizes, heads),
        out_shape=(
            shape(tok, part),
            shape(tok, part),
            shape(shard, inner),
            shape(shard, inner),
            shape(shard, 2 * N),
            shape(heads, shard),
            shape(shard, inner),
            shape(8, inner + 2 * N),
            shape(1, part),
        ),
        in_specs=[SCALARS] + [INSIDE] * 6 + [ANYWHERE] * 20,
        out_specs=(ANYWHERE, ANYWHERE, ANYWHERE, ANYWHERE, INSIDE, INSIDE, ANYWHERE, INSIDE, INSIDE),
        scratch_shapes=[
            floats(tp, tok, part),
            floats(fsdp, shard, 2 * tok),
            floats(8 + tok, inner),
            floats(8 + tok, 2 * N),
            floats(tok, 128),
            floats(tok, inner),
            floats(tok, 2 * N),
            floats(inner, N),
            floats(2 * tok, inner),
            floats(side, 2 * tok),
            halves(2 * tok, inner),
            halves(2 * tok, inner),
            halves(shard, 2 * tok),
            halves(shard, 2 * tok),
            floats(fsdp, shard, inner),
            floats(fsdp, shard, inner),
            floats(fsdp, side, shard),
            *landing(shard, inner),
            *landing(shard, inner),
            *landing(shard, inner),
            *landing(side, shard),
            floats(fsdp, shard, inner),
            floats(2, part, inner),
            floats(2 * fsdp * side, shard),
            floats(tok, 2 * N),
            halves(tok, side),
            halves(tok, side),
            floats(2 * N, tok),
            floats(tp - 1, share, tok),
            floats(2 * N, shard),
            floats(tp, tok, part),
            floats(tp, tok, part),
            floats(max(4, tp - 1), tok, part),
            floats(max(4, tp - 1), tok, part),
            floats(8, tok),
            floats(tp - 1, 8, tok),
            floats(tok, part),
            floats(tok, part),
            floats(tok, part),
            floats(tok, part),
            floats(inner, N),
            floats(inner, N),
            floats(tok, N),
            floats(tok, N),
            floats(8 + tok, inner),
            floats(8 + tok, 2 * N),
            floats(8, inner),
            floats(8, 2 * N),
            floats(tok, tok),
            floats(tok, tok),
            floats(tok, tok),
            floats(tok, 128),
            floats(tok, 128),
            floats(128, tok),
            floats(tok, 128),
            floats(tok, 128),
            floats(tok, 128),
            floats(128, tok),
            floats(1, inner),
            floats(8, inner + 2 * N),
            floats(1 + 2 * hops, 8, inner + 2 * N),
            floats(tp - 1, 8, 2 * N),
            floats(1, part),
            floats(2 * fsdp - 1, 1, part),
            pltpu.SemaphoreType.DMA((copies,)),
            pltpu.SemaphoreType.DMA((copies,)),
            pltpu.SemaphoreType.DMA((24 + 3 * tp,)),
        ],
        compiler_params=pltpu.CompilerParams(collective_id=1, has_side_effects=True, vmem_limit_bytes=VMEM_LIMIT),
        name="backward",
    )(*operands)


def last_kernel(heads, small, gain, bc, dt, *refs):
    large, outs, held, sems = refs[:5], refs[5:21], refs[21:26], refs[26]
    loads = [pltpu.make_async_copy(src, dst, sems.at[0, k]) for k, (src, dst) in enumerate(zip(large, held))]
    stores = [pltpu.make_async_copy(src, dst, sems.at[1, k]) for k, (src, dst) in enumerate(zip(held, outs))]
    for load in loads:
        load.start()
    for load, store in zip(loads, stores):
        load.wait()
        store.start()
    grad_bc, grad_dt, taps_x, bias_x, taps_s, bias_s, dt_bias, a_log, d_skip, gate_gain, gain_in = outs[5:]
    inner = taps_x.shape[1]
    grad_bc[...] = bc[...]
    grad_dt[...] = dt[...]
    taps_x[...] = small[0:4, 0:inner]
    bias_x[...] = small[4:5, 0:inner]
    taps_s[...] = small[0:4, inner : inner + 2 * N]
    bias_s[...] = small[4:5, inner : inner + 2 * N]
    dt_bias[...] = small[5:6, inner : inner + heads]
    a_log[...] = small[6:7, inner : inner + heads]
    d_skip[...] = small[7:8, inner : inner + heads]
    gate_gain[...] = small[5:6, 0:inner]
    gain_in[...] = gain[...]
    for store in stores:
        store.wait()


def last_call(heads, small, gain, bc, dt, *large):
    inner, part = small.shape[1] - 2 * N, gain.shape[1]
    few = [
        bc.shape,
        dt.shape,
        (4, inner),
        (1, inner),
        (4, 2 * N),
        (1, 2 * N),
        (1, heads),
        (1, heads),
        (1, heads),
        (1, inner),
        (1, part),
    ]
    return pl.pallas_call(
        functools.partial(last_kernel, heads),
        out_shape=tuple([shape(*value.shape) for value in large] + [shape(*dims) for dims in few]),
        in_specs=[INSIDE] * 4 + [ANYWHERE] * 5,
        out_specs=tuple([ANYWHERE] * 5 + [INSIDE] * len(few)),
        scratch_shapes=[floats(*value.shape) for value in large] + [pltpu.SemaphoreType.DMA((2, 5))],
        compiler_params=pltpu.CompilerParams(vmem_limit_bytes=VMEM_LIMIT),
        name="results",
    )(small, gain, bc, dt, *large)


def shards(
    inputs,
    cotangent,
    seq_lengths,
    slots,
    gain_in,
    w_z,
    w_x,
    w_dt,
    w_bc,
    w_out,
    conv_x,
    conv_x_bias,
    conv_bc,
    conv_bc_bias,
    dt_bias,
    a_log,
    d_skip,
    gate_gain,
):
    sizes = (lax.axis_size("fsdp"), lax.axis_size("ctx"), lax.axis_size("tp"))
    tok, width = inputs.shape
    shard, inner = w_x.shape
    heads = w_dt.shape[1]
    tp = sizes[2]
    operands = (
        seq_lengths,
        slots[None],
        gain_in[None],
        conv_x,
        conv_x_bias[None],
        conv_bc,
        conv_bc_bias[None],
        dt_bias[None],
        a_log[None],
        d_skip[None],
        gate_gain[None],
        w_bc,
        w_dt.T,
        inputs,
        cotangent,
        w_x,
        w_z,
        w_out,
    )
    params_c, params_s, tokens, up, n_pairs, p_recv, *kept = forward_call(sizes, operands, heads)
    pre_x, pre_s, raw, conv_x_kept, conv_s_kept, normal_y, d_gate, d_mixed, gain_row, *rest = kept
    operands = (
        seq_lengths,
        slots[None],
        p_recv,
        gain_in.reshape(tp, 1, width // tp),
        params_c,
        params_s,
        gain_row,
        tokens,
        up,
        n_pairs,
        pre_x,
        pre_s,
        raw,
        conv_x_kept,
        conv_s_kept,
        normal_y,
        d_gate,
        d_mixed,
        *rest,
    )
    result, grad_input, grad_z, grad_x, grad_bc, grad_dt, grad_out, small, gain = backward_call(
        sizes, heads, operands, tok, width, shard, inner
    )
    outs = last_call(heads, small, gain, grad_bc, grad_dt, result, grad_input, grad_z, grad_x, grad_out)
    result, grad_input, grad_z, grad_x, grad_out, grad_bc, grad_dt, taps_x, bias_x, taps_s, bias_s, *few = outs
    return (
        result,
        grad_input,
        grad_z,
        grad_x,
        grad_dt.T,
        grad_bc,
        grad_out,
        taps_x,
        bias_x[0],
        taps_s,
        bias_s[0],
        *[value[0] for value in few],
    )


def solution(mesh):
    return jax.shard_map(
        shards,
        mesh=mesh,
        in_specs=(
            P(("fsdp", "ctx"), None),
            P(("fsdp", "ctx"), None),
            P("fsdp", None),
            P(("fsdp", "ctx")),
            P(),
            P(("fsdp", "ctx"), "tp"),
            P(("fsdp", "ctx"), "tp"),
            P(("fsdp", "ctx"), "tp"),
            P(("fsdp", "ctx"), None),
            P(("fsdp", "ctx"), "tp"),
            P(None, "tp"),
            P("tp"),
            P(),
            P(),
            P("tp"),
            P("tp"),
            P("tp"),
            P("tp"),
        ),
        out_specs=(
            P(("fsdp", "ctx"), "tp"),
            P(("fsdp", "ctx"), "tp"),
            P(("fsdp", "ctx"), "tp"),
            P(("fsdp", "ctx"), "tp"),
            P(("fsdp", "ctx"), "tp"),
            P(("fsdp", "ctx"), None),
            P(("fsdp", "ctx"), "tp"),
            P(None, "tp"),
            P("tp"),
            P(),
            P(),
            P("tp"),
            P("tp"),
            P("tp"),
            P("tp"),
            P("tp"),
        ),
        check_vma=False,
    )
```

```python
import functools
import math

import jax
import jax.numpy as jnp
from jax import lax
from jax.experimental import pallas as pl
from jax.experimental.pallas import tpu as pltpu
from jax.sharding import PartitionSpec as P

N = 128
SPAN = 256
INNER = 4096
EPSILON = 1e-05
F32 = jnp.float32
BF16 = jnp.bfloat16
MESH = pl.DeviceIdType.MESH
NN = (((1,), (0,)), ((), ()))
NT = (((1,), (1,)), ((), ()))
TN = (((0,), (0,)), ((), ()))
VMEM_LIMIT = 62 << 20


def split2(value):
    high = value.astype(BF16)
    return high, (value - high.astype(F32)).astype(BF16)


def split3(value):
    high = value.astype(BF16)
    rest = value - high.astype(F32)
    middle = rest.astype(BF16)
    return high, middle, (rest - middle.astype(F32)).astype(BF16)


def dot1(left, right, dims):
    return lax.dot_general(left, right, dims, preferred_element_type=F32)


def dot_split(left, right, dims):
    (lh, ll), (rh, rl) = left, right
    return dot1(lh, rh, dims) + (dot1(lh, rl, dims) + dot1(ll, rh, dims))


def dot3(left, right, dims):
    return dot_split(split2(left), split2(right), dims)


def pick(table, value, dims):
    parts = split3(value)
    return dot1(table, parts[0], dims) + dot1(table, parts[1], dims) + dot1(table, parts[2], dims)


def iota(shape, dim):
    return lax.broadcasted_iota(jnp.int32, shape, dim)


class Place:
    def __init__(self, fsdp, ctx, tp):
        self.fsdp, self.n_ctx, self.tp = fsdp, ctx, tp
        self.side = math.isqrt(fsdp)
        assert self.side * self.side == fsdp and ctx == 2
        self.f = lax.axis_index("fsdp")
        self.c = lax.axis_index("ctx")
        self.z = lax.axis_index("tp")
        self.y, self.x = self.f // self.side, self.f % self.side

    def chip(self, dy, dx):
        side = self.side
        return ((self.y + dy + side) % side) * side + (self.x + dx + side) % side

    def block(self, dy, dx, core):
        return self.chip(dy, dx) * 2 + core

    def at(self, dy, dx):
        return (self.chip(dy, dx), self.c, self.z)

    def sibling(self):
        return (self.f, 1 - self.c, self.z)

    def plane(self):
        out = []
        for df in range(self.fsdp):
            for dc in range(2):
                if df or dc:
                    to_f = (self.f + df) % self.fsdp
                    from_f = (self.f - df + self.fsdp) % self.fsdp
                    core = (self.c + dc) % 2
                    out.append(((to_f, core, self.z), to_f * 2 + core, from_f * 2 + core))
        return out

    def column(self):
        out = []
        for dz in range(1, self.tp):
            to_z = (self.z + dz) % self.tp
            out.append(((self.f, self.c, to_z), to_z, (self.z - dz + self.tp) % self.tp))
        return out


class Links:
    def __init__(self, send, recv, local):
        self.send, self.recv, self.local = send, recv, local
        self.used, self.used_local = 0, 0
        self.open = []

    def remote(self, src, dst, device):
        k = self.used
        self.used += 1
        copy = pltpu.make_async_remote_copy(
            src_ref=src,
            dst_ref=dst,
            send_sem=self.send.at[k],
            recv_sem=self.recv.at[k],
            device_id=device,
            device_id_type=MESH,
        )
        copy.start()
        self.open.append(copy)
        return copy

    def plan(self, src, dst, device, lands_as=None):
        k = self.used
        self.used += 1
        copy = pltpu.make_async_remote_copy(
            src_ref=src,
            dst_ref=dst,
            send_sem=self.send.at[k],
            recv_sem=self.recv.at[k if lands_as is None else lands_as.slot],
            device_id=device,
            device_id_type=MESH,
        )
        copy.slot = k
        return copy

    def move(self, src, dst):
        k = self.used_local
        self.used_local += 1
        copy = pltpu.make_async_copy(src, dst, self.local.at[k])
        copy.start()
        return copy

    def settle(self, copies):
        for copy in copies:
            copy.wait_send()
            self.open = [other for other in self.open if other is not copy]

    def finish(self):
        assert self.used <= self.send.shape[0] and self.used_local <= self.local.shape[0]
        self.settle(list(self.open))


def greet(devices):
    barrier = pltpu.get_barrier_semaphore()
    for device in devices:
        pl.semaphore_signal(barrier, inc=1, device_id=device, device_id_type=MESH)


def greeted(devices):
    pl.semaphore_wait(pltpu.get_barrier_semaphore(), len(devices))


class Spread:
    def __init__(self, place, links, slices):
        self.place, self.links, self.slices = place, links, slices
        self.line = place.tp == 4
        z, mine = place.z, slices.at[place.z]
        if not self.line:
            self.copies = [links.remote(mine, mine, device) for device, _, _ in place.column()]
            return
        self.copies = [links.remote(mine, mine, (place.f, place.c, z ^ d)) for d in (1, 2)]
        self.inner = (z == 1) | (z == 2)
        across = links.plan(mine, mine, (place.f, place.c, 3 - z))
        onward = slices.at[z ^ 2]
        self.onward = links.plan(onward, onward, (place.f, place.c, z ^ 1), across)
        self.across = across

        @pl.when(self.inner)
        def _():
            across.start()

    def forward(self):
        if self.line:
            self.copies.pop().wait_recv()

            @pl.when(self.inner)
            def _():
                self.onward.start()

    def finish(self):
        for copy in self.copies:
            copy.wait_recv()
        if self.line:
            self.across.wait_recv()

            @pl.when(self.inner)
            def _():
                self.across.wait_send()
                self.onward.wait_send()


class Gather:
    def __init__(self, place, links, shard, whole):
        self.place, self.links, self.shard, self.whole = place, links, shard, whole
        self.rows = shard.shape[0]
        self.near = 0

    def rows_of(self, block, start=0, count=None):
        count = self.rows if count is None else count
        return self.whole.at[pl.ds(pl.multiple_of(block * self.rows + start, 8), count)]

    def part(self, block, half):
        return self.rows_of(block, half * (self.rows // 2), self.rows // 2)

    def start(self):
        p, steps = self.place, range(1, self.place.side)
        me = p.block(0, 0, p.c)
        self.row, self.col = [[], []], [[], []]
        for turn in range(2):
            for d in steps:
                shard = self.shard.at[pl.ds(turn * (self.rows // 2), self.rows // 2)]
                self.row[turn].append(self.links.remote(shard, self.part(me, turn), p.at(0, d)))
                shard = self.shard.at[pl.ds((1 - turn) * (self.rows // 2), self.rows // 2)]
                self.col[turn].append(self.links.remote(shard, self.part(me, 1 - turn), p.at(d, 0)))
        mine = self.rows_of(me)
        self.pair = [self.links.remote(self.shard, mine, p.sibling())]
        self.own = self.links.move(self.shard, mine)

    def forward(self):
        p, steps = self.place, range(1, self.place.side)
        self.half_a, self.half_b = [], []
        for k, d in enumerate(steps):
            self.row[0][k].wait_recv()
            part = self.part(p.block(0, -d, p.c), 0)
            self.half_a += [self.links.remote(part, part, p.at(e, 0)) for e in steps]
        for k, e in enumerate(steps):
            self.col[0][k].wait_recv()
            part = self.part(p.block(-e, 0, p.c), 1)
            self.half_b += [self.links.remote(part, part, p.at(0, d)) for d in steps]
        for k, d in enumerate(steps):
            self.row[1][k].wait_recv()
            whole = self.rows_of(p.block(0, -d, p.c))
            self.pair.append(self.links.remote(whole, whole, p.sibling()))
        for k, e in enumerate(steps):
            self.col[1][k].wait_recv()
            whole = self.rows_of(p.block(-e, 0, p.c))
            self.pair.append(self.links.remote(whole, whole, p.sibling()))

    def share(self):
        p, steps, half = self.place, range(1, self.place.side), self.rows // 2
        k = 0
        for d in steps:
            for e in steps:
                self.half_a[k].wait_recv()
                part = self.rows_of(p.block(-e, -d, p.c), 0, half)
                self.pair.append(self.links.remote(part, part, p.sibling()))
                k += 1
        k = 0
        for e in steps:
            for d in steps:
                self.half_b[k].wait_recv()
                part = self.rows_of(p.block(-e, -d, p.c), half, half)
                self.pair.append(self.links.remote(part, part, p.sibling()))
                k += 1

    def finish_near(self):
        self.own.wait()
        self.near = 1 + 2 * (self.place.side - 1)
        for copy in self.pair[: self.near]:
            copy.wait_recv()

    def finish(self):
        if self.near == 0:
            self.finish_near()
        for copy in self.pair[self.near :]:
            copy.wait_recv()


def gather_copies(side):
    steps = side - 1
    return 6 * steps + 1 + 4 * steps * steps


def down_lanes(row):
    return jnp.broadcast_to(row, (128, row.shape[1])).T


def leaving(slots, tok, groups):
    slots = down_lanes(slots.astype(F32)).astype(jnp.int32)
    targets = slots >> (tok.bit_length() - 1)
    lanes = iota((tok, 128), 1)
    member = (targets == lanes).astype(F32)
    earlier = (iota((tok, tok), 0) > iota((tok, tok), 1)).astype(BF16)
    ranks = jnp.sum(dot1(earlier, member.astype(BF16), NN) * member, axis=1, keepdims=True)
    send_at = (targets[:, :1] * (tok // groups)).astype(F32) + ranks
    leave = (send_at == iota((tok, tok), 1).astype(F32)).astype(BF16)
    places = jnp.where(ranks == lanes.astype(F32), (slots - targets * tok).astype(F32), 0.0)
    return leave, dot1(member.astype(BF16), places.astype(BF16), TN)


def arrived(rows, tok, per_pair):
    groups = rows.shape[0]
    rows = jnp.concatenate([rows, jnp.zeros((128 - groups, 128), F32)], axis=0)
    token, lanes = iota((tok, 128), 0), iota((tok, 128), 1)
    spread = dot1((token // per_pair == lanes).astype(BF16), rows.astype(BF16), NN)
    place = jnp.sum(jnp.where(token % per_pair == lanes, spread, 0.0), axis=1, keepdims=True)
    return jnp.broadcast_to(place, (tok, 128))


def settling(places, tok):
    return (places[:, :1] == iota((tok, tok), 1).astype(F32)).astype(BF16)


def halve(value_ref, high, low):
    @pl.loop(0, value_ref.shape[1] // 128)
    def _(n):
        cols = pl.ds(pl.multiple_of(n * 128, 128), 128)
        high[:, cols], low[:, cols] = split2(value_ref[:, cols])


def project(left_high, left_low, whole, chips, out, tile, first_row, fresh):
    _, rows, width = left_high.shape

    @pl.loop(0, whole.shape[1] // tile)
    def _(n):
        cols = pl.ds(pl.multiple_of(n * tile, 128), tile)
        total = jnp.zeros((rows, tile), F32) if fresh else out[first_row : first_row + rows, cols]
        for chip in chips:
            at = pl.ds(chip * width if isinstance(chip, int) else pl.multiple_of(chip * width, 8), width)
            total = total + dot_split((left_high[chip], left_low[chip]), split2(whole[at, cols]), NN)
        out[first_row : first_row + rows, cols] = total


def weight_block(left_ref, high, low, left_high, left_low, out):
    left_high[...], left_low[...] = split2(left_ref[...])

    @pl.loop(0, high.shape[1] // 512)
    def _(n):
        cols = pl.ds(pl.multiple_of(n * 512, 128), 512)
        out[:, cols] = dot_split((left_high[...], left_low[...]), (high[:, cols], low[:, cols]), NN)


def times_rows(high, low, rows_ref, out, fresh):
    tile = min(256, rows_ref.shape[0])
    for n in range(rows_ref.shape[0] // tile):
        at = slice(n * tile, (n + 1) * tile)
        value = dot_split((high[...], low[...]), split2(rows_ref[at, :]), NT)
        out[:, at] = value if fresh else out[:, at] + value


class Scatter:
    def __init__(self, place, links, source, blocks, first, second=None):
        self.place, self.links, self.blocks = place, links, blocks
        self.first, self.second = first, second
        self.half = source.shape[1] // 2
        self.source = source
        self.copies_a, self.copies_b = {}, {}

    def order(self):
        side = self.place.side
        hops = [(dy, dx) for dy in range(side) for dx in range(side)]
        return sorted(hops, key=lambda hop: -(hop[0] > 0) - (hop[1] > 0))

    def halves(self, dy, dx, blocks=None):
        ref = (self.blocks if blocks is None else blocks).at[self.place.chip(dy, dx)]
        return ref.at[pl.ds(0, self.half)], ref.at[pl.ds(self.half, self.half)]

    def send(self, dy, dx):
        p, side = self.place, self.place.side
        upper, lower = self.halves(dy, dx, self.source)
        if dy:
            target = self.first[0].at[dy - 1, (p.x + dx) % side]
            self.copies_a[dy, dx] = self.links.remote(upper, target, p.at(dy, 0))
        if dx:
            target = self.first[1].at[dx - 1, (p.y + dy) % side]
            self.copies_b[dy, dx] = self.links.remote(lower, target, p.at(0, dx))

    def send_all(self):
        for hop in self.order():
            self.send(*hop)

    def land(self):
        for copy in [*self.copies_a.values(), *self.copies_b.values()]:
            copy.wait_recv()

    def pass_on(self):
        p, side = self.place, self.place.side
        self.last_a, self.last_b = [], []
        for d in list(range(1, side)) + [0]:
            upper, _ = self.halves(0, d)
            total = upper[...]
            for e in range(1, side):
                if (e, d) in self.copies_a:
                    self.copies_a[e, d].wait_recv()
                total = total + self.first[0][e - 1, (p.x + d) % side]
            upper[...] = total
            if d:
                self.last_a.append(self.links.remote(upper, self.second[0].at[d - 1], p.at(0, d)))
            _, lower = self.halves(d, 0)
            total = lower[...]
            for e in range(1, side):
                if (d, e) in self.copies_b:
                    self.copies_b[d, e].wait_recv()
                total = total + self.first[1][e - 1, (p.y + d) % side]
            lower[...] = total
            if d:
                self.last_b.append(self.links.remote(lower, self.second[1].at[d - 1], p.at(d, 0)))

    def finish(self):
        for k, (copies, part) in enumerate(zip((self.last_a, self.last_b), self.halves(0, 0))):
            total = part[...]
            for d, copy in enumerate(copies):
                copy.wait_recv()
                total = total + self.second[k][d]
            part[...] = total
        return self.blocks.at[self.place.chip(0, 0)]


class Shares:
    def __init__(self, place, links, parts, landing):
        self.place, self.links, self.parts, self.landing = place, links, parts, landing
        self.line = place.tp == 4
        z = place.z
        self.copies = []
        if self.line:
            self.turns = [z ^ 3, z ^ 2, z ^ 1, z]
            self.inner = (z == 1) | (z == 2)
        else:
            self.turns = [(z + d + 1) % place.tp for d in range(place.tp)]

    def send(self, k):
        place, z = self.place, self.place.z
        if k == place.tp - 1:
            return
        part = self.parts.at[self.turns[k]]
        if not self.line:
            self.copies.append(self.links.remote(part, self.landing.at[k], (place.f, place.c, self.turns[k])))
            return
        if k == 0:
            self.direct = self.links.plan(part, self.landing.at[2], (place.f, place.c, z ^ 3))
            self.extra = self.links.plan(part, self.landing.at[3], (place.f, place.c, z ^ 1))

            @pl.when(self.inner)
            def _():
                self.direct.start()

            @pl.when(jnp.logical_not(self.inner))
            def _():
                self.extra.start()

        elif k == 1:
            self.across = self.links.plan(part, self.landing.at[1], (place.f, place.c, z ^ 2))

            @pl.when(jnp.logical_not(self.inner))
            def _():
                self.across.start()

        else:
            self.copies.append(self.links.remote(part, self.landing.at[0], (place.f, place.c, z ^ 1)))

    def forward(self):
        if self.line:

            @pl.when(self.inner)
            def _():
                self.extra.wait_recv()
                part = self.parts.at[self.place.z ^ 2]
                part[...] = part[...] + self.landing[3]
                self.across.start()

    def finish(self):
        own = self.parts.at[self.place.z]
        total = own[...]
        for k, copy in enumerate(self.copies):
            copy.wait_recv()
            total = total + self.landing[k]
        if self.line:
            self.across.wait_recv()
            total = total + self.landing[1]
            self.across.wait_send()
        own[...] = total
        if self.line:

            @pl.when(self.inner)
            def _():
                self.direct.wait()
                own[...] = own[...] + self.landing[2]

            @pl.when(jnp.logical_not(self.inner))
            def _():
                self.extra.wait_send()


def silu_slope(value):
    gate = jax.nn.sigmoid(value)
    return gate * (1.0 + value * (1.0 - gate))


def softplus(value):
    return jnp.maximum(value, 0.0) + jnp.log1p(jnp.exp(-jnp.abs(value)))


def segments(lengths, position):
    bound, seg = 0, jnp.zeros_like(position)
    for k in range(lengths.shape[1]):
        bound = bound + lengths[0, k]
        seg = seg + (bound <= position).astype(jnp.int32)
    return seg


def same_before(lengths, first, tok, distance):
    position = first + iota((tok, 128), 0)
    return (segments(lengths, position) == segments(lengths, position - distance)).astype(F32)


def wide(table, width):
    return jnp.concatenate([table] * (width // 128), axis=1)


def column_of(table, head):
    lanes = iota(table.shape, 1)
    return jnp.sum(jnp.where(lanes == head, table, 0.0), axis=1, keepdims=True)


def pair_columns(table, pair):
    first, second = column_of(table, 2 * pair), column_of(table, 2 * pair + 1)
    return jnp.where(iota(table.shape, 1) < 64, first, second)


class Steps:
    def __init__(self, raw, params_s, lengths, first):
        tok = raw.shape[0]
        shifted = raw + params_s[5:6, :128]
        self.slope = jax.nn.sigmoid(shifted)
        self.step = softplus(shifted)
        self.rate = -jnp.exp(params_s[6:7, :128])
        until = (iota((tok, tok), 0) >= iota((tok, tok), 1)).astype(BF16)
        self.total = pick(until, self.step * self.rate, NN)
        position = first + iota((tok, 128), 0)
        seg = segments(lengths, position)
        before = segments(lengths, jnp.full((tok, 128), first - 1, jnp.int32))
        last = segments(lengths, jnp.full((tok, 128), first + tok - 1, jnp.int32))
        self.reading = jnp.exp(self.total) * (seg == before).astype(F32)
        self.fading = jnp.exp(self.total[tok - 1 : tok] - self.total) * (seg == last).astype(F32)
        self.tail = self.fading * self.step


def closed(lengths, first, tok, flipped):
    rows, cols = first + iota((tok, tok), 0), first + iota((tok, tok), 1)
    order = rows <= cols if flipped else rows >= cols
    seg_rows = segments(lengths, first + iota((tok, 1), 0))
    seg_cols = segments(lengths, first + iota((1, tok), 1))
    return jnp.where(order & (seg_rows == seg_cols), 0.0, -1e30)


def convolve(padded, params, lengths, first, conv, act):
    tok, tile = conv.shape[0], 128
    same = [same_before(lengths, first, tok, 3 - k) for k in range(3)]

    @pl.loop(0, conv.shape[1] // tile)
    def _(n):
        cols = pl.ds(pl.multiple_of(n * tile, 128), tile)
        total = params[4:5, cols] + params[3:4, cols] * padded[8 : 8 + tok, cols]
        for k in range(3):
            total = total + params[k : k + 1, cols] * (padded[5 + k : 5 + k + tok, cols] * same[k])
        conv[:, cols] = total
        act[:, cols] = total * jax.nn.sigmoid(total)


def forward_kernel(
    sizes,
    lengths,
    slots_in,
    gain,
    taps_x,
    bias_x,
    taps_s,
    bias_s,
    dt_bias,
    a_log,
    d_skip,
    gate_gain,
    w_bc,
    w_dt,
    x_in,
    c_in,
    w_x,
    w_z,
    w_out,
    params_c,
    params_s,
    tokens_out,
    up_out,
    n_pairs_out,
    p_out,
    pre_x_out,
    pre_s_out,
    raw_out,
    conv_x_out,
    conv_s_out,
    ny_out,
    dz_out,
    dmix_out,
    gain_row,
    state_out,
    g_out,
    gz_out,
    land_a,
    land_b,
    wx_out,
    ws_out,
    wz_out,
    wo_out,
    wx,
    ws,
    wz,
    wo,
    ws_own,
    x_own,
    c_own,
    x_sort,
    c_sort,
    p_sort,
    p_recv,
    x_recv,
    c_recv,
    tokens,
    n_high,
    n_low,
    turned,
    n_pairs,
    c_pairs,
    pre_x,
    pre_s,
    raw,
    bc_rows,
    tail_x,
    tail_s,
    conv_x,
    conv_s,
    act_x,
    act_s,
    totals,
    step_rows,
    open_,
    scores,
    state,
    state_in,
    mixed,
    gate_pre,
    d_normal,
    ny_both,
    high,
    low,
    left_high,
    left_low,
    sums,
    sums_recv,
    inner_sums,
    inner_recv,
    send,
    recv,
    local,
):
    place = Place(*sizes)
    links = Links(send, recv, local)
    tok, groups = x_own.shape[0], 2 * place.fsdp
    per_pair = tok // groups
    part = x_own.shape[1]
    inner = act_x.shape[1]
    pairs = inner // 128
    heads = d_skip.shape[1]
    share = 2 * N // place.tp
    shard_rows = n_pairs.shape[1]
    chip_rows = 2 * shard_rows
    first = place.c * tok
    lanes = iota((tok, 128), 1)
    part_cols = pl.ds(pl.multiple_of(place.z * part, 128), part)
    load_x = links.move(x_in.at[:, part_cols], x_own)
    load_c = links.move(c_in.at[:, part_cols], c_own)
    plane, column = place.plane(), place.column()
    partners = [entry[0] for entry in plane] + [entry[0] for entry in column]
    greet(partners)

    leave, places = leaving(slots_in[...], tok, groups)
    p_sort[...] = jnp.broadcast_to(places[0:groups, None, :], (groups, 8, 128))
    load_x.wait()
    x_sort[...] = pick(leave, x_own[...], TN)
    greeted(partners)
    g_x, g_s, g_z, g_o = [Gather(place, links, shard, whole) for shard, whole in ((w_x, wx), (ws_own, ws), (w_z, wz), (w_out, wo))]

    def rows(group):
        return pl.ds(pl.multiple_of(group * per_pair, 8), per_pair)

    def route(source, target, at):
        mine = at(place.f * 2 + place.c)
        copies = [links.remote(source.at[at(to)], target.at[mine], device) for device, to, _ in plane]
        return copies, links.move(source.at[mine], target.at[mine])

    routes_x = [route(p_sort, p_recv, lambda group: group), route(x_sort, x_recv.at[place.z], rows)]
    g_x.start()

    def share_of(turn):
        return pl.ds(pl.multiple_of(turn * share, 8), share)

    bc_rows[:, 0:shard_rows] = w_bc[...].T
    ws_own[...] = jnp.zeros_like(ws_own)
    ws_own[0:heads, :] = w_dt[...]
    ws_own[heads : heads + share, :] = bc_rows[share_of(place.z), 0:shard_rows]
    g_s.start()
    load_c.wait()
    c_sort[...] = pick(leave, c_own[...], TN)
    routes_c = [route(c_sort, c_recv.at[place.z], rows)]

    params_c[0:4, :] = taps_x[...]
    params_c[4:5, :] = bias_x[...]
    params_c[6:7, :] = gate_gain[...]
    params_c[7:8, :] = jnp.zeros((1, inner), F32)
    for q in range(pairs):
        both = [d_skip[0:1, 2 * q + s : 2 * q + s + 1] for s in range(2)]
        params_c[5:6, q * 128 : (q + 1) * 128] = jnp.where(lanes[0:1] < 64, both[0], both[1])
    params_s[...] = jnp.zeros_like(params_s)
    params_s[0:4, :] = taps_s[...]
    params_s[4:5, :] = bias_s[...]
    params_s[5:6, 0:heads] = dt_bias[...]
    params_s[6:7, 0:heads] = a_log[...]

    def arrive(routes):
        for copies, own in routes:
            own.wait()
            for copy in copies:
                copy.wait_recv()

    arrive(routes_x)
    spread_x = Spread(place, links, x_recv)
    g_x.forward()
    g_s.forward()
    g_z.start()
    spread_x.forward()
    arrive(routes_c)
    g_s.share()
    stores = []
    spread_x.finish()
    p_out[...] = arrived(p_recv[:, 0, :], tok, per_pair)
    settle = settling(p_out, tok)
    squares = jnp.zeros((tok, 1), F32)
    for k in range(place.tp):
        value = pick(settle, x_recv[k], TN)
        tokens[k] = value
        squares = squares + jnp.sum(value * value, axis=1, keepdims=True)
    scale = lax.rsqrt(squares / (place.tp * part) + EPSILON)
    own_cols = pl.ds(pl.multiple_of(place.c * tok, 128), tok)
    own_rows = pl.ds(pl.multiple_of(place.c * tok, 128), tok)
    chips_here = part // chip_rows

    def keep_left(k, value):
        for j in range(chips_here):
            piece = value[:, j * chip_rows : (j + 1) * chip_rows]
            n_high[k * chips_here + j], n_low[k * chips_here + j] = split2(piece)
        turned[k * part : (k + 1) * part, :] = value.T

    def exchange_blocks(pairs_ref):
        copies, kept = [], []
        for q in range(place.fsdp):
            there = turned.at[pl.ds(pl.multiple_of((2 * q + 1 - place.c) * shard_rows, 8), shard_rows)]
            here = turned.at[pl.ds(pl.multiple_of((2 * q + place.c) * shard_rows, 8), shard_rows)]
            copies.append(links.remote(there, pairs_ref.at[q, :, own_cols], place.sibling()))
            kept.append(links.move(here, pairs_ref.at[q, :, own_cols]))
        return copies, kept

    for k in range(place.tp):
        keep_left(k, tokens[k] * scale * gain[:, k * part : (k + 1) * part])
    pairs_n, kept_n = exchange_blocks(n_pairs)
    stores.append(links.move(tokens, tokens_out))

    every = list(range(place.fsdp))
    g_s.finish()
    raw[...] = jnp.zeros_like(raw)
    side_rows = ws_own.shape[0]
    total = jnp.zeros((tok, side_rows), F32)
    for block in range(2 * place.fsdp):
        at = slice(block % 2 * shard_rows, (block % 2 + 1) * shard_rows)
        left = (n_high[block // 2, :, at], n_low[block // 2, :, at])
        total = total + dot_split(left, split2(ws[block * side_rows : (block + 1) * side_rows, :]), NT)
    raw[:, 0:side_rows] = total
    bc_turned = raw[...].T
    bc_rows[share_of(place.z), :] = bc_turned[heads : heads + share]
    mine = bc_rows.at[share_of(place.z)]
    spread_bc = [links.remote(mine, mine, device) for device, _, _ in column]
    spread_c = Spread(place, links, c_recv)
    g_x.share()
    g_x.finish()
    keep_wx = links.move(wx, wx_out)
    stores += [links.move(ws, ws_out)]
    project(n_high, n_low, wx, every, pre_x, 512, 8, True)
    halo = [links.remote(pre_x.at[pl.ds(tok, 8)], tail_x, place.sibling())]
    g_z.forward()
    g_o.start()

    raw[...] = jnp.where(lanes < heads, raw[...], 0.0)
    steps = Steps(raw[...], params_s, lengths, first)
    totals[...] = steps.total
    step_rows[0] = steps.total.T
    step_rows[1] = steps.step.T
    open_[...] = closed(lengths, first, tok, False)
    for copy in spread_bc:
        copy.wait_recv()
    pre_s[8 : 8 + tok, :] = bc_rows[...].T
    halo.append(links.remote(pre_s.at[pl.ds(tok, 8)], tail_s, place.sibling()))
    for copy in halo:
        copy.wait_recv()
    second = (place.c > 0).astype(F32)
    pre_x[0:8, :] = tail_x[...] * second
    pre_s[0:8, :] = tail_s[...] * second
    convolve(pre_s, params_s, lengths, first, conv_s, act_s)
    convolve(pre_x, params_c, lengths, first, conv_x, act_x)
    b_parts = split2(act_s[:, :N])
    c_parts = split2(act_s[:, N:])
    scores[...] = dot_split(c_parts, b_parts, NT)
    tail_table, reading_table = steps.tail, steps.reading

    @pl.loop(0, pairs)
    def _(q):
        cols = pl.ds(pl.multiple_of(q * 128, 128), 128)
        faded = act_x[:, cols] * pair_columns(tail_table, q)
        state[cols, :] = dot_split(split2(faded), b_parts, TN)

    pass_state = links.remote(state, state_in, place.sibling())
    spread_c.forward()
    pass_state.wait_recv()

    @pl.loop(0, pairs)
    def _(q):
        cols = pl.ds(pl.multiple_of(q * 128, 128), 128)
        channels = act_x[:, cols]
        entered = state_in[cols, :] * second
        state_in[cols, :] = entered
        out = params_c[5:6, cols] * channels
        out = out + pair_columns(reading_table, q) * dot_split(c_parts, split2(entered), NT)
        for s in range(2):
            head = 2 * q + s
            gaps = column_of(totals[...], head) - step_rows[0, pl.ds(head, 1), :] + open_[...]
            weights = jnp.exp(gaps) * scores[...] * step_rows[1, pl.ds(head, 1), :]
            own = jnp.where((lanes < 64) == (s == 0), channels, 0.0)
            out = out + dot3(weights, own, NN)
        mixed[:, cols] = out

    stores += [
        links.move(pre_x, pre_x_out),
        links.move(pre_s, pre_s_out),
        links.move(raw, raw_out),
        links.move(conv_x, conv_x_out),
        links.move(conv_s, conv_s_out),
        links.move(state_in, state_out),
    ]
    g_z.share()
    g_z.finish()
    stores.append(links.move(wz, wz_out))
    project(n_high, n_low, wz, every, gate_pre, 512, 0, True)

    def over_tiles(body, carry):
        def step(n, carry):
            return body(pl.ds(pl.multiple_of(n * 128, 128), 128), carry)

        return lax.fori_loop(0, pairs, step, carry)

    def gated_at(cols):
        z = gate_pre[:, cols]
        return mixed[:, cols] * (z * jax.nn.sigmoid(z))

    def add_squares(cols, total):
        gated = gated_at(cols)
        return total + gated * gated

    zeros = jnp.zeros((tok, 128), F32)
    square_sum = over_tiles(add_squares, zeros)
    sums[...] = jnp.broadcast_to(jnp.sum(square_sum, axis=1, keepdims=True), (tok, 128)).T[0:8, :]
    copies = [links.remote(sums, sums_recv.at[k], device) for k, (device, _, _) in enumerate(column)]

    spread_c.finish()
    for copy in pairs_n:
        copy.wait_recv()
    links.settle(pairs_n)
    for copy in kept_n:
        copy.wait()
    stores.append(links.move(n_pairs, n_pairs_out))
    for k in range(place.tp):
        upstream = pick(settle, c_recv[k], TN)
        keep_left(k, upstream)

        @pl.when(place.z == k)
        def _():
            x_own[...] = upstream

    pairs_c, kept_c = exchange_blocks(c_pairs)
    stores.append(links.move(x_own, up_out))

    for copy in copies:
        copy.wait_recv()
    total = sums[...]
    for k in range(place.tp - 1):
        total = total + sums_recv[k]
    gscale = lax.rsqrt(down_lanes(total[0:1]) / INNER + EPSILON)

    def normalise(cols, carry):
        ny_both[own_rows, cols] = gated_at(cols) * gscale * params_c[6:7, cols]
        return carry

    over_tiles(normalise, 0)
    g_o.forward()
    give_ny = links.remote(ny_both.at[own_rows], ny_both.at[own_rows], place.sibling())
    keep_ny = links.move(ny_both.at[own_rows], ny_out)

    near = [place.f] + [place.chip(0, d) for d in range(1, place.side)] + [place.chip(d, 0) for d in range(1, place.side)]
    far = [place.chip(e, d) for e in range(1, place.side) for d in range(1, place.side)]
    for copy in kept_c:
        copy.wait()
    for copy in pairs_c:
        copy.wait_recv()
    give_ny.wait_recv()
    halve(ny_both, high, low)
    keep_wx.wait()
    links.settle(g_x.half_a + g_x.half_b + g_x.pair)
    blocks_o = wx.reshape(2, place.fsdp, shard_rows, inner).at[0]
    blocks_z = wx.reshape(2, place.fsdp, shard_rows, inner).at[1]
    for q in range(place.fsdp):
        weight_block(c_pairs.at[q], high, low, left_high, left_low, blocks_o.at[q])
    stores.append(links.move(blocks_o, g_out))
    sum_o = Scatter(place, links, blocks_o, blocks_o, (land_a, land_b))
    sum_o.send_all()
    def keep_rows(chip):
        at = pl.ds(pl.multiple_of(chip * chip_rows, 8), chip_rows)
        stores.append(links.move(wo.at[at], wo_out.at[at]))

    g_o.finish_near()
    for chip in near:
        keep_rows(chip)
    project(n_high, n_low, wo, near, d_normal, 512, 0, True)
    g_o.share()
    g_o.finish()
    for chip in far:
        keep_rows(chip)
    project(n_high, n_low, wo, far, d_normal, 512, 0, False)

    def add_inner(cols, total):
        return total + d_normal[:, cols] * params_c[6:7, cols] * gated_at(cols)

    inner_sum = over_tiles(add_inner, zeros)
    inner_sums[...] = jnp.broadcast_to(jnp.sum(inner_sum, axis=1, keepdims=True), (tok, 128)).T[0:8, :]
    copies = [links.remote(inner_sums, inner_recv.at[k], device) for k, (device, _, _) in enumerate(column)]
    links.settle([give_ny])
    keep_ny.wait()
    for copy in copies:
        copy.wait_recv()
    total = inner_sums[...]
    for k in range(place.tp - 1):
        total = total + inner_recv[k]
    pull = gscale * gscale * gscale * down_lanes(total[0:1]) / INNER

    def shape_all(cols, carry):
        z, y, upward, weight = gate_pre[:, cols], mixed[:, cols], d_normal[:, cols], params_c[6:7, cols]
        gate = jax.nn.sigmoid(z)
        act = z * gate
        gated = y * act
        d_gated = gscale * weight * upward - gated * pull
        d_normal[:, cols] = d_gated * act
        ny_both[own_rows, cols] = d_gated * y * gate * (1.0 + z * (1.0 - gate))
        gain_row[:, cols] = jnp.sum(upward * gated * gscale, axis=0, keepdims=True)
        return carry

    over_tiles(shape_all, 0)
    give_dz = links.remote(ny_both.at[own_rows], ny_both.at[own_rows], place.sibling())
    stores += [links.move(ny_both.at[own_rows], dz_out), links.move(d_normal, dmix_out)]
    give_dz.wait_recv()
    halve(ny_both, high, low)
    for q in range(place.fsdp):
        weight_block(n_pairs.at[q], high, low, left_high, left_low, blocks_z.at[q])
        stores.append(links.move(blocks_z.at[q], gz_out.at[q]))
    sum_o.land()
    for store in stores:
        store.wait()
    links.finish()


def backward_kernel(
    sizes,
    heads,
    lengths,
    slots_in,
    p_recv,
    gain,
    params_c,
    params_s,
    gain_row,
    tokens_in,
    up_in,
    n_pairs_in,
    pre_x_in,
    pre_s_in,
    raw_in,
    conv_x_in,
    conv_s_in,
    ny_in,
    dz_in,
    dmix_in,
    state_in_hbm,
    g_in,
    gz_in,
    land_a_in,
    land_b_in,
    wx_in,
    ws_in,
    wz_in,
    wo_in,
    result,
    grad_input,
    grad_z,
    grad_x,
    grad_bc,
    grad_dt,
    grad_out,
    small_out,
    gain_out,
    tokens,
    n_pairs,
    pre_x,
    pre_s,
    raw,
    conv_x,
    conv_s,
    state_in,
    dx_both,
    ds_both,
    high,
    low,
    left_high,
    left_low,
    blocks_o,
    blocks_z,
    blocks_s,
    o1a, o1b, o2a, o2b,
    z1a, z1b, z2a, z2b,
    x1a, x1b, x2a, x2b,
    s1a, s1b, s2a, s2b,
    blocks_x,
    stream,
    ws,
    d_bc,
    ds_high,
    ds_low,
    bc_rows,
    bc_recv,
    bc_grad,
    part_r,
    part_t,
    recv_r,
    recv_t,
    row_sums,
    row_recv,
    home_r,
    home_t,
    back_r,
    back_t,
    d_state,
    d_state_recv,
    d_b,
    d_c,
    pad_x,
    pad_s,
    head_x,
    head_s,
    open_,
    scores,
    d_scores,
    totals,
    steps_col,
    total_rows,
    grad_total,
    grad_step,
    grad_tail,
    grad_rows,
    skip_row,
    small,
    small_recv,
    small_z,
    gain_own,
    gain_recv,
    send,
    recv,
    local,
):
    place = Place(*sizes)
    links = Links(send, recv, local)
    tok, groups = tokens.shape[1], 2 * place.fsdp
    per_pair = tok // groups
    part = tokens.shape[2]
    inner = conv_x.shape[1]
    pairs = inner // 128
    first = place.c * tok
    own_rows = pl.ds(pl.multiple_of(place.c * tok, 128), tok)
    plane, column = place.plane(), place.column()

    partners = [entry[0] for entry in plane] + [entry[0] for entry in column]
    greet(partners)
    shares_r, shares_t = Shares(place, links, part_r, recv_r), Shares(place, links, part_t, recv_t)
    turns = shares_r.turns
    schedule = [(weight, turn) for weight in (wo_in, wx_in, wz_in) for turn in turns]
    fetched = []

    def fetch():
        k = len(fetched)
        if k < len(schedule):
            weight, turn = schedule[k]
            src = weight.at[pl.ds(pl.multiple_of(turn * part, 8), part)]
            fetched.append(links.move(src, stream.at[k % 2]))

    def weight_slice(k):
        fetched[k].wait()
        return stream.at[k % 2]

    greeted(partners)
    sum_o = Scatter(place, links, g_in, blocks_o, (o1a, o1b), (o2a, o2b))
    sum_z = Scatter(place, links, gz_in, blocks_z, (z1a, z1b), (z2a, z2b))
    sum_z.send_all()
    loads = {}
    loads["ny"] = links.move(ny_in, dx_both.at[own_rows])
    fetch()
    fetch()
    for name, src, dst in (
        ("g", g_in, blocks_o),
        ("land_a", land_a_in, o1a),
        ("land_b", land_b_in, o1b),
        ("raw", raw_in, raw),
        ("conv_s", conv_s_in, conv_s),
        ("dmix", dmix_in, pad_x.at[pl.ds(0, tok)]),
        ("state", state_in_hbm, state_in),
        ("conv_x", conv_x_in, conv_x),
        ("n_pairs", n_pairs_in, n_pairs),
        ("gz", gz_in, blocks_z),
        ("pre_x", pre_x_in, pre_x),
        ("pre_s", pre_s_in, pre_s),
        ("tokens", tokens_in, tokens),
        ("up", up_in, home_t),
        ("ws", ws_in, ws),
    ):
        loads[name] = links.move(src, dst)

    loads["ny"].wait()
    halve(dx_both.at[own_rows], high.at[own_rows], low.at[own_rows])

    def product(k, turn, fresh, out):
        ref = weight_slice(k)
        times_rows(high.at[own_rows], low.at[own_rows], ref, out, fresh)
        fetch()

    for k, turn in enumerate(turns):
        product(k, turn, True, part_r.at[turn])
        shares_r.send(k)
        if k == min(1, place.tp - 1):
            for name in ("g", "land_a", "land_b"):
                loads[name].wait()
            sum_o.pass_on()

    loads["raw"].wait()
    loads["conv_s"].wait()
    steps = Steps(raw[...], params_s, lengths, first)
    totals[...] = steps.total
    steps_col[...] = steps.step
    total_rows[...] = steps.total.T
    open_[...] = closed(lengths, first, tok, True)
    act_s = conv_s[...] * jax.nn.sigmoid(conv_s[...])
    b_parts, c_parts = split2(act_s[:, :N]), split2(act_s[:, N:])
    scores[...] = dot_split(b_parts, c_parts, NT)
    reading_table, tail_table = steps.reading, steps.tail
    grad_total[...] = jnp.zeros((tok, 128), F32)
    grad_step[...] = jnp.zeros((tok, 128), F32)
    grad_tail[...] = jnp.zeros((tok, 128), F32)
    d_c[...] = jnp.zeros((tok, N), F32)
    d_b[...] = jnp.zeros((tok, N), F32)
    d_scores[...] = jnp.zeros((tok, tok), F32)
    grad_rows[...] = jnp.zeros((128, tok), F32)
    lanes = iota((tok, 128), 1)

    def put(ref, head, value):
        ref[...] = ref[...] + jnp.where(lanes == head, value, 0.0)

    def by_head(value, s):
        return jnp.sum(jnp.where((lanes < 64) == (s == 0), value, 0.0), axis=1, keepdims=True)

    loads["dmix"].wait()
    loads["state"].wait()

    @pl.loop(0, pairs)
    def _(q):
        cols = pl.ds(pl.multiple_of(q * 128, 128), 128)
        upward = pad_x[0:tok, cols] * pair_columns(reading_table, q)
        parts = split2(upward)
        entered = split2(state_in[cols, :])
        d_c[...] = d_c[...] + dot_split(parts, entered, NN)
        d_state[cols, :] = dot_split(parts, c_parts, TN)
        read = upward * dot_split(c_parts, entered, NT)
        for s in range(2):
            put(grad_total, 2 * q + s, by_head(read, s))

    give_state = links.remote(d_state, d_state_recv, place.sibling())

    shares_r.forward()

    loads["conv_x"].wait()
    give_state.wait_recv()
    first_half = (place.c == 0).astype(F32)

    @pl.loop(0, pairs)
    def _(q):
        cols = pl.ds(pl.multiple_of(q * 128, 128), 128)
        conv = conv_x[:, cols]
        gate = jax.nn.sigmoid(conv)
        channels = conv * gate
        upward = pad_x[0:tok, cols]
        ended = split2(d_state_recv[cols, :] * first_half)
        tail = pair_columns(tail_table, q)
        from_end = dot_split(b_parts, ended, NT)
        d_b[...] = d_b[...] + dot_split(split2(channels * tail), ended, NN)
        into = params_c[5:6, cols] * upward + tail * from_end
        skip_row[:, cols] = jnp.sum(upward * channels, axis=0, keepdims=True)
        end_part = channels * from_end
        x_parts = split2(channels)
        for s in range(2):
            head = 2 * q + s
            put(grad_tail, head, by_head(end_part, s))
            step_col = column_of(steps_col[...], head)
            gaps = total_rows[pl.ds(head, 1), :] - column_of(totals[...], head) + open_[...]
            decay = jnp.exp(gaps)
            up_parts = split2(jnp.where((lanes < 64) == (s == 0), upward, 0.0))
            reach = dot_split(x_parts, up_parts, NT) * decay
            d_scores[...] = d_scores[...] + reach * step_col
            reach = reach * scores[...]
            put(grad_step, head, jnp.sum(reach, axis=1, keepdims=True))
            grad_rows[pl.ds(head, 1), :] = jnp.sum(reach * step_col, axis=0, keepdims=True)
            into = into + dot3(decay * scores[...] * step_col, jnp.where((lanes < 64) == (s == 0), upward, 0.0), NN)
        pad_x[0:tok, cols] = into * gate * (1.0 + conv * (1.0 - gate))

    loads["dz"] = links.move(dz_in, conv_x)

    score_parts = split2(d_scores[...])
    slope_s = silu_slope(conv_s[...])
    pad_s[0:tok, 0:N] = (d_b[...] + dot_split(score_parts, c_parts, NN)) * slope_s[:, :N]
    pad_s[0:tok, N : 2 * N] = (d_c[...] + dot_split(score_parts, b_parts, TN)) * slope_s[:, N:]
    halo = [
        links.remote(pad_x.at[pl.ds(0, 8)], head_x, place.sibling()),
        links.remote(pad_s.at[pl.ds(0, 8)], head_s, place.sibling()),
    ]
    step_now = steps_col[...]
    faded = grad_tail[...] * tail_table
    d_total = grad_total[...] + grad_rows[...].T - grad_step[...] * step_now - faded
    at_end = iota((tok, 128), 0) == tok - 1
    d_total = d_total + jnp.where(at_end, jnp.sum(faded, axis=0, keepdims=True), 0.0)
    onward = (iota((tok, tok), 1) >= iota((tok, tok), 0)).astype(BF16)
    d_log = pick(onward, d_total, NN)
    d_step = grad_step[...] + grad_tail[...] * steps.fading + d_log * steps.rate
    d_raw = jnp.where(lanes < heads, d_step * steps.slope, 0.0)
    small[...] = jnp.zeros_like(small)
    small[5:6, inner : inner + 128] = jnp.sum(d_raw, axis=0, keepdims=True)
    small[6:7, inner : inner + 128] = jnp.sum(d_log * step_now, axis=0, keepdims=True) * steps.rate
    head_of = (iota((inner, 128), 0) // (inner // heads) == iota((inner, 128), 1)).astype(BF16)
    skips = jnp.broadcast_to(skip_row[...], (8, inner))
    small[7:8, inner : inner + 128] = sum(dot1(piece, head_of, NN) for piece in split3(skips))[0:1]
    small[5:6, 0:inner] = gain_row[...]

    loads["pre_x"].wait()
    loads["pre_s"].wait()
    for copy in halo:
        copy.wait_recv()
    pad_x[tok : tok + 8, :] = head_x[...] * first_half
    pad_s[tok : tok + 8, :] = head_s[...] * first_half
    same = [same_before(lengths, first, tok, 3 - k) for k in range(3)]
    same_next = [same_before(lengths, first + 3 - k, tok, 3 - k) for k in range(3)]

    def back(padded, pre, params, out, start, n):
        cols = pl.ds(pl.multiple_of(n * 128, 128), 128)
        small_cols = pl.ds(pl.multiple_of(start + n * 128, 128), 128)
        here = padded[0:tok, cols]
        total = params[3:4, cols] * here
        small[3:4, small_cols] = jnp.sum(here * pre[8 : 8 + tok, cols], axis=0, keepdims=True)
        small[4:5, small_cols] = jnp.sum(here, axis=0, keepdims=True)
        for k in range(3):
            total = total + params[k : k + 1, cols] * (padded[3 - k : 3 - k + tok, cols] * same_next[k])
            value = here * (pre[5 + k : 5 + k + tok, cols] * same[k])
            small[k : k + 1, small_cols] = jnp.sum(value, axis=0, keepdims=True)
        out[:, cols] = total

    @pl.loop(0, pairs)
    def _(n):
        back(pad_x, pre_x, params_c, dx_both.at[own_rows], 0, n)

    give_dx = links.remote(dx_both.at[own_rows], dx_both.at[own_rows], place.sibling())

    @pl.loop(0, 2 * N // 128)
    def _(n):
        back(pad_s, pre_s, params_s, d_bc, inner, n)

    share = 2 * N // place.tp
    bc_rows[...] = d_bc[...].T

    def share_of(turn):
        return pl.ds(pl.multiple_of(turn * share, 8), share)

    give_bc = [
        links.remote(bc_rows.at[share_of(to_z)], bc_recv.at[k], device) for k, (device, to_z, _) in enumerate(column)
    ]

    hops_of = [
        [place.sibling()],
        [place.at(0, d) for d in range(1, place.side)],
        [place.at(d, 0) for d in range(1, place.side)],
    ]
    small_copies = []

    def hop_small(step):
        slot = sum(len(devices) for devices in hops_of[:step])
        for device in hops_of[step]:
            small_copies.append(links.remote(small, small_recv.at[slot], device))
            slot += 1

    def land_small(step):
        slot = sum(len(devices) for devices in hops_of[:step])
        total = small[...]
        links.settle(small_copies[slot:])
        for copy in small_copies[slot:]:
            copy.wait_recv()
            total = total + small_recv[slot]
            slot += 1
        small[...] = total

    hop_small(0)
    give_dx.wait_recv()
    loads["n_pairs"].wait()
    sum_x = Scatter(place, links, blocks_x, blocks_x, (x1a, x1b), (x2a, x2b))
    halve(dx_both, high, low)
    for hop in sum_x.order():
        block = place.chip(*hop)
        weight_block(n_pairs.at[block], high, low, left_high, left_low, blocks_x.at[block])
        sum_x.send(*hop)
    loads["gz"].wait()
    sum_z.pass_on()
    land_small(0)
    hop_small(1)

    for k, turn in enumerate(turns):
        product(place.tp + k, turn, True, part_t.at[turn])
    loads["dz"].wait()
    halve(conv_x, high.at[own_rows], low.at[own_rows])
    loads["tokens"].wait()
    loads["ws"].wait()
    for copy in give_bc:
        copy.wait_recv()
    summed = bc_rows[share_of(place.z), :]
    for k in range(place.tp - 1):
        summed = summed + bc_recv[k]
    own_cols = pl.ds(pl.multiple_of(place.c * tok, 128), tok)
    ds_both[0:heads, own_cols] = d_raw.T[0:heads, :]
    ds_both[heads : heads + share, own_cols] = summed
    side_rows = ds_both.shape[0]
    if side_rows > heads + share:
        ds_both[heads + share :, own_cols] = jnp.zeros((side_rows - heads - share, tok), F32)
    give_ds = links.remote(ds_both.at[:, own_cols], ds_both.at[:, own_cols], place.sibling())
    ds_high[...], ds_low[...] = split2(ds_both[:, own_cols].T)
    give_ds.wait_recv()
    sum_s = Scatter(place, links, blocks_s, blocks_s, (s1a, s1b), (s2a, s2b))
    ds_parts = split2(ds_both[...])
    for hop in sum_s.order():
        block = place.chip(*hop)
        sum_s.blocks[block] = dot_split(ds_parts, split2(n_pairs[block]), NT)
        sum_s.send(*hop)
    row_sum = jnp.zeros((tok, 1), F32)
    squares = jnp.zeros((tok, 1), F32)
    for k, turn in enumerate(turns):
        out = part_t.at[turn]
        product(2 * place.tp + k, turn, False, out)
        shard_rows = ws.shape[1]
        for j in range(part // shard_rows):
            at = pl.ds(pl.multiple_of((turn * (part // shard_rows) + j) * side_rows, 8), side_rows)
            cols = slice(j * shard_rows, (j + 1) * shard_rows)
            out[:, cols] = out[:, cols] + dot_split((ds_high[...], ds_low[...]), split2(ws[at, :]), NN)
        shares_t.send(k)
        value = tokens[turn]
        row_sum = row_sum + jnp.sum(out[...] * gain[turn] * value, axis=1, keepdims=True)
        squares = squares + jnp.sum(value * value, axis=1, keepdims=True)
    row_sums[...] = jnp.where(lanes == 0, row_sum, 0.0).T[0:8, :]
    give_rows = [links.remote(row_sums, row_recv.at[k], device) for k, (device, _, _) in enumerate(column)]

    land_small(1)
    hop_small(2)
    stores = [links.move(sum_o.finish(), grad_out)]

    settle = settling(p_recv, tok)

    def rows(group):
        return pl.ds(pl.multiple_of(group * per_pair, 8), per_pair)

    def homeward(value, home, back_ref):
        home[...] = pick(settle, value, NN)
        at = rows(place.f * 2 + place.c)
        copies = [links.remote(home.at[rows(to)], back_ref.at[at], device) for device, to, _ in plane]
        return copies + [links.move(home.at[at], back_ref.at[at])]

    shares_r.finish()
    value = tokens[place.z] + part_r[place.z]
    way_r = homeward(value, home_r, back_r)

    shares_t.forward()
    sum_s.pass_on()
    sum_x.pass_on()
    stores.append(links.move(sum_z.finish(), grad_z))

    land_small(2)
    bc_cols = pl.ds(inner, 2 * N)
    give_small = [links.remote(small.at[:, bc_cols], small_z.at[j], device) for j, (device, _, _) in enumerate(column)]
    last = sum_s.finish()
    give_grad = [
        links.remote(last.at[pl.ds(heads, share)], bc_grad.at[share_of(place.z)], device) for device, _, _ in column
    ]
    bc_grad[share_of(place.z), :] = last[heads : heads + share, :]
    grad_dt[...] = last[0:heads, :]
    for copy in give_rows:
        copy.wait_recv()
    total = row_sums[...]
    for k in range(place.tp - 1):
        total = total + row_recv[k]
    shares_t.finish()
    d_normed = part_t[place.z]
    row_sum = jnp.concatenate([total, jnp.zeros((120, tok), F32)], axis=0).T[:, 0:1]
    width = place.tp * part
    scale = lax.rsqrt(squares / width + EPSILON)
    scaled = tokens[place.z] * scale
    gain_own[...] = jnp.sum(d_normed * scaled, axis=0, keepdims=True)
    give_gain = [links.remote(gain_own, gain_recv.at[j], device) for j, (device, _, _) in enumerate(plane)]
    loads["up"].wait()
    value = home_t[...] + scale * gain[place.z] * d_normed - scaled * (scale * scale * row_sum / width)
    way_t = homeward(value, home_t, back_t)

    stores.append(links.move(sum_x.finish(), grad_x))
    leave, _ = leaving(slots_in[...], tok, groups)
    for way, home, back_ref, out in ((way_r, home_r, back_r, result), (way_t, home_t, back_t, grad_input)):
        for copy in way[:-1]:
            copy.wait_recv()
        way[-1].wait()
        links.settle(way[:-1])
        home[...] = pick(leave, back_ref[...], NN)
        stores.append(links.move(home, out))
    total = gain_own[...]
    for j, copy in enumerate(give_gain):
        copy.wait_recv()
        total = total + gain_recv[j]
    gain_out[...] = total
    for copy in give_small:
        copy.wait_recv()
    small_out[...] = small[...]
    over_tp = small[0:5, inner : inner + 2 * N]
    for k in range(place.tp - 1):
        over_tp = over_tp + small_z[k, 0:5, :]
    small_out[0:5, inner : inner + 2 * N] = over_tp
    for copy in give_grad:
        copy.wait_recv()
    grad_bc[...] = bc_grad[...].T
    for store in stores:
        store.wait()
    links.finish()


ANYWHERE = pl.BlockSpec(memory_space=pl.ANY)
INSIDE = pl.BlockSpec(memory_space=pltpu.VMEM)
SCALARS = pl.BlockSpec(memory_space=pltpu.SMEM)


def shape(*dims):
    return jax.ShapeDtypeStruct(dims, F32)


def floats(*dims):
    return pltpu.VMEM(dims, F32)


def halves(*dims):
    return pltpu.VMEM(dims, BF16)


def side_height(heads, tp):
    return -(-(heads + 2 * N // tp) // 16) * 16


def forward_call(sizes, operands, heads):
    fsdp, _, tp = sizes
    inputs, w_x = operands[13], operands[15]
    tok, width = inputs.shape
    shard, inner = w_x.shape
    depth = shard * 2 * fsdp
    part = width // tp
    side = side_height(heads, tp)
    copies = 4 * gather_copies(math.isqrt(fsdp)) + 3 * (2 * fsdp - 1) + 8 * tp + 4 * fsdp + 8
    grid = math.isqrt(fsdp)
    landing = (grid - 1, grid, shard // 2, inner)
    outs = [
        (shape(8, inner), INSIDE),
        (shape(8, 2 * N), INSIDE),
        (shape(tp, tok, part), ANYWHERE),
        (shape(tok, part), ANYWHERE),
        (shape(fsdp, shard, 2 * tok), ANYWHERE),
        (shape(tok, 128), INSIDE),
        (shape(8 + tok, inner), ANYWHERE),
        (shape(8 + tok, 2 * N), ANYWHERE),
        (shape(tok, 128), ANYWHERE),
        (shape(tok, inner), ANYWHERE),
        (shape(tok, 2 * N), ANYWHERE),
        (shape(tok, inner), ANYWHERE),
        (shape(tok, inner), ANYWHERE),
        (shape(tok, inner), ANYWHERE),
        (shape(1, inner), INSIDE),
        (shape(inner, N), ANYWHERE),
        (shape(fsdp, shard, inner), ANYWHERE),
        (shape(fsdp, shard, inner), ANYWHERE),
        (shape(*landing), ANYWHERE),
        (shape(*landing), ANYWHERE),
        (shape(depth, inner), ANYWHERE),
        (shape(2 * fsdp * side, shard), ANYWHERE),
        (shape(depth, inner), ANYWHERE),
        (shape(depth, inner), ANYWHERE),
    ]
    return pl.pallas_call(
        functools.partial(forward_kernel, sizes),
        out_shape=tuple(out for out, _ in outs),
        in_specs=[SCALARS] + [INSIDE] * 12 + [ANYWHERE] * 5,
        out_specs=tuple(spec for _, spec in outs),
        scratch_shapes=[
            floats(depth, inner),
            floats(2 * fsdp * side, shard),
            floats(depth, inner),
            floats(depth, inner),
            floats(side, shard),
            floats(tok, part),
            floats(tok, part),
            floats(tok, part),
            floats(tok, part),
            floats(2 * fsdp, 8, 128),
            floats(2 * fsdp, 8, 128),
            floats(tp, tok, part),
            floats(tp, tok, part),
            floats(tp, tok, part),
            halves(fsdp, tok, 2 * shard),
            halves(fsdp, tok, 2 * shard),
            floats(width, tok),
            floats(fsdp, shard, 2 * tok),
            floats(fsdp, shard, 2 * tok),
            floats(8 + tok, inner),
            floats(8 + tok, 2 * N),
            floats(tok, 128),
            floats(2 * N, max(tok, shard)),
            floats(8, inner),
            floats(8, 2 * N),
            floats(tok, inner),
            floats(tok, 2 * N),
            floats(tok, inner),
            floats(tok, 2 * N),
            floats(tok, 128),
            floats(2, 128, tok),
            floats(tok, tok),
            floats(tok, tok),
            floats(inner, N),
            floats(inner, N),
            floats(tok, inner),
            floats(tok, inner),
            floats(tok, inner),
            floats(2 * tok, inner),
            halves(2 * tok, inner),
            halves(2 * tok, inner),
            halves(shard, 2 * tok),
            halves(shard, 2 * tok),
            floats(8, tok),
            floats(tp - 1, 8, tok),
            floats(8, tok),
            floats(tp - 1, 8, tok),
            pltpu.SemaphoreType.DMA((copies,)),
            pltpu.SemaphoreType.DMA((copies,)),
            pltpu.SemaphoreType.DMA((48 + 3 * fsdp,)),
        ],
        compiler_params=pltpu.CompilerParams(collective_id=0, has_side_effects=True, vmem_limit_bytes=VMEM_LIMIT),
        name="forward",
    )(*operands)


def backward_call(sizes, heads, operands, tok, width, shard, inner):
    fsdp, _, tp = sizes
    grid = math.isqrt(fsdp)
    part = width // tp
    share = 2 * N // tp
    side = side_height(heads, tp)
    hops = grid - 1
    copies = 4 + 4 * (2 * hops * grid + 2 * hops) + 9 * tp + 3 * (2 * fsdp) + 2 * hops + 4

    def landing(rows, columns):
        return [
            floats(hops, grid, rows // 2, columns),
            floats(hops, grid, rows // 2, columns),
            floats(hops, rows // 2, columns),
            floats(hops, rows // 2, columns),
        ]

    return pl.pallas_call(
        functools.partial(backward_kernel, sizes, heads),
        out_shape=(
            shape(tok, part),
            shape(tok, part),
            shape(shard, inner),
            shape(shard, inner),
            shape(shard, 2 * N),
            shape(heads, shard),
            shape(shard, inner),
            shape(8, inner + 2 * N),
            shape(1, part),
        ),
        in_specs=[SCALARS] + [INSIDE] * 6 + [ANYWHERE] * 20,
        out_specs=(ANYWHERE, ANYWHERE, ANYWHERE, ANYWHERE, INSIDE, INSIDE, ANYWHERE, INSIDE, INSIDE),
        scratch_shapes=[
            floats(tp, tok, part),
            floats(fsdp, shard, 2 * tok),
            floats(8 + tok, inner),
            floats(8 + tok, 2 * N),
            floats(tok, 128),
            floats(tok, inner),
            floats(tok, 2 * N),
            floats(inner, N),
            floats(2 * tok, inner),
            floats(side, 2 * tok),
            halves(2 * tok, inner),
            halves(2 * tok, inner),
            halves(shard, 2 * tok),
            halves(shard, 2 * tok),
            floats(fsdp, shard, inner),
            floats(fsdp, shard, inner),
            floats(fsdp, side, shard),
            *landing(shard, inner),
            *landing(shard, inner),
            *landing(shard, inner),
            *landing(side, shard),
            floats(fsdp, shard, inner),
            floats(2, part, inner),
            floats(2 * fsdp * side, shard),
            floats(tok, 2 * N),
            halves(tok, side),
            halves(tok, side),
            floats(2 * N, tok),
            floats(tp - 1, share, tok),
            floats(2 * N, shard),
            floats(tp, tok, part),
            floats(tp, tok, part),
            floats(max(4, tp - 1), tok, part),
            floats(max(4, tp - 1), tok, part),
            floats(8, tok),
            floats(tp - 1, 8, tok),
            floats(tok, part),
            floats(tok, part),
            floats(tok, part),
            floats(tok, part),
            floats(inner, N),
            floats(inner, N),
            floats(tok, N),
            floats(tok, N),
            floats(8 + tok, inner),
            floats(8 + tok, 2 * N),
            floats(8, inner),
            floats(8, 2 * N),
            floats(tok, tok),
            floats(tok, tok),
            floats(tok, tok),
            floats(tok, 128),
            floats(tok, 128),
            floats(128, tok),
            floats(tok, 128),
            floats(tok, 128),
            floats(tok, 128),
            floats(128, tok),
            floats(1, inner),
            floats(8, inner + 2 * N),
            floats(1 + 2 * hops, 8, inner + 2 * N),
            floats(tp - 1, 8, 2 * N),
            floats(1, part),
            floats(2 * fsdp - 1, 1, part),
            pltpu.SemaphoreType.DMA((copies,)),
            pltpu.SemaphoreType.DMA((copies,)),
            pltpu.SemaphoreType.DMA((24 + 3 * tp,)),
        ],
        compiler_params=pltpu.CompilerParams(collective_id=1, has_side_effects=True, vmem_limit_bytes=VMEM_LIMIT),
        name="backward",
    )(*operands)


def last_kernel(heads, small, gain, dt, *refs):
    large, outs, held, sems = refs[:6], refs[6:22], refs[22:28], refs[28]
    loads, stores = [], []
    for k, (src, hold, dst) in enumerate(zip(large, held, outs)):
        loads.append(pltpu.make_async_copy(src, hold, sems.at[0, k]))
        stores.append(pltpu.make_async_copy(hold, dst, sems.at[1, k]))
    for load in loads:
        load.start()
    for load, store in zip(loads, stores):
        load.wait()
        store.start()
    grad_dt, taps_x, bias_x, taps_s, bias_s, dt_bias, a_log, d_skip, gate_gain, gain_in = outs[6:]
    inner = taps_x.shape[1]
    grad_dt[...] = dt[...]
    taps_x[...] = small[0:4, 0:inner]
    bias_x[...] = small[4:5, 0:inner]
    taps_s[...] = small[0:4, inner : inner + 2 * N]
    bias_s[...] = small[4:5, inner : inner + 2 * N]
    dt_bias[...] = small[5:6, inner : inner + heads]
    a_log[...] = small[6:7, inner : inner + heads]
    d_skip[...] = small[7:8, inner : inner + heads]
    gate_gain[...] = small[5:6, 0:inner]
    gain_in[...] = gain[...]
    for store in stores:
        store.wait()


def last_call(heads, small, gain, dt, *large):
    inner, part = small.shape[1] - 2 * N, gain.shape[1]
    few = [
        dt.shape,
        (4, inner),
        (1, inner),
        (4, 2 * N),
        (1, 2 * N),
        (1, heads),
        (1, heads),
        (1, heads),
        (1, inner),
        (1, part),
    ]
    return pl.pallas_call(
        functools.partial(last_kernel, heads),
        out_shape=tuple([shape(*value.shape) for value in large] + [shape(*dims) for dims in few]),
        in_specs=[INSIDE] * 3 + [ANYWHERE] * 6,
        out_specs=tuple([ANYWHERE] * 6 + [INSIDE] * len(few)),
        scratch_shapes=[floats(*value.shape) for value in large] + [pltpu.SemaphoreType.DMA((2, 6))],
        compiler_params=pltpu.CompilerParams(vmem_limit_bytes=VMEM_LIMIT),
        name="results",
    )(small, gain, dt, *large)


def shards(
    inputs,
    cotangent,
    seq_lengths,
    slots,
    gain_in,
    w_z,
    w_x,
    w_dt,
    w_bc,
    w_out,
    conv_x,
    conv_x_bias,
    conv_bc,
    conv_bc_bias,
    dt_bias,
    a_log,
    d_skip,
    gate_gain,
):
    sizes = (lax.axis_size("fsdp"), lax.axis_size("ctx"), lax.axis_size("tp"))
    tok, width = inputs.shape
    shard, inner = w_x.shape
    heads = w_dt.shape[1]
    tp = sizes[2]
    operands = (
        seq_lengths,
        slots[None],
        gain_in[None],
        conv_x,
        conv_x_bias[None],
        conv_bc,
        conv_bc_bias[None],
        dt_bias[None],
        a_log[None],
        d_skip[None],
        gate_gain[None],
        w_bc,
        w_dt.T,
        inputs,
        cotangent,
        w_x,
        w_z,
        w_out,
    )
    params_c, params_s, tokens, up, n_pairs, p_recv, *kept = forward_call(sizes, operands, heads)
    pre_x, pre_s, raw, conv_x_kept, conv_s_kept, normal_y, d_gate, d_mixed, gain_row, *rest = kept
    operands = (
        seq_lengths,
        slots[None],
        p_recv,
        gain_in.reshape(tp, 1, width // tp),
        params_c,
        params_s,
        gain_row,
        tokens,
        up,
        n_pairs,
        pre_x,
        pre_s,
        raw,
        conv_x_kept,
        conv_s_kept,
        normal_y,
        d_gate,
        d_mixed,
        *rest,
    )
    result, grad_input, grad_z, grad_x, grad_bc, grad_dt, grad_out, small, gain = backward_call(
        sizes, heads, operands, tok, width, shard, inner
    )
    outs = last_call(heads, small, gain, grad_dt, result, grad_input, grad_z, grad_x, grad_out, grad_bc)
    result, grad_input, grad_z, grad_x, grad_out, grad_bc, grad_dt, taps_x, bias_x, taps_s, bias_s, *few = outs
    return (
        result,
        grad_input,
        grad_z,
        grad_x,
        grad_dt.T,
        grad_bc,
        grad_out,
        taps_x,
        bias_x[0],
        taps_s,
        bias_s[0],
        *[value[0] for value in few],
    )


def solution(mesh):
    return jax.shard_map(
        shards,
        mesh=mesh,
        in_specs=(
            P(("fsdp", "ctx"), None),
            P(("fsdp", "ctx"), None),
            P("fsdp", None),
            P(("fsdp", "ctx")),
            P(),
            P(("fsdp", "ctx"), "tp"),
            P(("fsdp", "ctx"), "tp"),
            P(("fsdp", "ctx"), "tp"),
            P(("fsdp", "ctx"), None),
            P(("fsdp", "ctx"), "tp"),
            P(None, "tp"),
            P("tp"),
            P(),
            P(),
            P("tp"),
            P("tp"),
            P("tp"),
            P("tp"),
        ),
        out_specs=(
            P(("fsdp", "ctx"), "tp"),
            P(("fsdp", "ctx"), "tp"),
            P(("fsdp", "ctx"), "tp"),
            P(("fsdp", "ctx"), "tp"),
            P(("fsdp", "ctx"), "tp"),
            P(("fsdp", "ctx"), None),
            P(("fsdp", "ctx"), "tp"),
            P(None, "tp"),
            P("tp"),
            P(),
            P(),
            P("tp"),
            P("tp"),
            P("tp"),
            P("tp"),
            P("tp"),
        ),
        check_vma=False,
    )
```

```python
import functools
import math

import jax
import jax.numpy as jnp
from jax import lax
from jax.experimental import pallas as pl
from jax.experimental.pallas import tpu as pltpu
from jax.sharding import PartitionSpec as P

N = 128
SPAN = 256
INNER = 4096
EPSILON = 1e-05
F32 = jnp.float32
BF16 = jnp.bfloat16
MESH = pl.DeviceIdType.MESH
NN = (((1,), (0,)), ((), ()))
NT = (((1,), (1,)), ((), ()))
TN = (((0,), (0,)), ((), ()))
VMEM_LIMIT = 62 << 20


def split2(value):
    high = value.astype(BF16)
    return high, (value - high.astype(F32)).astype(BF16)


def split3(value):
    high = value.astype(BF16)
    rest = value - high.astype(F32)
    middle = rest.astype(BF16)
    return high, middle, (rest - middle.astype(F32)).astype(BF16)


def dot1(left, right, dims):
    return lax.dot_general(left, right, dims, preferred_element_type=F32)


def dot_split(left, right, dims):
    (lh, ll), (rh, rl) = left, right
    return dot1(lh, rh, dims) + (dot1(lh, rl, dims) + dot1(ll, rh, dims))


def dot3(left, right, dims):
    return dot_split(split2(left), split2(right), dims)


def pick(table, value, dims):
    parts = split3(value)
    return dot1(table, parts[0], dims) + dot1(table, parts[1], dims) + dot1(table, parts[2], dims)


def iota(shape, dim):
    return lax.broadcasted_iota(jnp.int32, shape, dim)


class Place:
    def __init__(self, fsdp, ctx, tp):
        self.fsdp, self.n_ctx, self.tp = fsdp, ctx, tp
        self.side = math.isqrt(fsdp)
        assert self.side * self.side == fsdp and ctx == 2
        self.f = lax.axis_index("fsdp")
        self.c = lax.axis_index("ctx")
        self.z = lax.axis_index("tp")
        self.y, self.x = self.f // self.side, self.f % self.side

    def chip(self, dy, dx):
        side = self.side
        return ((self.y + dy + side) % side) * side + (self.x + dx + side) % side

    def block(self, dy, dx, core):
        return self.chip(dy, dx) * 2 + core

    def at(self, dy, dx):
        return (self.chip(dy, dx), self.c, self.z)

    def sibling(self):
        return (self.f, 1 - self.c, self.z)

    def plane(self):
        out = []
        for df in range(self.fsdp):
            for dc in range(2):
                if df or dc:
                    to_f = (self.f + df) % self.fsdp
                    from_f = (self.f - df + self.fsdp) % self.fsdp
                    core = (self.c + dc) % 2
                    out.append(((to_f, core, self.z), to_f * 2 + core, from_f * 2 + core))
        return out

    def column(self):
        out = []
        for dz in range(1, self.tp):
            to_z = (self.z + dz) % self.tp
            out.append(((self.f, self.c, to_z), to_z, (self.z - dz + self.tp) % self.tp))
        return out


class Links:
    def __init__(self, send, recv, local):
        self.send, self.recv, self.local = send, recv, local
        self.used, self.used_local = 0, 0
        self.open = []

    def remote(self, src, dst, device):
        k = self.used
        self.used += 1
        copy = pltpu.make_async_remote_copy(
            src_ref=src,
            dst_ref=dst,
            send_sem=self.send.at[k],
            recv_sem=self.recv.at[k],
            device_id=device,
            device_id_type=MESH,
        )
        copy.start()
        self.open.append(copy)
        return copy

    def plan(self, src, dst, device, lands_as=None):
        k = self.used
        self.used += 1
        copy = pltpu.make_async_remote_copy(
            src_ref=src,
            dst_ref=dst,
            send_sem=self.send.at[k],
            recv_sem=self.recv.at[k if lands_as is None else lands_as.slot],
            device_id=device,
            device_id_type=MESH,
        )
        copy.slot = k
        return copy

    def move(self, src, dst):
        k = self.used_local
        self.used_local += 1
        copy = pltpu.make_async_copy(src, dst, self.local.at[k])
        copy.start()
        return copy

    def settle(self, copies):
        for copy in copies:
            copy.wait_send()
            self.open = [other for other in self.open if other is not copy]

    def finish(self):
        assert self.used <= self.send.shape[0] and self.used_local <= self.local.shape[0]
        self.settle(list(self.open))


def greet(devices):
    barrier = pltpu.get_barrier_semaphore()
    for device in devices:
        pl.semaphore_signal(barrier, inc=1, device_id=device, device_id_type=MESH)


def greeted(devices):
    pl.semaphore_wait(pltpu.get_barrier_semaphore(), len(devices))


class Spread:
    def __init__(self, place, links, slices):
        self.place, self.links, self.slices = place, links, slices
        self.line = place.tp == 4
        z, mine = place.z, slices.at[place.z]
        if not self.line:
            self.copies = [links.remote(mine, mine, device) for device, _, _ in place.column()]
            return
        self.copies = [links.remote(mine, mine, (place.f, place.c, z ^ d)) for d in (1, 2)]
        self.inner = (z == 1) | (z == 2)
        across = links.plan(mine, mine, (place.f, place.c, 3 - z))
        onward = slices.at[z ^ 2]
        self.onward = links.plan(onward, onward, (place.f, place.c, z ^ 1), across)
        self.across = across

        @pl.when(self.inner)
        def _():
            across.start()

    def forward(self):
        if self.line:
            self.copies.pop().wait_recv()

            @pl.when(self.inner)
            def _():
                self.onward.start()

    def finish(self):
        for copy in self.copies:
            copy.wait_recv()
        if self.line:
            self.across.wait_recv()

            @pl.when(self.inner)
            def _():
                self.across.wait_send()
                self.onward.wait_send()


class Gather:
    def __init__(self, place, links, shard, whole):
        self.place, self.links, self.shard, self.whole = place, links, shard, whole
        self.rows = shard.shape[0]
        self.near = 0

    def rows_of(self, block, start=0, count=None):
        count = self.rows if count is None else count
        return self.whole.at[pl.ds(pl.multiple_of(block * self.rows + start, 8), count)]

    def part(self, block, half):
        return self.rows_of(block, half * (self.rows // 2), self.rows // 2)

    def start(self):
        p, steps = self.place, range(1, self.place.side)
        me = p.block(0, 0, p.c)
        self.row, self.col = [[], []], [[], []]
        for turn in range(2):
            for d in steps:
                shard = self.shard.at[pl.ds(turn * (self.rows // 2), self.rows // 2)]
                self.row[turn].append(self.links.remote(shard, self.part(me, turn), p.at(0, d)))
                shard = self.shard.at[pl.ds((1 - turn) * (self.rows // 2), self.rows // 2)]
                self.col[turn].append(self.links.remote(shard, self.part(me, 1 - turn), p.at(d, 0)))
        mine = self.rows_of(me)
        self.pair = [self.links.remote(self.shard, mine, p.sibling())]
        self.own = self.links.move(self.shard, mine)

    def forward(self):
        p, steps = self.place, range(1, self.place.side)
        self.half_a, self.half_b = [], []
        for k, d in enumerate(steps):
            self.row[0][k].wait_recv()
            part = self.part(p.block(0, -d, p.c), 0)
            self.half_a += [self.links.remote(part, part, p.at(e, 0)) for e in steps]
        for k, e in enumerate(steps):
            self.col[0][k].wait_recv()
            part = self.part(p.block(-e, 0, p.c), 1)
            self.half_b += [self.links.remote(part, part, p.at(0, d)) for d in steps]
        for k, d in enumerate(steps):
            self.row[1][k].wait_recv()
            whole = self.rows_of(p.block(0, -d, p.c))
            self.pair.append(self.links.remote(whole, whole, p.sibling()))
        for k, e in enumerate(steps):
            self.col[1][k].wait_recv()
            whole = self.rows_of(p.block(-e, 0, p.c))
            self.pair.append(self.links.remote(whole, whole, p.sibling()))

    def share(self):
        p, steps, half = self.place, range(1, self.place.side), self.rows // 2
        k = 0
        for d in steps:
            for e in steps:
                self.half_a[k].wait_recv()
                part = self.rows_of(p.block(-e, -d, p.c), 0, half)
                self.pair.append(self.links.remote(part, part, p.sibling()))
                k += 1
        k = 0
        for e in steps:
            for d in steps:
                self.half_b[k].wait_recv()
                part = self.rows_of(p.block(-e, -d, p.c), half, half)
                self.pair.append(self.links.remote(part, part, p.sibling()))
                k += 1

    def finish_near(self):
        self.own.wait()
        self.near = 1 + 2 * (self.place.side - 1)
        for copy in self.pair[: self.near]:
            copy.wait_recv()

    def finish(self):
        if self.near == 0:
            self.finish_near()
        for copy in self.pair[self.near :]:
            copy.wait_recv()


def gather_copies(side):
    steps = side - 1
    return 6 * steps + 1 + 4 * steps * steps


def down_lanes(row):
    return jnp.broadcast_to(row, (128, row.shape[1])).T


def leaving(slots, tok, groups):
    slots = down_lanes(slots.astype(F32)).astype(jnp.int32)
    targets = slots >> (tok.bit_length() - 1)
    lanes = iota((tok, 128), 1)
    member = (targets == lanes).astype(F32)
    earlier = (iota((tok, tok), 0) > iota((tok, tok), 1)).astype(BF16)
    ranks = jnp.sum(dot1(earlier, member.astype(BF16), NN) * member, axis=1, keepdims=True)
    send_at = (targets[:, :1] * (tok // groups)).astype(F32) + ranks
    leave = (send_at == iota((tok, tok), 1).astype(F32)).astype(BF16)
    places = jnp.where(ranks == lanes.astype(F32), (slots - targets * tok).astype(F32), 0.0)
    return leave, dot1(member.astype(BF16), places.astype(BF16), TN)


def arrived(rows, tok, per_pair):
    groups = rows.shape[0]
    rows = jnp.concatenate([rows, jnp.zeros((128 - groups, 128), F32)], axis=0)
    token, lanes = iota((tok, 128), 0), iota((tok, 128), 1)
    spread = dot1((token // per_pair == lanes).astype(BF16), rows.astype(BF16), NN)
    place = jnp.sum(jnp.where(token % per_pair == lanes, spread, 0.0), axis=1, keepdims=True)
    return jnp.broadcast_to(place, (tok, 128))


def settling(places, tok):
    return (places[:, :1] == iota((tok, tok), 1).astype(F32)).astype(BF16)


def halve(value_ref, high, low):
    @pl.loop(0, value_ref.shape[1] // 128)
    def _(n):
        cols = pl.ds(pl.multiple_of(n * 128, 128), 128)
        high[:, cols], low[:, cols] = split2(value_ref[:, cols])


def project(left_high, left_low, whole, chips, out, tile, first_row, fresh):
    _, rows, width = left_high.shape

    @pl.loop(0, whole.shape[1] // tile)
    def _(n):
        cols = pl.ds(pl.multiple_of(n * tile, 128), tile)
        total = jnp.zeros((rows, tile), F32) if fresh else out[first_row : first_row + rows, cols]
        for chip in chips:
            at = pl.ds(chip * width if isinstance(chip, int) else pl.multiple_of(chip * width, 8), width)
            total = total + dot_split((left_high[chip], left_low[chip]), split2(whole[at, cols]), NN)
        out[first_row : first_row + rows, cols] = total


def weight_block(left_ref, high, low, left_high, left_low, out):
    left_high[...], left_low[...] = split2(left_ref[...])

    @pl.loop(0, high.shape[1] // 512)
    def _(n):
        cols = pl.ds(pl.multiple_of(n * 512, 128), 512)
        out[:, cols] = dot_split((left_high[...], left_low[...]), (high[:, cols], low[:, cols]), NN)


def times_rows(high, low, rows_ref, out, fresh):
    tile = min(256, rows_ref.shape[0])
    for n in range(rows_ref.shape[0] // tile):
        at = slice(n * tile, (n + 1) * tile)
        value = dot_split((high[...], low[...]), split2(rows_ref[at, :]), NT)
        out[:, at] = value if fresh else out[:, at] + value


class Scatter:
    def __init__(self, place, links, source, blocks, first, second=None):
        self.place, self.links, self.blocks = place, links, blocks
        self.first, self.second = first, second
        self.half = source.shape[1] // 2
        self.source = source
        self.copies_a, self.copies_b = {}, {}

    def order(self):
        side = self.place.side
        hops = [(dy, dx) for dy in range(side) for dx in range(side)]
        return sorted(hops, key=lambda hop: -(hop[0] > 0) - (hop[1] > 0))

    def halves(self, dy, dx, blocks=None):
        ref = (self.blocks if blocks is None else blocks).at[self.place.chip(dy, dx)]
        return ref.at[pl.ds(0, self.half)], ref.at[pl.ds(self.half, self.half)]

    def send(self, dy, dx):
        p, side = self.place, self.place.side
        upper, lower = self.halves(dy, dx, self.source)
        if dy:
            target = self.first[0].at[dy - 1, (p.x + dx) % side]
            self.copies_a[dy, dx] = self.links.remote(upper, target, p.at(dy, 0))
        if dx:
            target = self.first[1].at[dx - 1, (p.y + dy) % side]
            self.copies_b[dy, dx] = self.links.remote(lower, target, p.at(0, dx))

    def send_all(self):
        for hop in self.order():
            self.send(*hop)

    def land(self):
        for copy in [*self.copies_a.values(), *self.copies_b.values()]:
            copy.wait_recv()

    def pass_on(self):
        p, side = self.place, self.place.side
        self.last_a, self.last_b = [], []
        for d in list(range(1, side)) + [0]:
            upper, _ = self.halves(0, d)
            total = upper[...]
            for e in range(1, side):
                if (e, d) in self.copies_a:
                    self.copies_a[e, d].wait_recv()
                total = total + self.first[0][e - 1, (p.x + d) % side]
            upper[...] = total
            if d:
                self.last_a.append(self.links.remote(upper, self.second[0].at[d - 1], p.at(0, d)))
            _, lower = self.halves(d, 0)
            total = lower[...]
            for e in range(1, side):
                if (d, e) in self.copies_b:
                    self.copies_b[d, e].wait_recv()
                total = total + self.first[1][e - 1, (p.y + d) % side]
            lower[...] = total
            if d:
                self.last_b.append(self.links.remote(lower, self.second[1].at[d - 1], p.at(d, 0)))

    def finish(self):
        for k, (copies, part) in enumerate(zip((self.last_a, self.last_b), self.halves(0, 0))):
            total = part[...]
            for d, copy in enumerate(copies):
                copy.wait_recv()
                total = total + self.second[k][d]
            part[...] = total
        return self.blocks.at[self.place.chip(0, 0)]


class Shares:
    def __init__(self, place, links, parts, landing):
        self.place, self.links, self.parts, self.landing = place, links, parts, landing
        self.line = place.tp == 4
        z = place.z
        self.copies = []
        if self.line:
            self.turns = [z ^ 3, z ^ 2, z ^ 1, z]
            self.inner = (z == 1) | (z == 2)
        else:
            self.turns = [(z + d + 1) % place.tp for d in range(place.tp)]

    def send(self, k):
        place, z = self.place, self.place.z
        if k == place.tp - 1:
            return
        part = self.parts.at[self.turns[k]]
        if not self.line:
            self.copies.append(self.links.remote(part, self.landing.at[k], (place.f, place.c, self.turns[k])))
            return
        if k == 0:
            self.direct = self.links.plan(part, self.landing.at[2], (place.f, place.c, z ^ 3))
            self.extra = self.links.plan(part, self.landing.at[3], (place.f, place.c, z ^ 1))

            @pl.when(self.inner)
            def _():
                self.direct.start()

            @pl.when(jnp.logical_not(self.inner))
            def _():
                self.extra.start()

        elif k == 1:
            self.across = self.links.plan(part, self.landing.at[1], (place.f, place.c, z ^ 2))

            @pl.when(jnp.logical_not(self.inner))
            def _():
                self.across.start()

        else:
            self.copies.append(self.links.remote(part, self.landing.at[0], (place.f, place.c, z ^ 1)))

    def forward(self):
        if self.line:

            @pl.when(self.inner)
            def _():
                self.extra.wait_recv()
                part = self.parts.at[self.place.z ^ 2]
                part[...] = part[...] + self.landing[3]
                self.across.start()

    def finish(self):
        own = self.parts.at[self.place.z]
        total = own[...]
        for k, copy in enumerate(self.copies):
            copy.wait_recv()
            total = total + self.landing[k]
        if self.line:
            self.across.wait_recv()
            total = total + self.landing[1]
            self.across.wait_send()
        own[...] = total
        if self.line:

            @pl.when(self.inner)
            def _():
                self.direct.wait()
                own[...] = own[...] + self.landing[2]

            @pl.when(jnp.logical_not(self.inner))
            def _():
                self.extra.wait_send()


def silu_slope(value):
    gate = jax.nn.sigmoid(value)
    return gate * (1.0 + value * (1.0 - gate))


def softplus(value):
    return jnp.maximum(value, 0.0) + jnp.log1p(jnp.exp(-jnp.abs(value)))


def segments(lengths, position):
    bound, seg = 0, jnp.zeros_like(position)
    for k in range(lengths.shape[1]):
        bound = bound + lengths[0, k]
        seg = seg + (bound <= position).astype(jnp.int32)
    return seg


def same_before(lengths, first, tok, distance):
    position = first + iota((tok, 128), 0)
    return (segments(lengths, position) == segments(lengths, position - distance)).astype(F32)


def wide(table, width):
    return jnp.concatenate([table] * (width // 128), axis=1)


def column_of(table, head):
    lanes = iota(table.shape, 1)
    return jnp.sum(jnp.where(lanes == head, table, 0.0), axis=1, keepdims=True)


def pair_columns(table, pair):
    first, second = column_of(table, 2 * pair), column_of(table, 2 * pair + 1)
    return jnp.where(iota(table.shape, 1) < 64, first, second)


class Steps:
    def __init__(self, raw, params_s, lengths, first):
        tok = raw.shape[0]
        shifted = raw + params_s[5:6, :128]
        self.slope = jax.nn.sigmoid(shifted)
        self.step = softplus(shifted)
        self.rate = -jnp.exp(params_s[6:7, :128])
        until = (iota((tok, tok), 0) >= iota((tok, tok), 1)).astype(BF16)
        self.total = pick(until, self.step * self.rate, NN)
        position = first + iota((tok, 128), 0)
        seg = segments(lengths, position)
        before = segments(lengths, jnp.full((tok, 128), first - 1, jnp.int32))
        last = segments(lengths, jnp.full((tok, 128), first + tok - 1, jnp.int32))
        self.reading = jnp.exp(self.total) * (seg == before).astype(F32)
        self.fading = jnp.exp(self.total[tok - 1 : tok] - self.total) * (seg == last).astype(F32)
        self.tail = self.fading * self.step


def closed(lengths, first, tok, flipped):
    rows, cols = first + iota((tok, tok), 0), first + iota((tok, tok), 1)
    order = rows <= cols if flipped else rows >= cols
    seg_rows = segments(lengths, first + iota((tok, 1), 0))
    seg_cols = segments(lengths, first + iota((1, tok), 1))
    return jnp.where(order & (seg_rows == seg_cols), 0.0, -1e30)


def convolve(padded, params, lengths, first, conv, act):
    tok, tile = conv.shape[0], 128
    same = [same_before(lengths, first, tok, 3 - k) for k in range(3)]

    @pl.loop(0, conv.shape[1] // tile)
    def _(n):
        cols = pl.ds(pl.multiple_of(n * tile, 128), tile)
        total = params[4:5, cols] + params[3:4, cols] * padded[8 : 8 + tok, cols]
        for k in range(3):
            total = total + params[k : k + 1, cols] * (padded[5 + k : 5 + k + tok, cols] * same[k])
        conv[:, cols] = total
        act[:, cols] = total * jax.nn.sigmoid(total)


def forward_kernel(
    sizes,
    lengths,
    slots_in_hbm,
    gain_hbm,
    taps_x_hbm,
    bias_x_hbm,
    taps_s_hbm,
    bias_s_hbm,
    dt_bias_hbm,
    a_log_hbm,
    d_skip_hbm,
    gate_gain_hbm,
    w_bc_hbm,
    w_dt_hbm,
    x_in,
    c_in,
    w_x,
    w_z,
    w_out,
    params_c_hbm,
    params_s_hbm,
    tokens_out,
    up_out,
    n_pairs_out,
    p_out_hbm,
    pre_x_out,
    pre_s_out,
    raw_out,
    conv_x_out,
    conv_s_out,
    ny_out,
    dz_out,
    dmix_out,
    gain_row_hbm,
    state_out,
    g_out,
    gz_out,
    land_a,
    land_b,
    wx_out,
    ws_out,
    wz_out,
    wo_out,
    slots_in,
    gain,
    taps_x,
    bias_x,
    taps_s,
    bias_s,
    dt_bias,
    a_log,
    d_skip,
    gate_gain,
    w_bc,
    w_dt,
    params_c,
    params_s,
    p_out,
    gain_row,
    wx,
    ws,
    wz,
    wo,
    ws_own,
    x_own,
    c_own,
    x_sort,
    c_sort,
    p_sort,
    p_recv,
    x_recv,
    c_recv,
    tokens,
    n_high,
    n_low,
    turned,
    n_pairs,
    c_pairs,
    pre_x,
    pre_s,
    raw,
    bc_rows,
    tail_x,
    tail_s,
    conv_x,
    conv_s,
    act_x,
    act_s,
    totals,
    step_rows,
    open_,
    scores,
    state,
    state_in,
    mixed,
    gate_pre,
    d_normal,
    ny_both,
    high,
    low,
    left_high,
    left_low,
    sums,
    sums_recv,
    inner_sums,
    inner_recv,
    send,
    recv,
    local,
):
    place = Place(*sizes)
    links = Links(send, recv, local)
    tok, groups = x_own.shape[0], 2 * place.fsdp
    per_pair = tok // groups
    part = x_own.shape[1]
    inner = act_x.shape[1]
    pairs = inner // 128
    heads = d_skip.shape[1]
    share = 2 * N // place.tp
    shard_rows = n_pairs.shape[1]
    chip_rows = 2 * shard_rows
    first = place.c * tok
    lanes = iota((tok, 128), 1)
    part_cols = pl.ds(pl.multiple_of(place.z * part, 128), part)
    load_x = links.move(x_in.at[:, part_cols], x_own)
    first_loads = [links.move(slots_in_hbm, slots_in)]
    load_c = links.move(c_in.at[:, part_cols], c_own)
    first_loads += [
        links.move(gain_hbm, gain),
        links.move(taps_x_hbm, taps_x),
        links.move(bias_x_hbm, bias_x),
        links.move(taps_s_hbm, taps_s),
        links.move(bias_s_hbm, bias_s),
        links.move(dt_bias_hbm, dt_bias),
        links.move(a_log_hbm, a_log),
        links.move(d_skip_hbm, d_skip),
        links.move(gate_gain_hbm, gate_gain),
        links.move(w_bc_hbm, w_bc),
        links.move(w_dt_hbm, w_dt),
    ]
    plane, column = place.plane(), place.column()
    partners = [entry[0] for entry in plane] + [entry[0] for entry in column]
    greet(partners)

    first_loads[0].wait()
    leave, places = leaving(slots_in[...], tok, groups)
    p_sort[...] = jnp.broadcast_to(places[0:groups, None, :], (groups, 8, 128))
    load_x.wait()
    x_sort[...] = pick(leave, x_own[...], TN)
    greeted(partners)
    g_x, g_s, g_z, g_o = [Gather(place, links, shard, whole) for shard, whole in ((w_x, wx), (ws_own, ws), (w_z, wz), (w_out, wo))]

    def rows(group):
        return pl.ds(pl.multiple_of(group * per_pair, 8), per_pair)

    def route(source, target, at):
        mine = at(place.f * 2 + place.c)
        copies = [links.remote(source.at[at(to)], target.at[mine], device) for device, to, _ in plane]
        return copies, links.move(source.at[mine], target.at[mine])

    routes_x = [route(p_sort, p_recv, lambda group: group), route(x_sort, x_recv.at[place.z], rows)]
    g_x.start()

    def share_of(turn):
        return pl.ds(pl.multiple_of(turn * share, 8), share)

    for load in first_loads[1:]:
        load.wait()
    bc_rows[:, 0:shard_rows] = w_bc[...].T
    ws_own[...] = jnp.zeros_like(ws_own)
    ws_own[0:heads, :] = w_dt[...]
    ws_own[heads : heads + share, :] = bc_rows[share_of(place.z), 0:shard_rows]
    g_s.start()
    load_c.wait()
    c_sort[...] = pick(leave, c_own[...], TN)
    routes_c = [route(c_sort, c_recv.at[place.z], rows)]

    params_c[0:4, :] = taps_x[...]
    params_c[4:5, :] = bias_x[...]
    params_c[6:7, :] = gate_gain[...]
    params_c[7:8, :] = jnp.zeros((1, inner), F32)
    for q in range(pairs):
        both = [d_skip[0:1, 2 * q + s : 2 * q + s + 1] for s in range(2)]
        params_c[5:6, q * 128 : (q + 1) * 128] = jnp.where(lanes[0:1] < 64, both[0], both[1])
    params_s[...] = jnp.zeros_like(params_s)
    params_s[0:4, :] = taps_s[...]
    params_s[4:5, :] = bias_s[...]
    params_s[5:6, 0:heads] = dt_bias[...]
    params_s[6:7, 0:heads] = a_log[...]

    def arrive(routes):
        for copies, own in routes:
            own.wait()
            for copy in copies:
                copy.wait_recv()

    arrive(routes_x)
    spread_x = Spread(place, links, x_recv)
    g_x.forward()
    g_s.forward()
    g_z.start()
    spread_x.forward()
    arrive(routes_c)
    g_s.share()
    stores = [links.move(params_c, params_c_hbm), links.move(params_s, params_s_hbm)]
    spread_x.finish()
    p_out[...] = arrived(p_recv[:, 0, :], tok, per_pair)
    stores.append(links.move(p_out, p_out_hbm))
    settle = settling(p_out, tok)
    squares = jnp.zeros((tok, 1), F32)
    for k in range(place.tp):
        value = pick(settle, x_recv[k], TN)
        tokens[k] = value
        squares = squares + jnp.sum(value * value, axis=1, keepdims=True)
    scale = lax.rsqrt(squares / (place.tp * part) + EPSILON)
    own_cols = pl.ds(pl.multiple_of(place.c * tok, 128), tok)
    own_rows = pl.ds(pl.multiple_of(place.c * tok, 128), tok)
    chips_here = part // chip_rows

    def keep_left(k, value):
        for j in range(chips_here):
            piece = value[:, j * chip_rows : (j + 1) * chip_rows]
            n_high[k * chips_here + j], n_low[k * chips_here + j] = split2(piece)
        turned[k * part : (k + 1) * part, :] = value.T

    def exchange_blocks(pairs_ref):
        copies, kept = [], []
        for q in range(place.fsdp):
            there = turned.at[pl.ds(pl.multiple_of((2 * q + 1 - place.c) * shard_rows, 8), shard_rows)]
            here = turned.at[pl.ds(pl.multiple_of((2 * q + place.c) * shard_rows, 8), shard_rows)]
            copies.append(links.remote(there, pairs_ref.at[q, :, own_cols], place.sibling()))
            kept.append(links.move(here, pairs_ref.at[q, :, own_cols]))
        return copies, kept

    for k in range(place.tp):
        keep_left(k, tokens[k] * scale * gain[:, k * part : (k + 1) * part])
    pairs_n, kept_n = exchange_blocks(n_pairs)
    stores.append(links.move(tokens, tokens_out))

    every = list(range(place.fsdp))
    g_s.finish()
    raw[...] = jnp.zeros_like(raw)
    side_rows = ws_own.shape[0]
    total = jnp.zeros((tok, side_rows), F32)
    for block in range(2 * place.fsdp):
        at = slice(block % 2 * shard_rows, (block % 2 + 1) * shard_rows)
        left = (n_high[block // 2, :, at], n_low[block // 2, :, at])
        total = total + dot_split(left, split2(ws[block * side_rows : (block + 1) * side_rows, :]), NT)
    raw[:, 0:side_rows] = total
    bc_turned = raw[...].T
    bc_rows[share_of(place.z), :] = bc_turned[heads : heads + share]
    mine = bc_rows.at[share_of(place.z)]
    spread_bc = [links.remote(mine, mine, device) for device, _, _ in column]
    spread_c = Spread(place, links, c_recv)
    g_x.share()
    g_x.finish()
    keep_wx = links.move(wx, wx_out)
    stores += [links.move(ws, ws_out)]
    project(n_high, n_low, wx, every, pre_x, 512, 8, True)
    halo = [links.remote(pre_x.at[pl.ds(tok, 8)], tail_x, place.sibling())]
    g_z.forward()
    g_o.start()

    raw[...] = jnp.where(lanes < heads, raw[...], 0.0)
    steps = Steps(raw[...], params_s, lengths, first)
    totals[...] = steps.total
    step_rows[0] = steps.total.T
    step_rows[1] = steps.step.T
    open_[...] = closed(lengths, first, tok, False)
    for copy in spread_bc:
        copy.wait_recv()
    pre_s[8 : 8 + tok, :] = bc_rows[...].T
    halo.append(links.remote(pre_s.at[pl.ds(tok, 8)], tail_s, place.sibling()))
    for copy in halo:
        copy.wait_recv()
    second = (place.c > 0).astype(F32)
    pre_x[0:8, :] = tail_x[...] * second
    pre_s[0:8, :] = tail_s[...] * second
    convolve(pre_s, params_s, lengths, first, conv_s, act_s)
    convolve(pre_x, params_c, lengths, first, conv_x, act_x)
    b_parts = split2(act_s[:, :N])
    c_parts = split2(act_s[:, N:])
    scores[...] = dot_split(c_parts, b_parts, NT)
    tail_table, reading_table = steps.tail, steps.reading

    @pl.loop(0, pairs)
    def _(q):
        cols = pl.ds(pl.multiple_of(q * 128, 128), 128)
        faded = act_x[:, cols] * pair_columns(tail_table, q)
        state[cols, :] = dot_split(split2(faded), b_parts, TN)

    pass_state = links.remote(state, state_in, place.sibling())
    spread_c.forward()
    pass_state.wait_recv()

    @pl.loop(0, pairs)
    def _(q):
        cols = pl.ds(pl.multiple_of(q * 128, 128), 128)
        channels = act_x[:, cols]
        entered = state_in[cols, :] * second
        state_in[cols, :] = entered
        out = params_c[5:6, cols] * channels
        out = out + pair_columns(reading_table, q) * dot_split(c_parts, split2(entered), NT)
        for s in range(2):
            head = 2 * q + s
            gaps = column_of(totals[...], head) - step_rows[0, pl.ds(head, 1), :] + open_[...]
            weights = jnp.exp(gaps) * scores[...] * step_rows[1, pl.ds(head, 1), :]
            own = jnp.where((lanes < 64) == (s == 0), channels, 0.0)
            out = out + dot3(weights, own, NN)
        mixed[:, cols] = out

    stores += [
        links.move(pre_x, pre_x_out),
        links.move(pre_s, pre_s_out),
        links.move(raw, raw_out),
        links.move(conv_x, conv_x_out),
        links.move(conv_s, conv_s_out),
        links.move(state_in, state_out),
    ]
    g_z.share()
    g_z.finish()
    stores.append(links.move(wz, wz_out))
    project(n_high, n_low, wz, every, gate_pre, 512, 0, True)

    def over_tiles(body, carry):
        def step(n, carry):
            return body(pl.ds(pl.multiple_of(n * 128, 128), 128), carry)

        return lax.fori_loop(0, pairs, step, carry)

    def gated_at(cols):
        z = gate_pre[:, cols]
        return mixed[:, cols] * (z * jax.nn.sigmoid(z))

    def add_squares(cols, total):
        gated = gated_at(cols)
        return total + gated * gated

    zeros = jnp.zeros((tok, 128), F32)
    square_sum = over_tiles(add_squares, zeros)
    sums[...] = jnp.broadcast_to(jnp.sum(square_sum, axis=1, keepdims=True), (tok, 128)).T[0:8, :]
    copies = [links.remote(sums, sums_recv.at[k], device) for k, (device, _, _) in enumerate(column)]

    spread_c.finish()
    for copy in pairs_n:
        copy.wait_recv()
    links.settle(pairs_n)
    for copy in kept_n:
        copy.wait()
    stores.append(links.move(n_pairs, n_pairs_out))
    for k in range(place.tp):
        upstream = pick(settle, c_recv[k], TN)
        keep_left(k, upstream)

        @pl.when(place.z == k)
        def _():
            x_own[...] = upstream

    pairs_c, kept_c = exchange_blocks(c_pairs)
    stores.append(links.move(x_own, up_out))

    for copy in copies:
        copy.wait_recv()
    total = sums[...]
    for k in range(place.tp - 1):
        total = total + sums_recv[k]
    gscale = lax.rsqrt(down_lanes(total[0:1]) / INNER + EPSILON)

    def normalise(cols, carry):
        ny_both[own_rows, cols] = gated_at(cols) * gscale * params_c[6:7, cols]
        return carry

    over_tiles(normalise, 0)
    g_o.forward()
    give_ny = links.remote(ny_both.at[own_rows], ny_both.at[own_rows], place.sibling())
    keep_ny = links.move(ny_both.at[own_rows], ny_out)

    near = [place.f] + [place.chip(0, d) for d in range(1, place.side)] + [place.chip(d, 0) for d in range(1, place.side)]
    far = [place.chip(e, d) for e in range(1, place.side) for d in range(1, place.side)]
    for copy in kept_c:
        copy.wait()
    for copy in pairs_c:
        copy.wait_recv()
    give_ny.wait_recv()
    halve(ny_both, high, low)
    keep_wx.wait()
    links.settle(g_x.half_a + g_x.half_b + g_x.pair)
    blocks_o = wx.reshape(2, place.fsdp, shard_rows, inner).at[0]
    blocks_z = wx.reshape(2, place.fsdp, shard_rows, inner).at[1]
    for q in range(place.fsdp):
        weight_block(c_pairs.at[q], high, low, left_high, left_low, blocks_o.at[q])
    stores.append(links.move(blocks_o, g_out))
    sum_o = Scatter(place, links, blocks_o, blocks_o, (land_a, land_b))
    sum_o.send_all()
    def keep_rows(chip):
        at = pl.ds(pl.multiple_of(chip * chip_rows, 8), chip_rows)
        stores.append(links.move(wo.at[at], wo_out.at[at]))

    g_o.finish_near()
    for chip in near:
        keep_rows(chip)
    project(n_high, n_low, wo, near, d_normal, 512, 0, True)
    g_o.share()
    g_o.finish()
    for chip in far:
        keep_rows(chip)
    project(n_high, n_low, wo, far, d_normal, 512, 0, False)

    def add_inner(cols, total):
        return total + d_normal[:, cols] * params_c[6:7, cols] * gated_at(cols)

    inner_sum = over_tiles(add_inner, zeros)
    inner_sums[...] = jnp.broadcast_to(jnp.sum(inner_sum, axis=1, keepdims=True), (tok, 128)).T[0:8, :]
    copies = [links.remote(inner_sums, inner_recv.at[k], device) for k, (device, _, _) in enumerate(column)]
    links.settle([give_ny])
    keep_ny.wait()
    for copy in copies:
        copy.wait_recv()
    total = inner_sums[...]
    for k in range(place.tp - 1):
        total = total + inner_recv[k]
    pull = gscale * gscale * gscale * down_lanes(total[0:1]) / INNER

    def shape_all(cols, carry):
        z, y, upward, weight = gate_pre[:, cols], mixed[:, cols], d_normal[:, cols], params_c[6:7, cols]
        gate = jax.nn.sigmoid(z)
        act = z * gate
        gated = y * act
        d_gated = gscale * weight * upward - gated * pull
        d_normal[:, cols] = d_gated * act
        ny_both[own_rows, cols] = d_gated * y * gate * (1.0 + z * (1.0 - gate))
        gain_row[:, cols] = jnp.sum(upward * gated * gscale, axis=0, keepdims=True)
        return carry

    over_tiles(shape_all, 0)
    give_dz = links.remote(ny_both.at[own_rows], ny_both.at[own_rows], place.sibling())
    stores += [links.move(ny_both.at[own_rows], dz_out), links.move(d_normal, dmix_out), links.move(gain_row, gain_row_hbm)]
    give_dz.wait_recv()
    halve(ny_both, high, low)
    for q in range(place.fsdp):
        weight_block(n_pairs.at[q], high, low, left_high, left_low, blocks_z.at[q])
        stores.append(links.move(blocks_z.at[q], gz_out.at[q]))
    sum_o.land()
    for store in stores:
        store.wait()
    links.finish()


def backward_kernel(
    sizes,
    heads,
    lengths,
    slots_in_hbm,
    p_recv_hbm,
    gain_hbm,
    params_c_hbm,
    params_s_hbm,
    gain_row_hbm,
    tokens_in,
    up_in,
    n_pairs_in,
    pre_x_in,
    pre_s_in,
    raw_in,
    conv_x_in,
    conv_s_in,
    ny_in,
    dz_in,
    dmix_in,
    state_in_hbm,
    g_in,
    gz_in,
    land_a_in,
    land_b_in,
    wx_in,
    ws_in,
    wz_in,
    wo_in,
    result,
    grad_input,
    grad_z,
    grad_x,
    grad_bc_hbm,
    grad_dt_hbm,
    grad_out,
    small_out_hbm,
    gain_out_hbm,
    slots_in,
    p_recv,
    gain,
    params_c,
    params_s,
    gain_row,
    grad_bc,
    grad_dt,
    small_out,
    gain_out,
    tokens,
    n_pairs,
    pre_x,
    pre_s,
    raw,
    conv_x,
    conv_s,
    state_in,
    dx_both,
    ds_both,
    high,
    low,
    left_high,
    left_low,
    blocks_o,
    blocks_z,
    blocks_s,
    o1a, o1b, o2a, o2b,
    z1a, z1b, z2a, z2b,
    x1a, x1b, x2a, x2b,
    s1a, s1b, s2a, s2b,
    blocks_x,
    stream,
    ws,
    d_bc,
    ds_high,
    ds_low,
    bc_rows,
    bc_recv,
    bc_grad,
    part_r,
    part_t,
    recv_r,
    recv_t,
    row_sums,
    row_recv,
    home_r,
    home_t,
    back_r,
    back_t,
    d_state,
    d_state_recv,
    d_b,
    d_c,
    pad_x,
    pad_s,
    head_x,
    head_s,
    open_,
    scores,
    d_scores,
    totals,
    steps_col,
    total_rows,
    grad_total,
    grad_step,
    grad_tail,
    grad_rows,
    skip_row,
    small,
    small_recv,
    small_z,
    gain_own,
    gain_recv,
    send,
    recv,
    local,
):
    place = Place(*sizes)
    links = Links(send, recv, local)
    tok, groups = tokens.shape[1], 2 * place.fsdp
    per_pair = tok // groups
    part = tokens.shape[2]
    inner = conv_x.shape[1]
    pairs = inner // 128
    first = place.c * tok
    own_rows = pl.ds(pl.multiple_of(place.c * tok, 128), tok)
    plane, column = place.plane(), place.column()

    partners = [entry[0] for entry in plane] + [entry[0] for entry in column]
    greet(partners)
    shares_r, shares_t = Shares(place, links, part_r, recv_r), Shares(place, links, part_t, recv_t)
    turns = shares_r.turns
    schedule = [(weight, turn) for weight in (wo_in, wx_in, wz_in) for turn in turns]
    fetched = []

    def fetch():
        k = len(fetched)
        if k < len(schedule):
            weight, turn = schedule[k]
            src = weight.at[pl.ds(pl.multiple_of(turn * part, 8), part)]
            fetched.append(links.move(src, stream.at[k % 2]))

    def weight_slice(k):
        fetched[k].wait()
        return stream.at[k % 2]

    greeted(partners)
    sum_o = Scatter(place, links, g_in, blocks_o, (o1a, o1b), (o2a, o2b))
    sum_z = Scatter(place, links, gz_in, blocks_z, (z1a, z1b), (z2a, z2b))
    sum_z.send_all()
    loads = {}
    loads["ny"] = links.move(ny_in, dx_both.at[own_rows])
    fetch()
    fetch()
    few = [
        links.move(slots_in_hbm, slots_in),
        links.move(p_recv_hbm, p_recv),
        links.move(gain_hbm, gain),
        links.move(params_c_hbm, params_c),
        links.move(params_s_hbm, params_s),
        links.move(gain_row_hbm, gain_row),
    ]
    for name, src, dst in (
        ("g", g_in, blocks_o),
        ("land_a", land_a_in, o1a),
        ("land_b", land_b_in, o1b),
        ("raw", raw_in, raw),
        ("conv_s", conv_s_in, conv_s),
        ("dmix", dmix_in, pad_x.at[pl.ds(0, tok)]),
        ("state", state_in_hbm, state_in),
        ("conv_x", conv_x_in, conv_x),
        ("n_pairs", n_pairs_in, n_pairs),
        ("gz", gz_in, blocks_z),
        ("pre_x", pre_x_in, pre_x),
        ("pre_s", pre_s_in, pre_s),
        ("tokens", tokens_in, tokens),
        ("up", up_in, home_t),
        ("ws", ws_in, ws),
    ):
        loads[name] = links.move(src, dst)

    loads["ny"].wait()
    halve(dx_both.at[own_rows], high.at[own_rows], low.at[own_rows])

    def product(k, turn, fresh, out):
        ref = weight_slice(k)
        times_rows(high.at[own_rows], low.at[own_rows], ref, out, fresh)
        fetch()

    for k, turn in enumerate(turns):
        product(k, turn, True, part_r.at[turn])
        shares_r.send(k)
        if k == min(1, place.tp - 1):
            for name in ("g", "land_a", "land_b"):
                loads[name].wait()
            sum_o.pass_on()

    for load in few:
        load.wait()
    loads["raw"].wait()
    loads["conv_s"].wait()
    steps = Steps(raw[...], params_s, lengths, first)
    totals[...] = steps.total
    steps_col[...] = steps.step
    total_rows[...] = steps.total.T
    open_[...] = closed(lengths, first, tok, True)
    act_s = conv_s[...] * jax.nn.sigmoid(conv_s[...])
    b_parts, c_parts = split2(act_s[:, :N]), split2(act_s[:, N:])
    scores[...] = dot_split(b_parts, c_parts, NT)
    reading_table, tail_table = steps.reading, steps.tail
    grad_total[...] = jnp.zeros((tok, 128), F32)
    grad_step[...] = jnp.zeros((tok, 128), F32)
    grad_tail[...] = jnp.zeros((tok, 128), F32)
    d_c[...] = jnp.zeros((tok, N), F32)
    d_b[...] = jnp.zeros((tok, N), F32)
    d_scores[...] = jnp.zeros((tok, tok), F32)
    grad_rows[...] = jnp.zeros((128, tok), F32)
    lanes = iota((tok, 128), 1)

    def put(ref, head, value):
        ref[...] = ref[...] + jnp.where(lanes == head, value, 0.0)

    def by_head(value, s):
        return jnp.sum(jnp.where((lanes < 64) == (s == 0), value, 0.0), axis=1, keepdims=True)

    loads["dmix"].wait()
    loads["state"].wait()

    @pl.loop(0, pairs)
    def _(q):
        cols = pl.ds(pl.multiple_of(q * 128, 128), 128)
        upward = pad_x[0:tok, cols] * pair_columns(reading_table, q)
        parts = split2(upward)
        entered = split2(state_in[cols, :])
        d_c[...] = d_c[...] + dot_split(parts, entered, NN)
        d_state[cols, :] = dot_split(parts, c_parts, TN)
        read = upward * dot_split(c_parts, entered, NT)
        for s in range(2):
            put(grad_total, 2 * q + s, by_head(read, s))

    give_state = links.remote(d_state, d_state_recv, place.sibling())

    shares_r.forward()

    loads["conv_x"].wait()
    give_state.wait_recv()
    first_half = (place.c == 0).astype(F32)

    @pl.loop(0, pairs)
    def _(q):
        cols = pl.ds(pl.multiple_of(q * 128, 128), 128)
        conv = conv_x[:, cols]
        gate = jax.nn.sigmoid(conv)
        channels = conv * gate
        upward = pad_x[0:tok, cols]
        ended = split2(d_state_recv[cols, :] * first_half)
        tail = pair_columns(tail_table, q)
        from_end = dot_split(b_parts, ended, NT)
        d_b[...] = d_b[...] + dot_split(split2(channels * tail), ended, NN)
        into = params_c[5:6, cols] * upward + tail * from_end
        skip_row[:, cols] = jnp.sum(upward * channels, axis=0, keepdims=True)
        end_part = channels * from_end
        x_parts = split2(channels)
        for s in range(2):
            head = 2 * q + s
            put(grad_tail, head, by_head(end_part, s))
            step_col = column_of(steps_col[...], head)
            gaps = total_rows[pl.ds(head, 1), :] - column_of(totals[...], head) + open_[...]
            decay = jnp.exp(gaps)
            up_parts = split2(jnp.where((lanes < 64) == (s == 0), upward, 0.0))
            reach = dot_split(x_parts, up_parts, NT) * decay
            d_scores[...] = d_scores[...] + reach * step_col
            reach = reach * scores[...]
            put(grad_step, head, jnp.sum(reach, axis=1, keepdims=True))
            grad_rows[pl.ds(head, 1), :] = jnp.sum(reach * step_col, axis=0, keepdims=True)
            into = into + dot3(decay * scores[...] * step_col, jnp.where((lanes < 64) == (s == 0), upward, 0.0), NN)
        pad_x[0:tok, cols] = into * gate * (1.0 + conv * (1.0 - gate))

    loads["dz"] = links.move(dz_in, conv_x)

    score_parts = split2(d_scores[...])
    slope_s = silu_slope(conv_s[...])
    pad_s[0:tok, 0:N] = (d_b[...] + dot_split(score_parts, c_parts, NN)) * slope_s[:, :N]
    pad_s[0:tok, N : 2 * N] = (d_c[...] + dot_split(score_parts, b_parts, TN)) * slope_s[:, N:]
    halo = [
        links.remote(pad_x.at[pl.ds(0, 8)], head_x, place.sibling()),
        links.remote(pad_s.at[pl.ds(0, 8)], head_s, place.sibling()),
    ]
    step_now = steps_col[...]
    faded = grad_tail[...] * tail_table
    d_total = grad_total[...] + grad_rows[...].T - grad_step[...] * step_now - faded
    at_end = iota((tok, 128), 0) == tok - 1
    d_total = d_total + jnp.where(at_end, jnp.sum(faded, axis=0, keepdims=True), 0.0)
    onward = (iota((tok, tok), 1) >= iota((tok, tok), 0)).astype(BF16)
    d_log = pick(onward, d_total, NN)
    d_step = grad_step[...] + grad_tail[...] * steps.fading + d_log * steps.rate
    d_raw = jnp.where(lanes < heads, d_step * steps.slope, 0.0)
    small[...] = jnp.zeros_like(small)
    small[5:6, inner : inner + 128] = jnp.sum(d_raw, axis=0, keepdims=True)
    small[6:7, inner : inner + 128] = jnp.sum(d_log * step_now, axis=0, keepdims=True) * steps.rate
    head_of = (iota((inner, 128), 0) // (inner // heads) == iota((inner, 128), 1)).astype(BF16)
    skips = jnp.broadcast_to(skip_row[...], (8, inner))
    small[7:8, inner : inner + 128] = sum(dot1(piece, head_of, NN) for piece in split3(skips))[0:1]
    small[5:6, 0:inner] = gain_row[...]

    loads["pre_x"].wait()
    loads["pre_s"].wait()
    for copy in halo:
        copy.wait_recv()
    pad_x[tok : tok + 8, :] = head_x[...] * first_half
    pad_s[tok : tok + 8, :] = head_s[...] * first_half
    same = [same_before(lengths, first, tok, 3 - k) for k in range(3)]
    same_next = [same_before(lengths, first + 3 - k, tok, 3 - k) for k in range(3)]

    def back(padded, pre, params, out, start, n):
        cols = pl.ds(pl.multiple_of(n * 128, 128), 128)
        small_cols = pl.ds(pl.multiple_of(start + n * 128, 128), 128)
        here = padded[0:tok, cols]
        total = params[3:4, cols] * here
        small[3:4, small_cols] = jnp.sum(here * pre[8 : 8 + tok, cols], axis=0, keepdims=True)
        small[4:5, small_cols] = jnp.sum(here, axis=0, keepdims=True)
        for k in range(3):
            total = total + params[k : k + 1, cols] * (padded[3 - k : 3 - k + tok, cols] * same_next[k])
            value = here * (pre[5 + k : 5 + k + tok, cols] * same[k])
            small[k : k + 1, small_cols] = jnp.sum(value, axis=0, keepdims=True)
        out[:, cols] = total

    @pl.loop(0, pairs)
    def _(n):
        back(pad_x, pre_x, params_c, dx_both.at[own_rows], 0, n)

    give_dx = links.remote(dx_both.at[own_rows], dx_both.at[own_rows], place.sibling())

    @pl.loop(0, 2 * N // 128)
    def _(n):
        back(pad_s, pre_s, params_s, d_bc, inner, n)

    share = 2 * N // place.tp
    bc_rows[...] = d_bc[...].T

    def share_of(turn):
        return pl.ds(pl.multiple_of(turn * share, 8), share)

    give_bc = [
        links.remote(bc_rows.at[share_of(to_z)], bc_recv.at[k], device) for k, (device, to_z, _) in enumerate(column)
    ]

    hops_of = [
        [place.sibling()],
        [place.at(0, d) for d in range(1, place.side)],
        [place.at(d, 0) for d in range(1, place.side)],
    ]
    small_copies = []

    def hop_small(step):
        slot = sum(len(devices) for devices in hops_of[:step])
        for device in hops_of[step]:
            small_copies.append(links.remote(small, small_recv.at[slot], device))
            slot += 1

    def land_small(step):
        slot = sum(len(devices) for devices in hops_of[:step])
        total = small[...]
        links.settle(small_copies[slot:])
        for copy in small_copies[slot:]:
            copy.wait_recv()
            total = total + small_recv[slot]
            slot += 1
        small[...] = total

    hop_small(0)
    give_dx.wait_recv()
    loads["n_pairs"].wait()
    sum_x = Scatter(place, links, blocks_x, blocks_x, (x1a, x1b), (x2a, x2b))
    halve(dx_both, high, low)
    for hop in sum_x.order():
        block = place.chip(*hop)
        weight_block(n_pairs.at[block], high, low, left_high, left_low, blocks_x.at[block])
        sum_x.send(*hop)
    loads["gz"].wait()
    sum_z.pass_on()
    land_small(0)
    hop_small(1)

    for k, turn in enumerate(turns):
        product(place.tp + k, turn, True, part_t.at[turn])
    loads["dz"].wait()
    halve(conv_x, high.at[own_rows], low.at[own_rows])
    loads["tokens"].wait()
    loads["ws"].wait()
    for copy in give_bc:
        copy.wait_recv()
    summed = bc_rows[share_of(place.z), :]
    for k in range(place.tp - 1):
        summed = summed + bc_recv[k]
    own_cols = pl.ds(pl.multiple_of(place.c * tok, 128), tok)
    ds_both[0:heads, own_cols] = d_raw.T[0:heads, :]
    ds_both[heads : heads + share, own_cols] = summed
    side_rows = ds_both.shape[0]
    if side_rows > heads + share:
        ds_both[heads + share :, own_cols] = jnp.zeros((side_rows - heads - share, tok), F32)
    give_ds = links.remote(ds_both.at[:, own_cols], ds_both.at[:, own_cols], place.sibling())
    ds_high[...], ds_low[...] = split2(ds_both[:, own_cols].T)
    give_ds.wait_recv()
    sum_s = Scatter(place, links, blocks_s, blocks_s, (s1a, s1b), (s2a, s2b))
    ds_parts = split2(ds_both[...])
    for hop in sum_s.order():
        block = place.chip(*hop)
        sum_s.blocks[block] = dot_split(ds_parts, split2(n_pairs[block]), NT)
        sum_s.send(*hop)
    row_sum = jnp.zeros((tok, 1), F32)
    squares = jnp.zeros((tok, 1), F32)
    for k, turn in enumerate(turns):
        out = part_t.at[turn]
        product(2 * place.tp + k, turn, False, out)
        shard_rows = ws.shape[1]
        for j in range(part // shard_rows):
            at = pl.ds(pl.multiple_of((turn * (part // shard_rows) + j) * side_rows, 8), side_rows)
            cols = slice(j * shard_rows, (j + 1) * shard_rows)
            out[:, cols] = out[:, cols] + dot_split((ds_high[...], ds_low[...]), split2(ws[at, :]), NN)
        shares_t.send(k)
        value = tokens[turn]
        row_sum = row_sum + jnp.sum(out[...] * gain[turn] * value, axis=1, keepdims=True)
        squares = squares + jnp.sum(value * value, axis=1, keepdims=True)
    row_sums[...] = jnp.where(lanes == 0, row_sum, 0.0).T[0:8, :]
    give_rows = [links.remote(row_sums, row_recv.at[k], device) for k, (device, _, _) in enumerate(column)]

    land_small(1)
    hop_small(2)
    stores = [links.move(sum_o.finish(), grad_out)]

    settle = settling(p_recv, tok)

    def rows(group):
        return pl.ds(pl.multiple_of(group * per_pair, 8), per_pair)

    def homeward(value, home, back_ref):
        home[...] = pick(settle, value, NN)
        at = rows(place.f * 2 + place.c)
        copies = [links.remote(home.at[rows(to)], back_ref.at[at], device) for device, to, _ in plane]
        return copies + [links.move(home.at[at], back_ref.at[at])]

    shares_r.finish()
    value = tokens[place.z] + part_r[place.z]
    way_r = homeward(value, home_r, back_r)

    shares_t.forward()
    sum_s.pass_on()
    sum_x.pass_on()
    stores.append(links.move(sum_z.finish(), grad_z))

    land_small(2)
    bc_cols = pl.ds(inner, 2 * N)
    give_small = [links.remote(small.at[:, bc_cols], small_z.at[j], device) for j, (device, _, _) in enumerate(column)]
    last = sum_s.finish()
    give_grad = [
        links.remote(last.at[pl.ds(heads, share)], bc_grad.at[share_of(place.z)], device) for device, _, _ in column
    ]
    bc_grad[share_of(place.z), :] = last[heads : heads + share, :]
    grad_dt[...] = last[0:heads, :]
    stores.append(links.move(grad_dt, grad_dt_hbm))
    for copy in give_rows:
        copy.wait_recv()
    total = row_sums[...]
    for k in range(place.tp - 1):
        total = total + row_recv[k]
    shares_t.finish()
    d_normed = part_t[place.z]
    row_sum = jnp.concatenate([total, jnp.zeros((120, tok), F32)], axis=0).T[:, 0:1]
    width = place.tp * part
    scale = lax.rsqrt(squares / width + EPSILON)
    scaled = tokens[place.z] * scale
    gain_own[...] = jnp.sum(d_normed * scaled, axis=0, keepdims=True)
    give_gain = [links.remote(gain_own, gain_recv.at[j], device) for j, (device, _, _) in enumerate(plane)]
    loads["up"].wait()
    value = home_t[...] + scale * gain[place.z] * d_normed - scaled * (scale * scale * row_sum / width)
    way_t = homeward(value, home_t, back_t)

    stores.append(links.move(sum_x.finish(), grad_x))
    leave, _ = leaving(slots_in[...], tok, groups)
    for way, home, back_ref, out in ((way_r, home_r, back_r, result), (way_t, home_t, back_t, grad_input)):
        for copy in way[:-1]:
            copy.wait_recv()
        way[-1].wait()
        links.settle(way[:-1])
        home[...] = pick(leave, back_ref[...], NN)
        stores.append(links.move(home, out))
    total = gain_own[...]
    for j, copy in enumerate(give_gain):
        copy.wait_recv()
        total = total + gain_recv[j]
    gain_out[...] = total
    stores.append(links.move(gain_out, gain_out_hbm))
    for copy in give_small:
        copy.wait_recv()
    small_out[...] = small[...]
    over_tp = small[0:5, inner : inner + 2 * N]
    for k in range(place.tp - 1):
        over_tp = over_tp + small_z[k, 0:5, :]
    small_out[0:5, inner : inner + 2 * N] = over_tp
    stores.append(links.move(small_out, small_out_hbm))
    for copy in give_grad:
        copy.wait_recv()
    grad_bc[...] = bc_grad[...].T
    stores.append(links.move(grad_bc, grad_bc_hbm))
    for store in stores:
        store.wait()
    links.finish()


ANYWHERE = pl.BlockSpec(memory_space=pl.ANY)
INSIDE = pl.BlockSpec(memory_space=pltpu.VMEM)
SCALARS = pl.BlockSpec(memory_space=pltpu.SMEM)


def shape(*dims):
    return jax.ShapeDtypeStruct(dims, F32)


def floats(*dims):
    return pltpu.VMEM(dims, F32)


def halves(*dims):
    return pltpu.VMEM(dims, BF16)


def side_height(heads, tp):
    return -(-(heads + 2 * N // tp) // 16) * 16


def forward_call(sizes, operands, heads):
    fsdp, _, tp = sizes
    inputs, w_x = operands[13], operands[15]
    tok, width = inputs.shape
    shard, inner = w_x.shape
    depth = shard * 2 * fsdp
    part = width // tp
    side = side_height(heads, tp)
    copies = 4 * gather_copies(math.isqrt(fsdp)) + 3 * (2 * fsdp - 1) + 8 * tp + 4 * fsdp + 8
    grid = math.isqrt(fsdp)
    landing = (grid - 1, grid, shard // 2, inner)
    outs = [
        (shape(8, inner), ANYWHERE),
        (shape(8, 2 * N), ANYWHERE),
        (shape(tp, tok, part), ANYWHERE),
        (shape(tok, part), ANYWHERE),
        (shape(fsdp, shard, 2 * tok), ANYWHERE),
        (shape(tok, 128), ANYWHERE),
        (shape(8 + tok, inner), ANYWHERE),
        (shape(8 + tok, 2 * N), ANYWHERE),
        (shape(tok, 128), ANYWHERE),
        (shape(tok, inner), ANYWHERE),
        (shape(tok, 2 * N), ANYWHERE),
        (shape(tok, inner), ANYWHERE),
        (shape(tok, inner), ANYWHERE),
        (shape(tok, inner), ANYWHERE),
        (shape(1, inner), ANYWHERE),
        (shape(inner, N), ANYWHERE),
        (shape(fsdp, shard, inner), ANYWHERE),
        (shape(fsdp, shard, inner), ANYWHERE),
        (shape(*landing), ANYWHERE),
        (shape(*landing), ANYWHERE),
        (shape(depth, inner), ANYWHERE),
        (shape(2 * fsdp * side, shard), ANYWHERE),
        (shape(depth, inner), ANYWHERE),
        (shape(depth, inner), ANYWHERE),
    ]
    return pl.pallas_call(
        functools.partial(forward_kernel, sizes),
        out_shape=tuple(out for out, _ in outs),
        in_specs=[SCALARS] + [ANYWHERE] * 17,
        out_specs=tuple(spec for _, spec in outs),
        scratch_shapes=[
            pltpu.VMEM((1, tok), jnp.int32),
            *[floats(*operand.shape) for operand in operands[2:13]],
            floats(8, inner),
            floats(8, 2 * N),
            floats(tok, 128),
            floats(1, inner),
            floats(depth, inner),
            floats(2 * fsdp * side, shard),
            floats(depth, inner),
            floats(depth, inner),
            floats(side, shard),
            floats(tok, part),
            floats(tok, part),
            floats(tok, part),
            floats(tok, part),
            floats(2 * fsdp, 8, 128),
            floats(2 * fsdp, 8, 128),
            floats(tp, tok, part),
            floats(tp, tok, part),
            floats(tp, tok, part),
            halves(fsdp, tok, 2 * shard),
            halves(fsdp, tok, 2 * shard),
            floats(width, tok),
            floats(fsdp, shard, 2 * tok),
            floats(fsdp, shard, 2 * tok),
            floats(8 + tok, inner),
            floats(8 + tok, 2 * N),
            floats(tok, 128),
            floats(2 * N, max(tok, shard)),
            floats(8, inner),
            floats(8, 2 * N),
            floats(tok, inner),
            floats(tok, 2 * N),
            floats(tok, inner),
            floats(tok, 2 * N),
            floats(tok, 128),
            floats(2, 128, tok),
            floats(tok, tok),
            floats(tok, tok),
            floats(inner, N),
            floats(inner, N),
            floats(tok, inner),
            floats(tok, inner),
            floats(tok, inner),
            floats(2 * tok, inner),
            halves(2 * tok, inner),
            halves(2 * tok, inner),
            halves(shard, 2 * tok),
            halves(shard, 2 * tok),
            floats(8, tok),
            floats(tp - 1, 8, tok),
            floats(8, tok),
            floats(tp - 1, 8, tok),
            pltpu.SemaphoreType.DMA((copies,)),
            pltpu.SemaphoreType.DMA((copies,)),
            pltpu.SemaphoreType.DMA((64 + 4 * fsdp,)),
        ],
        compiler_params=pltpu.CompilerParams(collective_id=0, has_side_effects=True, vmem_limit_bytes=VMEM_LIMIT),
        name="forward",
    )(*operands)


def backward_call(sizes, heads, operands, tok, width, shard, inner):
    fsdp, _, tp = sizes
    grid = math.isqrt(fsdp)
    part = width // tp
    share = 2 * N // tp
    side = side_height(heads, tp)
    hops = grid - 1
    copies = 4 + 4 * (2 * hops * grid + 2 * hops) + 9 * tp + 3 * (2 * fsdp) + 2 * hops + 4

    def landing(rows, columns):
        return [
            floats(hops, grid, rows // 2, columns),
            floats(hops, grid, rows // 2, columns),
            floats(hops, rows // 2, columns),
            floats(hops, rows // 2, columns),
        ]

    return pl.pallas_call(
        functools.partial(backward_kernel, sizes, heads),
        out_shape=(
            shape(tok, part),
            shape(tok, part),
            shape(shard, inner),
            shape(shard, inner),
            shape(shard, 2 * N),
            shape(heads, shard),
            shape(shard, inner),
            shape(8, inner + 2 * N),
            shape(1, part),
        ),
        in_specs=[SCALARS] + [ANYWHERE] * 26,
        out_specs=(ANYWHERE,) * 9,
        scratch_shapes=[
            pltpu.VMEM((1, tok), jnp.int32),
            *[floats(*operand.shape) for operand in operands[2:7]],
            floats(shard, 2 * N),
            floats(heads, shard),
            floats(8, inner + 2 * N),
            floats(1, part),
            floats(tp, tok, part),
            floats(fsdp, shard, 2 * tok),
            floats(8 + tok, inner),
            floats(8 + tok, 2 * N),
            floats(tok, 128),
            floats(tok, inner),
            floats(tok, 2 * N),
            floats(inner, N),
            floats(2 * tok, inner),
            floats(side, 2 * tok),
            halves(2 * tok, inner),
            halves(2 * tok, inner),
            halves(shard, 2 * tok),
            halves(shard, 2 * tok),
            floats(fsdp, shard, inner),
            floats(fsdp, shard, inner),
            floats(fsdp, side, shard),
            *landing(shard, inner),
            *landing(shard, inner),
            *landing(shard, inner),
            *landing(side, shard),
            floats(fsdp, shard, inner),
            floats(2, part, inner),
            floats(2 * fsdp * side, shard),
            floats(tok, 2 * N),
            halves(tok, side),
            halves(tok, side),
            floats(2 * N, tok),
            floats(tp - 1, share, tok),
            floats(2 * N, shard),
            floats(tp, tok, part),
            floats(tp, tok, part),
            floats(max(4, tp - 1), tok, part),
            floats(max(4, tp - 1), tok, part),
            floats(8, tok),
            floats(tp - 1, 8, tok),
            floats(tok, part),
            floats(tok, part),
            floats(tok, part),
            floats(tok, part),
            floats(inner, N),
            floats(inner, N),
            floats(tok, N),
            floats(tok, N),
            floats(8 + tok, inner),
            floats(8 + tok, 2 * N),
            floats(8, inner),
            floats(8, 2 * N),
            floats(tok, tok),
            floats(tok, tok),
            floats(tok, tok),
            floats(tok, 128),
            floats(tok, 128),
            floats(128, tok),
            floats(tok, 128),
            floats(tok, 128),
            floats(tok, 128),
            floats(128, tok),
            floats(1, inner),
            floats(8, inner + 2 * N),
            floats(1 + 2 * hops, 8, inner + 2 * N),
            floats(tp - 1, 8, 2 * N),
            floats(1, part),
            floats(2 * fsdp - 1, 1, part),
            pltpu.SemaphoreType.DMA((copies,)),
            pltpu.SemaphoreType.DMA((copies,)),
            pltpu.SemaphoreType.DMA((40 + 3 * tp,)),
        ],
        compiler_params=pltpu.CompilerParams(collective_id=1, has_side_effects=True, vmem_limit_bytes=VMEM_LIMIT),
        name="backward",
    )(*operands)


def last_kernel(heads, small, gain, dt, *refs):
    large, outs, held, sems = refs[:6], refs[6:22], refs[22:28], refs[28]
    loads, stores = [], []
    for k, (src, hold, dst) in enumerate(zip(large, held, outs)):
        loads.append(pltpu.make_async_copy(src, hold, sems.at[0, k]))
        stores.append(pltpu.make_async_copy(hold, dst, sems.at[1, k]))
    for load in loads:
        load.start()
    for load, store in zip(loads, stores):
        load.wait()
        store.start()
    grad_dt, taps_x, bias_x, taps_s, bias_s, dt_bias, a_log, d_skip, gate_gain, gain_in = outs[6:]
    inner = taps_x.shape[1]
    grad_dt[...] = dt[...]
    taps_x[...] = small[0:4, 0:inner]
    bias_x[...] = small[4:5, 0:inner]
    taps_s[...] = small[0:4, inner : inner + 2 * N]
    bias_s[...] = small[4:5, inner : inner + 2 * N]
    dt_bias[...] = small[5:6, inner : inner + heads]
    a_log[...] = small[6:7, inner : inner + heads]
    d_skip[...] = small[7:8, inner : inner + heads]
    gate_gain[...] = small[5:6, 0:inner]
    gain_in[...] = gain[...]
    for store in stores:
        store.wait()


def last_call(heads, small, gain, dt, *large):
    inner, part = small.shape[1] - 2 * N, gain.shape[1]
    few = [
        dt.shape,
        (4, inner),
        (1, inner),
        (4, 2 * N),
        (1, 2 * N),
        (1, heads),
        (1, heads),
        (1, heads),
        (1, inner),
        (1, part),
    ]
    return pl.pallas_call(
        functools.partial(last_kernel, heads),
        out_shape=tuple([shape(*value.shape) for value in large] + [shape(*dims) for dims in few]),
        in_specs=[INSIDE] * 3 + [ANYWHERE] * 6,
        out_specs=tuple([ANYWHERE] * 6 + [INSIDE] * len(few)),
        scratch_shapes=[floats(*value.shape) for value in large] + [pltpu.SemaphoreType.DMA((2, 6))],
        compiler_params=pltpu.CompilerParams(vmem_limit_bytes=VMEM_LIMIT),
        name="results",
    )(small, gain, dt, *large)


def shards(
    inputs,
    cotangent,
    seq_lengths,
    slots,
    gain_in,
    w_z,
    w_x,
    w_dt,
    w_bc,
    w_out,
    conv_x,
    conv_x_bias,
    conv_bc,
    conv_bc_bias,
    dt_bias,
    a_log,
    d_skip,
    gate_gain,
):
    sizes = (lax.axis_size("fsdp"), lax.axis_size("ctx"), lax.axis_size("tp"))
    tok, width = inputs.shape
    shard, inner = w_x.shape
    heads = w_dt.shape[1]
    tp = sizes[2]
    operands = (
        seq_lengths,
        slots[None],
        gain_in[None],
        conv_x,
        conv_x_bias[None],
        conv_bc,
        conv_bc_bias[None],
        dt_bias[None],
        a_log[None],
        d_skip[None],
        gate_gain[None],
        w_bc,
        w_dt.T,
        inputs,
        cotangent,
        w_x,
        w_z,
        w_out,
    )
    params_c, params_s, tokens, up, n_pairs, p_recv, *kept = forward_call(sizes, operands, heads)
    pre_x, pre_s, raw, conv_x_kept, conv_s_kept, normal_y, d_gate, d_mixed, gain_row, *rest = kept
    operands = (
        seq_lengths,
        slots[None],
        p_recv,
        gain_in.reshape(tp, 1, width // tp),
        params_c,
        params_s,
        gain_row,
        tokens,
        up,
        n_pairs,
        pre_x,
        pre_s,
        raw,
        conv_x_kept,
        conv_s_kept,
        normal_y,
        d_gate,
        d_mixed,
        *rest,
    )
    result, grad_input, grad_z, grad_x, grad_bc, grad_dt, grad_out, small, gain = backward_call(
        sizes, heads, operands, tok, width, shard, inner
    )
    outs = last_call(heads, small, gain, grad_dt, result, grad_input, grad_z, grad_x, grad_out, grad_bc)
    result, grad_input, grad_z, grad_x, grad_out, grad_bc, grad_dt, taps_x, bias_x, taps_s, bias_s, *few = outs
    return (
        result,
        grad_input,
        grad_z,
        grad_x,
        grad_dt.T,
        grad_bc,
        grad_out,
        taps_x,
        bias_x[0],
        taps_s,
        bias_s[0],
        *[value[0] for value in few],
    )


def solution(mesh):
    return jax.shard_map(
        shards,
        mesh=mesh,
        in_specs=(
            P(("fsdp", "ctx"), None),
            P(("fsdp", "ctx"), None),
            P("fsdp", None),
            P(("fsdp", "ctx")),
            P(),
            P(("fsdp", "ctx"), "tp"),
            P(("fsdp", "ctx"), "tp"),
            P(("fsdp", "ctx"), "tp"),
            P(("fsdp", "ctx"), None),
            P(("fsdp", "ctx"), "tp"),
            P(None, "tp"),
            P("tp"),
            P(),
            P(),
            P("tp"),
            P("tp"),
            P("tp"),
            P("tp"),
        ),
        out_specs=(
            P(("fsdp", "ctx"), "tp"),
            P(("fsdp", "ctx"), "tp"),
            P(("fsdp", "ctx"), "tp"),
            P(("fsdp", "ctx"), "tp"),
            P(("fsdp", "ctx"), "tp"),
            P(("fsdp", "ctx"), None),
            P(("fsdp", "ctx"), "tp"),
            P(None, "tp"),
            P("tp"),
            P(),
            P(),
            P("tp"),
            P("tp"),
            P("tp"),
            P("tp"),
            P("tp"),
        ),
        check_vma=False,
    )
```

```python
import functools
import math

import jax
import jax.numpy as jnp
from jax import lax
from jax.experimental import pallas as pl
from jax.experimental.pallas import tpu as pltpu
from jax.sharding import PartitionSpec as P

N = 128
SPAN = 256
INNER = 4096
EPSILON = 1e-05
F32 = jnp.float32
BF16 = jnp.bfloat16
MESH = pl.DeviceIdType.MESH
NN = (((1,), (0,)), ((), ()))
NT = (((1,), (1,)), ((), ()))
TN = (((0,), (0,)), ((), ()))
VMEM_LIMIT = 62 << 20


def split2(value):
    high = value.astype(BF16)
    return high, (value - high.astype(F32)).astype(BF16)


def split3(value):
    high = value.astype(BF16)
    rest = value - high.astype(F32)
    middle = rest.astype(BF16)
    return high, middle, (rest - middle.astype(F32)).astype(BF16)


def dot1(left, right, dims):
    return lax.dot_general(left, right, dims, preferred_element_type=F32)


def dot_split(left, right, dims):
    (lh, ll), (rh, rl) = left, right
    return dot1(lh, rh, dims) + (dot1(lh, rl, dims) + dot1(ll, rh, dims))


def dot3(left, right, dims):
    return dot_split(split2(left), split2(right), dims)


def pick(table, value, dims):
    parts = split3(value)
    return dot1(table, parts[0], dims) + dot1(table, parts[1], dims) + dot1(table, parts[2], dims)


def iota(shape, dim):
    return lax.broadcasted_iota(jnp.int32, shape, dim)


class Place:
    def __init__(self, fsdp, ctx, tp):
        self.fsdp, self.n_ctx, self.tp = fsdp, ctx, tp
        self.side = math.isqrt(fsdp)
        assert self.side * self.side == fsdp and ctx == 2
        self.f = lax.axis_index("fsdp")
        self.c = lax.axis_index("ctx")
        self.z = lax.axis_index("tp")
        self.y, self.x = self.f // self.side, self.f % self.side

    def chip(self, dy, dx):
        side = self.side
        return ((self.y + dy + side) % side) * side + (self.x + dx + side) % side

    def block(self, dy, dx, core):
        return self.chip(dy, dx) * 2 + core

    def at(self, dy, dx):
        return (self.chip(dy, dx), self.c, self.z)

    def sibling(self):
        return (self.f, 1 - self.c, self.z)

    def plane(self):
        out = []
        for df in range(self.fsdp):
            for dc in range(2):
                if df or dc:
                    to_f = (self.f + df) % self.fsdp
                    from_f = (self.f - df + self.fsdp) % self.fsdp
                    core = (self.c + dc) % 2
                    out.append(((to_f, core, self.z), to_f * 2 + core, from_f * 2 + core))
        return out

    def column(self):
        out = []
        for dz in range(1, self.tp):
            to_z = (self.z + dz) % self.tp
            out.append(((self.f, self.c, to_z), to_z, (self.z - dz + self.tp) % self.tp))
        return out


class Links:
    def __init__(self, send, recv, local):
        self.send, self.recv, self.local = send, recv, local
        self.used, self.used_local = 0, 0
        self.open = []

    def remote(self, src, dst, device):
        k = self.used
        self.used += 1
        copy = pltpu.make_async_remote_copy(
            src_ref=src,
            dst_ref=dst,
            send_sem=self.send.at[k],
            recv_sem=self.recv.at[k],
            device_id=device,
            device_id_type=MESH,
        )
        copy.start()
        self.open.append(copy)
        return copy

    def plan(self, src, dst, device, lands_as=None):
        k = self.used
        self.used += 1
        copy = pltpu.make_async_remote_copy(
            src_ref=src,
            dst_ref=dst,
            send_sem=self.send.at[k],
            recv_sem=self.recv.at[k if lands_as is None else lands_as.slot],
            device_id=device,
            device_id_type=MESH,
        )
        copy.slot = k
        return copy

    def move(self, src, dst):
        k = self.used_local
        self.used_local += 1
        copy = pltpu.make_async_copy(src, dst, self.local.at[k])
        copy.start()
        return copy

    def settle(self, copies):
        for copy in copies:
            copy.wait_send()
            self.open = [other for other in self.open if other is not copy]

    def finish(self):
        assert self.used <= self.send.shape[0] and self.used_local <= self.local.shape[0]
        self.settle(list(self.open))


def greet(devices):
    barrier = pltpu.get_barrier_semaphore()
    for device in devices:
        pl.semaphore_signal(barrier, inc=1, device_id=device, device_id_type=MESH)


def greeted(devices):
    pl.semaphore_wait(pltpu.get_barrier_semaphore(), len(devices))


class Spread:
    def __init__(self, place, links, slices):
        self.place, self.links, self.slices = place, links, slices
        self.line = place.tp == 4
        z, mine = place.z, slices.at[place.z]
        if not self.line:
            self.copies = [links.remote(mine, mine, device) for device, _, _ in place.column()]
            return
        self.copies = [links.remote(mine, mine, (place.f, place.c, z ^ d)) for d in (1, 2)]
        self.inner = (z == 1) | (z == 2)
        across = links.plan(mine, mine, (place.f, place.c, 3 - z))
        onward = slices.at[z ^ 2]
        self.onward = links.plan(onward, onward, (place.f, place.c, z ^ 1), across)
        self.across = across

        @pl.when(self.inner)
        def _():
            across.start()

    def forward(self):
        if self.line:
            self.copies.pop().wait_recv()

            @pl.when(self.inner)
            def _():
                self.onward.start()

    def finish(self):
        for copy in self.copies:
            copy.wait_recv()
        if self.line:
            self.across.wait_recv()

            @pl.when(self.inner)
            def _():
                self.across.wait_send()
                self.onward.wait_send()


class Gather:
    def __init__(self, place, links, shard, whole):
        self.place, self.links, self.shard, self.whole = place, links, shard, whole
        self.rows = shard.shape[0]
        self.near = 0

    def rows_of(self, block, start=0, count=None):
        count = self.rows if count is None else count
        return self.whole.at[pl.ds(pl.multiple_of(block * self.rows + start, 8), count)]

    def part(self, block, half):
        return self.rows_of(block, half * (self.rows // 2), self.rows // 2)

    def start(self):
        p, steps = self.place, range(1, self.place.side)
        me = p.block(0, 0, p.c)
        self.row, self.col = [[], []], [[], []]
        for turn in range(2):
            for d in steps:
                shard = self.shard.at[pl.ds(turn * (self.rows // 2), self.rows // 2)]
                self.row[turn].append(self.links.remote(shard, self.part(me, turn), p.at(0, d)))
                shard = self.shard.at[pl.ds((1 - turn) * (self.rows // 2), self.rows // 2)]
                self.col[turn].append(self.links.remote(shard, self.part(me, 1 - turn), p.at(d, 0)))
        mine = self.rows_of(me)
        self.pair = [self.links.remote(self.shard, mine, p.sibling())]
        self.own = self.links.move(self.shard, mine)

    def forward(self):
        p, steps = self.place, range(1, self.place.side)
        self.half_a, self.half_b = [], []
        for k, d in enumerate(steps):
            self.row[0][k].wait_recv()
            part = self.part(p.block(0, -d, p.c), 0)
            self.half_a += [self.links.remote(part, part, p.at(e, 0)) for e in steps]
        for k, e in enumerate(steps):
            self.col[0][k].wait_recv()
            part = self.part(p.block(-e, 0, p.c), 1)
            self.half_b += [self.links.remote(part, part, p.at(0, d)) for d in steps]
        for k, d in enumerate(steps):
            self.row[1][k].wait_recv()
            whole = self.rows_of(p.block(0, -d, p.c))
            self.pair.append(self.links.remote(whole, whole, p.sibling()))
        for k, e in enumerate(steps):
            self.col[1][k].wait_recv()
            whole = self.rows_of(p.block(-e, 0, p.c))
            self.pair.append(self.links.remote(whole, whole, p.sibling()))

    def share(self):
        p, steps, half = self.place, range(1, self.place.side), self.rows // 2
        k = 0
        for d in steps:
            for e in steps:
                self.half_a[k].wait_recv()
                part = self.rows_of(p.block(-e, -d, p.c), 0, half)
                self.pair.append(self.links.remote(part, part, p.sibling()))
                k += 1
        k = 0
        for e in steps:
            for d in steps:
                self.half_b[k].wait_recv()
                part = self.rows_of(p.block(-e, -d, p.c), half, half)
                self.pair.append(self.links.remote(part, part, p.sibling()))
                k += 1

    def finish_near(self):
        self.own.wait()
        self.near = 1 + 2 * (self.place.side - 1)
        for copy in self.pair[: self.near]:
            copy.wait_recv()

    def finish(self):
        if self.near == 0:
            self.finish_near()
        for copy in self.pair[self.near :]:
            copy.wait_recv()


def gather_copies(side):
    steps = side - 1
    return 6 * steps + 1 + 4 * steps * steps


def down_lanes(row):
    return jnp.broadcast_to(row, (128, row.shape[1])).T


def leaving(slots, tok, groups):
    slots = down_lanes(slots.astype(F32)).astype(jnp.int32)
    targets = slots >> (tok.bit_length() - 1)
    lanes = iota((tok, 128), 1)
    member = (targets == lanes).astype(F32)
    earlier = (iota((tok, tok), 0) > iota((tok, tok), 1)).astype(BF16)
    ranks = jnp.sum(dot1(earlier, member.astype(BF16), NN) * member, axis=1, keepdims=True)
    send_at = (targets[:, :1] * (tok // groups)).astype(F32) + ranks
    leave = (send_at == iota((tok, tok), 1).astype(F32)).astype(BF16)
    places = jnp.where(ranks == lanes.astype(F32), (slots - targets * tok).astype(F32), 0.0)
    return leave, dot1(member.astype(BF16), places.astype(BF16), TN)


def arrived(rows, tok, per_pair):
    groups = rows.shape[0]
    rows = jnp.concatenate([rows, jnp.zeros((128 - groups, 128), F32)], axis=0)
    token, lanes = iota((tok, 128), 0), iota((tok, 128), 1)
    spread = dot1((token // per_pair == lanes).astype(BF16), rows.astype(BF16), NN)
    place = jnp.sum(jnp.where(token % per_pair == lanes, spread, 0.0), axis=1, keepdims=True)
    return jnp.broadcast_to(place, (tok, 128))


def settling(places, tok):
    return (places[:, :1] == iota((tok, tok), 1).astype(F32)).astype(BF16)


def halve(value_ref, high, low):
    @pl.loop(0, value_ref.shape[1] // 128)
    def _(n):
        cols = pl.ds(pl.multiple_of(n * 128, 128), 128)
        high[:, cols], low[:, cols] = split2(value_ref[:, cols])


def project(left_high, left_low, whole, chips, out, tile, first_row, fresh):
    _, rows, width = left_high.shape

    @pl.loop(0, whole.shape[1] // tile)
    def _(n):
        cols = pl.ds(pl.multiple_of(n * tile, 128), tile)
        total = jnp.zeros((rows, tile), F32) if fresh else out[first_row : first_row + rows, cols]
        for chip in chips:
            at = pl.ds(chip * width if isinstance(chip, int) else pl.multiple_of(chip * width, 8), width)
            total = total + dot_split((left_high[chip], left_low[chip]), split2(whole[at, cols]), NN)
        out[first_row : first_row + rows, cols] = total


def weight_block(left_ref, high, low, left_high, left_low, out):
    left_high[...], left_low[...] = split2(left_ref[...])

    @pl.loop(0, high.shape[1] // 512)
    def _(n):
        cols = pl.ds(pl.multiple_of(n * 512, 128), 512)
        out[:, cols] = dot_split((left_high[...], left_low[...]), (high[:, cols], low[:, cols]), NN)


def times_rows(high, low, rows_ref, out, fresh):
    tile = min(256, rows_ref.shape[0])
    for n in range(rows_ref.shape[0] // tile):
        at = slice(n * tile, (n + 1) * tile)
        value = dot_split((high[...], low[...]), split2(rows_ref[at, :]), NT)
        out[:, at] = value if fresh else out[:, at] + value


class Scatter:
    def __init__(self, place, links, source, blocks, first, second=None):
        self.place, self.links, self.blocks = place, links, blocks
        self.first, self.second = first, second
        self.half = source.shape[1] // 2
        self.source = source
        self.copies_a, self.copies_b = {}, {}

    def order(self):
        side = self.place.side
        hops = [(dy, dx) for dy in range(side) for dx in range(side)]
        return sorted(hops, key=lambda hop: -(hop[0] > 0) - (hop[1] > 0))

    def halves(self, dy, dx, blocks=None):
        ref = (self.blocks if blocks is None else blocks).at[self.place.chip(dy, dx)]
        return ref.at[pl.ds(0, self.half)], ref.at[pl.ds(self.half, self.half)]

    def send(self, dy, dx):
        p, side = self.place, self.place.side
        upper, lower = self.halves(dy, dx, self.source)
        if dy:
            target = self.first[0].at[dy - 1, (p.x + dx) % side]
            self.copies_a[dy, dx] = self.links.remote(upper, target, p.at(dy, 0))
        if dx:
            target = self.first[1].at[dx - 1, (p.y + dy) % side]
            self.copies_b[dy, dx] = self.links.remote(lower, target, p.at(0, dx))

    def send_all(self):
        for hop in self.order():
            self.send(*hop)

    def land(self):
        for copy in [*self.copies_a.values(), *self.copies_b.values()]:
            copy.wait_recv()

    def pass_on(self):
        p, side = self.place, self.place.side
        self.last_a, self.last_b = [], []
        for d in list(range(1, side)) + [0]:
            upper, _ = self.halves(0, d)
            total = upper[...]
            for e in range(1, side):
                if (e, d) in self.copies_a:
                    self.copies_a[e, d].wait_recv()
                total = total + self.first[0][e - 1, (p.x + d) % side]
            upper[...] = total
            if d:
                self.last_a.append(self.links.remote(upper, self.second[0].at[d - 1], p.at(0, d)))
            _, lower = self.halves(d, 0)
            total = lower[...]
            for e in range(1, side):
                if (d, e) in self.copies_b:
                    self.copies_b[d, e].wait_recv()
                total = total + self.first[1][e - 1, (p.y + d) % side]
            lower[...] = total
            if d:
                self.last_b.append(self.links.remote(lower, self.second[1].at[d - 1], p.at(d, 0)))

    def finish(self):
        for k, (copies, part) in enumerate(zip((self.last_a, self.last_b), self.halves(0, 0))):
            total = part[...]
            for d, copy in enumerate(copies):
                copy.wait_recv()
                total = total + self.second[k][d]
            part[...] = total
        return self.blocks.at[self.place.chip(0, 0)]


class Shares:
    def __init__(self, place, links, parts, landing):
        self.place, self.links, self.parts, self.landing = place, links, parts, landing
        self.line = place.tp == 4
        z = place.z
        self.copies = []
        if self.line:
            self.turns = [z ^ 3, z ^ 2, z ^ 1, z]
            self.inner = (z == 1) | (z == 2)
        else:
            self.turns = [(z + d + 1) % place.tp for d in range(place.tp)]

    def send(self, k):
        place, z = self.place, self.place.z
        if k == place.tp - 1:
            return
        part = self.parts.at[self.turns[k]]
        if not self.line:
            self.copies.append(self.links.remote(part, self.landing.at[k], (place.f, place.c, self.turns[k])))
            return
        if k == 0:
            self.direct = self.links.plan(part, self.landing.at[2], (place.f, place.c, z ^ 3))
            self.extra = self.links.plan(part, self.landing.at[3], (place.f, place.c, z ^ 1))

            @pl.when(self.inner)
            def _():
                self.direct.start()

            @pl.when(jnp.logical_not(self.inner))
            def _():
                self.extra.start()

        elif k == 1:
            self.across = self.links.plan(part, self.landing.at[1], (place.f, place.c, z ^ 2))

            @pl.when(jnp.logical_not(self.inner))
            def _():
                self.across.start()

        else:
            self.copies.append(self.links.remote(part, self.landing.at[0], (place.f, place.c, z ^ 1)))

    def forward(self):
        if self.line:

            @pl.when(self.inner)
            def _():
                self.extra.wait_recv()
                part = self.parts.at[self.place.z ^ 2]
                part[...] = part[...] + self.landing[3]
                self.across.start()

    def finish(self):
        own = self.parts.at[self.place.z]
        total = own[...]
        for k, copy in enumerate(self.copies):
            copy.wait_recv()
            total = total + self.landing[k]
        if self.line:
            self.across.wait_recv()
            total = total + self.landing[1]
            self.across.wait_send()
        own[...] = total
        if self.line:

            @pl.when(self.inner)
            def _():
                self.direct.wait()
                own[...] = own[...] + self.landing[2]

            @pl.when(jnp.logical_not(self.inner))
            def _():
                self.extra.wait_send()


def silu_slope(value):
    gate = jax.nn.sigmoid(value)
    return gate * (1.0 + value * (1.0 - gate))


def softplus(value):
    return jnp.maximum(value, 0.0) + jnp.log1p(jnp.exp(-jnp.abs(value)))


def segments(lengths, position):
    bound, seg = 0, jnp.zeros_like(position)
    for k in range(lengths.shape[1]):
        bound = bound + lengths[0, k]
        seg = seg + (bound <= position).astype(jnp.int32)
    return seg


def same_before(lengths, first, tok, distance):
    position = first + iota((tok, 128), 0)
    return (segments(lengths, position) == segments(lengths, position - distance)).astype(F32)


def wide(table, width):
    return jnp.concatenate([table] * (width // 128), axis=1)


def column_of(table, head):
    lanes = iota(table.shape, 1)
    return jnp.sum(jnp.where(lanes == head, table, 0.0), axis=1, keepdims=True)


def pair_columns(table, pair):
    first, second = column_of(table, 2 * pair), column_of(table, 2 * pair + 1)
    return jnp.where(iota(table.shape, 1) < 64, first, second)


class Steps:
    def __init__(self, raw, params_s, lengths, first):
        tok = raw.shape[0]
        shifted = raw + params_s[5:6, :128]
        self.slope = jax.nn.sigmoid(shifted)
        self.step = softplus(shifted)
        self.rate = -jnp.exp(params_s[6:7, :128])
        until = (iota((tok, tok), 0) >= iota((tok, tok), 1)).astype(BF16)
        self.total = pick(until, self.step * self.rate, NN)
        position = first + iota((tok, 128), 0)
        seg = segments(lengths, position)
        before = segments(lengths, jnp.full((tok, 128), first - 1, jnp.int32))
        last = segments(lengths, jnp.full((tok, 128), first + tok - 1, jnp.int32))
        self.reading = jnp.exp(self.total) * (seg == before).astype(F32)
        self.fading = jnp.exp(self.total[tok - 1 : tok] - self.total) * (seg == last).astype(F32)
        self.tail = self.fading * self.step


def closed(lengths, first, tok, flipped):
    rows, cols = first + iota((tok, tok), 0), first + iota((tok, tok), 1)
    order = rows <= cols if flipped else rows >= cols
    seg_rows = segments(lengths, first + iota((tok, 1), 0))
    seg_cols = segments(lengths, first + iota((1, tok), 1))
    return jnp.where(order & (seg_rows == seg_cols), 0.0, -1e30)


def convolve(padded, params, lengths, first, conv, act):
    tok, tile = conv.shape[0], 128
    same = [same_before(lengths, first, tok, 3 - k) for k in range(3)]

    @pl.loop(0, conv.shape[1] // tile)
    def _(n):
        cols = pl.ds(pl.multiple_of(n * tile, 128), tile)
        total = params[4:5, cols] + params[3:4, cols] * padded[8 : 8 + tok, cols]
        for k in range(3):
            total = total + params[k : k + 1, cols] * (padded[5 + k : 5 + k + tok, cols] * same[k])
        conv[:, cols] = total
        act[:, cols] = total * jax.nn.sigmoid(total)


def forward_kernel(
    sizes,
    lengths,
    slots_in_hbm,
    gain_hbm,
    taps_x_hbm,
    bias_x_hbm,
    taps_s_hbm,
    bias_s_hbm,
    dt_bias_hbm,
    a_log_hbm,
    d_skip_hbm,
    gate_gain_hbm,
    w_bc_hbm,
    w_dt_hbm,
    x_in,
    c_in,
    w_x,
    w_z,
    w_out,
    params_c_hbm,
    params_s_hbm,
    tokens_out,
    up_out,
    n_pairs_out,
    p_out_hbm,
    pre_x_out,
    pre_s_out,
    raw_out,
    conv_x_out,
    conv_s_out,
    ny_out,
    dz_out,
    dmix_out,
    gain_row_hbm,
    state_out,
    g_out,
    gz_out,
    land_a,
    land_b,
    wx_out,
    ws_out,
    wz_out,
    wo_out,
    slots_in,
    gain,
    taps_x,
    bias_x,
    taps_s,
    bias_s,
    dt_bias,
    a_log,
    d_skip,
    gate_gain,
    w_bc,
    w_dt,
    params_c,
    params_s,
    p_out,
    gain_row,
    wx,
    ws,
    wz,
    wo,
    ws_own,
    x_own,
    c_own,
    x_sort,
    c_sort,
    p_sort,
    p_recv,
    x_recv,
    c_recv,
    tokens,
    n_high,
    n_low,
    turned,
    n_pairs,
    c_pairs,
    pre_x,
    pre_s,
    raw,
    bc_rows,
    tail_x,
    tail_s,
    conv_x,
    conv_s,
    act_x,
    act_s,
    totals,
    step_rows,
    open_,
    scores,
    state,
    state_in,
    mixed,
    gate_pre,
    d_normal,
    ny_both,
    high,
    low,
    left_high,
    left_low,
    sums,
    sums_recv,
    inner_sums,
    inner_recv,
    send,
    recv,
    local,
):
    place = Place(*sizes)
    links = Links(send, recv, local)
    tok, groups = x_own.shape[0], 2 * place.fsdp
    per_pair = tok // groups
    part = x_own.shape[1]
    inner = act_x.shape[1]
    pairs = inner // 128
    heads = d_skip.shape[1]
    share = 2 * N // place.tp
    shard_rows = n_pairs.shape[1]
    chip_rows = 2 * shard_rows
    first = place.c * tok
    lanes = iota((tok, 128), 1)
    part_cols = pl.ds(pl.multiple_of(place.z * part, 128), part)
    load_x = links.move(x_in.at[:, part_cols], x_own)
    first_loads = [links.move(slots_in_hbm, slots_in)]
    load_c = links.move(c_in.at[:, part_cols], c_own)
    first_loads += [
        links.move(gain_hbm, gain),
        links.move(taps_x_hbm, taps_x),
        links.move(bias_x_hbm, bias_x),
        links.move(taps_s_hbm, taps_s),
        links.move(bias_s_hbm, bias_s),
        links.move(dt_bias_hbm, dt_bias),
        links.move(a_log_hbm, a_log),
        links.move(d_skip_hbm, d_skip),
        links.move(gate_gain_hbm, gate_gain),
        links.move(w_bc_hbm, w_bc),
        links.move(w_dt_hbm, w_dt),
    ]
    plane, column = place.plane(), place.column()
    partners = [entry[0] for entry in plane] + [entry[0] for entry in column]
    greet(partners)

    first_loads[0].wait()
    leave, places = leaving(slots_in[...], tok, groups)
    p_sort[...] = jnp.broadcast_to(places[0:groups, None, :], (groups, 8, 128))
    load_x.wait()
    x_sort[...] = pick(leave, x_own[...], TN)
    greeted(partners)
    g_x, g_s, g_z, g_o = [Gather(place, links, shard, whole) for shard, whole in ((w_x, wx), (ws_own, ws), (w_z, wz), (w_out, wo))]

    def rows(group):
        return pl.ds(pl.multiple_of(group * per_pair, 8), per_pair)

    def route(source, target, at):
        mine = at(place.f * 2 + place.c)
        copies = [links.remote(source.at[at(to)], target.at[mine], device) for device, to, _ in plane]
        return copies, links.move(source.at[mine], target.at[mine])

    routes_x = [route(p_sort, p_recv, lambda group: group), route(x_sort, x_recv.at[place.z], rows)]
    g_x.start()

    def share_of(turn):
        return pl.ds(pl.multiple_of(turn * share, 8), share)

    for load in first_loads[1:]:
        load.wait()
    bc_rows[:, 0:shard_rows] = w_bc[...].T
    ws_own[...] = jnp.zeros_like(ws_own)
    ws_own[0:heads, :] = w_dt[...]
    ws_own[heads : heads + share, :] = bc_rows[share_of(place.z), 0:shard_rows]
    g_s.start()
    load_c.wait()
    c_sort[...] = pick(leave, c_own[...], TN)
    routes_c = [route(c_sort, c_recv.at[place.z], rows)]

    params_c[0:4, :] = taps_x[...]
    params_c[4:5, :] = bias_x[...]
    params_c[6:7, :] = gate_gain[...]
    params_c[7:8, :] = jnp.zeros((1, inner), F32)
    for q in range(pairs):
        both = [d_skip[0:1, 2 * q + s : 2 * q + s + 1] for s in range(2)]
        params_c[5:6, q * 128 : (q + 1) * 128] = jnp.where(lanes[0:1] < 64, both[0], both[1])
    params_s[...] = jnp.zeros_like(params_s)
    params_s[0:4, :] = taps_s[...]
    params_s[4:5, :] = bias_s[...]
    params_s[5:6, 0:heads] = dt_bias[...]
    params_s[6:7, 0:heads] = a_log[...]

    def arrive(routes):
        for copies, own in routes:
            own.wait()
            for copy in copies:
                copy.wait_recv()

    arrive(routes_x)
    spread_x = Spread(place, links, x_recv)
    g_x.forward()
    g_s.forward()
    g_z.start()
    spread_x.forward()
    arrive(routes_c)
    g_s.share()
    stores = [links.move(params_c, params_c_hbm), links.move(params_s, params_s_hbm)]
    spread_x.finish()
    p_out[...] = arrived(p_recv[:, 0, :], tok, per_pair)
    stores.append(links.move(p_out, p_out_hbm))
    settle = settling(p_out, tok)
    squares = jnp.zeros((tok, 1), F32)
    for k in range(place.tp):
        value = pick(settle, x_recv[k], TN)
        tokens[k] = value
        squares = squares + jnp.sum(value * value, axis=1, keepdims=True)
    scale = lax.rsqrt(squares / (place.tp * part) + EPSILON)
    own_cols = pl.ds(pl.multiple_of(place.c * tok, 128), tok)
    own_rows = pl.ds(pl.multiple_of(place.c * tok, 128), tok)
    chips_here = part // chip_rows

    def keep_left(k, value):
        for j in range(chips_here):
            piece = value[:, j * chip_rows : (j + 1) * chip_rows]
            n_high[k * chips_here + j], n_low[k * chips_here + j] = split2(piece)
        turned[k * part : (k + 1) * part, :] = value.T

    def exchange_blocks(pairs_ref):
        copies, kept = [], []
        for q in range(place.fsdp):
            there = turned.at[pl.ds(pl.multiple_of((2 * q + 1 - place.c) * shard_rows, 8), shard_rows)]
            here = turned.at[pl.ds(pl.multiple_of((2 * q + place.c) * shard_rows, 8), shard_rows)]
            copies.append(links.remote(there, pairs_ref.at[q, :, own_cols], place.sibling()))
            kept.append(links.move(here, pairs_ref.at[q, :, own_cols]))
        return copies, kept

    for k in range(place.tp):
        keep_left(k, tokens[k] * scale * gain[:, k * part : (k + 1) * part])
    pairs_n, kept_n = exchange_blocks(n_pairs)
    stores.append(links.move(tokens, tokens_out))

    every = list(range(place.fsdp))
    g_s.finish()
    raw[...] = jnp.zeros_like(raw)
    side_rows = ws_own.shape[0]
    total = jnp.zeros((tok, side_rows), F32)
    for block in range(2 * place.fsdp):
        at = slice(block % 2 * shard_rows, (block % 2 + 1) * shard_rows)
        left = (n_high[block // 2, :, at], n_low[block // 2, :, at])
        total = total + dot_split(left, split2(ws[block * side_rows : (block + 1) * side_rows, :]), NT)
    raw[:, 0:side_rows] = total
    bc_turned = raw[...].T
    bc_rows[share_of(place.z), :] = bc_turned[heads : heads + share]
    mine = bc_rows.at[share_of(place.z)]
    spread_bc = [links.remote(mine, mine, device) for device, _, _ in column]
    spread_c = Spread(place, links, c_recv)
    g_x.share()
    g_x.finish()
    keep_wx = links.move(wx, wx_out)
    stores += [links.move(ws, ws_out)]
    project(n_high, n_low, wx, every, pre_x, 512, 8, True)
    halo = [links.remote(pre_x.at[pl.ds(tok, 8)], tail_x, place.sibling())]
    g_z.forward()
    g_o.start()

    raw[...] = jnp.where(lanes < heads, raw[...], 0.0)
    steps = Steps(raw[...], params_s, lengths, first)
    totals[...] = steps.total
    step_rows[0] = steps.total.T
    step_rows[1] = steps.step.T
    open_[...] = closed(lengths, first, tok, False)
    for copy in spread_bc:
        copy.wait_recv()
    pre_s[8 : 8 + tok, :] = bc_rows[...].T
    halo.append(links.remote(pre_s.at[pl.ds(tok, 8)], tail_s, place.sibling()))
    for copy in halo:
        copy.wait_recv()
    second = (place.c > 0).astype(F32)
    pre_x[0:8, :] = tail_x[...] * second
    pre_s[0:8, :] = tail_s[...] * second
    convolve(pre_s, params_s, lengths, first, conv_s, act_s)
    convolve(pre_x, params_c, lengths, first, conv_x, act_x)
    b_parts = split2(act_s[:, :N])
    c_parts = split2(act_s[:, N:])
    scores[...] = dot_split(c_parts, b_parts, NT)
    tail_table, reading_table = steps.tail, steps.reading

    @pl.loop(0, pairs)
    def _(q):
        cols = pl.ds(pl.multiple_of(q * 128, 128), 128)
        faded = act_x[:, cols] * pair_columns(tail_table, q)
        state[cols, :] = dot_split(split2(faded), b_parts, TN)

    pass_state = links.remote(state, state_in, place.sibling())
    spread_c.forward()
    pass_state.wait_recv()

    @pl.loop(0, pairs)
    def _(q):
        cols = pl.ds(pl.multiple_of(q * 128, 128), 128)
        channels = act_x[:, cols]
        entered = state_in[cols, :] * second
        state_in[cols, :] = entered
        out = params_c[5:6, cols] * channels
        out = out + pair_columns(reading_table, q) * dot_split(c_parts, split2(entered), NT)
        for s in range(2):
            head = 2 * q + s
            gaps = column_of(totals[...], head) - step_rows[0, pl.ds(head, 1), :] + open_[...]
            weights = jnp.exp(gaps) * scores[...] * step_rows[1, pl.ds(head, 1), :]
            own = jnp.where((lanes < 64) == (s == 0), channels, 0.0)
            out = out + dot3(weights, own, NN)
        mixed[:, cols] = out

    stores += [
        links.move(pre_x, pre_x_out),
        links.move(pre_s, pre_s_out),
        links.move(raw, raw_out),
        links.move(conv_x, conv_x_out),
        links.move(conv_s, conv_s_out),
        links.move(state_in, state_out),
    ]
    g_z.share()
    g_z.finish()
    stores.append(links.move(wz, wz_out))
    project(n_high, n_low, wz, every, gate_pre, 512, 0, True)

    def over_tiles(body, carry):
        def step(n, carry):
            return body(pl.ds(pl.multiple_of(n * 128, 128), 128), carry)

        return lax.fori_loop(0, pairs, step, carry)

    def gated_at(cols):
        z = gate_pre[:, cols]
        return mixed[:, cols] * (z * jax.nn.sigmoid(z))

    def add_squares(cols, total):
        gated = gated_at(cols)
        return total + gated * gated

    zeros = jnp.zeros((tok, 128), F32)
    square_sum = over_tiles(add_squares, zeros)
    sums[...] = jnp.broadcast_to(jnp.sum(square_sum, axis=1, keepdims=True), (tok, 128)).T[0:8, :]
    copies = [links.remote(sums, sums_recv.at[k], device) for k, (device, _, _) in enumerate(column)]

    spread_c.finish()
    for copy in pairs_n:
        copy.wait_recv()
    links.settle(pairs_n)
    for copy in kept_n:
        copy.wait()
    stores.append(links.move(n_pairs, n_pairs_out))
    for k in range(place.tp):
        upstream = pick(settle, c_recv[k], TN)
        keep_left(k, upstream)

        @pl.when(place.z == k)
        def _():
            x_own[...] = upstream

    pairs_c, kept_c = exchange_blocks(c_pairs)
    stores.append(links.move(x_own, up_out))

    for copy in copies:
        copy.wait_recv()
    total = sums[...]
    for k in range(place.tp - 1):
        total = total + sums_recv[k]
    gscale = lax.rsqrt(down_lanes(total[0:1]) / INNER + EPSILON)

    def normalise(cols, carry):
        ny_both[own_rows, cols] = gated_at(cols) * gscale * params_c[6:7, cols]
        return carry

    over_tiles(normalise, 0)
    g_o.forward()
    give_ny = links.remote(ny_both.at[own_rows], ny_both.at[own_rows], place.sibling())
    keep_ny = links.move(ny_both.at[own_rows], ny_out)

    near = [place.f] + [place.chip(0, d) for d in range(1, place.side)] + [place.chip(d, 0) for d in range(1, place.side)]
    far = [place.chip(e, d) for e in range(1, place.side) for d in range(1, place.side)]
    for copy in kept_c:
        copy.wait()
    for copy in pairs_c:
        copy.wait_recv()
    give_ny.wait_recv()
    halve(ny_both, high, low)
    keep_wx.wait()
    links.settle(g_x.half_a + g_x.half_b + g_x.pair)
    blocks_o = wx.reshape(2, place.fsdp, shard_rows, inner).at[0]
    blocks_z = wx.reshape(2, place.fsdp, shard_rows, inner).at[1]
    for q in range(place.fsdp):
        weight_block(c_pairs.at[q], high, low, left_high, left_low, blocks_o.at[q])
    stores.append(links.move(blocks_o, g_out))
    sum_o = Scatter(place, links, blocks_o, blocks_o, (land_a, land_b))
    sum_o.send_all()
    def keep_rows(chip):
        at = pl.ds(pl.multiple_of(chip * chip_rows, 8), chip_rows)
        stores.append(links.move(wo.at[at], wo_out.at[at]))

    g_o.finish_near()
    for chip in near:
        keep_rows(chip)
    project(n_high, n_low, wo, near, d_normal, 512, 0, True)
    g_o.share()
    g_o.finish()
    for chip in far:
        keep_rows(chip)
    project(n_high, n_low, wo, far, d_normal, 512, 0, False)

    def add_inner(cols, total):
        return total + d_normal[:, cols] * params_c[6:7, cols] * gated_at(cols)

    inner_sum = over_tiles(add_inner, zeros)
    inner_sums[...] = jnp.broadcast_to(jnp.sum(inner_sum, axis=1, keepdims=True), (tok, 128)).T[0:8, :]
    copies = [links.remote(inner_sums, inner_recv.at[k], device) for k, (device, _, _) in enumerate(column)]
    links.settle([give_ny])
    keep_ny.wait()
    for copy in copies:
        copy.wait_recv()
    total = inner_sums[...]
    for k in range(place.tp - 1):
        total = total + inner_recv[k]
    pull = gscale * gscale * gscale * down_lanes(total[0:1]) / INNER

    def shape_all(cols, carry):
        z, y, upward, weight = gate_pre[:, cols], mixed[:, cols], d_normal[:, cols], params_c[6:7, cols]
        gate = jax.nn.sigmoid(z)
        act = z * gate
        gated = y * act
        d_gated = gscale * weight * upward - gated * pull
        d_normal[:, cols] = d_gated * act
        ny_both[own_rows, cols] = d_gated * y * gate * (1.0 + z * (1.0 - gate))
        gain_row[:, cols] = jnp.sum(upward * gated * gscale, axis=0, keepdims=True)
        return carry

    over_tiles(shape_all, 0)
    give_dz = links.remote(ny_both.at[own_rows], ny_both.at[own_rows], place.sibling())
    stores += [links.move(ny_both.at[own_rows], dz_out), links.move(d_normal, dmix_out), links.move(gain_row, gain_row_hbm)]
    give_dz.wait_recv()
    halve(ny_both, high, low)
    for q in range(place.fsdp):
        weight_block(n_pairs.at[q], high, low, left_high, left_low, blocks_z.at[q])
        stores.append(links.move(blocks_z.at[q], gz_out.at[q]))
    sum_o.land()
    for store in stores:
        store.wait()
    links.finish()


def backward_kernel(
    sizes,
    heads,
    lengths,
    slots_in_hbm,
    p_recv_hbm,
    gain_hbm,
    params_c_hbm,
    params_s_hbm,
    gain_row_hbm,
    tokens_in,
    up_in,
    n_pairs_in,
    pre_x_in,
    pre_s_in,
    raw_in,
    conv_x_in,
    conv_s_in,
    ny_in,
    dz_in,
    dmix_in,
    state_in_hbm,
    g_in,
    gz_in,
    land_a_in,
    land_b_in,
    wx_in,
    ws_in,
    wz_in,
    wo_in,
    result,
    grad_input,
    grad_z,
    grad_x,
    grad_bc_hbm,
    grad_dt_hbm,
    grad_out,
    small_out_hbm,
    gain_out_hbm,
    slots_in,
    p_recv,
    gain,
    params_c,
    params_s,
    gain_row,
    grad_bc,
    grad_dt,
    small_out,
    gain_out,
    tokens,
    n_pairs,
    pre_x,
    pre_s,
    raw,
    conv_x,
    conv_s,
    state_in,
    dx_both,
    ds_both,
    high,
    low,
    left_high,
    left_low,
    blocks_o,
    blocks_z,
    blocks_s,
    o1a, o1b, o2a, o2b,
    z1a, z1b, z2a, z2b,
    x1a, x1b, x2a, x2b,
    s1a, s1b, s2a, s2b,
    blocks_x,
    stream,
    ws,
    d_bc,
    ds_high,
    ds_low,
    bc_rows,
    bc_recv,
    bc_grad,
    part_r,
    part_t,
    recv_r,
    recv_t,
    row_sums,
    row_recv,
    home_r,
    home_t,
    back_r,
    back_t,
    d_state,
    d_state_recv,
    d_b,
    d_c,
    pad_x,
    pad_s,
    head_x,
    head_s,
    open_,
    scores,
    d_scores,
    totals,
    steps_col,
    total_rows,
    grad_total,
    grad_step,
    grad_tail,
    grad_rows,
    skip_row,
    small,
    small_recv,
    small_z,
    gain_own,
    gain_recv,
    send,
    recv,
    local,
):
    place = Place(*sizes)
    links = Links(send, recv, local)
    tok, groups = tokens.shape[1], 2 * place.fsdp
    per_pair = tok // groups
    part = tokens.shape[2]
    inner = conv_x.shape[1]
    pairs = inner // 128
    first = place.c * tok
    own_rows = pl.ds(pl.multiple_of(place.c * tok, 128), tok)
    plane, column = place.plane(), place.column()

    partners = [entry[0] for entry in plane] + [entry[0] for entry in column]
    greet(partners)
    shares_r, shares_t = Shares(place, links, part_r, recv_r), Shares(place, links, part_t, recv_t)
    turns = shares_r.turns
    schedule = [(weight, turn) for weight in (wo_in, wx_in, wz_in) for turn in turns]
    fetched = []

    def fetch():
        k = len(fetched)
        if k < len(schedule):
            weight, turn = schedule[k]
            src = weight.at[pl.ds(pl.multiple_of(turn * part, 8), part)]
            fetched.append(links.move(src, stream.at[k % 2]))

    def weight_slice(k):
        fetched[k].wait()
        return stream.at[k % 2]

    greeted(partners)
    sum_o = Scatter(place, links, g_in, blocks_o, (o1a, o1b), (o2a, o2b))
    sum_z = Scatter(place, links, gz_in, blocks_z, (z1a, z1b), (z2a, z2b))
    sum_z.send_all()
    loads = {}
    loads["ny"] = links.move(ny_in, dx_both.at[own_rows])
    fetch()
    fetch()
    few = [
        links.move(slots_in_hbm, slots_in),
        links.move(p_recv_hbm, p_recv),
        links.move(gain_hbm, gain),
        links.move(params_c_hbm, params_c),
        links.move(params_s_hbm, params_s),
        links.move(gain_row_hbm, gain_row),
    ]
    for name, src, dst in (
        ("g", g_in, blocks_o),
        ("land_a", land_a_in, o1a),
        ("land_b", land_b_in, o1b),
        ("raw", raw_in, raw),
        ("conv_s", conv_s_in, conv_s),
        ("dmix", dmix_in, pad_x.at[pl.ds(0, tok)]),
        ("state", state_in_hbm, state_in),
        ("conv_x", conv_x_in, conv_x),
        ("n_pairs", n_pairs_in, n_pairs),
        ("gz", gz_in, blocks_z),
        ("pre_x", pre_x_in, pre_x),
        ("pre_s", pre_s_in, pre_s),
        ("tokens", tokens_in, tokens),
        ("up", up_in, home_t),
        ("ws", ws_in, ws),
    ):
        loads[name] = links.move(src, dst)

    loads["ny"].wait()
    halve(dx_both.at[own_rows], high.at[own_rows], low.at[own_rows])

    def product(k, turn, fresh, out):
        ref = weight_slice(k)
        times_rows(high.at[own_rows], low.at[own_rows], ref, out, fresh)
        fetch()

    for k, turn in enumerate(turns):
        product(k, turn, True, part_r.at[turn])
        shares_r.send(k)
        if k == min(1, place.tp - 1):
            for name in ("g", "land_a", "land_b"):
                loads[name].wait()
            sum_o.pass_on()

    for load in few:
        load.wait()
    loads["raw"].wait()
    loads["conv_s"].wait()
    steps = Steps(raw[...], params_s, lengths, first)
    totals[...] = steps.total
    steps_col[...] = steps.step
    total_rows[...] = steps.total.T
    open_[...] = closed(lengths, first, tok, True)
    act_s = conv_s[...] * jax.nn.sigmoid(conv_s[...])
    b_parts, c_parts = split2(act_s[:, :N]), split2(act_s[:, N:])
    scores[...] = dot_split(b_parts, c_parts, NT)
    reading_table, tail_table = steps.reading, steps.tail
    grad_total[...] = jnp.zeros((tok, 128), F32)
    grad_step[...] = jnp.zeros((tok, 128), F32)
    grad_tail[...] = jnp.zeros((tok, 128), F32)
    d_c[...] = jnp.zeros((tok, N), F32)
    d_b[...] = jnp.zeros((tok, N), F32)
    d_scores[...] = jnp.zeros((tok, tok), F32)
    grad_rows[...] = jnp.zeros((128, tok), F32)
    lanes = iota((tok, 128), 1)

    def put(ref, head, value):
        ref[...] = ref[...] + jnp.where(lanes == head, value, 0.0)

    def by_head(value, s):
        return jnp.sum(jnp.where((lanes < 64) == (s == 0), value, 0.0), axis=1, keepdims=True)

    loads["dmix"].wait()
    loads["state"].wait()

    @pl.loop(0, pairs)
    def _(q):
        cols = pl.ds(pl.multiple_of(q * 128, 128), 128)
        upward = pad_x[0:tok, cols] * pair_columns(reading_table, q)
        parts = split2(upward)
        entered = split2(state_in[cols, :])
        d_c[...] = d_c[...] + dot_split(parts, entered, NN)
        d_state[cols, :] = dot_split(parts, c_parts, TN)
        read = upward * dot_split(c_parts, entered, NT)
        for s in range(2):
            put(grad_total, 2 * q + s, by_head(read, s))

    give_state = links.remote(d_state, d_state_recv, place.sibling())

    shares_r.forward()

    loads["conv_x"].wait()
    give_state.wait_recv()
    first_half = (place.c == 0).astype(F32)

    @pl.loop(0, pairs)
    def _(q):
        cols = pl.ds(pl.multiple_of(q * 128, 128), 128)
        conv = conv_x[:, cols]
        gate = jax.nn.sigmoid(conv)
        channels = conv * gate
        upward = pad_x[0:tok, cols]
        ended = split2(d_state_recv[cols, :] * first_half)
        tail = pair_columns(tail_table, q)
        from_end = dot_split(b_parts, ended, NT)
        d_b[...] = d_b[...] + dot_split(split2(channels * tail), ended, NN)
        into = params_c[5:6, cols] * upward + tail * from_end
        skip_row[:, cols] = jnp.sum(upward * channels, axis=0, keepdims=True)
        end_part = channels * from_end
        x_parts = split2(channels)
        for s in range(2):
            head = 2 * q + s
            put(grad_tail, head, by_head(end_part, s))
            step_col = column_of(steps_col[...], head)
            gaps = total_rows[pl.ds(head, 1), :] - column_of(totals[...], head) + open_[...]
            decay = jnp.exp(gaps)
            up_parts = split2(jnp.where((lanes < 64) == (s == 0), upward, 0.0))
            reach = dot_split(x_parts, up_parts, NT) * decay
            d_scores[...] = d_scores[...] + reach * step_col
            reach = reach * scores[...]
            put(grad_step, head, jnp.sum(reach, axis=1, keepdims=True))
            grad_rows[pl.ds(head, 1), :] = jnp.sum(reach * step_col, axis=0, keepdims=True)
            into = into + dot3(decay * scores[...] * step_col, jnp.where((lanes < 64) == (s == 0), upward, 0.0), NN)
        pad_x[0:tok, cols] = into * gate * (1.0 + conv * (1.0 - gate))

    loads["dz"] = links.move(dz_in, conv_x)

    score_parts = split2(d_scores[...])
    slope_s = silu_slope(conv_s[...])
    pad_s[0:tok, 0:N] = (d_b[...] + dot_split(score_parts, c_parts, NN)) * slope_s[:, :N]
    pad_s[0:tok, N : 2 * N] = (d_c[...] + dot_split(score_parts, b_parts, TN)) * slope_s[:, N:]
    halo = [
        links.remote(pad_x.at[pl.ds(0, 8)], head_x, place.sibling()),
        links.remote(pad_s.at[pl.ds(0, 8)], head_s, place.sibling()),
    ]
    step_now = steps_col[...]
    faded = grad_tail[...] * tail_table
    d_total = grad_total[...] + grad_rows[...].T - grad_step[...] * step_now - faded
    at_end = iota((tok, 128), 0) == tok - 1
    d_total = d_total + jnp.where(at_end, jnp.sum(faded, axis=0, keepdims=True), 0.0)
    onward = (iota((tok, tok), 1) >= iota((tok, tok), 0)).astype(BF16)
    d_log = pick(onward, d_total, NN)
    d_step = grad_step[...] + grad_tail[...] * steps.fading + d_log * steps.rate
    d_raw = jnp.where(lanes < heads, d_step * steps.slope, 0.0)
    small[...] = jnp.zeros_like(small)
    small[5:6, inner : inner + 128] = jnp.sum(d_raw, axis=0, keepdims=True)
    small[6:7, inner : inner + 128] = jnp.sum(d_log * step_now, axis=0, keepdims=True) * steps.rate
    head_of = (iota((inner, 128), 0) // (inner // heads) == iota((inner, 128), 1)).astype(BF16)
    skips = jnp.broadcast_to(skip_row[...], (8, inner))
    small[7:8, inner : inner + 128] = sum(dot1(piece, head_of, NN) for piece in split3(skips))[0:1]
    small[5:6, 0:inner] = gain_row[...]

    loads["pre_x"].wait()
    loads["pre_s"].wait()
    for copy in halo:
        copy.wait_recv()
    pad_x[tok : tok + 8, :] = head_x[...] * first_half
    pad_s[tok : tok + 8, :] = head_s[...] * first_half
    same = [same_before(lengths, first, tok, 3 - k) for k in range(3)]
    same_next = [same_before(lengths, first + 3 - k, tok, 3 - k) for k in range(3)]

    def back(padded, pre, params, out, start, n):
        cols = pl.ds(pl.multiple_of(n * 128, 128), 128)
        small_cols = pl.ds(pl.multiple_of(start + n * 128, 128), 128)
        here = padded[0:tok, cols]
        total = params[3:4, cols] * here
        small[3:4, small_cols] = jnp.sum(here * pre[8 : 8 + tok, cols], axis=0, keepdims=True)
        small[4:5, small_cols] = jnp.sum(here, axis=0, keepdims=True)
        for k in range(3):
            total = total + params[k : k + 1, cols] * (padded[3 - k : 3 - k + tok, cols] * same_next[k])
            value = here * (pre[5 + k : 5 + k + tok, cols] * same[k])
            small[k : k + 1, small_cols] = jnp.sum(value, axis=0, keepdims=True)
        out[:, cols] = total

    @pl.loop(0, pairs)
    def _(n):
        back(pad_x, pre_x, params_c, dx_both.at[own_rows], 0, n)

    give_dx = links.remote(dx_both.at[own_rows], dx_both.at[own_rows], place.sibling())

    @pl.loop(0, 2 * N // 128)
    def _(n):
        back(pad_s, pre_s, params_s, d_bc, inner, n)

    share = 2 * N // place.tp
    bc_rows[...] = d_bc[...].T

    def share_of(turn):
        return pl.ds(pl.multiple_of(turn * share, 8), share)

    give_bc = [
        links.remote(bc_rows.at[share_of(to_z)], bc_recv.at[k], device) for k, (device, to_z, _) in enumerate(column)
    ]

    hops_of = [
        [place.sibling()],
        [place.at(0, d) for d in range(1, place.side)],
        [place.at(d, 0) for d in range(1, place.side)],
    ]
    small_copies = []

    def hop_small(step):
        slot = sum(len(devices) for devices in hops_of[:step])
        for device in hops_of[step]:
            small_copies.append(links.remote(small, small_recv.at[slot], device))
            slot += 1

    def land_small(step):
        slot = sum(len(devices) for devices in hops_of[:step])
        total = small[...]
        links.settle(small_copies[slot:])
        for copy in small_copies[slot:]:
            copy.wait_recv()
            total = total + small_recv[slot]
            slot += 1
        small[...] = total

    hop_small(0)
    give_dx.wait_recv()
    loads["n_pairs"].wait()
    sum_x = Scatter(place, links, blocks_x, blocks_x, (x1a, x1b), (x2a, x2b))
    halve(dx_both, high, low)
    for hop in sum_x.order():
        block = place.chip(*hop)
        weight_block(n_pairs.at[block], high, low, left_high, left_low, blocks_x.at[block])
        sum_x.send(*hop)
    loads["gz"].wait()
    sum_z.pass_on()
    land_small(0)
    hop_small(1)

    for k, turn in enumerate(turns):
        product(place.tp + k, turn, True, part_t.at[turn])
    loads["dz"].wait()
    halve(conv_x, high.at[own_rows], low.at[own_rows])
    loads["tokens"].wait()
    loads["ws"].wait()
    for copy in give_bc:
        copy.wait_recv()
    summed = bc_rows[share_of(place.z), :]
    for k in range(place.tp - 1):
        summed = summed + bc_recv[k]
    own_cols = pl.ds(pl.multiple_of(place.c * tok, 128), tok)
    ds_both[0:heads, own_cols] = d_raw.T[0:heads, :]
    ds_both[heads : heads + share, own_cols] = summed
    side_rows = ds_both.shape[0]
    if side_rows > heads + share:
        ds_both[heads + share :, own_cols] = jnp.zeros((side_rows - heads - share, tok), F32)
    give_ds = links.remote(ds_both.at[:, own_cols], ds_both.at[:, own_cols], place.sibling())
    ds_high[...], ds_low[...] = split2(ds_both[:, own_cols].T)
    give_ds.wait_recv()
    sum_s = Scatter(place, links, blocks_s, blocks_s, (s1a, s1b), (s2a, s2b))
    ds_parts = split2(ds_both[...])
    for hop in sum_s.order():
        block = place.chip(*hop)
        sum_s.blocks[block] = dot_split(ds_parts, split2(n_pairs[block]), NT)
        sum_s.send(*hop)
    row_sum = jnp.zeros((tok, 1), F32)
    squares = jnp.zeros((tok, 1), F32)
    for k, turn in enumerate(turns):
        out = part_t.at[turn]
        product(2 * place.tp + k, turn, False, out)
        shard_rows = ws.shape[1]
        for j in range(part // shard_rows):
            at = pl.ds(pl.multiple_of((turn * (part // shard_rows) + j) * side_rows, 8), side_rows)
            cols = slice(j * shard_rows, (j + 1) * shard_rows)
            out[:, cols] = out[:, cols] + dot_split((ds_high[...], ds_low[...]), split2(ws[at, :]), NN)
        shares_t.send(k)
        value = tokens[turn]
        row_sum = row_sum + jnp.sum(out[...] * gain[turn] * value, axis=1, keepdims=True)
        squares = squares + jnp.sum(value * value, axis=1, keepdims=True)
    row_sums[...] = jnp.where(lanes == 0, row_sum, 0.0).T[0:8, :]
    give_rows = [links.remote(row_sums, row_recv.at[k], device) for k, (device, _, _) in enumerate(column)]

    land_small(1)
    hop_small(2)
    stores = [links.move(sum_o.finish(), grad_out)]

    settle = settling(p_recv, tok)

    def rows(group):
        return pl.ds(pl.multiple_of(group * per_pair, 8), per_pair)

    def homeward(value, home, back_ref):
        home[...] = pick(settle, value, NN)
        at = rows(place.f * 2 + place.c)
        copies = [links.remote(home.at[rows(to)], back_ref.at[at], device) for device, to, _ in plane]
        return copies + [links.move(home.at[at], back_ref.at[at])]

    shares_r.finish()
    value = tokens[place.z] + part_r[place.z]
    way_r = homeward(value, home_r, back_r)

    shares_t.forward()
    sum_s.pass_on()
    sum_x.pass_on()
    stores.append(links.move(sum_z.finish(), grad_z))

    land_small(2)
    bc_cols = pl.ds(inner, 2 * N)
    give_small = [links.remote(small.at[:, bc_cols], small_z.at[j], device) for j, (device, _, _) in enumerate(column)]
    last = sum_s.finish()
    give_grad = [
        links.remote(last.at[pl.ds(heads, share)], bc_grad.at[share_of(place.z)], device) for device, _, _ in column
    ]
    bc_grad[share_of(place.z), :] = last[heads : heads + share, :]
    grad_dt[...] = last[0:heads, :]
    stores.append(links.move(grad_dt, grad_dt_hbm))
    for copy in give_rows:
        copy.wait_recv()
    total = row_sums[...]
    for k in range(place.tp - 1):
        total = total + row_recv[k]
    shares_t.finish()
    d_normed = part_t[place.z]
    row_sum = jnp.concatenate([total, jnp.zeros((120, tok), F32)], axis=0).T[:, 0:1]
    width = place.tp * part
    scale = lax.rsqrt(squares / width + EPSILON)
    scaled = tokens[place.z] * scale
    gain_own[...] = jnp.sum(d_normed * scaled, axis=0, keepdims=True)
    give_gain = [links.remote(gain_own, gain_recv.at[j], device) for j, (device, _, _) in enumerate(plane)]
    loads["up"].wait()
    value = home_t[...] + scale * gain[place.z] * d_normed - scaled * (scale * scale * row_sum / width)
    way_t = homeward(value, home_t, back_t)

    stores.append(links.move(sum_x.finish(), grad_x))
    leave, _ = leaving(slots_in[...], tok, groups)
    total = gain_own[...]
    for j, copy in enumerate(give_gain):
        copy.wait_recv()
        total = total + gain_recv[j]
    gain_out[...] = total
    stores.append(links.move(gain_out, gain_out_hbm))
    for copy in give_small:
        copy.wait_recv()
    small_out[...] = small[...]
    over_tp = small[0:5, inner : inner + 2 * N]
    for k in range(place.tp - 1):
        over_tp = over_tp + small_z[k, 0:5, :]
    small_out[0:5, inner : inner + 2 * N] = over_tp
    stores.append(links.move(small_out, small_out_hbm))
    for copy in give_grad:
        copy.wait_recv()
    grad_bc[...] = bc_grad[...].T
    stores.append(links.move(grad_bc, grad_bc_hbm))
    for way, home, back_ref, out in ((way_r, home_r, back_r, result), (way_t, home_t, back_t, grad_input)):
        for copy in way[:-1]:
            copy.wait_recv()
        way[-1].wait()
        links.settle(way[:-1])
        home[...] = pick(leave, back_ref[...], NN)
        stores.append(links.move(home, out))
    for store in stores:
        store.wait()
    links.finish()


ANYWHERE = pl.BlockSpec(memory_space=pl.ANY)
INSIDE = pl.BlockSpec(memory_space=pltpu.VMEM)
SCALARS = pl.BlockSpec(memory_space=pltpu.SMEM)


def shape(*dims):
    return jax.ShapeDtypeStruct(dims, F32)


def floats(*dims):
    return pltpu.VMEM(dims, F32)


def halves(*dims):
    return pltpu.VMEM(dims, BF16)


def side_height(heads, tp):
    return -(-(heads + 2 * N // tp) // 16) * 16


def forward_call(sizes, operands, heads):
    fsdp, _, tp = sizes
    inputs, w_x = operands[13], operands[15]
    tok, width = inputs.shape
    shard, inner = w_x.shape
    depth = shard * 2 * fsdp
    part = width // tp
    side = side_height(heads, tp)
    copies = 4 * gather_copies(math.isqrt(fsdp)) + 3 * (2 * fsdp - 1) + 8 * tp + 4 * fsdp + 8
    grid = math.isqrt(fsdp)
    landing = (grid - 1, grid, shard // 2, inner)
    outs = [
        (shape(8, inner), ANYWHERE),
        (shape(8, 2 * N), ANYWHERE),
        (shape(tp, tok, part), ANYWHERE),
        (shape(tok, part), ANYWHERE),
        (shape(fsdp, shard, 2 * tok), ANYWHERE),
        (shape(tok, 128), ANYWHERE),
        (shape(8 + tok, inner), ANYWHERE),
        (shape(8 + tok, 2 * N), ANYWHERE),
        (shape(tok, 128), ANYWHERE),
        (shape(tok, inner), ANYWHERE),
        (shape(tok, 2 * N), ANYWHERE),
        (shape(tok, inner), ANYWHERE),
        (shape(tok, inner), ANYWHERE),
        (shape(tok, inner), ANYWHERE),
        (shape(1, inner), ANYWHERE),
        (shape(inner, N), ANYWHERE),
        (shape(fsdp, shard, inner), ANYWHERE),
        (shape(fsdp, shard, inner), ANYWHERE),
        (shape(*landing), ANYWHERE),
        (shape(*landing), ANYWHERE),
        (shape(depth, inner), ANYWHERE),
        (shape(2 * fsdp * side, shard), ANYWHERE),
        (shape(depth, inner), ANYWHERE),
        (shape(depth, inner), ANYWHERE),
    ]
    return pl.pallas_call(
        functools.partial(forward_kernel, sizes),
        out_shape=tuple(out for out, _ in outs),
        in_specs=[SCALARS] + [ANYWHERE] * 17,
        out_specs=tuple(spec for _, spec in outs),
        scratch_shapes=[
            pltpu.VMEM((1, tok), jnp.int32),
            *[floats(*operand.shape) for operand in operands[2:13]],
            floats(8, inner),
            floats(8, 2 * N),
            floats(tok, 128),
            floats(1, inner),
            floats(depth, inner),
            floats(2 * fsdp * side, shard),
            floats(depth, inner),
            floats(depth, inner),
            floats(side, shard),
            floats(tok, part),
            floats(tok, part),
            floats(tok, part),
            floats(tok, part),
            floats(2 * fsdp, 8, 128),
            floats(2 * fsdp, 8, 128),
            floats(tp, tok, part),
            floats(tp, tok, part),
            floats(tp, tok, part),
            halves(fsdp, tok, 2 * shard),
            halves(fsdp, tok, 2 * shard),
            floats(width, tok),
            floats(fsdp, shard, 2 * tok),
            floats(fsdp, shard, 2 * tok),
            floats(8 + tok, inner),
            floats(8 + tok, 2 * N),
            floats(tok, 128),
            floats(2 * N, max(tok, shard)),
            floats(8, inner),
            floats(8, 2 * N),
            floats(tok, inner),
            floats(tok, 2 * N),
            floats(tok, inner),
            floats(tok, 2 * N),
            floats(tok, 128),
            floats(2, 128, tok),
            floats(tok, tok),
            floats(tok, tok),
            floats(inner, N),
            floats(inner, N),
            floats(tok, inner),
            floats(tok, inner),
            floats(tok, inner),
            floats(2 * tok, inner),
            halves(2 * tok, inner),
            halves(2 * tok, inner),
            halves(shard, 2 * tok),
            halves(shard, 2 * tok),
            floats(8, tok),
            floats(tp - 1, 8, tok),
            floats(8, tok),
            floats(tp - 1, 8, tok),
            pltpu.SemaphoreType.DMA((copies,)),
            pltpu.SemaphoreType.DMA((copies,)),
            pltpu.SemaphoreType.DMA((64 + 4 * fsdp,)),
        ],
        compiler_params=pltpu.CompilerParams(collective_id=0, has_side_effects=True, vmem_limit_bytes=VMEM_LIMIT),
        name="forward",
    )(*operands)


def backward_call(sizes, heads, operands, tok, width, shard, inner):
    fsdp, _, tp = sizes
    grid = math.isqrt(fsdp)
    part = width // tp
    share = 2 * N // tp
    side = side_height(heads, tp)
    hops = grid - 1
    copies = 4 + 4 * (2 * hops * grid + 2 * hops) + 9 * tp + 3 * (2 * fsdp) + 2 * hops + 4

    def landing(rows, columns):
        return [
            floats(hops, grid, rows // 2, columns),
            floats(hops, grid, rows // 2, columns),
            floats(hops, rows // 2, columns),
            floats(hops, rows // 2, columns),
        ]

    return pl.pallas_call(
        functools.partial(backward_kernel, sizes, heads),
        out_shape=(
            shape(tok, part),
            shape(tok, part),
            shape(shard, inner),
            shape(shard, inner),
            shape(shard, 2 * N),
            shape(heads, shard),
            shape(shard, inner),
            shape(8, inner + 2 * N),
            shape(1, part),
        ),
        in_specs=[SCALARS] + [ANYWHERE] * 26,
        out_specs=(ANYWHERE,) * 9,
        scratch_shapes=[
            pltpu.VMEM((1, tok), jnp.int32),
            *[floats(*operand.shape) for operand in operands[2:7]],
            floats(shard, 2 * N),
            floats(heads, shard),
            floats(8, inner + 2 * N),
            floats(1, part),
            floats(tp, tok, part),
            floats(fsdp, shard, 2 * tok),
            floats(8 + tok, inner),
            floats(8 + tok, 2 * N),
            floats(tok, 128),
            floats(tok, inner),
            floats(tok, 2 * N),
            floats(inner, N),
            floats(2 * tok, inner),
            floats(side, 2 * tok),
            halves(2 * tok, inner),
            halves(2 * tok, inner),
            halves(shard, 2 * tok),
            halves(shard, 2 * tok),
            floats(fsdp, shard, inner),
            floats(fsdp, shard, inner),
            floats(fsdp, side, shard),
            *landing(shard, inner),
            *landing(shard, inner),
            *landing(shard, inner),
            *landing(side, shard),
            floats(fsdp, shard, inner),
            floats(2, part, inner),
            floats(2 * fsdp * side, shard),
            floats(tok, 2 * N),
            halves(tok, side),
            halves(tok, side),
            floats(2 * N, tok),
            floats(tp - 1, share, tok),
            floats(2 * N, shard),
            floats(tp, tok, part),
            floats(tp, tok, part),
            floats(max(4, tp - 1), tok, part),
            floats(max(4, tp - 1), tok, part),
            floats(8, tok),
            floats(tp - 1, 8, tok),
            floats(tok, part),
            floats(tok, part),
            floats(tok, part),
            floats(tok, part),
            floats(inner, N),
            floats(inner, N),
            floats(tok, N),
            floats(tok, N),
            floats(8 + tok, inner),
            floats(8 + tok, 2 * N),
            floats(8, inner),
            floats(8, 2 * N),
            floats(tok, tok),
            floats(tok, tok),
            floats(tok, tok),
            floats(tok, 128),
            floats(tok, 128),
            floats(128, tok),
            floats(tok, 128),
            floats(tok, 128),
            floats(tok, 128),
            floats(128, tok),
            floats(1, inner),
            floats(8, inner + 2 * N),
            floats(1 + 2 * hops, 8, inner + 2 * N),
            floats(tp - 1, 8, 2 * N),
            floats(1, part),
            floats(2 * fsdp - 1, 1, part),
            pltpu.SemaphoreType.DMA((copies,)),
            pltpu.SemaphoreType.DMA((copies,)),
            pltpu.SemaphoreType.DMA((40 + 3 * tp,)),
        ],
        compiler_params=pltpu.CompilerParams(collective_id=1, has_side_effects=True, vmem_limit_bytes=VMEM_LIMIT),
        name="backward",
    )(*operands)


def last_kernel(heads, small, gain, dt, *refs):
    large, outs, held, sems = refs[:6], refs[6:22], refs[22:28], refs[28]
    loads, stores = [], []
    for k, (src, hold, dst) in enumerate(zip(large, held, outs)):
        loads.append(pltpu.make_async_copy(src, hold, sems.at[0, k]))
        stores.append(pltpu.make_async_copy(hold, dst, sems.at[1, k]))
    for load in loads:
        load.start()
    for load, store in zip(loads, stores):
        load.wait()
        store.start()
    grad_dt, taps_x, bias_x, taps_s, bias_s, dt_bias, a_log, d_skip, gate_gain, gain_in = outs[6:]
    inner = taps_x.shape[1]
    grad_dt[...] = dt[...]
    taps_x[...] = small[0:4, 0:inner]
    bias_x[...] = small[4:5, 0:inner]
    taps_s[...] = small[0:4, inner : inner + 2 * N]
    bias_s[...] = small[4:5, inner : inner + 2 * N]
    dt_bias[...] = small[5:6, inner : inner + heads]
    a_log[...] = small[6:7, inner : inner + heads]
    d_skip[...] = small[7:8, inner : inner + heads]
    gate_gain[...] = small[5:6, 0:inner]
    gain_in[...] = gain[...]
    for store in stores:
        store.wait()


def last_call(heads, small, gain, dt, *large):
    inner, part = small.shape[1] - 2 * N, gain.shape[1]
    few = [
        dt.shape,
        (4, inner),
        (1, inner),
        (4, 2 * N),
        (1, 2 * N),
        (1, heads),
        (1, heads),
        (1, heads),
        (1, inner),
        (1, part),
    ]
    return pl.pallas_call(
        functools.partial(last_kernel, heads),
        out_shape=tuple([shape(*value.shape) for value in large] + [shape(*dims) for dims in few]),
        in_specs=[INSIDE] * 3 + [ANYWHERE] * 6,
        out_specs=tuple([ANYWHERE] * 6 + [INSIDE] * len(few)),
        scratch_shapes=[floats(*value.shape) for value in large] + [pltpu.SemaphoreType.DMA((2, 6))],
        compiler_params=pltpu.CompilerParams(vmem_limit_bytes=VMEM_LIMIT),
        name="results",
    )(small, gain, dt, *large)


def shards(
    inputs,
    cotangent,
    seq_lengths,
    slots,
    gain_in,
    w_z,
    w_x,
    w_dt,
    w_bc,
    w_out,
    conv_x,
    conv_x_bias,
    conv_bc,
    conv_bc_bias,
    dt_bias,
    a_log,
    d_skip,
    gate_gain,
):
    sizes = (lax.axis_size("fsdp"), lax.axis_size("ctx"), lax.axis_size("tp"))
    tok, width = inputs.shape
    shard, inner = w_x.shape
    heads = w_dt.shape[1]
    tp = sizes[2]
    operands = (
        seq_lengths,
        slots[None],
        gain_in[None],
        conv_x,
        conv_x_bias[None],
        conv_bc,
        conv_bc_bias[None],
        dt_bias[None],
        a_log[None],
        d_skip[None],
        gate_gain[None],
        w_bc,
        w_dt.T,
        inputs,
        cotangent,
        w_x,
        w_z,
        w_out,
    )
    params_c, params_s, tokens, up, n_pairs, p_recv, *kept = forward_call(sizes, operands, heads)
    pre_x, pre_s, raw, conv_x_kept, conv_s_kept, normal_y, d_gate, d_mixed, gain_row, *rest = kept
    operands = (
        seq_lengths,
        slots[None],
        p_recv,
        gain_in.reshape(tp, 1, width // tp),
        params_c,
        params_s,
        gain_row,
        tokens,
        up,
        n_pairs,
        pre_x,
        pre_s,
        raw,
        conv_x_kept,
        conv_s_kept,
        normal_y,
        d_gate,
        d_mixed,
        *rest,
    )
    result, grad_input, grad_z, grad_x, grad_bc, grad_dt, grad_out, small, gain = backward_call(
        sizes, heads, operands, tok, width, shard, inner
    )
    outs = last_call(heads, small, gain, grad_dt, result, grad_input, grad_z, grad_x, grad_out, grad_bc)
    result, grad_input, grad_z, grad_x, grad_out, grad_bc, grad_dt, taps_x, bias_x, taps_s, bias_s, *few = outs
    return (
        result,
        grad_input,
        grad_z,
        grad_x,
        grad_dt.T,
        grad_bc,
        grad_out,
        taps_x,
        bias_x[0],
        taps_s,
        bias_s[0],
        *[value[0] for value in few],
    )


def solution(mesh):
    return jax.shard_map(
        shards,
        mesh=mesh,
        in_specs=(
            P(("fsdp", "ctx"), None),
            P(("fsdp", "ctx"), None),
            P("fsdp", None),
            P(("fsdp", "ctx")),
            P(),
            P(("fsdp", "ctx"), "tp"),
            P(("fsdp", "ctx"), "tp"),
            P(("fsdp", "ctx"), "tp"),
            P(("fsdp", "ctx"), None),
            P(("fsdp", "ctx"), "tp"),
            P(None, "tp"),
            P("tp"),
            P(),
            P(),
            P("tp"),
            P("tp"),
            P("tp"),
            P("tp"),
        ),
        out_specs=(
            P(("fsdp", "ctx"), "tp"),
            P(("fsdp", "ctx"), "tp"),
            P(("fsdp", "ctx"), "tp"),
            P(("fsdp", "ctx"), "tp"),
            P(("fsdp", "ctx"), "tp"),
            P(("fsdp", "ctx"), None),
            P(("fsdp", "ctx"), "tp"),
            P(None, "tp"),
            P("tp"),
            P(),
            P(),
            P("tp"),
            P("tp"),
            P("tp"),
            P("tp"),
            P("tp"),
        ),
        check_vma=False,
    )
```
